32 devices in a mesh: dp: 2 (over y), tm: 4 (over x, core), height: 4 (over z).
Axes of the slice: x: 2, y: 2, z: 4, core: 2. Of those that a mesh axis runs over, the one named last changes fastest.
Arguments:
- low_frames: bfloat16 [2, 16, 16, 32, 256], P('dp', 'tm', 'height'), may hold values from -6 to 6
- spatial_weight: bfloat16 [3, 3, 256, 256], replicated, may hold values from -0.125 to 0.125
- temporal_weight: bfloat16 [3, 256, 256], replicated, may hold values from -0.21875 to 0.21875
- cotangent: bfloat16 [2, 16, 32, 64, 256], P('dp', 'tm', 'height'), may hold values from -6 to 6
Outputs:
- section_out: bfloat16 [2, 16, 32, 64, 256], P('dp', 'tm', 'height')
- input_grad: bfloat16 [2, 16, 16, 32, 256], P('dp', 'tm', 'height')
- spatial_grad: float32 [3, 3, 256, 256], replicated
- temporal_grad: float32 [3, 256, 256], replicated
The draws below stay inside these ranges and needn't reach their ends.
All inputs are finite; a program needn't handle non-finite values.
Results may differ from the reference program's by a relative error of at most 0.0033.
Values may be sent and summed in bfloat16 or wider, within the bound.
No kernel may reach another device: no remote copies, remote signals or barrier semaphores. Data moves between devices by JAX's collectives and lax.ppermute only.
A program may use at most 64 MiB of HBM per device.

```python
import jax
import jax.numpy as jnp
from jax import lax

C = 256
WL = 32
CLIPS = 2
FRAMES = 16
ROWS_IN = 16


def block_scale(key, dims, shards, low, high):
    factor_of, own = 1.0, jax.random.fold_in(key, 6)
    for axis_at, parts in shards:
        draws = jnp.exp(jax.random.uniform(jax.random.fold_in(own, axis_at), (parts,), jnp.float32, low / len(shards), high / len(shards)))
        factor_of = factor_of * jnp.repeat(draws, dims[axis_at] // parts).reshape([-1 if axis == axis_at else 1 for axis in range(len(dims))])
    return factor_of


def normal_values(stream_key, dims, deviation, most, shards=(), held_as=jnp.bfloat16):
    entries = jax.random.normal(stream_key, dims, jnp.float32) * deviation
    if len(shards) > 0:
        entries = block_scale(stream_key, dims, shards, -0.22, 0.18) * entries
    return jnp.clip(entries, min=-most, max=most).astype(held_as)


def setup_inputs(seed: int = 0) -> dict:
    keys = jax.random.split(jax.random.key(seed), 5)
    low_frames = normal_values(keys[0], (CLIPS, FRAMES, ROWS_IN, WL, C), 1.0, 6.0, ((0, 2), (1, 4), (2, 4)))
    spatial_weight = normal_values(keys[1], (3, 3, C, C), (9 * C) ** -0.5, 0.125)
    temporal_weight = normal_values(keys[2], (3, C, C), (3 * C) ** -0.5, 0.21875)
    cotangent = normal_values(keys[3], (CLIPS, FRAMES, 2 * ROWS_IN, 2 * WL, C), 1.0, 6.0, ((0, 2), (1, 4), (2, 4)))
    return dict(low_frames=low_frames, spatial_weight=spatial_weight, temporal_weight=temporal_weight, cotangent=cotangent)


def spatial_apply(padded, weights, rows, cols):
    chan = weights.shape[-1]
    total = jnp.zeros((padded.shape[0] * rows * cols, chan), jnp.float32)
    for i in range(3):
        for j in range(3):
            piece = padded[:, i:i + rows, j:j + cols, :].reshape(-1, chan)
            total = total + jnp.dot(piece, weights[i, j], preferred_element_type=jnp.float32)
    return total


def one_clip(args):
    low, spatial_weight, temporal_weight, grad_out = args
    frames, rows_low, cols_low, chan = low.shape
    rows = 2 * rows_low
    cols = 2 * cols_low
    upsampled = jnp.repeat(jnp.repeat(low, 2, axis=1), 2, axis=2)
    padded = jnp.pad(upsampled, ((0, 0), (1, 1), (1, 1), (0, 0)))
    pre = spatial_apply(padded, spatial_weight, rows, cols)
    act = jax.nn.silu(pre).astype(jnp.bfloat16).reshape(frames, rows, cols, chan)
    act_ext = jnp.concatenate([jnp.zeros((2, rows, cols, chan), jnp.bfloat16), act], 0)
    mixed = upsampled.reshape(-1, chan).astype(jnp.float32)
    for k in range(3):
        mixed = mixed + jnp.dot(act_ext[2 - k:2 - k + frames].reshape(-1, chan), temporal_weight[k], preferred_element_type=jnp.float32)
    section_out = mixed.astype(jnp.bfloat16).reshape(frames, rows, cols, chan)
    grad_ext = jnp.concatenate([grad_out, jnp.zeros((2, rows, cols, chan), jnp.bfloat16)], 0)
    grad_flat = grad_out.reshape(-1, chan)
    act_grad = jnp.zeros((frames * rows * cols, chan), jnp.float32)
    tgrads = []
    for k in range(3):
        act_grad = act_grad + jnp.dot(grad_ext[k:k + frames].reshape(-1, chan), temporal_weight[k].T, preferred_element_type=jnp.float32)
        tgrads.append(lax.dot_general(act_ext[2 - k:2 - k + frames].reshape(-1, chan), grad_flat, (((0,), (0,)), ((), ())), preferred_element_type=jnp.float32))
    sig = jax.nn.sigmoid(pre)
    pre_grad = (act_grad * (sig * (1.0 + pre * (1.0 - sig)))).astype(jnp.bfloat16)
    sgrads = []
    for i in range(3):
        for j in range(3):
            piece = padded[:, i:i + rows, j:j + cols, :].reshape(-1, chan)
            sgrads.append(lax.dot_general(piece, pre_grad, (((0,), (0,)), ((), ())), preferred_element_type=jnp.float32))
    grad_pad = jnp.pad(pre_grad.reshape(frames, rows, cols, chan), ((0, 0), (1, 1), (1, 1), (0, 0)))
    total = grad_out.reshape(-1, chan).astype(jnp.float32)
    for i in range(3):
        for j in range(3):
            piece = grad_pad[:, 2 - i:2 - i + rows, 2 - j:2 - j + cols, :].reshape(-1, chan)
            total = total + jnp.dot(piece, spatial_weight[i, j].T, preferred_element_type=jnp.float32)
    input_grad = total.reshape(frames, rows_low, 2, cols_low, 2, chan).sum(axis=(2, 4)).astype(jnp.bfloat16)
    return section_out, input_grad, jnp.stack(sgrads).reshape(3, 3, chan, chan), jnp.stack(tgrads)


def reference(low_frames, spatial_weight, temporal_weight, cotangent):
    clips = low_frames.shape[0]
    outs = []
    grads_in = []
    sgrad = jnp.zeros(spatial_weight.shape, jnp.float32)
    tgrad = jnp.zeros(temporal_weight.shape, jnp.float32)
    for clip in range(clips):
        section_out, input_grad, sg, tg = one_clip((low_frames[clip], spatial_weight, temporal_weight, cotangent[clip]))
        outs.append(section_out)
        grads_in.append(input_grad)
        sgrad = sgrad + sg
        tgrad = tgrad + tg
    return jnp.stack(outs), jnp.stack(grads_in), sgrad, tgrad
```

```python
import functools

import jax
import jax.numpy as jnp
from jax import lax
from jax.sharding import PartitionSpec as P

AXES = ("dp", "tm", "height")


class Slots:
    def __init__(self, mesh):
        self.sizes = [mesh.shape[axis] for axis in AXES]
        bits = []
        for at in (1, 0, 2):
            bits += [(at, bit) for bit in range(self.sizes[at].bit_length() - 1)]
        self.core = next((b for b in bits if self.same_chip(mesh, b)), bits[0])
        others = [b for b in bits if b != self.core]
        self.first = others[0]
        self.second = next(b for b in others if b[0] != self.first[0])
        self.rest = {}
        for at, bit in others:
            if (at, bit) not in (self.first, self.second):
                self.rest.setdefault(at, []).append(bit)

    def same_chip(self, mesh, place):
        at, bit = place
        where = [0, 0, 0]
        here = mesh.devices[tuple(where)]
        where[at] = 1 << bit
        there = mesh.devices[tuple(where)]
        return tuple(getattr(here, "coords", (0,))) == tuple(getattr(there, "coords", (1,)))

    def index(self, place):
        return (place[0] * self.sizes[1] + place[1]) * self.sizes[2] + place[2]

    def pairs(self, partner):
        d, t, h = self.sizes
        places = [(i, j, k) for i in range(d) for j in range(t) for k in range(h)]
        return [(self.index(p), self.index(partner(p))) for p in places]

    def flip(self, place, at, mask):
        return tuple(v ^ mask if i == at else v for i, v in enumerate(place))

    def swap_core(self, place):
        return self.flip(place, self.core[0], 1 << self.core[1])

    def swap(self, stage):
        def partner(place):
            on_core = place[self.core[0]] >> self.core[1] & 1
            at, bit = (self.first, self.second)[on_core ^ stage]
            return self.flip(place, at, 1 << bit)

        return partner

    def code(self):
        def bit_of(place):
            return lax.axis_index(AXES[place[0]]) >> place[1] & 1

        return bit_of(self.core), bit_of(self.first), bit_of(self.second)

    def send(self, block, partner):
        return lax.ppermute(block, AXES, self.pairs(partner))

    def reduce(self, slots):
        n = slots.shape[0]
        kept = slots[: n // 2] + self.send(slots[n // 2 :], self.swap_core)
        for stage in (0, 1):
            n = kept.shape[0]
            sent = self.send(kept[n // 2 :].astype(jnp.bfloat16), self.swap(stage))
            kept = kept[: n // 2] + sent.astype(jnp.float32)
        for at, bits in self.rest.items():
            masks = [0]
            for bit in bits:
                masks += [m | 1 << bit for m in masks]
            mine = kept.astype(jnp.bfloat16)
            parts = [mine] + [
                self.send(mine, lambda p, m=m: self.flip(p, at, m)) for m in masks[1:]
            ]
            parts = [p.astype(jnp.float32) for p in parts]
            while len(parts) > 1:
                parts = [parts[i] + parts[i + 1] for i in range(0, len(parts), 2)]
            kept = parts[0]
        total = kept.astype(jnp.bfloat16)
        for partner in (self.swap(1), self.swap(0), self.swap_core):
            total = jnp.concatenate([total, self.send(total, partner)], axis=0)
        return total


def swapped(block, bit, axis):
    return jnp.where(bit == 1, jnp.flip(block, axis), block)


def to_slots(pieces, code):
    core, a, b = code
    view = pieces.reshape((2, 2, 2) + pieces.shape[1:])
    low = swapped(swapped(view[0], a, 0), b, 1)
    high = swapped(swapped(view[1], b, 0), a, 1)
    return swapped(jnp.stack([low, high]), core, 0).reshape(pieces.shape)


def from_slots(slots, code):
    core, a, b = code
    view = swapped(slots.reshape((2, 2, 2) + slots.shape[1:]), core, 0)
    low = swapped(swapped(view[0], a, 0), b, 1)
    high = swapped(swapped(view[1], b, 0), a, 1)
    return jnp.stack([low, high]).reshape(slots.shape)


def extended(block, sides, width):
    for axis, dim in sides:
        count = lax.axis_size(axis)
        forward = [(i, i + 1) for i in range(count - 1)]
        backward = [(target, source) for source, target in forward]
        low = lax.ppermute(
            lax.slice_in_dim(block, block.shape[dim] - width, None, axis=dim), axis, forward
        )
        high = lax.ppermute(lax.slice_in_dim(block, 0, width, axis=dim), axis, backward)
        block = jnp.concatenate([low, block, high], axis=dim)
    return block


def shifted(block, axis, distance):
    devices = range(lax.axis_size(axis))
    route = [(i - distance, i) for i in devices if i - distance in devices]
    return lax.ppermute(block, axis, route)


def spatial_apply(padded, weights, rows, cols):
    chan = weights.shape[-1]
    total = jnp.zeros((padded.shape[0] * rows * cols, chan), jnp.float32)
    for i in range(3):
        for j in range(3):
            piece = padded[:, i : i + rows, j : j + cols, :].reshape(-1, chan)
            total = total + jnp.dot(piece, weights[i, j], preferred_element_type=jnp.float32)
    return total


def on_device(slots, low_frames, spatial_weight, temporal_weight, cotangent):
    low = low_frames[0]
    grad_out = cotangent[0]
    frames, rows_low, cols_low, chan = low.shape
    rows = 2 * rows_low
    cols = 2 * cols_low
    low_ext = extended(low, (("height", 1),), 1)
    upsampled = jnp.repeat(jnp.repeat(low_ext, 2, axis=1), 2, axis=2)[:, 1:-1]
    padded = jnp.pad(upsampled, ((0, 0), (0, 0), (1, 1), (0, 0)))
    pre = spatial_apply(padded, spatial_weight, rows, cols)
    act = jax.nn.silu(pre).astype(jnp.bfloat16).reshape(frames, rows, cols, chan)
    earlier = shifted(act[frames - 2 :], "tm", 1)
    act_ext = jnp.concatenate([earlier, act], 0)
    mixed = padded[:, 1:-1, 1:-1, :].reshape(-1, chan).astype(jnp.float32)
    for k in range(3):
        mixed = mixed + jnp.dot(
            act_ext[2 - k : 2 - k + frames].reshape(-1, chan),
            temporal_weight[k],
            preferred_element_type=jnp.float32,
        )
    section_out = mixed.astype(jnp.bfloat16).reshape(1, frames, rows, cols, chan)
    later = shifted(grad_out[:2], "tm", -1)
    grad_ext = jnp.concatenate([grad_out, later], 0)
    grad_flat = grad_out.reshape(-1, chan)
    act_grad = jnp.zeros((frames * rows * cols, chan), jnp.float32)
    tgrads = []
    for k in range(3):
        act_grad = act_grad + jnp.dot(
            grad_ext[k : k + frames].reshape(-1, chan),
            temporal_weight[k].T,
            preferred_element_type=jnp.float32,
        )
        tgrads.append(
            lax.dot_general(
                act.reshape(-1, chan),
                grad_ext[k : k + frames].reshape(-1, chan),
                (((0,), (0,)), ((), ())),
                preferred_element_type=jnp.float32,
            )
        )
    temporal_grad = jnp.stack(tgrads)
    sig = jax.nn.sigmoid(pre)
    pre_grad = (act_grad * (sig * (1.0 + pre * (1.0 - sig)))).astype(jnp.bfloat16)
    sgrads = []
    for i in range(3):
        for j in range(3):
            piece = padded[:, i : i + rows, j : j + cols, :].reshape(-1, chan)
            sgrads.append(
                lax.dot_general(
                    piece, pre_grad, (((0,), (0,)), ((), ())), preferred_element_type=jnp.float32
                )
            )
    spatial_grad = jnp.stack(sgrads).reshape(3, 3, chan, chan)
    grad_rows = extended(pre_grad.reshape(frames, rows, cols, chan), (("height", 1),), 1)
    grad_pad = jnp.pad(grad_rows, ((0, 0), (0, 0), (1, 1), (0, 0)))
    total = grad_flat.astype(jnp.float32)
    for i in range(3):
        for j in range(3):
            piece = grad_pad[:, 2 - i : 2 - i + rows, 2 - j : 2 - j + cols, :].reshape(-1, chan)
            total = total + jnp.dot(
                piece, spatial_weight[i, j].T, preferred_element_type=jnp.float32
            )
    input_grad = (
        total.reshape(frames, rows_low, 2, cols_low, 2, chan).sum(axis=(2, 4)).astype(jnp.bfloat16)
    )
    code = slots.code()
    taps = jnp.concatenate([spatial_grad.reshape(9, chan, chan), temporal_grad])
    pieces = taps.reshape(12, 8, chan // 8, chan).transpose(1, 0, 2, 3)
    pieces = from_slots(slots.reduce(to_slots(pieces, code)), code)
    taps = pieces.transpose(1, 0, 2, 3).reshape(12, chan, chan).astype(jnp.float32)
    spatial_grad, temporal_grad = taps[:9].reshape(3, 3, chan, chan), taps[9:]
    return (section_out, input_grad[None], spatial_grad, temporal_grad)


def solution(mesh):
    in_specs = (P("dp", "tm", "height", None, None), P(), P(), P("dp", "tm", "height", None, None))
    out_specs = (P("dp", "tm", "height", None, None), P("dp", "tm", "height", None, None), P(), P())
    return jax.shard_map(
        functools.partial(on_device, Slots(mesh)), mesh=mesh, in_specs=in_specs, out_specs=out_specs, check_vma=False
    )
```

```python
import functools

import jax
import jax.numpy as jnp
from jax import lax
from jax.sharding import Mesh
from jax.sharding import PartitionSpec as P


class Bits:
    def __init__(self, mesh):
        self.axes = {}
        for name in mesh.axis_names:
            count = mesh.shape[name].bit_length() - 1
            self.axes[name] = tuple(f"{name}{bit}" for bit in reversed(range(count)))
        names = [bit for bits in self.axes.values() for bit in bits]
        self.mesh = Mesh(mesh.devices.reshape([2] * len(names)), tuple(names))
        self.core = next((n for n in names if self.same_chip(n)), self.axes["tm"][-1])
        self.near = []
        for bits in self.axes.values():
            self.near += [b for b in bits if b != self.core][-1:]
        self.far = [n for n in names if n != self.core and n not in self.near]

    def same_chip(self, name):
        at = [1 if n == name else 0 for n in self.mesh.axis_names]
        here = self.mesh.devices[tuple([0] * len(at))]
        there = self.mesh.devices[tuple(at)]
        return tuple(getattr(here, "coords", (0,))) == tuple(getattr(there, "coords", (1,)))

    def swap(self, block, axis):
        return lax.ppermute(block, axis, [(0, 1), (1, 0)])

    def reduce(self, pieces):
        near, parts = tuple(self.near), pieces.shape[1]
        on_core = lax.axis_index(self.core) == 1
        mine = jnp.where(on_core, pieces[1], pieces[0])
        other = jnp.where(on_core, pieces[0], pieces[1])
        kept = (mine + self.swap(other, self.core)).astype(jnp.bfloat16)
        got = lax.all_to_all(kept, near, 0, 0, tiled=True).astype(jnp.float32)
        total = got.sum(0)
        for axis in self.far:
            own = total.astype(jnp.bfloat16)
            total = own.astype(jnp.float32) + self.swap(own, axis).astype(jnp.float32)
        total = total.astype(jnp.bfloat16)
        spread = jnp.broadcast_to(total, (parts,) + total.shape)
        half = lax.all_to_all(spread, near, 0, 0, tiled=True)
        theirs = self.swap(half, self.core)
        return jnp.stack([jnp.where(on_core, theirs, half), jnp.where(on_core, half, theirs)])


def extended(block, sides, width):
    for axis, dim in sides:
        count = lax.axis_size(axis)
        forward = [(i, i + 1) for i in range(count - 1)]
        backward = [(target, source) for source, target in forward]
        low = lax.ppermute(
            lax.slice_in_dim(block, block.shape[dim] - width, None, axis=dim), axis, forward
        )
        high = lax.ppermute(lax.slice_in_dim(block, 0, width, axis=dim), axis, backward)
        block = jnp.concatenate([low, block, high], axis=dim)
    return block


def shifted(block, axis, distance):
    devices = range(lax.axis_size(axis))
    route = [(i - distance, i) for i in devices if i - distance in devices]
    return lax.ppermute(block, axis, route)


def spatial_apply(padded, weights, rows, cols):
    chan = weights.shape[-1]
    total = jnp.zeros((padded.shape[0] * rows * cols, chan), jnp.float32)
    for i in range(3):
        for j in range(3):
            piece = padded[:, i : i + rows, j : j + cols, :].reshape(-1, chan)
            total = total + jnp.dot(piece, weights[i, j], preferred_element_type=jnp.float32)
    return total


def on_device(bits, low_frames, spatial_weight, temporal_weight, cotangent):
    low = low_frames[0]
    grad_out = cotangent[0]
    frames, rows_low, cols_low, chan = low.shape
    rows = 2 * rows_low
    cols = 2 * cols_low
    low_ext = extended(low, ((bits.axes["height"], 1),), 1)
    upsampled = jnp.repeat(jnp.repeat(low_ext, 2, axis=1), 2, axis=2)[:, 1:-1]
    padded = jnp.pad(upsampled, ((0, 0), (0, 0), (1, 1), (0, 0)))
    pre = spatial_apply(padded, spatial_weight, rows, cols)
    act = jax.nn.silu(pre).astype(jnp.bfloat16).reshape(frames, rows, cols, chan)
    earlier = shifted(act[frames - 2 :], bits.axes["tm"], 1)
    act_ext = jnp.concatenate([earlier, act], 0)
    mixed = padded[:, 1:-1, 1:-1, :].reshape(-1, chan).astype(jnp.float32)
    for k in range(3):
        mixed = mixed + jnp.dot(
            act_ext[2 - k : 2 - k + frames].reshape(-1, chan),
            temporal_weight[k],
            preferred_element_type=jnp.float32,
        )
    section_out = mixed.astype(jnp.bfloat16).reshape(1, frames, rows, cols, chan)
    later = shifted(grad_out[:2], bits.axes["tm"], -1)
    grad_ext = jnp.concatenate([grad_out, later], 0)
    grad_flat = grad_out.reshape(-1, chan)
    act_grad = jnp.zeros((frames * rows * cols, chan), jnp.float32)
    tgrads = []
    for k in range(3):
        act_grad = act_grad + jnp.dot(
            grad_ext[k : k + frames].reshape(-1, chan),
            temporal_weight[k].T,
            preferred_element_type=jnp.float32,
        )
        tgrads.append(
            lax.dot_general(
                act.reshape(-1, chan),
                grad_ext[k : k + frames].reshape(-1, chan),
                (((0,), (0,)), ((), ())),
                preferred_element_type=jnp.float32,
            )
        )
    temporal_grad = jnp.stack(tgrads)
    sig = jax.nn.sigmoid(pre)
    pre_grad = (act_grad * (sig * (1.0 + pre * (1.0 - sig)))).astype(jnp.bfloat16)
    sgrads = []
    for i in range(3):
        for j in range(3):
            piece = padded[:, i : i + rows, j : j + cols, :].reshape(-1, chan)
            sgrads.append(
                lax.dot_general(
                    piece, pre_grad, (((0,), (0,)), ((), ())), preferred_element_type=jnp.float32
                )
            )
    spatial_grad = jnp.stack(sgrads).reshape(3, 3, chan, chan)
    grad_rows = extended(pre_grad.reshape(frames, rows, cols, chan), ((bits.axes["height"], 1),), 1)
    grad_pad = jnp.pad(grad_rows, ((0, 0), (0, 0), (1, 1), (0, 0)))
    total = grad_flat.astype(jnp.float32)
    for i in range(3):
        for j in range(3):
            piece = grad_pad[:, 2 - i : 2 - i + rows, 2 - j : 2 - j + cols, :].reshape(-1, chan)
            total = total + jnp.dot(
                piece, spatial_weight[i, j].T, preferred_element_type=jnp.float32
            )
    input_grad = (
        total.reshape(frames, rows_low, 2, cols_low, 2, chan).sum(axis=(2, 4)).astype(jnp.bfloat16)
    )
    taps = jnp.concatenate([spatial_grad.reshape(9, chan, chan), temporal_grad])
    parts = 1 << len(bits.near)
    pieces = taps.reshape(12, 2, parts, chan // (2 * parts), chan).transpose(1, 2, 0, 3, 4)
    pieces = bits.reduce(pieces).astype(jnp.float32)
    taps = pieces.transpose(2, 0, 1, 3, 4).reshape(12, chan, chan)
    spatial_grad, temporal_grad = taps[:9].reshape(3, 3, chan, chan), taps[9:]
    return (section_out, input_grad[None], spatial_grad, temporal_grad)


def solution(mesh):
    bits = Bits(mesh)
    block = P(*(bits.axes[name] for name in ("dp", "tm", "height")), None, None)
    return jax.shard_map(
        functools.partial(on_device, bits),
        mesh=bits.mesh,
        in_specs=(block, P(), P(), block),
        out_specs=(block, block, P(), P()),
        check_vma=False,
    )
```

```python
import functools

import jax
import jax.numpy as jnp
from jax import lax
from jax.experimental import pallas as pl
from jax.experimental.pallas import tpu as pltpu
from jax.sharding import Mesh
from jax.sharding import PartitionSpec as P


class Bits:
    def __init__(self, mesh):
        self.axes = {}
        for name in mesh.axis_names:
            count = mesh.shape[name].bit_length() - 1
            self.axes[name] = tuple(f"{name}{bit}" for bit in reversed(range(count)))
        names = [bit for bits in self.axes.values() for bit in bits]
        self.mesh = Mesh(mesh.devices.reshape([2] * len(names)), tuple(names))
        self.core = next((n for n in names if self.same_chip(n)), self.axes["tm"][-1])
        self.near = []
        for bits in self.axes.values():
            self.near += [b for b in bits if b != self.core][-1:]
        self.far = [n for n in names if n != self.core and n not in self.near]

    def same_chip(self, name):
        at = [1 if n == name else 0 for n in self.mesh.axis_names]
        here = self.mesh.devices[tuple([0] * len(at))]
        there = self.mesh.devices[tuple(at)]
        return tuple(getattr(here, "coords", (0,))) == tuple(getattr(there, "coords", (1,)))

    def swap(self, block, axis):
        return lax.ppermute(block, axis, [(0, 1), (1, 0)])

    def shift(self, block, name, distance):
        axes = self.axes[name]
        devices = range(1 << len(axes))
        route = [(i - distance, i) for i in devices if i - distance in devices]
        return lax.ppermute(block, axes, route)

    def reduce(self, mine, other):
        near = tuple(self.near)
        kept = (mine + self.swap(other, self.core)).astype(jnp.bfloat16)
        got = lax.all_to_all(kept, near, 0, 0, tiled=True).astype(jnp.float32)
        total = got.sum(0)
        for axis in self.far:
            own = total.astype(jnp.bfloat16)
            total = own.astype(jnp.float32) + self.swap(own, axis).astype(jnp.float32)
        total = total.astype(jnp.bfloat16)
        spread = jnp.broadcast_to(total, kept.shape)
        half = lax.all_to_all(spread, near, 0, 0, tiled=True)
        return half, self.swap(half, self.core)


SIDES = ((0, 0), (0, 1), (1, 0), (1, 1))
VMEM = pltpu.CompilerParams(vmem_limit_bytes=56 * 2**20)


def product(left, right):
    return jnp.dot(left, right, preferred_element_type=jnp.float32)


def product_nt(left, right):
    return lax.dot_general(left, right, (((1,), (1,)), ((), ())), preferred_element_type=jnp.float32)


def rows_at_once(rows_low, cols_low):
    return max(n for n in (1, 2, 4, 8) if rows_low % n == 0 and (n == 1 or 4 * n * cols_low <= 256))


def by_side(count, cols_low, dtype=jnp.bfloat16):
    size = 4 * count * cols_low
    to = lax.broadcasted_iota(jnp.int32, (size, size), 0)
    at = lax.broadcasted_iota(jnp.int32, (size, size), 1)
    q, rest = to % cols_low, to // cols_low
    p, side = rest % count, rest // count
    return (at == (p * 2 + side // 2) * 2 * cols_low + 2 * q + side % 2).astype(jnp.float32).astype(dtype)


def from_side(count, cols_low, dtype=jnp.bfloat16):
    size = 4 * count * cols_low
    at = lax.broadcasted_iota(jnp.int32, (size, size), 0)
    to = lax.broadcasted_iota(jnp.int32, (size, size), 1)
    q, rest = to % cols_low, to // cols_low
    p, side = rest % count, rest // count
    return (at == (p * 2 + side // 2) * 2 * cols_low + 2 * q + side % 2).astype(jnp.float32).astype(dtype)


def box(count, cols_low, dtype=jnp.bfloat16):
    size = 4 * count * cols_low
    to = lax.broadcasted_iota(jnp.int32, (size // 4, size), 0)
    at = lax.broadcasted_iota(jnp.int32, (size // 4, size), 1)
    p, q = at // (4 * cols_low), at % (2 * cols_low) // 2
    return (to == p * cols_low + q).astype(jnp.float32).astype(dtype)


def column(rows, cols_low, chan):
    return lax.broadcasted_iota(jnp.int32, (rows, chan), 0) % cols_low


def from_left(x, at):
    return jnp.where(at == 0, 0.0, pltpu.roll(x, 1, 0))


def from_right(x, at, last):
    return jnp.where(at == last, 0.0, pltpu.roll(x, x.shape[0] - 1, 0))


def grads_kernel(core_ref, low_ref, up_ref, down_ref, cot_ref, later_ref, ws_ref, wt_ref,
                 act_ref, pg_ref, mine_ref, other_ref, cot_side, acc):
    frame, frames = pl.program_id(0), pl.num_programs(0)
    _, rows_low, cols_low, chan = low_ref.shape
    count = rows_low * cols_low
    group = rows_at_once(rows_low, cols_low)
    span = group * cols_low
    order = by_side(group, cols_low)

    def sort_frame(source, slot):
        for n in range(rows_low // group):
            block = source[2 * group * n : 2 * group * (n + 1)].reshape(4 * span, chan)
            block = product(order, block).astype(jnp.bfloat16).reshape(4, span, chan)
            cot_side[slot, :, n * span : (n + 1) * span, :] = block

    @pl.when(frame == 0)
    def _():
        for n in range(2):
            sort_frame(cot_ref.at[n], n)

    @pl.when(frame + 2 < frames)
    def _():
        sort_frame(cot_ref.at[jnp.minimum(frame + 2, frames - 1)], frame + 2)

    @pl.when(frame + 2 >= frames)
    def _():
        sort_frame(later_ref.at[jnp.maximum(frame + 2 - frames, 0)], frame + 2)

    low = jnp.concatenate([up_ref[0], low_ref[0], down_ref[0]], axis=0)
    flat = low.reshape(-1, chan)
    rows = [[], []]
    for j in range(3):
        taps = [product(flat, ws_ref[i, j]).reshape(low.shape) for i in range(3)]
        even = taps[0][:rows_low] + (taps[1] + taps[2])[1 : rows_low + 1]
        odd = (taps[0] + taps[1])[1 : rows_low + 1] + taps[2][2:]
        rows[0].append(even.reshape(count, chan))
        rows[1].append(odd.reshape(count, chan))
    at = column(count, cols_low, chan)
    pres = []
    for a in range(2):
        first, second, third = rows[a]
        pres.append(from_left(first, at) + (second + third))
        pres.append((first + second) + from_right(third, at, cols_low - 1))

    acts, pgs = [], []
    for side, pre in enumerate(pres):
        sig = jax.nn.sigmoid(pre)
        acts.append((pre * sig).astype(jnp.bfloat16))
        act_grad = product_nt(cot_side[frame, side], wt_ref[0])
        for k in (1, 2):
            act_grad = act_grad + product_nt(cot_side[frame + k, side], wt_ref[k])
        pgs.append((act_grad * (sig * (1.0 + pre * (1.0 - sig)))).astype(jnp.bfloat16))
        act_ref[0, side] = acts[side]
        pg_ref[0, side] = pgs[side]

    sums = []
    wide = flat.astype(jnp.float32)
    at = column(wide.shape[0], cols_low, chan)
    moved = [from_left(wide, at), wide, from_right(wide, at, cols_low - 1)]
    turned = {}
    for dc in range(3):
        view = moved[dc].astype(jnp.bfloat16).reshape(low.shape)
        for dr in range(3):
            turned[dr - 1, dc - 1] = view[dr : dr + rows_low].reshape(count, chan).T
    pg = jnp.concatenate(pgs, axis=0)
    for i in range(3):
        for j in range(3):
            left = jnp.concatenate([turned[(a + i - 1) // 2, (b + j - 1) // 2] for a, b in SIDES], axis=1)
            sums.append(product(left, pg))
    act = jnp.concatenate(acts, axis=0).T
    for k in range(3):
        sums.append(product(act, cot_side[frame + k].reshape(4 * count, chan)))

    @pl.when(frame == 0)
    def _():
        for tap, value in enumerate(sums):
            acc[tap] = value

    @pl.when(frame > 0)
    def _():
        for tap, value in enumerate(sums):
            acc[tap] += value

    @pl.when(frame == frames - 1)
    def _():
        parts = mine_ref.shape[0]
        half = chan // 2
        size = half // parts
        core = core_ref[0]
        for out, start in ((mine_ref, core * half), (other_ref, half - core * half)):
            for n in range(parts):
                for tap in range(12):
                    begin = pl.multiple_of(start + n * size, size)
                    out[n, tap * size : (tap + 1) * size, :] = acc[tap, pl.ds(begin, size), :]


def whole(shape):
    return pl.BlockSpec(shape, lambda f: (0,) * len(shape))


def each(shape):
    return pl.BlockSpec((1,) + tuple(shape[1:]), lambda f: (f,) + (0,) * (len(shape) - 1))


SCALAR = pl.BlockSpec(memory_space=pltpu.SMEM)


def weight_grads(core, parts, low, up, down, cot, later, ws, wt):
    frames, rows_low, cols_low, chan = low.shape
    count = rows_low * cols_low
    side = (frames, 4, count, chan)
    piece = (parts, 12 * (chan // (2 * parts)), chan)
    flops = 2 * 2048 * chan * chan * 20
    return pl.pallas_call(
        grads_kernel,
        grid=(frames,),
        in_specs=[SCALAR, each(low.shape), each(up.shape), each(down.shape),
                  whole(cot.shape), whole(later.shape), whole(ws.shape), whole(wt.shape)],
        out_specs=[each(side), each(side), whole(piece), whole(piece)],
        out_shape=[jax.ShapeDtypeStruct(side, jnp.bfloat16)] * 2
        + [jax.ShapeDtypeStruct(piece, jnp.float32)] * 2,
        scratch_shapes=[pltpu.VMEM((frames + 2, 4, count, chan), jnp.bfloat16),
                        pltpu.VMEM((12, chan, chan), jnp.float32)],
        compiler_params=VMEM,
        cost_estimate=pl.CostEstimate(flops=flops, bytes_accessed=8 * 2**20, transcendentals=frames * 4 * count * chan),
        name="weight_grads",
    )(core, low, up, down, cot, later, ws, wt)


def section_kernel(act_ref, low_ref, wt_ref, out_ref):
    frame = pl.program_id(0)
    _, rows_low, cols_low, chan = low_ref.shape
    group = rows_at_once(rows_low, cols_low)
    span = group * cols_low
    order = from_side(group, cols_low)
    low = low_ref[0].reshape(-1, chan).astype(jnp.float32)
    mixed = []
    for side in range(4):
        total = low
        for k in range(3):
            total = total + product(act_ref[frame + 2 - k, side], wt_ref[k])
        mixed.append(total.astype(jnp.bfloat16))
    for n in range(rows_low // group):
        block = jnp.concatenate([m[n * span : (n + 1) * span] for m in mixed], axis=0)
        block = product(order, block).astype(jnp.bfloat16)
        out_ref[0, 2 * group * n : 2 * group * (n + 1)] = block.reshape(2 * group, 2 * cols_low, chan)


def section(act_ext, low, wt):
    frames, rows_low, cols_low, chan = low.shape
    out = (frames, 2 * rows_low, 2 * cols_low, chan)
    return pl.pallas_call(
        section_kernel,
        grid=(frames,),
        in_specs=[whole(act_ext.shape), each(low.shape), whole(wt.shape)],
        out_specs=each(out),
        out_shape=jax.ShapeDtypeStruct(out, jnp.bfloat16),
        compiler_params=VMEM,
        cost_estimate=pl.CostEstimate(flops=2 * 2048 * chan * chan * 4, bytes_accessed=3 * 2**20, transcendentals=0),
        name="section",
    )(act_ext, low, wt)


def input_kernel(pg_ref, up_ref, down_ref, cot_ref, ws_ref, out_ref):
    _, rows_low, cols_low, chan = out_ref.shape
    group = rows_at_once(rows_low, cols_low)
    span = group * cols_low
    place = box(group, cols_low)
    count = rows_low * cols_low
    total = jnp.concatenate(
        [product(place, cot_ref[0, 2 * group * n : 2 * group * (n + 1)].reshape(4 * span, chan))
         for n in range(rows_low // group)], axis=0)
    tall = (rows_low + 1, cols_low, chan)
    at = column(tall[0] * cols_low, cols_low, chan)
    own = [pg_ref[0, side].astype(jnp.float32) for side in range(4)]
    above = [up_ref[0, b].astype(jnp.float32) for b in range(2)]
    below = [down_ref[0, b].astype(jnp.float32) for b in range(2)]
    even = [jnp.concatenate([own[b], below[b]], axis=0) for b in range(2)]
    odd = [jnp.concatenate([above[b], own[2 + b]], axis=0) for b in range(2)]
    for j in range(3):
        pair = []
        for first, second in (even, odd):
            if j == 0:
                value = second + from_right(first, at, cols_low - 1)
            elif j == 1:
                value = first + second
            else:
                value = first + from_left(second, at)
            pair.append(value.reshape(tall))
        top, low = pair
        for i, value in enumerate((low[1:] + top[1:], top[:-1] + low[1:], low[:-1] + top[:-1])):
            value = value.reshape(count, chan)
            high = value.astype(jnp.bfloat16)
            rest = (value - high.astype(jnp.float32)).astype(jnp.bfloat16)
            total = total + product_nt(high, ws_ref[i, j]) + product_nt(rest, ws_ref[i, j])
    out_ref[0] = total.astype(jnp.bfloat16).reshape(rows_low, cols_low, chan)


def input_grads(pg, up, down, cot, ws, low_shape):
    chan = low_shape[-1]
    return pl.pallas_call(
        input_kernel,
        grid=(low_shape[0],),
        in_specs=[each(pg.shape), each(up.shape), each(down.shape), each(cot.shape), whole(ws.shape)],
        out_specs=each(low_shape),
        out_shape=jax.ShapeDtypeStruct(low_shape, jnp.bfloat16),
        compiler_params=VMEM,
        cost_estimate=pl.CostEstimate(flops=2 * 2048 * chan * chan * 6, bytes_accessed=4 * 2**20, transcendentals=0),
        name="input_grads",
    )(pg, up, down, cot, ws)


def place_kernel(core_ref, half_ref, theirs_ref, spatial_ref, temporal_ref):
    parts, rows, chan = half_ref.shape
    size = rows // 12
    half = chan // 2
    core = core_ref[0]
    for source, start in ((half_ref, core * half), (theirs_ref, half - core * half)):
        for n in range(parts):
            begin = pl.multiple_of(start + n * size, size)
            for tap in range(12):
                value = source[n, tap * size : (tap + 1) * size, :].astype(jnp.float32)
                if tap < 9:
                    spatial_ref[tap // 3, tap % 3, pl.ds(begin, size), :] = value
                else:
                    temporal_ref[tap - 9, pl.ds(begin, size), :] = value


def place(core, half, theirs, chan):
    full = pl.BlockSpec(memory_space=pltpu.VMEM)
    return pl.pallas_call(
        place_kernel,
        in_specs=[SCALAR, full, full],
        out_specs=[full, full],
        out_shape=[jax.ShapeDtypeStruct((3, 3, chan, chan), jnp.float32),
                   jax.ShapeDtypeStruct((3, chan, chan), jnp.float32)],
        compiler_params=VMEM,
        name="place",
    )(core, half, theirs)


def on_device(bits, low_frames, spatial_weight, temporal_weight, cotangent):
    low, cot = low_frames[0], cotangent[0]
    frames, rows_low, cols_low, chan = low.shape
    core = lax.axis_index(bits.core).astype(jnp.int32).reshape(1)
    up = bits.shift(low[:, -1:], "height", 1)
    down = bits.shift(low[:, :1], "height", -1)
    later = bits.shift(cot[:2], "tm", -1)
    act, pg, mine, other = weight_grads(
        core, 1 << len(bits.near), low, up, down, cot, later, spatial_weight, temporal_weight
    )
    half, theirs = bits.reduce(mine, other)
    earlier = bits.shift(act[frames - 2 :], "tm", 1)
    section_out = section(jnp.concatenate([earlier, act], axis=0), low, temporal_weight)
    above = bits.shift(pg[:, 2:, -cols_low:], "height", 1)
    below = bits.shift(pg[:, :2, :cols_low], "height", -1)
    input_grad = input_grads(pg, above, below, cot, spatial_weight, low.shape)
    spatial_grad, temporal_grad = place(core, half, theirs, chan)
    return section_out[None], input_grad[None], spatial_grad, temporal_grad


def solution(mesh):
    bits = Bits(mesh)
    block = P(*(bits.axes[name] for name in ("dp", "tm", "height")), None, None)
    return jax.shard_map(
        functools.partial(on_device, bits),
        mesh=bits.mesh,
        in_specs=(block, P(), P(), block),
        out_specs=(block, block, P(), P()),
        check_vma=False,
    )
```

```python
import functools

import jax
import jax.numpy as jnp
from jax import lax
from jax.experimental import pallas as pl
from jax.experimental.pallas import tpu as pltpu
from jax.sharding import Mesh
from jax.sharding import PartitionSpec as P


class Bits:
    def __init__(self, mesh):
        self.axes = {}
        for name in mesh.axis_names:
            count = mesh.shape[name].bit_length() - 1
            self.axes[name] = tuple(f"{name}{bit}" for bit in reversed(range(count)))
        names = [bit for bits in self.axes.values() for bit in bits]
        self.mesh = Mesh(mesh.devices.reshape([2] * len(names)), tuple(names))
        self.core = next((n for n in names if self.same_chip(n)), self.axes["tm"][-1])
        self.near = []
        for bits in self.axes.values():
            self.near += [b for b in bits if b != self.core][-1:]
        self.far = [n for n in names if n != self.core and n not in self.near]

    def same_chip(self, name):
        at = [1 if n == name else 0 for n in self.mesh.axis_names]
        here = self.mesh.devices[tuple([0] * len(at))]
        there = self.mesh.devices[tuple(at)]
        return tuple(getattr(here, "coords", (0,))) == tuple(getattr(there, "coords", (1,)))

    def swap(self, block, axis):
        return lax.ppermute(block, axis, [(0, 1), (1, 0)])

    def shift(self, block, name, distance):
        axes = self.axes[name]
        devices = range(1 << len(axes))
        route = [(i - distance, i) for i in devices if i - distance in devices]
        return lax.ppermute(block, axes, route)

    def halves(self, mine, other):
        return (mine + self.swap(other, self.core)).astype(jnp.bfloat16)

    def exchange(self, parts):
        return lax.all_to_all(parts, tuple(self.near), 0, 0, tiled=True)

    def gather(self, total, parts):
        for axis in self.far:
            own = total.astype(jnp.bfloat16)
            total = own.astype(jnp.float32) + self.swap(own, axis).astype(jnp.float32)
        total = total.astype(jnp.bfloat16)
        spread = jnp.broadcast_to(total, (parts,) + total.shape)
        half = self.exchange(spread)
        return half, self.swap(half, self.core)


SIDES = ((0, 0), (0, 1), (1, 0), (1, 1))
VMEM = pltpu.CompilerParams(vmem_limit_bytes=56 * 2**20)


def product(left, right):
    return jnp.dot(left, right, preferred_element_type=jnp.float32)


def product_nt(left, right):
    return lax.dot_general(left, right, (((1,), (1,)), ((), ())), preferred_element_type=jnp.float32)


def rows_at_once(rows_low, cols_low):
    return max(n for n in (1, 2, 4, 8) if rows_low % n == 0 and (n == 1 or 4 * n * cols_low <= 256))


def by_side(count, cols_low, dtype=jnp.bfloat16):
    size = 4 * count * cols_low
    to = lax.broadcasted_iota(jnp.int32, (size, size), 0)
    at = lax.broadcasted_iota(jnp.int32, (size, size), 1)
    q, rest = to % cols_low, to // cols_low
    p, side = rest % count, rest // count
    return (at == (p * 2 + side // 2) * 2 * cols_low + 2 * q + side % 2).astype(jnp.float32).astype(dtype)


def from_side(count, cols_low, dtype=jnp.bfloat16):
    size = 4 * count * cols_low
    at = lax.broadcasted_iota(jnp.int32, (size, size), 0)
    to = lax.broadcasted_iota(jnp.int32, (size, size), 1)
    q, rest = to % cols_low, to // cols_low
    p, side = rest % count, rest // count
    return (at == (p * 2 + side // 2) * 2 * cols_low + 2 * q + side % 2).astype(jnp.float32).astype(dtype)


def box(count, cols_low, dtype=jnp.bfloat16):
    size = 4 * count * cols_low
    to = lax.broadcasted_iota(jnp.int32, (size // 4, size), 0)
    at = lax.broadcasted_iota(jnp.int32, (size // 4, size), 1)
    p, q = at // (4 * cols_low), at % (2 * cols_low) // 2
    return (to == p * cols_low + q).astype(jnp.float32).astype(dtype)


def column(rows, cols_low, chan):
    return lax.broadcasted_iota(jnp.int32, (rows, chan), 0) % cols_low


def from_left(x, at):
    return jnp.where(at == 0, 0.0, pltpu.roll(x, 1, 0))


def from_right(x, at, last):
    return jnp.where(at == last, 0.0, pltpu.roll(x, x.shape[0] - 1, 0))


def grads_kernel(core_ref, low_ref, up_ref, down_ref, cot_ref, later_ref, ws_ref, wt_ref,
                 act_ref, pg_ref, mine_ref, other_ref, cot_side, acc):
    frame, frames = pl.program_id(0), pl.num_programs(0)
    _, rows_low, cols_low, chan = low_ref.shape
    count = rows_low * cols_low
    group = rows_at_once(rows_low, cols_low)
    span = group * cols_low
    order = by_side(group, cols_low)

    def sort_frame(source, slot):
        for n in range(rows_low // group):
            block = source[2 * group * n : 2 * group * (n + 1)].reshape(4 * span, chan)
            block = product(order, block).astype(jnp.bfloat16).reshape(4, span, chan)
            cot_side[slot, :, n * span : (n + 1) * span, :] = block

    @pl.when(frame == 0)
    def _():
        for n in range(2):
            sort_frame(cot_ref.at[n], n)

    @pl.when(frame + 2 < frames)
    def _():
        sort_frame(cot_ref.at[jnp.minimum(frame + 2, frames - 1)], frame + 2)

    @pl.when(frame + 2 >= frames)
    def _():
        sort_frame(later_ref.at[jnp.maximum(frame + 2 - frames, 0)], frame + 2)

    low = jnp.concatenate([up_ref[0], low_ref[0], down_ref[0]], axis=0)
    flat = low.reshape(-1, chan)
    rows = [[], []]
    for j in range(3):
        taps = [product(flat, ws_ref[i, j]).reshape(low.shape) for i in range(3)]
        even = taps[0][:rows_low] + (taps[1] + taps[2])[1 : rows_low + 1]
        odd = (taps[0] + taps[1])[1 : rows_low + 1] + taps[2][2:]
        rows[0].append(even.reshape(count, chan))
        rows[1].append(odd.reshape(count, chan))
    at = column(count, cols_low, chan)
    pres = []
    for a in range(2):
        first, second, third = rows[a]
        pres.append(from_left(first, at) + (second + third))
        pres.append((first + second) + from_right(third, at, cols_low - 1))

    acts, pgs = [], []
    for side, pre in enumerate(pres):
        sig = jax.nn.sigmoid(pre)
        acts.append((pre * sig).astype(jnp.bfloat16))
        act_grad = product_nt(cot_side[frame, side], wt_ref[0])
        for k in (1, 2):
            act_grad = act_grad + product_nt(cot_side[frame + k, side], wt_ref[k])
        pgs.append((act_grad * (sig * (1.0 + pre * (1.0 - sig)))).astype(jnp.bfloat16))
        act_ref[0, side] = acts[side]
        pg_ref[0, side] = pgs[side]

    sums = []
    wide = flat.astype(jnp.float32)
    at = column(wide.shape[0], cols_low, chan)
    moved = [from_left(wide, at), wide, from_right(wide, at, cols_low - 1)]
    turned = {}
    for dc in range(3):
        view = moved[dc].astype(jnp.bfloat16).reshape(low.shape)
        for dr in range(3):
            turned[dr - 1, dc - 1] = view[dr : dr + rows_low].reshape(count, chan).T
    pg = jnp.concatenate(pgs, axis=0)
    for i in range(3):
        for j in range(3):
            left = jnp.concatenate([turned[(a + i - 1) // 2, (b + j - 1) // 2] for a, b in SIDES], axis=1)
            sums.append(product(left, pg))
    act = jnp.concatenate(acts, axis=0).T
    for k in range(3):
        sums.append(product(act, cot_side[frame + k].reshape(4 * count, chan)))

    @pl.when(frame == 0)
    def _():
        for tap, value in enumerate(sums):
            acc[tap] = value

    @pl.when(frame > 0)
    def _():
        for tap, value in enumerate(sums):
            acc[tap] += value

    @pl.when(frame == frames - 1)
    def _():
        parts = mine_ref.shape[0]
        half = chan // 2
        size = half // parts
        core = core_ref[0]
        for out, start in ((mine_ref, core * half), (other_ref, half - core * half)):
            for n in range(parts):
                for tap in range(12):
                    begin = pl.multiple_of(start + n * size, size)
                    out[n, tap * size : (tap + 1) * size, :] = acc[tap, pl.ds(begin, size), :]


def whole(shape):
    return pl.BlockSpec(shape, lambda f: (0,) * len(shape))


def each(shape):
    return pl.BlockSpec((1,) + tuple(shape[1:]), lambda f: (f,) + (0,) * (len(shape) - 1))


SCALAR = pl.BlockSpec(memory_space=pltpu.SMEM)
UNREAD = pl.BlockSpec(memory_space=pl.ANY)


def weight_grads(core, parts, low, up, down, cot, later, ws, wt):
    frames, rows_low, cols_low, chan = low.shape
    count = rows_low * cols_low
    side = (frames, 4, count, chan)
    piece = (parts, 12 * (chan // (2 * parts)), chan)
    flops = 2 * 2048 * chan * chan * 20
    return pl.pallas_call(
        grads_kernel,
        grid=(frames,),
        in_specs=[SCALAR, each(low.shape), each(up.shape), each(down.shape),
                  whole(cot.shape), whole(later.shape), whole(ws.shape), whole(wt.shape)],
        out_specs=[each(side), each(side), whole(piece), whole(piece)],
        out_shape=[jax.ShapeDtypeStruct(side, jnp.bfloat16)] * 2
        + [jax.ShapeDtypeStruct(piece, jnp.float32)] * 2,
        scratch_shapes=[pltpu.VMEM((frames + 2, 4, count, chan), jnp.bfloat16),
                        pltpu.VMEM((12, chan, chan), jnp.float32)],
        compiler_params=VMEM,
        cost_estimate=pl.CostEstimate(flops=flops, bytes_accessed=8 * 2**20, transcendentals=frames * 4 * count * chan),
        name="weight_grads",
    )(core, low, up, down, cot, later, ws, wt)


def section_kernel(act_ref, low_ref, wt_ref, _, out_ref):
    frame = pl.program_id(0)
    _, rows_low, cols_low, chan = low_ref.shape
    group = rows_at_once(rows_low, cols_low)
    span = group * cols_low
    order = from_side(group, cols_low)
    low = low_ref[0].reshape(-1, chan).astype(jnp.float32)
    mixed = []
    for side in range(4):
        total = low
        for k in range(3):
            total = total + product(act_ref[frame + 2 - k, side], wt_ref[k])
        mixed.append(total.astype(jnp.bfloat16))
    for n in range(rows_low // group):
        block = jnp.concatenate([m[n * span : (n + 1) * span] for m in mixed], axis=0)
        block = product(order, block).astype(jnp.bfloat16)
        out_ref[0, 2 * group * n : 2 * group * (n + 1)] = block.reshape(2 * group, 2 * cols_low, chan)


def section(act_ext, low, wt, before):
    frames, rows_low, cols_low, chan = low.shape
    out = (frames, 2 * rows_low, 2 * cols_low, chan)
    return pl.pallas_call(
        section_kernel,
        grid=(frames,),
        in_specs=[whole(act_ext.shape), each(low.shape), whole(wt.shape), UNREAD],
        out_specs=each(out),
        out_shape=jax.ShapeDtypeStruct(out, jnp.bfloat16),
        compiler_params=VMEM,
        cost_estimate=pl.CostEstimate(flops=2 * 2048 * chan * chan * 4, bytes_accessed=3 * 2**20, transcendentals=0),
        name="section",
    )(act_ext, low, wt, before)


def input_kernel(pg_ref, up_ref, down_ref, cot_ref, ws_ref, _, out_ref):
    _, rows_low, cols_low, chan = out_ref.shape
    group = rows_at_once(rows_low, cols_low)
    span = group * cols_low
    place = box(group, cols_low)
    count = rows_low * cols_low
    total = jnp.concatenate(
        [product(place, cot_ref[0, 2 * group * n : 2 * group * (n + 1)].reshape(4 * span, chan))
         for n in range(rows_low // group)], axis=0)
    tall = (rows_low + 1, cols_low, chan)
    at = column(tall[0] * cols_low, cols_low, chan)
    own = [pg_ref[0, side].astype(jnp.float32) for side in range(4)]
    above = [up_ref[0, b].astype(jnp.float32) for b in range(2)]
    below = [down_ref[0, b].astype(jnp.float32) for b in range(2)]
    even = [jnp.concatenate([own[b], below[b]], axis=0) for b in range(2)]
    odd = [jnp.concatenate([above[b], own[2 + b]], axis=0) for b in range(2)]
    for j in range(3):
        pair = []
        for first, second in (even, odd):
            if j == 0:
                value = second + from_right(first, at, cols_low - 1)
            elif j == 1:
                value = first + second
            else:
                value = first + from_left(second, at)
            pair.append(value.reshape(tall))
        top, low = pair
        for i, value in enumerate((low[1:] + top[1:], top[:-1] + low[1:], low[:-1] + top[:-1])):
            value = value.reshape(count, chan)
            high = value.astype(jnp.bfloat16)
            rest = (value - high.astype(jnp.float32)).astype(jnp.bfloat16)
            total = total + product_nt(high, ws_ref[i, j]) + product_nt(rest, ws_ref[i, j])
    out_ref[0] = total.astype(jnp.bfloat16).reshape(rows_low, cols_low, chan)


def input_grads(pg, up, down, cot, ws, before, low_shape):
    chan = low_shape[-1]
    return pl.pallas_call(
        input_kernel,
        grid=(low_shape[0],),
        in_specs=[each(pg.shape), each(up.shape), each(down.shape), each(cot.shape), whole(ws.shape), UNREAD],
        out_specs=each(low_shape),
        out_shape=jax.ShapeDtypeStruct(low_shape, jnp.bfloat16),
        compiler_params=VMEM,
        cost_estimate=pl.CostEstimate(flops=2 * 2048 * chan * chan * 6, bytes_accessed=4 * 2**20, transcendentals=0),
        name="input_grads",
    )(pg, up, down, cot, ws, before)


def place_kernel(core_ref, half_ref, theirs_ref, spatial_ref, temporal_ref):
    parts, rows, chan = half_ref.shape
    size = rows // 12
    half = chan // 2
    core = core_ref[0]
    for source, start in ((half_ref, core * half), (theirs_ref, half - core * half)):
        for n in range(parts):
            begin = pl.multiple_of(start + n * size, size)
            for tap in range(12):
                value = source[n, tap * size : (tap + 1) * size, :].astype(jnp.float32)
                if tap < 9:
                    spatial_ref[tap // 3, tap % 3, pl.ds(begin, size), :] = value
                else:
                    temporal_ref[tap - 9, pl.ds(begin, size), :] = value


def place(core, half, theirs, chan):
    full = pl.BlockSpec(memory_space=pltpu.VMEM)
    return pl.pallas_call(
        place_kernel,
        in_specs=[SCALAR, full, full],
        out_specs=[full, full],
        out_shape=[jax.ShapeDtypeStruct((3, 3, chan, chan), jnp.float32),
                   jax.ShapeDtypeStruct((3, chan, chan), jnp.float32)],
        compiler_params=VMEM,
        name="place",
    )(core, half, theirs)


def sum_kernel(got_ref, *refs):
    total = got_ref[0].astype(jnp.float32)
    for n in range(1, got_ref.shape[0]):
        total = total + got_ref[n].astype(jnp.float32)
    refs[-1][...] = total


def sum_parts(got, *before):
    full = pl.BlockSpec(memory_space=pltpu.VMEM)
    return pl.pallas_call(
        sum_kernel,
        in_specs=[full] + [UNREAD] * len(before),
        out_specs=full,
        out_shape=jax.ShapeDtypeStruct(got.shape[1:], jnp.float32),
        compiler_params=VMEM,
        name="sum_parts",
    )(got, *before)


def on_device(bits, low_frames, spatial_weight, temporal_weight, cotangent):
    low, cot = low_frames[0], cotangent[0]
    frames, rows_low, cols_low, chan = low.shape
    core = lax.axis_index(bits.core).astype(jnp.int32).reshape(1)
    up = bits.shift(low[:, -1:], "height", 1)
    down = bits.shift(low[:, :1], "height", -1)
    later = bits.shift(cot[:2], "tm", -1)
    act, pg, mine, other = weight_grads(
        core, 1 << len(bits.near), low, up, down, cot, later, spatial_weight, temporal_weight
    )
    kept = bits.halves(mine, other)
    got = bits.exchange(kept)
    earlier = bits.shift(act[frames - 2 :], "tm", 1)
    section_out = section(jnp.concatenate([earlier, act], axis=0), low, temporal_weight, kept)
    above = bits.shift(pg[:, 2:, -cols_low:], "height", 1)
    below = bits.shift(pg[:, :2, :cols_low], "height", -1)
    input_grad = input_grads(pg, above, below, cot, spatial_weight, kept, low.shape)
    total = sum_parts(got, section_out, input_grad)
    half, theirs = bits.gather(total, got.shape[0])
    spatial_grad, temporal_grad = place(core, half, theirs, chan)
    return section_out[None], input_grad[None], spatial_grad, temporal_grad


def solution(mesh):
    bits = Bits(mesh)
    block = P(*(bits.axes[name] for name in ("dp", "tm", "height")), None, None)
    return jax.shard_map(
        functools.partial(on_device, bits),
        mesh=bits.mesh,
        in_specs=(block, P(), P(), block),
        out_specs=(block, block, P(), P()),
        check_vma=False,
    )
```

```python
import functools

import jax
import jax.numpy as jnp
from jax import lax
from jax.experimental import pallas as pl
from jax.experimental.pallas import tpu as pltpu
from jax.sharding import Mesh
from jax.sharding import PartitionSpec as P


class Bits:
    def __init__(self, mesh):
        self.axes = {}
        for name in mesh.axis_names:
            count = mesh.shape[name].bit_length() - 1
            self.axes[name] = tuple(f"{name}{bit}" for bit in reversed(range(count)))
        names = [bit for bits in self.axes.values() for bit in bits]
        self.mesh = Mesh(mesh.devices.reshape([2] * len(names)), tuple(names))
        self.core = next((n for n in names if self.same_chip(n)), self.axes["tm"][-1])
        self.near = []
        for bits in self.axes.values():
            self.near += [b for b in bits if b != self.core][-1:]
        self.far = [n for n in names if n != self.core and n not in self.near]

    def same_chip(self, name):
        at = [1 if n == name else 0 for n in self.mesh.axis_names]
        here = self.mesh.devices[tuple([0] * len(at))]
        there = self.mesh.devices[tuple(at)]
        return tuple(getattr(here, "coords", (0,))) == tuple(getattr(there, "coords", (1,)))

    def swap(self, block, axis):
        return lax.ppermute(block, axis, [(0, 1), (1, 0)])

    def shift(self, block, name, distance):
        axes = self.axes[name]
        devices = range(1 << len(axes))
        route = [(i - distance, i) for i in devices if i - distance in devices]
        return lax.ppermute(block, axes, route)

    def exchange(self, parts):
        return lax.all_to_all(parts, tuple(self.near), 0, 0, tiled=True)

    def gather(self, total, parts):
        for axis in self.far:
            total = (total.astype(jnp.float32) + self.swap(total, axis).astype(jnp.float32)).astype(jnp.bfloat16)
        spread = jnp.broadcast_to(total, (parts,) + total.shape)
        half = self.exchange(spread)
        return half, self.swap(half, self.core)


SIDES = ((0, 0), (0, 1), (1, 0), (1, 1))


def grant(mib):
    return pltpu.CompilerParams(vmem_limit_bytes=mib * 2**20)


def product(left, right):
    return jnp.dot(left, right, preferred_element_type=jnp.float32)


def product_nt(left, right):
    return lax.dot_general(left, right, (((1,), (1,)), ((), ())), preferred_element_type=jnp.float32)


def rows_at_once(rows_low, cols_low):
    return max(n for n in (1, 2, 4, 8) if rows_low % n == 0 and (n == 1 or 4 * n * cols_low <= 256))


def by_side(count, cols_low, dtype=jnp.bfloat16):
    size = 4 * count * cols_low
    to = lax.broadcasted_iota(jnp.int32, (size, size), 0)
    at = lax.broadcasted_iota(jnp.int32, (size, size), 1)
    q, rest = to % cols_low, to // cols_low
    p, side = rest % count, rest // count
    return (at == (p * 2 + side // 2) * 2 * cols_low + 2 * q + side % 2).astype(jnp.float32).astype(dtype)


def from_side(count, cols_low, dtype=jnp.bfloat16):
    size = 4 * count * cols_low
    at = lax.broadcasted_iota(jnp.int32, (size, size), 0)
    to = lax.broadcasted_iota(jnp.int32, (size, size), 1)
    q, rest = to % cols_low, to // cols_low
    p, side = rest % count, rest // count
    return (at == (p * 2 + side // 2) * 2 * cols_low + 2 * q + side % 2).astype(jnp.float32).astype(dtype)


def box(count, cols_low, dtype=jnp.bfloat16):
    size = 4 * count * cols_low
    to = lax.broadcasted_iota(jnp.int32, (size // 4, size), 0)
    at = lax.broadcasted_iota(jnp.int32, (size // 4, size), 1)
    p, q = at // (4 * cols_low), at % (2 * cols_low) // 2
    return (to == p * cols_low + q).astype(jnp.float32).astype(dtype)


def column(rows, cols_low, chan):
    return lax.broadcasted_iota(jnp.int32, (rows, chan), 0) % cols_low


def from_left(x, at):
    return jnp.where(at == 0, 0.0, pltpu.roll(x, 1, 0))


def from_right(x, at, last):
    return jnp.where(at == last, 0.0, pltpu.roll(x, x.shape[0] - 1, 0))


def sort_columns(source, target, cols_low):
    rows_low, chan = source.shape[0] // 2, source.shape[2]
    group = rows_at_once(rows_low, cols_low)
    span = group * cols_low
    order = by_side(group, cols_low)
    for n in range(rows_low // group):
        block = source[2 * group * n : 2 * group * (n + 1)].reshape(4 * span, chan)
        block = product(order, block).astype(jnp.bfloat16).reshape(4, span, chan)
        target[:, n * span : (n + 1) * span, :] = block


def forward_kernel(low_ref, up_ref, down_ref, cot_ref, ws_ref, act_ref, slope_ref, cot_side):
    _, rows_low, cols_low, chan = low_ref.shape
    count = rows_low * cols_low
    low = jnp.concatenate([up_ref[0], low_ref[0], down_ref[0]], axis=0)
    flat = low.reshape(-1, chan)
    rows = [[], []]
    for j in range(3):
        taps = [product(flat, ws_ref[i, j]).reshape(low.shape) for i in range(3)]
        even = taps[0][:rows_low] + (taps[1] + taps[2])[1 : rows_low + 1]
        odd = (taps[0] + taps[1])[1 : rows_low + 1] + taps[2][2:]
        rows[0].append(even.reshape(count, chan))
        rows[1].append(odd.reshape(count, chan))
    at = column(count, cols_low, chan)
    for a in range(2):
        first, second, third = rows[a]
        for b in range(2):
            if b == 0:
                pre = from_left(first, at) + (second + third)
            else:
                pre = (first + second) + from_right(third, at, cols_low - 1)
            sig = jax.nn.sigmoid(pre)
            act_ref[0, 2 * a + b] = (pre * sig).astype(jnp.bfloat16)
            slope_ref[0, 2 * a + b] = sig * (1.0 + pre * (1.0 - sig))
    sort_columns(cot_ref.at[0], cot_side.at[0], cols_low)


def add_sums(low, act, pg, cots, out_ref):
    rows_low, cols_low, half = low.shape[0] - 2, low.shape[1], low.shape[2]
    count = rows_low * cols_low
    sums = []
    wide = low.reshape(-1, half).astype(jnp.float32)
    at = column(wide.shape[0], cols_low, half)
    moved = [from_left(wide, at), wide, from_right(wide, at, cols_low - 1)]
    turned = {}
    for dc in range(3):
        view = moved[dc].astype(jnp.bfloat16).reshape(low.shape)
        for dr in range(3):
            turned[dr - 1, dc - 1] = view[dr : dr + rows_low].reshape(count, half).T
    for i in range(3):
        for j in range(3):
            left = jnp.concatenate([turned[(a + i - 1) // 2, (b + j - 1) // 2] for a, b in SIDES], axis=1)
            sums.append(product(left, pg))
    act = act.T
    for cot in cots:
        sums.append(product(act, cot))

    def each_piece(store):
        parts = out_ref.shape[0]
        size = half // parts
        for tap, value in enumerate(sums):
            for n in range(parts):
                store(n, slice(tap * size, (tap + 1) * size), value[n * size : (n + 1) * size])

    @pl.when(pl.program_id(0) == 0)
    def _():
        def store(n, rows, value):
            out_ref[n, rows, :] = value

        each_piece(store)

    @pl.when(pl.program_id(0) > 0)
    def _():
        def store(n, rows, value):
            out_ref[n, rows, :] += value

        each_piece(store)


def backward_kernel(_, low_ref, up_ref, down_ref, act_ref, slope_ref, cot_ref, later_ref, wt_ref, pg_ref, ext_ref, out_ref):
    frame = pl.program_id(0)
    frames, _, count, chan = cot_ref.shape
    cols_low = low_ref.shape[2]

    @pl.when(frame == 0)
    def _():
        ext_ref[:frames] = cot_ref[...]
        for n in range(2):
            sort_columns(later_ref.at[n], ext_ref.at[frames + n], cols_low)

    pgs = []
    for side in range(4):
        act_grad = product_nt(ext_ref[frame, side], wt_ref[0])
        for k in (1, 2):
            act_grad = act_grad + product_nt(ext_ref[frame + k, side], wt_ref[k])
        pgs.append((act_grad * slope_ref[0, side]).astype(jnp.bfloat16))
        pg_ref[0, side] = pgs[side]
    low = jnp.concatenate([up_ref[0], low_ref[0], down_ref[0]], axis=0)
    act = act_ref[0].reshape(4 * count, -1)
    cots = [ext_ref[frame + k].reshape(4 * count, chan) for k in range(3)]
    add_sums(low, act, jnp.concatenate(pgs, axis=0), cots, out_ref)


def half_kernel(_, low_ref, up_ref, down_ref, act_ref, pg_ref, ext_ref, __, out_ref):
    frame = pl.program_id(0)
    _, _, count, chan = pg_ref.shape
    low = jnp.concatenate([up_ref[0], low_ref[0], down_ref[0]], axis=0)
    act = act_ref[0].reshape(4 * count, -1)
    cots = [ext_ref[frame + k].reshape(4 * count, chan) for k in range(3)]
    add_sums(low, act, pg_ref[0].reshape(4 * count, chan), cots, out_ref)


def whole(shape):
    return pl.BlockSpec(shape, lambda f, *_: (0,) * len(shape))


def each(shape):
    return pl.BlockSpec((1,) + tuple(shape[1:]), lambda f, *_: (f,) + (0,) * (len(shape) - 1))


def half_of(shape):
    block = (1,) + tuple(shape[1:-1]) + (shape[-1] // 2,)
    return pl.BlockSpec(block, lambda f, side: (f,) + (0,) * (len(shape) - 2) + (side[0],))


SCALAR = pl.BlockSpec(memory_space=pltpu.SMEM)
UNREAD = pl.BlockSpec(memory_space=pl.ANY)


def like(shape, dtype):
    return jax.ShapeDtypeStruct(shape, dtype)


TOKEN = like((8, 128), jnp.float32)


def cost(units, mib):
    return pl.CostEstimate(flops=units * 2 * 2048 * 256 * 256, bytes_accessed=mib * 2**20, transcendentals=0)


def forward(low, up, down, cot, ws):
    frames, rows_low, cols_low, chan = low.shape
    side = (frames, 4, rows_low * cols_low, chan)
    return pl.pallas_call(
        forward_kernel,
        grid=(frames,),
        in_specs=[each(low.shape), each(up.shape), each(down.shape), each(cot.shape), whole(ws.shape)],
        out_specs=[each(side)] * 3,
        out_shape=[like(side, jnp.bfloat16), like(side, jnp.float32), like(side, jnp.bfloat16)],
        compiler_params=grant(20),
        cost_estimate=cost(10, 8),
        name="forward",
    )(low, up, down, cot, ws)


def backward(side, parts, low, up, down, act, slope, cot, later, wt):
    frames, _, count, chan = act.shape
    ext = (frames + 2,) + act.shape[1:]
    piece = (parts, 12 * (chan // (2 * parts)), chan)
    return pl.pallas_call(
        backward_kernel,
        grid_spec=pltpu.PrefetchScalarGridSpec(
            num_scalar_prefetch=1,
            grid=(frames,),
            in_specs=[half_of(low.shape), half_of(up.shape), half_of(down.shape), half_of(act.shape),
                      each(slope.shape), whole(cot.shape), whole(later.shape), whole(wt.shape)],
            out_specs=[each(act.shape), whole(ext), whole(piece)],
        ),
        out_shape=[like(act.shape, jnp.bfloat16), like(ext, jnp.bfloat16), like(piece, jnp.float32)],
        compiler_params=grant(28),
        cost_estimate=cost(15, 10),
        name="backward",
    )(side, low, up, down, act, slope, cot, later, wt)


def half_grads(side, parts, low, up, down, act, pg, ext, before):
    frames, _, _, chan = act.shape
    piece = (parts, 12 * (chan // (2 * parts)), chan)
    return pl.pallas_call(
        half_kernel,
        grid_spec=pltpu.PrefetchScalarGridSpec(
            num_scalar_prefetch=1,
            grid=(frames,),
            in_specs=[half_of(low.shape), half_of(up.shape), half_of(down.shape), half_of(act.shape),
                      each(pg.shape), whole(ext.shape), UNREAD],
            out_specs=whole(piece),
        ),
        out_shape=like(piece, jnp.float32),
        compiler_params=grant(24),
        cost_estimate=cost(10, 6),
        name="half_grads",
    )(side, low, up, down, act, pg, ext, before)


def section_kernel(act_ref, low_ref, wt_ref, _, out_ref, token_ref):
    token_ref[...] = jnp.zeros_like(token_ref)
    frame = pl.program_id(0)
    _, rows_low, cols_low, chan = low_ref.shape
    group = rows_at_once(rows_low, cols_low)
    span = group * cols_low
    order = from_side(group, cols_low)
    low = low_ref[0].reshape(-1, chan).astype(jnp.float32)
    mixed = []
    for side in range(4):
        total = low
        for k in range(3):
            total = total + product(act_ref[frame + 2 - k, side], wt_ref[k])
        mixed.append(total.astype(jnp.bfloat16))
    for n in range(rows_low // group):
        block = jnp.concatenate([m[n * span : (n + 1) * span] for m in mixed], axis=0)
        block = product(order, block).astype(jnp.bfloat16)
        out_ref[0, 2 * group * n : 2 * group * (n + 1)] = block.reshape(2 * group, 2 * cols_low, chan)


def section(act_ext, low, wt, before):
    frames, rows_low, cols_low, chan = low.shape
    out = (frames, 2 * rows_low, 2 * cols_low, chan)
    return pl.pallas_call(
        section_kernel,
        grid=(frames,),
        in_specs=[whole(act_ext.shape), each(low.shape), whole(wt.shape), UNREAD],
        out_specs=[each(out), whole(TOKEN.shape)],
        out_shape=[like(out, jnp.bfloat16), TOKEN],
        compiler_params=grant(16),
        cost_estimate=pl.CostEstimate(flops=2 * 2048 * chan * chan * 4, bytes_accessed=3 * 2**20, transcendentals=0),
        name="section",
    )(act_ext, low, wt, before)


def input_kernel(pg_ref, up_ref, down_ref, cot_ref, ws_ref, _, out_ref, token_ref):
    token_ref[...] = jnp.zeros_like(token_ref)
    _, rows_low, cols_low, chan = out_ref.shape
    group = rows_at_once(rows_low, cols_low)
    span = group * cols_low
    place = box(group, cols_low)
    count = rows_low * cols_low
    total = jnp.concatenate(
        [product(place, cot_ref[0, 2 * group * n : 2 * group * (n + 1)].reshape(4 * span, chan))
         for n in range(rows_low // group)], axis=0)
    tall = (rows_low + 1, cols_low, chan)
    at = column(tall[0] * cols_low, cols_low, chan)
    own = [pg_ref[0, side].astype(jnp.float32) for side in range(4)]
    above = [up_ref[0, b].astype(jnp.float32) for b in range(2)]
    below = [down_ref[0, b].astype(jnp.float32) for b in range(2)]
    even = [jnp.concatenate([own[b], below[b]], axis=0) for b in range(2)]
    odd = [jnp.concatenate([above[b], own[2 + b]], axis=0) for b in range(2)]
    for j in range(3):
        pair = []
        for first, second in (even, odd):
            if j == 0:
                value = second + from_right(first, at, cols_low - 1)
            elif j == 1:
                value = first + second
            else:
                value = first + from_left(second, at)
            pair.append(value.reshape(tall))
        top, low = pair
        for i, value in enumerate((low[1:] + top[1:], top[:-1] + low[1:], low[:-1] + top[:-1])):
            value = value.reshape(count, chan)
            high = value.astype(jnp.bfloat16)
            rest = (value - high.astype(jnp.float32)).astype(jnp.bfloat16)
            total = total + product_nt(high, ws_ref[i, j]) + product_nt(rest, ws_ref[i, j])
    out_ref[0] = total.astype(jnp.bfloat16).reshape(rows_low, cols_low, chan)


def input_grads(pg, up, down, cot, ws, before, low_shape):
    chan = low_shape[-1]
    return pl.pallas_call(
        input_kernel,
        grid=(low_shape[0],),
        in_specs=[each(pg.shape), each(up.shape), each(down.shape), each(cot.shape), whole(ws.shape), UNREAD],
        out_specs=[each(low_shape), whole(TOKEN.shape)],
        out_shape=[like(low_shape, jnp.bfloat16), TOKEN],
        compiler_params=grant(20),
        cost_estimate=pl.CostEstimate(flops=2 * 2048 * chan * chan * 6, bytes_accessed=4 * 2**20, transcendentals=0),
        name="input_grads",
    )(pg, up, down, cot, ws, before)


def place_kernel(core_ref, half_ref, theirs_ref, spatial_ref, temporal_ref):
    parts, rows, chan = half_ref.shape
    size = rows // 12
    half = chan // 2
    core = core_ref[0]
    for source, start in ((half_ref, core * half), (theirs_ref, half - core * half)):
        for n in range(parts):
            begin = pl.multiple_of(start + n * size, size)
            for tap in range(12):
                value = source[n, tap * size : (tap + 1) * size, :].astype(jnp.float32)
                if tap < 9:
                    spatial_ref[tap // 3, tap % 3, pl.ds(begin, size), :] = value
                else:
                    temporal_ref[tap - 9, pl.ds(begin, size), :] = value


def place(core, half, theirs, chan):
    full = pl.BlockSpec(memory_space=pltpu.VMEM)
    return pl.pallas_call(
        place_kernel,
        in_specs=[SCALAR, full, full],
        out_specs=[full, full],
        out_shape=[jax.ShapeDtypeStruct((3, 3, chan, chan), jnp.float32),
                   jax.ShapeDtypeStruct((3, chan, chan), jnp.float32)],
        compiler_params=grant(10),
        name="place",
    )(core, half, theirs)


def add_kernel(mine_ref, theirs_ref, out_ref):
    out_ref[...] = (mine_ref[...] + theirs_ref[...]).astype(jnp.bfloat16)


def add_halves(mine, theirs):
    full = pl.BlockSpec(memory_space=pltpu.VMEM)
    return pl.pallas_call(
        add_kernel,
        in_specs=[full, full],
        out_specs=full,
        out_shape=like(mine.shape, jnp.bfloat16),
        compiler_params=grant(8),
        name="add_halves",
    )(mine, theirs)


def sum_kernel(got_ref, *refs):
    total = got_ref[0].astype(jnp.float32)
    for n in range(1, got_ref.shape[0]):
        total = total + got_ref[n].astype(jnp.float32)
    refs[-1][...] = total.astype(jnp.bfloat16)


def sum_parts(got, *before):
    full = pl.BlockSpec(memory_space=pltpu.VMEM)
    return pl.pallas_call(
        sum_kernel,
        in_specs=[full] + [UNREAD] * len(before),
        out_specs=full,
        out_shape=like(got.shape[1:], jnp.bfloat16),
        compiler_params=grant(4),
        name="sum_parts",
    )(got, *before)


def on_device(bits, low_frames, spatial_weight, temporal_weight, cotangent):
    low, cot = low_frames[0], cotangent[0]
    frames, rows_low, cols_low, chan = low.shape
    core = lax.axis_index(bits.core).astype(jnp.int32).reshape(1)
    up = bits.shift(low[:, -1:], "height", 1)
    down = bits.shift(low[:, :1], "height", -1)
    later = bits.shift(cot[:2], "tm", -1)
    parts = 1 << len(bits.near)
    act, slope, cot_side = forward(low, up, down, cot, spatial_weight)
    earlier = bits.shift(act[frames - 2 :], "tm", 1)
    pg, ext, other = backward(
        1 - core, parts, low, up, down, act, slope, cot_side, later, temporal_weight
    )
    theirs = bits.swap(other, bits.core)
    mine = half_grads(core, parts, low, up, down, act, pg, ext, earlier)
    kept = add_halves(mine, theirs)
    got = bits.exchange(kept)
    section_out, section_done = section(jnp.concatenate([earlier, act], axis=0), low, temporal_weight, kept)
    above = bits.shift(pg[:, 2:, -cols_low:], "height", 1)
    below = bits.shift(pg[:, :2, :cols_low], "height", -1)
    input_grad, input_done = input_grads(pg, above, below, cot, spatial_weight, kept, low.shape)
    total = sum_parts(got, section_done, input_done)
    half, theirs = bits.gather(total, got.shape[0])
    spatial_grad, temporal_grad = place(core, half, theirs, chan)
    return section_out[None], input_grad[None], spatial_grad, temporal_grad


def solution(mesh):
    bits = Bits(mesh)
    block = P(*(bits.axes[name] for name in ("dp", "tm", "height")), None, None)
    return jax.shard_map(
        functools.partial(on_device, bits),
        mesh=bits.mesh,
        in_specs=(block, P(), P(), block),
        out_specs=(block, block, P(), P()),
        check_vma=False,
    )
```

```python
import functools

import jax
import jax.numpy as jnp
from jax import lax
from jax.experimental import pallas as pl
from jax.experimental.pallas import tpu as pltpu
from jax.sharding import Mesh
from jax.sharding import PartitionSpec as P


class Bits:
    def __init__(self, mesh):
        self.axes = {}
        for name in mesh.axis_names:
            count = mesh.shape[name].bit_length() - 1
            self.axes[name] = tuple(f"{name}{bit}" for bit in reversed(range(count)))
        names = [bit for bits in self.axes.values() for bit in bits]
        self.mesh = Mesh(mesh.devices.reshape([2] * len(names)), tuple(names))
        self.core = next((n for n in names if self.same_chip(n)), self.axes["tm"][-1])
        self.near = []
        for bits in self.axes.values():
            self.near += [b for b in bits if b != self.core][-1:]
        self.far = [n for n in names if n != self.core and n not in self.near]

    def same_chip(self, name):
        at = [1 if n == name else 0 for n in self.mesh.axis_names]
        here = self.mesh.devices[tuple([0] * len(at))]
        there = self.mesh.devices[tuple(at)]
        return tuple(getattr(here, "coords", (0,))) == tuple(getattr(there, "coords", (1,)))

    def swap(self, block, axis):
        return lax.ppermute(block, axis, [(0, 1), (1, 0)])

    def shift(self, block, name, distance):
        axes = self.axes[name]
        devices = range(1 << len(axes))
        route = [(i - distance, i) for i in devices if i - distance in devices]
        return lax.ppermute(block, axes, route)

    def exchange(self, parts):
        return lax.all_to_all(parts, tuple(self.near), 0, 0, tiled=True)

    def rows(self, first, last):
        odd = lax.axis_index(self.axes["height"][-1]) == 1
        return self.pairs(jnp.where(odd, first, last), jnp.where(odd, last, first))

    def pairs(self, inner, outer):
        axes = self.axes["height"]
        low = range(1, (1 << len(axes)) - 1, 2)
        route = [(i, i + 1) for i in low] + [(i + 1, i) for i in low]
        return self.swap(inner, axes[-1]), lax.ppermute(outer, axes, route)

    def far_sums(self, total):
        for axis in self.far[:-1]:
            total = (total.astype(jnp.float32) + self.swap(total, axis).astype(jnp.float32)).astype(jnp.bfloat16)
        return total, self.swap(total, self.far[-1])


SIDES = ((0, 0), (0, 1), (1, 0), (1, 1))


def grant(mib):
    return pltpu.CompilerParams(vmem_limit_bytes=mib * 2**20)


def product(left, right):
    return jnp.dot(left, right, preferred_element_type=jnp.float32)


def product_nt(left, right):
    return lax.dot_general(left, right, (((1,), (1,)), ((), ())), preferred_element_type=jnp.float32)


def rows_at_once(rows_low, cols_low):
    return max(n for n in (1, 2, 4, 8) if rows_low % n == 0 and (n == 1 or 4 * n * cols_low <= 256))


def by_side(count, cols_low, dtype=jnp.bfloat16):
    size = 4 * count * cols_low
    to = lax.broadcasted_iota(jnp.int32, (size, size), 0)
    at = lax.broadcasted_iota(jnp.int32, (size, size), 1)
    q, rest = to % cols_low, to // cols_low
    p, side = rest % count, rest // count
    return (at == (p * 2 + side // 2) * 2 * cols_low + 2 * q + side % 2).astype(jnp.float32).astype(dtype)


def from_side(count, cols_low, dtype=jnp.bfloat16):
    size = 4 * count * cols_low
    at = lax.broadcasted_iota(jnp.int32, (size, size), 0)
    to = lax.broadcasted_iota(jnp.int32, (size, size), 1)
    q, rest = to % cols_low, to // cols_low
    p, side = rest % count, rest // count
    return (at == (p * 2 + side // 2) * 2 * cols_low + 2 * q + side % 2).astype(jnp.float32).astype(dtype)


def box(count, cols_low, dtype=jnp.bfloat16):
    size = 4 * count * cols_low
    to = lax.broadcasted_iota(jnp.int32, (size // 4, size), 0)
    at = lax.broadcasted_iota(jnp.int32, (size // 4, size), 1)
    p, q = at // (4 * cols_low), at % (2 * cols_low) // 2
    return (to == p * cols_low + q).astype(jnp.float32).astype(dtype)


def column(rows, cols_low, chan):
    return lax.broadcasted_iota(jnp.int32, (rows, chan), 0) % cols_low


def from_left(x, at):
    return jnp.where(at == 0, 0.0, pltpu.roll(x, 1, 0))


def from_right(x, at, last):
    return jnp.where(at == last, 0.0, pltpu.roll(x, x.shape[0] - 1, 0))


def sort_columns(source, target, cols_low):
    rows_low, chan = source.shape[0] // 2, source.shape[2]
    group = rows_at_once(rows_low, cols_low)
    span = group * cols_low
    order = by_side(group, cols_low)
    for n in range(rows_low // group):
        block = source[2 * group * n : 2 * group * (n + 1)].reshape(4 * span, chan)
        block = product(order, block).astype(jnp.bfloat16).reshape(4, span, chan)
        target[:, n * span : (n + 1) * span, :] = block


def tall(place_ref, low_ref, inner_ref, outer_ref):
    odd = place_ref[1] == 1
    up = jnp.where(odd, inner_ref[0], outer_ref[0])
    down = jnp.where(odd, outer_ref[0], inner_ref[0])
    return jnp.concatenate([up, low_ref[0], down], axis=0)


def spatial(low, ws_ref):
    rows_low, cols_low, chan = low.shape[0] - 2, low.shape[1], low.shape[2]
    count = rows_low * cols_low
    flat = low.reshape(-1, chan)
    rows = [[], []]
    for j in range(3):
        taps = [product(flat, ws_ref[i, j]).reshape(low.shape) for i in range(3)]
        even = taps[0][:rows_low] + (taps[1] + taps[2])[1 : rows_low + 1]
        odd = (taps[0] + taps[1])[1 : rows_low + 1] + taps[2][2:]
        rows[0].append(even.reshape(count, chan))
        rows[1].append(odd.reshape(count, chan))
    at = column(count, cols_low, chan)
    for first, second, third in rows:
        yield from_left(first, at) + (second + third)
        yield (first + second) + from_right(third, at, cols_low - 1)


def forward_kernel(place_ref, low_ref, inner_ref, outer_ref, cot_ref, ws_ref, act_ref, slope_ref, cot_side):
    low = tall(place_ref, low_ref, inner_ref, outer_ref)
    for side, pre in enumerate(spatial(low, ws_ref)):
        sig = jax.nn.sigmoid(pre)
        act_ref[0, side] = (pre * sig).astype(jnp.bfloat16)
        slope_ref[0, side] = sig * (1.0 + pre * (1.0 - sig))
    sort_columns(cot_ref.at[0], cot_side.at[0], low.shape[1])


def act_kernel(low_ref, ws_ref, act_ref):
    for side, pre in enumerate(spatial(low_ref[0], ws_ref)):
        act_ref[0, side] = (pre * jax.nn.sigmoid(pre)).astype(jnp.bfloat16)


def add_sums(low, act, pg, cots, out_ref):
    rows_low, cols_low, half = low.shape[0] - 2, low.shape[1], low.shape[2]
    count = rows_low * cols_low
    sums = []
    wide = low.reshape(-1, half).astype(jnp.float32)
    at = column(wide.shape[0], cols_low, half)
    moved = [from_left(wide, at), wide, from_right(wide, at, cols_low - 1)]
    turned = {}
    for dc in range(3):
        view = moved[dc].astype(jnp.bfloat16).reshape(low.shape)
        for dr in range(3):
            turned[dr - 1, dc - 1] = view[dr : dr + rows_low].reshape(count, half).T
    for i in range(3):
        for j in range(3):
            left = jnp.concatenate([turned[(a + i - 1) // 2, (b + j - 1) // 2] for a, b in SIDES], axis=1)
            sums.append(product(left, pg))
    act = act.T
    for cot in cots:
        sums.append(product(act, cot))

    def each_piece(store):
        parts = out_ref.shape[0]
        size = half // parts
        for tap, value in enumerate(sums):
            for n in range(parts):
                store(n, slice(tap * size, (tap + 1) * size), value[n * size : (n + 1) * size])

    @pl.when(pl.program_id(0) == 0)
    def _():
        def store(n, rows, value):
            out_ref[n, rows, :] = value

        each_piece(store)

    @pl.when(pl.program_id(0) > 0)
    def _():
        def store(n, rows, value):
            out_ref[n, rows, :] += value

        each_piece(store)


def backward_kernel(place_ref, low_ref, inner_ref, outer_ref, act_ref, slope_ref, cot_ref, later_ref, wt_ref, pg_ref, ext_ref, out_ref):
    frame = pl.program_id(0)
    frames, _, count, chan = cot_ref.shape
    cols_low = low_ref.shape[2]

    @pl.when(frame == 0)
    def _():
        ext_ref[:frames] = cot_ref[...]
        for n in range(2):
            sort_columns(later_ref.at[n], ext_ref.at[frames + n], cols_low)

    pgs = []
    for side in range(4):
        act_grad = product_nt(ext_ref[frame, side], wt_ref[0])
        for k in (1, 2):
            act_grad = act_grad + product_nt(ext_ref[frame + k, side], wt_ref[k])
        pgs.append((act_grad * slope_ref[0, side]).astype(jnp.bfloat16))
        pg_ref[0, side] = pgs[side]
    low = tall(place_ref, low_ref, inner_ref, outer_ref)
    act = act_ref[0].reshape(4 * count, -1)
    cots = [ext_ref[frame + k].reshape(4 * count, chan) for k in range(3)]
    add_sums(low, act, jnp.concatenate(pgs, axis=0), cots, out_ref)


def half_kernel(place_ref, low_ref, inner_ref, outer_ref, act_ref, pg_ref, ext_ref, out_ref):
    frame = pl.program_id(0)
    _, _, count, chan = pg_ref.shape
    low = tall(place_ref, low_ref, inner_ref, outer_ref)
    act = act_ref[0].reshape(4 * count, -1)
    cots = [ext_ref[frame + k].reshape(4 * count, chan) for k in range(3)]
    add_sums(low, act, pg_ref[0].reshape(4 * count, chan), cots, out_ref)


def whole(shape):
    return pl.BlockSpec(shape, lambda f, *_: (0,) * len(shape))


def each(shape):
    return pl.BlockSpec((1,) + tuple(shape[1:]), lambda f, *_: (f,) + (0,) * (len(shape) - 1))


def half_of(shape):
    block = (1,) + tuple(shape[1:-1]) + (shape[-1] // 2,)
    return pl.BlockSpec(block, lambda f, side: (f,) + (0,) * (len(shape) - 2) + (side[0],))


SCALAR = pl.BlockSpec(memory_space=pltpu.SMEM)
UNREAD = pl.BlockSpec(memory_space=pl.ANY)


def like(shape, dtype):
    return jax.ShapeDtypeStruct(shape, dtype)


TOKEN = like((8, 128), jnp.float32)


def cost(units, mib):
    return pl.CostEstimate(flops=units * 2 * 2048 * 256 * 256, bytes_accessed=mib * 2**20, transcendentals=0)


def in_hbm(array):
    return pltpu.with_memory_space_constraint(array, pltpu.HBM)


def forward(place, low, inner, outer, cot, ws):
    frames, rows_low, cols_low, chan = low.shape
    side = (frames, 4, rows_low * cols_low, chan)
    return pl.pallas_call(
        forward_kernel,
        grid=(frames,),
        in_specs=[SCALAR, each(low.shape), each(inner.shape), each(outer.shape), each(cot.shape), whole(ws.shape)],
        out_specs=[each(side)] * 3,
        out_shape=[like(side, jnp.bfloat16), like(side, jnp.float32), like(side, jnp.bfloat16)],
        compiler_params=grant(20),
        cost_estimate=cost(10, 8),
        name="forward",
    )(place, in_hbm(low), inner, outer, in_hbm(cot), in_hbm(ws))


def edges_kernel(place_ref, low_ref, inner_ref, outer_ref, pg_ref, _, tall_ref, pg_inner, pg_outer):
    cols_low = low_ref.shape[2]
    first = low_ref.shape[0] - tall_ref.shape[0]
    for n in range(tall_ref.shape[0]):
        at = pl.ds(first + n, 1)
        tall_ref[n] = tall(place_ref, low_ref.at[at], inner_ref.at[at], outer_ref.at[at])
    odd = place_ref[1] == 1
    top, bottom = pg_ref[:, :2, :cols_low, :], pg_ref[:, 2:, -cols_low:, :]
    pg_inner[...] = jnp.where(odd, top, bottom)
    pg_outer[...] = jnp.where(odd, bottom, top)


def edges(place, low, inner, outer, pg, before):
    frames, rows_low, cols_low, chan = low.shape
    full = pl.BlockSpec(memory_space=pltpu.VMEM)
    rows = like((frames, 2, cols_low, chan), jnp.bfloat16)
    return pl.pallas_call(
        edges_kernel,
        in_specs=[SCALAR, full, full, full, full, UNREAD],
        out_specs=[full] * 3,
        out_shape=[like((2, rows_low + 2, cols_low, chan), jnp.bfloat16), rows, rows],
        compiler_params=grant(8),
        name="edges",
    )(place, low, inner, outer, pg, before)


def earlier_act(low, ws):
    frames, rows_tall, cols_low, chan = low.shape
    side = (frames, 4, (rows_tall - 2) * cols_low, chan)
    return pl.pallas_call(
        act_kernel,
        grid=(frames,),
        in_specs=[each(low.shape), whole(ws.shape)],
        out_specs=each(side),
        out_shape=like(side, jnp.bfloat16),
        compiler_params=grant(16),
        cost_estimate=cost(4, 3),
        name="earlier_act",
    )(low, ws)


def backward(place, parts, low, inner, outer, act, slope, cot, later, wt):
    frames, _, count, chan = act.shape
    ext = (frames + 2,) + act.shape[1:]
    piece = (parts, 12 * (chan // (2 * parts)), chan)
    return pl.pallas_call(
        backward_kernel,
        grid_spec=pltpu.PrefetchScalarGridSpec(
            num_scalar_prefetch=1,
            grid=(frames,),
            in_specs=[half_of(low.shape), half_of(inner.shape), half_of(outer.shape), half_of(act.shape),
                      each(slope.shape), whole(cot.shape), whole(later.shape), whole(wt.shape)],
            out_specs=[each(act.shape), whole(ext), whole(piece)],
        ),
        out_shape=[like(act.shape, jnp.bfloat16), like(ext, jnp.bfloat16), like(piece, jnp.float32)],
        compiler_params=grant(28),
        cost_estimate=cost(15, 10),
        name="backward",
    )(place, low, inner, outer, act, slope, cot, later, in_hbm(wt))


def half_grads(place, parts, low, inner, outer, act, pg, ext):
    frames, _, _, chan = act.shape
    piece = (parts, 12 * (chan // (2 * parts)), chan)
    return pl.pallas_call(
        half_kernel,
        grid_spec=pltpu.PrefetchScalarGridSpec(
            num_scalar_prefetch=1,
            grid=(frames,),
            in_specs=[half_of(low.shape), half_of(inner.shape), half_of(outer.shape), half_of(act.shape),
                      each(pg.shape), whole(ext.shape)],
            out_specs=whole(piece),
        ),
        out_shape=like(piece, jnp.float32),
        compiler_params=grant(24),
        cost_estimate=cost(10, 6),
        name="half_grads",
    )(place, low, inner, outer, act, pg, ext)


def section_kernel(act_ref, low_ref, wt_ref, _, out_ref, token_ref):
    token_ref[...] = jnp.zeros_like(token_ref)
    frame = pl.program_id(0)
    _, rows_low, cols_low, chan = low_ref.shape
    group = rows_at_once(rows_low, cols_low)
    span = group * cols_low
    order = from_side(group, cols_low)
    low = low_ref[0].reshape(-1, chan).astype(jnp.float32)
    mixed = []
    for side in range(4):
        total = low
        for k in range(3):
            total = total + product(act_ref[frame + 2 - k, side], wt_ref[k])
        mixed.append(total.astype(jnp.bfloat16))
    for n in range(rows_low // group):
        block = jnp.concatenate([m[n * span : (n + 1) * span] for m in mixed], axis=0)
        block = product(order, block).astype(jnp.bfloat16)
        out_ref[0, 2 * group * n : 2 * group * (n + 1)] = block.reshape(2 * group, 2 * cols_low, chan)


def section(act_ext, low, wt, before):
    frames, rows_low, cols_low, chan = low.shape
    out = (frames, 2 * rows_low, 2 * cols_low, chan)
    return pl.pallas_call(
        section_kernel,
        grid=(frames,),
        in_specs=[whole(act_ext.shape), each(low.shape), whole(wt.shape), UNREAD],
        out_specs=[each(out), whole(TOKEN.shape)],
        out_shape=[like(out, jnp.bfloat16), TOKEN],
        compiler_params=grant(16),
        cost_estimate=pl.CostEstimate(flops=2 * 2048 * chan * chan * 4, bytes_accessed=3 * 2**20, transcendentals=0),
        name="section",
    )(act_ext, low, wt, before)


def input_kernel(place_ref, pg_ref, inner_ref, outer_ref, cot_ref, ws_ref, _, out_ref, token_ref):
    token_ref[...] = jnp.zeros_like(token_ref)
    _, rows_low, cols_low, chan = out_ref.shape
    group = rows_at_once(rows_low, cols_low)
    span = group * cols_low
    boxes = box(group, cols_low)
    count = rows_low * cols_low
    total = jnp.concatenate(
        [product(boxes, cot_ref[0, 2 * group * n : 2 * group * (n + 1)].reshape(4 * span, chan))
         for n in range(rows_low // group)], axis=0)
    higher = (rows_low + 1, cols_low, chan)
    at = column(higher[0] * cols_low, cols_low, chan)
    own = [pg_ref[0, side].astype(jnp.float32) for side in range(4)]
    odd_place = place_ref[1] == 1
    inner = [inner_ref[0, b].astype(jnp.float32) for b in range(2)]
    outer = [outer_ref[0, b].astype(jnp.float32) for b in range(2)]
    above = [jnp.where(odd_place, inner[b], outer[b]) for b in range(2)]
    below = [jnp.where(odd_place, outer[b], inner[b]) for b in range(2)]
    even = [jnp.concatenate([own[b], below[b]], axis=0) for b in range(2)]
    odd = [jnp.concatenate([above[b], own[2 + b]], axis=0) for b in range(2)]
    for j in range(3):
        pair = []
        for first, second in (even, odd):
            if j == 0:
                value = second + from_right(first, at, cols_low - 1)
            elif j == 1:
                value = first + second
            else:
                value = first + from_left(second, at)
            pair.append(value.reshape(higher))
        top, low = pair
        for i, value in enumerate((low[1:] + top[1:], top[:-1] + low[1:], low[:-1] + top[:-1])):
            value = value.reshape(count, chan)
            high = value.astype(jnp.bfloat16)
            rest = (value - high.astype(jnp.float32)).astype(jnp.bfloat16)
            total = total + product_nt(high, ws_ref[i, j]) + product_nt(rest, ws_ref[i, j])
    out_ref[0] = total.astype(jnp.bfloat16).reshape(rows_low, cols_low, chan)


def input_grads(place, pg, inner, outer, cot, ws, before, low_shape):
    chan = low_shape[-1]
    return pl.pallas_call(
        input_kernel,
        grid=(low_shape[0],),
        in_specs=[SCALAR, each(pg.shape), each(inner.shape), each(outer.shape), each(cot.shape), whole(ws.shape), UNREAD],
        out_specs=[each(low_shape), whole(TOKEN.shape)],
        out_shape=[like(low_shape, jnp.bfloat16), TOKEN],
        compiler_params=grant(20),
        cost_estimate=pl.CostEstimate(flops=2 * 2048 * chan * chan * 6, bytes_accessed=4 * 2**20, transcendentals=0),
        name="input_grads",
    )(place, pg, inner, outer, cot, ws, before)


def place_kernel(place_ref, half_ref, theirs_ref, _, spatial_ref, temporal_ref):
    parts, rows, chan = half_ref.shape
    size = rows // 12
    half = chan // 2
    core = place_ref[0]
    for source, start in ((half_ref, core * half), (theirs_ref, half - core * half)):
        for n in range(parts):
            begin = pl.multiple_of(start + n * size, size)
            for tap in range(12):
                value = source[n, tap * size : (tap + 1) * size, :].astype(jnp.float32)
                if tap < 9:
                    spatial_ref[tap // 3, tap % 3, pl.ds(begin, size), :] = value
                else:
                    temporal_ref[tap - 9, pl.ds(begin, size), :] = value


def put(place, half, theirs, chan, before):
    full = pl.BlockSpec(memory_space=pltpu.VMEM)
    return pl.pallas_call(
        place_kernel,
        in_specs=[SCALAR, full, full, UNREAD],
        out_specs=[full, full],
        out_shape=[jax.ShapeDtypeStruct((3, 3, chan, chan), jnp.float32),
                   jax.ShapeDtypeStruct((3, chan, chan), jnp.float32)],
        compiler_params=grant(10),
        name="place",
    )(place, half, theirs, before)


def add_kernel(mine_ref, theirs_ref, out_ref):
    out_ref[...] = (mine_ref[...] + theirs_ref[...]).astype(jnp.bfloat16)


def add_halves(mine, theirs):
    full = pl.BlockSpec(memory_space=pltpu.VMEM)
    return pl.pallas_call(
        add_kernel,
        in_specs=[full, full],
        out_specs=full,
        out_shape=like(mine.shape, jnp.bfloat16),
        compiler_params=grant(8),
        name="add_halves",
    )(mine, theirs)


def sum_kernel(got_ref, _, out_ref):
    total = got_ref[0].astype(jnp.float32)
    for n in range(1, got_ref.shape[0]):
        total = total + got_ref[n].astype(jnp.float32)
    out_ref[...] = total.astype(jnp.bfloat16)


def sum_parts(got, before):
    full = pl.BlockSpec(memory_space=pltpu.VMEM)
    return pl.pallas_call(
        sum_kernel,
        in_specs=[full, UNREAD],
        out_specs=full,
        out_shape=like(got.shape[1:], jnp.bfloat16),
        compiler_params=grant(4),
        name="sum_parts",
    )(got, before)


def spread_kernel(own_ref, theirs_ref, *refs):
    total = (own_ref[...].astype(jnp.float32) + theirs_ref[...].astype(jnp.float32)).astype(jnp.bfloat16)
    for n in range(refs[-1].shape[0]):
        refs[-1][n] = total


def spread(own, theirs, parts, *before):
    full = pl.BlockSpec(memory_space=pltpu.VMEM)
    return pl.pallas_call(
        spread_kernel,
        in_specs=[full, full] + [UNREAD] * len(before),
        out_specs=full,
        out_shape=like((parts,) + own.shape, jnp.bfloat16),
        compiler_params=grant(4),
        name="spread",
    )(own, theirs, *before)


def on_device(bits, low_frames, spatial_weight, temporal_weight, cotangent):
    low, cot = low_frames[0], cotangent[0]
    frames, rows_low, cols_low, chan = low.shape
    core = lax.axis_index(bits.core).astype(jnp.int32)
    odd = lax.axis_index(bits.axes["height"][-1]).astype(jnp.int32)
    mine, other = jnp.stack([core, odd]), jnp.stack([1 - core, odd])
    parts = 1 << len(bits.near)

    later = bits.shift(cot[:2], "tm", -1)
    inner, outer = bits.rows(low[:, :1], low[:, -1:])
    act, slope, cot_side = forward(mine, low, inner, outer, cot, spatial_weight)
    pg, ext, theirs = backward(
        other, parts, low, inner, outer, act, slope, cot_side, later, temporal_weight
    )
    theirs = bits.swap(theirs, bits.core)
    own = half_grads(mine, parts, low, inner, outer, act, pg, ext)
    kept = add_halves(own, theirs)
    got = bits.exchange(kept)

    edge, pg_inner, pg_outer = edges(mine, low, inner, outer, pg, kept)
    earlier = earlier_act(bits.shift(edge, "tm", 1), spatial_weight)
    pg_inner, pg_outer = bits.pairs(pg_inner, pg_outer)

    total, far = bits.far_sums(sum_parts(got, earlier))
    section_out, section_done = section(jnp.concatenate([earlier, act], axis=0), low, temporal_weight, total)
    totals = spread(total, far, parts, section_done, pg_inner, pg_outer)
    input_grad, input_done = input_grads(
        mine, pg, pg_inner, pg_outer, cot, spatial_weight, totals, low.shape
    )
    half = bits.exchange(totals)
    theirs = bits.swap(half, bits.core)
    spatial_grad, temporal_grad = put(mine, half, theirs, chan, input_done)
    return section_out[None], input_grad[None], spatial_grad, temporal_grad


def solution(mesh):
    bits = Bits(mesh)
    block = P(*(bits.axes[name] for name in ("dp", "tm", "height")), None, None)
    return jax.shard_map(
        functools.partial(on_device, bits),
        mesh=bits.mesh,
        in_specs=(block, P(), P(), block),
        out_specs=(block, block, P(), P()),
        check_vma=False,
    )
```

```python
import functools

import jax
import jax.numpy as jnp
from jax import lax
from jax.experimental import pallas as pl
from jax.experimental.pallas import tpu as pltpu
from jax.sharding import Mesh
from jax.sharding import PartitionSpec as P


class Bits:
    def __init__(self, mesh):
        self.axes = {}
        for name in mesh.axis_names:
            count = mesh.shape[name].bit_length() - 1
            self.axes[name] = tuple(f"{name}{bit}" for bit in reversed(range(count)))
        names = [bit for bits in self.axes.values() for bit in bits]
        self.mesh = Mesh(mesh.devices.reshape([2] * len(names)), tuple(names))
        self.core = next((n for n in names if self.same_chip(n)), self.axes["tm"][-1])
        self.near = []
        for bits in self.axes.values():
            self.near += [b for b in bits if b != self.core][-1:]
        self.far = [n for n in names if n != self.core and n not in self.near]

    def same_chip(self, name):
        at = [1 if n == name else 0 for n in self.mesh.axis_names]
        here = self.mesh.devices[tuple([0] * len(at))]
        there = self.mesh.devices[tuple(at)]
        return tuple(getattr(here, "coords", (0,))) == tuple(getattr(there, "coords", (1,)))

    def swap(self, block, axis):
        return lax.ppermute(block, axis, [(0, 1), (1, 0)])

    def shift(self, block, name, distance):
        axes = self.axes[name]
        devices = range(1 << len(axes))
        route = [(i - distance, i) for i in devices if i - distance in devices]
        return lax.ppermute(block, axes, route)

    def exchange(self, parts):
        return lax.all_to_all(parts, tuple(self.near), 0, 0, tiled=True)

    def pairs(self, inner, outer):
        axes = self.axes["height"]
        low = range(1, (1 << len(axes)) - 1, 2)
        route = [(i, i + 1) for i in low] + [(i + 1, i) for i in low]
        outer = lax.ppermute(outer, axes, route)
        return self.swap(inner, axes[-1]), outer

    def far_sums(self, total):
        for axis in self.far[:-1]:
            total = (total.astype(jnp.float32) + self.swap(total, axis).astype(jnp.float32)).astype(jnp.bfloat16)
        return total, self.swap(total, self.far[-1])


SIDES = ((0, 0), (0, 1), (1, 0), (1, 1))


def grant(mib):
    return pltpu.CompilerParams(vmem_limit_bytes=mib * 2**20)


def product(left, right):
    return jnp.dot(left, right, preferred_element_type=jnp.float32)


def product_nt(left, right):
    return lax.dot_general(left, right, (((1,), (1,)), ((), ())), preferred_element_type=jnp.float32)


def rows_at_once(rows_low, cols_low):
    return max(n for n in (1, 2, 4, 8) if rows_low % n == 0 and (n == 1 or 4 * n * cols_low <= 256))


def by_side(count, cols_low, dtype=jnp.bfloat16):
    size = 4 * count * cols_low
    to = lax.broadcasted_iota(jnp.int32, (size, size), 0)
    at = lax.broadcasted_iota(jnp.int32, (size, size), 1)
    q, rest = to % cols_low, to // cols_low
    p, side = rest % count, rest // count
    return (at == (p * 2 + side // 2) * 2 * cols_low + 2 * q + side % 2).astype(jnp.float32).astype(dtype)


def from_side(count, cols_low, dtype=jnp.bfloat16):
    size = 4 * count * cols_low
    at = lax.broadcasted_iota(jnp.int32, (size, size), 0)
    to = lax.broadcasted_iota(jnp.int32, (size, size), 1)
    q, rest = to % cols_low, to // cols_low
    p, side = rest % count, rest // count
    return (at == (p * 2 + side // 2) * 2 * cols_low + 2 * q + side % 2).astype(jnp.float32).astype(dtype)


def box(count, cols_low, dtype=jnp.bfloat16):
    size = 4 * count * cols_low
    to = lax.broadcasted_iota(jnp.int32, (size // 4, size), 0)
    at = lax.broadcasted_iota(jnp.int32, (size // 4, size), 1)
    p, q = at // (4 * cols_low), at % (2 * cols_low) // 2
    return (to == p * cols_low + q).astype(jnp.float32).astype(dtype)


def column(rows, cols_low, chan):
    return lax.broadcasted_iota(jnp.int32, (rows, chan), 0) % cols_low


def from_left(x, at):
    return jnp.where(at == 0, 0.0, pltpu.roll(x, 1, 0))


def from_right(x, at, last):
    return jnp.where(at == last, 0.0, pltpu.roll(x, x.shape[0] - 1, 0))


def sort_columns(source, target, cols_low):
    rows_low, chan = source.shape[0] // 2, source.shape[2]
    group = rows_at_once(rows_low, cols_low)
    span = group * cols_low
    order = by_side(group, cols_low)
    for n in range(rows_low // group):
        block = source[2 * group * n : 2 * group * (n + 1)].reshape(4 * span, chan)
        block = product(order, block).astype(jnp.bfloat16).reshape(4, span, chan)
        target[:, n * span : (n + 1) * span, :] = block


def tall(place_ref, low_ref, inner_ref, outer_ref):
    odd = place_ref[1] == 1
    up = jnp.where(odd, inner_ref[0], outer_ref[0])
    down = jnp.where(odd, outer_ref[0], inner_ref[0])
    return jnp.concatenate([up, low_ref[0], down], axis=0)


def spatial(low, ws_ref):
    rows_low, cols_low, chan = low.shape[0] - 2, low.shape[1], low.shape[2]
    count = rows_low * cols_low
    flat = low.reshape(-1, chan)
    rows = [[], []]
    for j in range(3):
        taps = [product(flat, ws_ref[i, j]).reshape(low.shape) for i in range(3)]
        even = taps[0][:rows_low] + (taps[1] + taps[2])[1 : rows_low + 1]
        odd = (taps[0] + taps[1])[1 : rows_low + 1] + taps[2][2:]
        rows[0].append(even.reshape(count, chan))
        rows[1].append(odd.reshape(count, chan))
    at = column(count, cols_low, chan)
    for first, second, third in rows:
        yield from_left(first, at) + (second + third)
        yield (first + second) + from_right(third, at, cols_low - 1)


def forward_kernel(place_ref, low_ref, inner_ref, outer_ref, ws_ref, act_ref, slope_ref):
    low = tall(place_ref, low_ref, inner_ref, outer_ref)
    for side, pre in enumerate(spatial(low, ws_ref)):
        sig = jax.nn.sigmoid(pre)
        act_ref[0, side] = (pre * sig).astype(jnp.bfloat16)
        slope_ref[0, side] = sig * (1.0 + pre * (1.0 - sig))


def act_kernel(low_ref, ws_ref, _, act_ref):
    for side, pre in enumerate(spatial(low_ref[0], ws_ref)):
        act_ref[0, side] = (pre * jax.nn.sigmoid(pre)).astype(jnp.bfloat16)


def add_sums(low, act, pg, cots, out_ref):
    rows_low, cols_low, half = low.shape[0] - 2, low.shape[1], low.shape[2]
    count = rows_low * cols_low
    sums = []
    wide = low.reshape(-1, half).astype(jnp.float32)
    at = column(wide.shape[0], cols_low, half)
    moved = [from_left(wide, at), wide, from_right(wide, at, cols_low - 1)]
    turned = {}
    for dc in range(3):
        view = moved[dc].astype(jnp.bfloat16).reshape(low.shape)
        for dr in range(3):
            turned[dr - 1, dc - 1] = view[dr : dr + rows_low].reshape(count, half).T
    for i in range(3):
        for j in range(3):
            left = jnp.concatenate([turned[(a + i - 1) // 2, (b + j - 1) // 2] for a, b in SIDES], axis=1)
            sums.append(product(left, pg))
    act = act.T
    for cot in cots:
        sums.append(product(act, cot))

    def each_piece(store):
        parts = out_ref.shape[0]
        size = half // parts
        for tap, value in enumerate(sums):
            for n in range(parts):
                store(n, slice(tap * size, (tap + 1) * size), value[n * size : (n + 1) * size])

    @pl.when(pl.program_id(0) == 0)
    def _():
        def store(n, rows, value):
            out_ref[n, rows, :] = value

        each_piece(store)

    @pl.when(pl.program_id(0) > 0)
    def _():
        def store(n, rows, value):
            out_ref[n, rows, :] += value

        each_piece(store)


def backward_kernel(place_ref, low_ref, inner_ref, outer_ref, act_ref, slope_ref, cot_ref, later_ref, wt_ref, pg_ref, ext_ref, out_ref):
    frame = pl.program_id(0)
    frames, _, count, chan = cot_ref.shape
    cols_low = low_ref.shape[2]

    @pl.when(frame == 0)
    def _():
        ext_ref[:frames] = cot_ref[...]
        for n in range(2):
            sort_columns(later_ref.at[n], ext_ref.at[frames + n], cols_low)

    pgs = []
    for side in range(4):
        act_grad = product_nt(ext_ref[frame, side], wt_ref[0])
        for k in (1, 2):
            act_grad = act_grad + product_nt(ext_ref[frame + k, side], wt_ref[k])
        pgs.append((act_grad * slope_ref[0, side]).astype(jnp.bfloat16))
        pg_ref[0, side] = pgs[side]
    low = tall(place_ref, low_ref, inner_ref, outer_ref)
    act = act_ref[0].reshape(4 * count, -1)
    cots = [ext_ref[frame + k].reshape(4 * count, chan) for k in range(3)]
    add_sums(low, act, jnp.concatenate(pgs, axis=0), cots, out_ref)


def half_kernel(place_ref, low_ref, inner_ref, outer_ref, act_ref, pg_ref, ext_ref, out_ref):
    frame = pl.program_id(0)
    _, _, count, chan = pg_ref.shape
    low = tall(place_ref, low_ref, inner_ref, outer_ref)
    act = act_ref[0].reshape(4 * count, -1)
    cots = [ext_ref[frame + k].reshape(4 * count, chan) for k in range(3)]
    add_sums(low, act, pg_ref[0].reshape(4 * count, chan), cots, out_ref)


def whole(shape):
    return pl.BlockSpec(shape, lambda f, *_: (0,) * len(shape))


def each(shape):
    return pl.BlockSpec((1,) + tuple(shape[1:]), lambda f, *_: (f,) + (0,) * (len(shape) - 1))


def half_of(shape):
    block = (1,) + tuple(shape[1:-1]) + (shape[-1] // 2,)
    return pl.BlockSpec(block, lambda f, side: (f,) + (0,) * (len(shape) - 2) + (side[0],))


SCALAR = pl.BlockSpec(memory_space=pltpu.SMEM)
UNREAD = pl.BlockSpec(memory_space=pl.ANY)


def like(shape, dtype):
    return jax.ShapeDtypeStruct(shape, dtype)


TOKEN = like((8, 128), jnp.float32)


def cost(units, mib):
    return pl.CostEstimate(flops=units * 2 * 2048 * 256 * 256, bytes_accessed=mib * 2**20, transcendentals=0)


def in_hbm(array):
    return pltpu.with_memory_space_constraint(array, pltpu.HBM)


FULL = pl.BlockSpec(memory_space=pltpu.VMEM)


def first_kernel(place_ref, low_ref, cot_ref, inner_ref, outer_ref, later_ref, sems):
    last = low_ref.shape[1] - 1
    odd = place_ref[1]
    copies = [
        pltpu.make_async_copy(cot_ref.at[0:2], later_ref, sems.at[0]),
        pltpu.make_async_copy(low_ref.at[:, pl.ds(last * (1 - odd), 1)], inner_ref, sems.at[1]),
        pltpu.make_async_copy(low_ref.at[:, pl.ds(last * odd, 1)], outer_ref, sems.at[2]),
    ]
    for copy in copies:
        copy.start()
    for copy in copies:
        copy.wait()


def first_messages(place, low, cot):
    row = like(low[:, :1].shape, low.dtype)
    return pl.pallas_call(
        first_kernel,
        in_specs=[SCALAR, UNREAD, UNREAD],
        out_specs=[FULL] * 3,
        out_shape=[row, row, like(cot[:2].shape, cot.dtype)],
        scratch_shapes=[pltpu.SemaphoreType.DMA((3,))],
        compiler_params=grant(4),
        name="first_messages",
    )(place, in_hbm(low), in_hbm(cot))


def load_kernel(low_hbm, cot_hbm, ws_hbm, wt_hbm, low_ref, ws_ref, wt_ref, side_ref, cot_ref, sems):
    frames, cols_low = low_ref.shape[0], low_ref.shape[2]
    copies = [pltpu.make_async_copy(cot_hbm.at[n], cot_ref.at[n], sems.at[n]) for n in range(frames)]
    pairs = ((low_hbm, low_ref), (ws_hbm, ws_ref), (wt_hbm, wt_ref))
    copies += [pltpu.make_async_copy(a, b, sems.at[frames + n]) for n, (a, b) in enumerate(pairs)]
    for copy in copies:
        copy.start()
    for n in range(frames):
        copies[n].wait()
        sort_columns(cot_ref.at[n], side_ref.at[n], cols_low)
    for copy in copies[frames:]:
        copy.wait()


def load(low, cot, ws, wt):
    frames, rows_low, cols_low, chan = low.shape
    return pl.pallas_call(
        load_kernel,
        in_specs=[UNREAD] * 4,
        out_specs=[FULL] * 4,
        out_shape=[like(low.shape, low.dtype), like(ws.shape, ws.dtype), like(wt.shape, wt.dtype),
                   like((frames, 4, rows_low * cols_low, chan), jnp.bfloat16)],
        scratch_shapes=[pltpu.VMEM(cot.shape, cot.dtype), pltpu.SemaphoreType.DMA((frames + 3,))],
        compiler_params=grant(12),
        cost_estimate=cost(2, 4),
        name="load",
    )(in_hbm(low), in_hbm(cot), in_hbm(ws), in_hbm(wt))


def nothing(*_):
    pass


def after(arrays, *before):
    return pl.pallas_call(
        nothing,
        in_specs=[UNREAD] * (len(arrays) + len(before)),
        out_specs=[UNREAD] * len(arrays),
        out_shape=[like(a.shape, a.dtype) for a in arrays],
        input_output_aliases={n: n for n in range(len(arrays))},
        name="after",
    )(*arrays, *before)


def forward(place, low, inner, outer, ws):
    frames, rows_low, cols_low, chan = low.shape
    side = (frames, 4, rows_low * cols_low, chan)
    return pl.pallas_call(
        forward_kernel,
        grid=(frames,),
        in_specs=[SCALAR, each(low.shape), each(inner.shape), each(outer.shape), whole(ws.shape)],
        out_specs=[each(side)] * 2,
        out_shape=[like(side, jnp.bfloat16), like(side, jnp.float32)],
        compiler_params=grant(20),
        cost_estimate=cost(10, 8),
        name="forward",
    )(place, low, inner, outer, ws)


def edges_kernel(place_ref, low_ref, inner_ref, outer_ref, pg_ref, _, tall_ref, pg_inner, pg_outer):
    cols_low = low_ref.shape[2]
    first = low_ref.shape[0] - tall_ref.shape[0]
    for n in range(tall_ref.shape[0]):
        at = pl.ds(first + n, 1)
        tall_ref[n] = tall(place_ref, low_ref.at[at], inner_ref.at[at], outer_ref.at[at])
    odd = place_ref[1] == 1
    top, bottom = pg_ref[:, :2, :cols_low, :], pg_ref[:, 2:, -cols_low:, :]
    pg_inner[...] = jnp.where(odd, top, bottom)
    pg_outer[...] = jnp.where(odd, bottom, top)


def edges(place, low, inner, outer, pg, before):
    frames, rows_low, cols_low, chan = low.shape
    full = pl.BlockSpec(memory_space=pltpu.VMEM)
    rows = like((frames, 2, cols_low, chan), jnp.bfloat16)
    return pl.pallas_call(
        edges_kernel,
        in_specs=[SCALAR, full, full, full, full, UNREAD],
        out_specs=[full] * 3,
        out_shape=[like((2, rows_low + 2, cols_low, chan), jnp.bfloat16), rows, rows],
        compiler_params=grant(8),
        name="edges",
    )(place, low, inner, outer, pg, before)


def earlier_act(low, ws, before):
    frames, rows_tall, cols_low, chan = low.shape
    side = (frames, 4, (rows_tall - 2) * cols_low, chan)
    return pl.pallas_call(
        act_kernel,
        grid=(frames,),
        in_specs=[each(low.shape), whole(ws.shape), UNREAD],
        out_specs=each(side),
        out_shape=like(side, jnp.bfloat16),
        compiler_params=grant(16),
        cost_estimate=cost(4, 3),
        name="earlier_act",
    )(low, ws, before)


def backward(place, parts, low, inner, outer, act, slope, cot, later, wt):
    frames, _, count, chan = act.shape
    ext = (frames + 2,) + act.shape[1:]
    piece = (parts, 12 * (chan // (2 * parts)), chan)
    return pl.pallas_call(
        backward_kernel,
        grid_spec=pltpu.PrefetchScalarGridSpec(
            num_scalar_prefetch=1,
            grid=(frames,),
            in_specs=[half_of(low.shape), half_of(inner.shape), half_of(outer.shape), half_of(act.shape),
                      each(slope.shape), whole(cot.shape), whole(later.shape), whole(wt.shape)],
            out_specs=[each(act.shape), whole(ext), whole(piece)],
        ),
        out_shape=[like(act.shape, jnp.bfloat16), like(ext, jnp.bfloat16), like(piece, jnp.float32)],
        compiler_params=grant(28),
        cost_estimate=cost(15, 10),
        name="backward",
    )(place, low, inner, outer, act, slope, cot, later, wt)


def half_grads(place, parts, low, inner, outer, act, pg, ext):
    frames, _, _, chan = act.shape
    piece = (parts, 12 * (chan // (2 * parts)), chan)
    return pl.pallas_call(
        half_kernel,
        grid_spec=pltpu.PrefetchScalarGridSpec(
            num_scalar_prefetch=1,
            grid=(frames,),
            in_specs=[half_of(low.shape), half_of(inner.shape), half_of(outer.shape), half_of(act.shape),
                      each(pg.shape), whole(ext.shape)],
            out_specs=whole(piece),
        ),
        out_shape=like(piece, jnp.float32),
        compiler_params=grant(24),
        cost_estimate=cost(10, 6),
        name="half_grads",
    )(place, low, inner, outer, act, pg, ext)


def section_kernel(act_ref, low_ref, wt_ref, _, out_ref, token_ref):
    token_ref[...] = jnp.zeros_like(token_ref)
    frame = pl.program_id(0)
    _, rows_low, cols_low, chan = low_ref.shape
    group = rows_at_once(rows_low, cols_low)
    span = group * cols_low
    order = from_side(group, cols_low)
    low = low_ref[0].reshape(-1, chan).astype(jnp.float32)
    mixed = []
    for side in range(4):
        total = low
        for k in range(3):
            total = total + product(act_ref[frame + 2 - k, side], wt_ref[k])
        mixed.append(total.astype(jnp.bfloat16))
    for n in range(rows_low // group):
        block = jnp.concatenate([m[n * span : (n + 1) * span] for m in mixed], axis=0)
        block = product(order, block).astype(jnp.bfloat16)
        out_ref[0, 2 * group * n : 2 * group * (n + 1)] = block.reshape(2 * group, 2 * cols_low, chan)


def section(act_ext, low, wt, before):
    frames, rows_low, cols_low, chan = low.shape
    out = (frames, 2 * rows_low, 2 * cols_low, chan)
    return pl.pallas_call(
        section_kernel,
        grid=(frames,),
        in_specs=[whole(act_ext.shape), each(low.shape), whole(wt.shape), UNREAD],
        out_specs=[each(out), whole(TOKEN.shape)],
        out_shape=[like(out, jnp.bfloat16), TOKEN],
        compiler_params=grant(16),
        cost_estimate=pl.CostEstimate(flops=2 * 2048 * chan * chan * 4, bytes_accessed=3 * 2**20, transcendentals=0),
        name="section",
    )(act_ext, low, wt, before)


def input_kernel(place_ref, pg_ref, inner_ref, outer_ref, cot_ref, ws_ref, _, out_ref, token_ref):
    token_ref[...] = jnp.zeros_like(token_ref)
    _, rows_low, cols_low, chan = out_ref.shape
    group = rows_at_once(rows_low, cols_low)
    span = group * cols_low
    boxes = box(group, cols_low)
    count = rows_low * cols_low
    total = jnp.concatenate(
        [product(boxes, cot_ref[0, 2 * group * n : 2 * group * (n + 1)].reshape(4 * span, chan))
         for n in range(rows_low // group)], axis=0)
    higher = (rows_low + 1, cols_low, chan)
    at = column(higher[0] * cols_low, cols_low, chan)
    own = [pg_ref[0, side].astype(jnp.float32) for side in range(4)]
    odd_place = place_ref[1] == 1
    inner = [inner_ref[0, b].astype(jnp.float32) for b in range(2)]
    outer = [outer_ref[0, b].astype(jnp.float32) for b in range(2)]
    above = [jnp.where(odd_place, inner[b], outer[b]) for b in range(2)]
    below = [jnp.where(odd_place, outer[b], inner[b]) for b in range(2)]
    even = [jnp.concatenate([own[b], below[b]], axis=0) for b in range(2)]
    odd = [jnp.concatenate([above[b], own[2 + b]], axis=0) for b in range(2)]
    for j in range(3):
        pair = []
        for first, second in (even, odd):
            if j == 0:
                value = second + from_right(first, at, cols_low - 1)
            elif j == 1:
                value = first + second
            else:
                value = first + from_left(second, at)
            pair.append(value.reshape(higher))
        top, low = pair
        for i, value in enumerate((low[1:] + top[1:], top[:-1] + low[1:], low[:-1] + top[:-1])):
            value = value.reshape(count, chan)
            high = value.astype(jnp.bfloat16)
            rest = (value - high.astype(jnp.float32)).astype(jnp.bfloat16)
            total = total + product_nt(high, ws_ref[i, j]) + product_nt(rest, ws_ref[i, j])
    out_ref[0] = total.astype(jnp.bfloat16).reshape(rows_low, cols_low, chan)


def input_grads(place, pg, inner, outer, cot, ws, before, low_shape):
    chan = low_shape[-1]
    return pl.pallas_call(
        input_kernel,
        grid=(low_shape[0],),
        in_specs=[SCALAR, each(pg.shape), each(inner.shape), each(outer.shape), each(cot.shape), whole(ws.shape), UNREAD],
        out_specs=[each(low_shape), whole(TOKEN.shape)],
        out_shape=[like(low_shape, jnp.bfloat16), TOKEN],
        compiler_params=grant(20),
        cost_estimate=pl.CostEstimate(flops=2 * 2048 * chan * chan * 6, bytes_accessed=4 * 2**20, transcendentals=0),
        name="input_grads",
    )(place, pg, inner, outer, cot, ws, before)


def put_kernel(place_ref, half_ref, *refs):
    spatial_ref, temporal_ref, wide, sems = refs[-4:]
    parts, rows, chan = half_ref.shape
    size, half = rows // 12, chan // 2
    for tap in range(12):
        for n in range(parts):
            wide[tap, n * size : (n + 1) * size, :] = half_ref[n, tap * size : (tap + 1) * size, :].astype(jnp.float32)
    to = pl.ds(pl.multiple_of(place_ref[0] * half, half), half)
    copies = []
    for tap in range(12):
        if tap < 9:
            target = spatial_ref.at[tap // 3, tap % 3, to]
        else:
            target = temporal_ref.at[tap - 9, to]
        copies.append(pltpu.make_async_copy(wide.at[tap], target, sems.at[tap]))
        copies[-1].start()
    for copy in copies:
        copy.wait()


def put(place, half, *done):
    chan = half.shape[-1]
    hbm = pl.BlockSpec(memory_space=pltpu.HBM)
    return pl.pallas_call(
        put_kernel,
        in_specs=[SCALAR, FULL] + [hbm] * len(done),
        out_specs=[hbm, hbm],
        out_shape=[like((3, 3, chan, chan), jnp.float32), like((3, chan, chan), jnp.float32)],
        input_output_aliases={2 + n: n for n in range(len(done))},
        scratch_shapes=[pltpu.VMEM((12, chan // 2, chan), jnp.float32), pltpu.SemaphoreType.DMA((12,))],
        compiler_params=grant(6),
        name="put",
    )(place, half, *done)


def add_kernel(mine_ref, theirs_ref, out_ref):
    out_ref[...] = (mine_ref[...] + theirs_ref[...]).astype(jnp.bfloat16)


def add_halves(mine, theirs):
    full = pl.BlockSpec(memory_space=pltpu.VMEM)
    return pl.pallas_call(
        add_kernel,
        in_specs=[full, full],
        out_specs=full,
        out_shape=like(mine.shape, jnp.bfloat16),
        compiler_params=grant(8),
        name="add_halves",
    )(mine, theirs)


def sum_kernel(got_ref, out_ref):
    total = got_ref[0].astype(jnp.float32)
    for n in range(1, got_ref.shape[0]):
        total = total + got_ref[n].astype(jnp.float32)
    out_ref[...] = total.astype(jnp.bfloat16)


def sum_parts(got):
    full = pl.BlockSpec(memory_space=pltpu.VMEM)
    return pl.pallas_call(
        sum_kernel,
        in_specs=[full],
        out_specs=full,
        out_shape=like(got.shape[1:], jnp.bfloat16),
        compiler_params=grant(4),
        name="sum_parts",
    )(got)


def spread_kernel(own_ref, theirs_ref, *refs):
    total = (own_ref[...].astype(jnp.float32) + theirs_ref[...].astype(jnp.float32)).astype(jnp.bfloat16)
    for n in range(refs[-1].shape[0]):
        refs[-1][n] = total


def spread(own, theirs, parts, *before):
    full = pl.BlockSpec(memory_space=pltpu.VMEM)
    return pl.pallas_call(
        spread_kernel,
        in_specs=[full, full] + [UNREAD] * len(before),
        out_specs=full,
        out_shape=like((parts,) + own.shape, jnp.bfloat16),
        compiler_params=grant(4),
        name="spread",
    )(own, theirs, *before)


def on_device(bits, low_frames, spatial_weight, temporal_weight, cotangent):
    low, cot = low_frames[0], cotangent[0]
    frames, rows_low, cols_low, chan = low.shape
    core = lax.axis_index(bits.core).astype(jnp.int32)
    odd = lax.axis_index(bits.axes["height"][-1]).astype(jnp.int32)
    mine, other = jnp.stack([core, odd]), jnp.stack([1 - core, odd])
    parts = 1 << len(bits.near)

    inner, outer, later = first_messages(mine, low, cot)
    later = bits.shift(later, "tm", -1)
    inner, outer = bits.pairs(inner, outer)
    low, ws, wt, cot_side = load(low, cot, spatial_weight, temporal_weight)
    act, slope = forward(mine, low, inner, outer, ws)
    pg, ext, theirs = backward(other, parts, low, inner, outer, act, slope, cot_side, later, wt)
    theirs = bits.swap(theirs, bits.core)
    own = half_grads(mine, parts, low, inner, outer, act, pg, ext)
    kept = add_halves(own, theirs)
    total = sum_parts(bits.exchange(kept))
    messages = after(edges(mine, low, inner, outer, pg, kept), total)
    total, far = bits.far_sums(total)
    edge, pg_inner, pg_outer = messages
    edge = bits.shift(edge, "tm", 1)
    pg_inner, pg_outer = bits.pairs(pg_inner, pg_outer)
    totals = spread(total, far, parts)
    earlier = earlier_act(edge, ws, totals)
    section_out, section_done = section(jnp.concatenate([earlier, act], axis=0), low, wt, totals)
    input_grad, input_done = input_grads(mine, pg, pg_inner, pg_outer, cot, ws, totals, low.shape)
    half, = after([bits.exchange(totals)], section_done, input_done)
    theirs = bits.swap(half, bits.core)
    spatial_grad, temporal_grad = put(other, theirs, *put(mine, half))
    return section_out[None], input_grad[None], spatial_grad, temporal_grad


def solution(mesh):
    bits = Bits(mesh)
    block = P(*(bits.axes[name] for name in ("dp", "tm", "height")), None, None)
    return jax.shard_map(
        functools.partial(on_device, bits),
        mesh=bits.mesh,
        in_specs=(block, P(), P(), block),
        out_specs=(block, block, P(), P()),
        check_vma=False,
    )
```

```python
import functools

import jax
import jax.numpy as jnp
from jax import lax
from jax.experimental import pallas as pl
from jax.experimental.pallas import tpu as pltpu
from jax.sharding import Mesh
from jax.sharding import PartitionSpec as P


class Bits:
    def __init__(self, mesh):
        self.axes = {}
        for name in mesh.axis_names:
            count = mesh.shape[name].bit_length() - 1
            self.axes[name] = tuple(f"{name}{bit}" for bit in reversed(range(count)))
        names = [bit for bits in self.axes.values() for bit in bits]
        self.mesh = Mesh(mesh.devices.reshape([2] * len(names)), tuple(names))
        self.core = next((n for n in names if self.same_chip(n)), self.axes["tm"][-1])
        self.near = []
        for bits in self.axes.values():
            self.near += [b for b in bits if b != self.core][-1:]
        self.far = [n for n in names if n != self.core and n not in self.near]

    def same_chip(self, name):
        at = [1 if n == name else 0 for n in self.mesh.axis_names]
        here = self.mesh.devices[tuple([0] * len(at))]
        there = self.mesh.devices[tuple(at)]
        return tuple(getattr(here, "coords", (0,))) == tuple(getattr(there, "coords", (1,)))

    def swap(self, block, axis):
        return lax.ppermute(block, axis, [(0, 1), (1, 0)])

    def shift(self, block, name, distance):
        axes = self.axes[name]
        devices = range(1 << len(axes))
        route = [(i - distance, i) for i in devices if i - distance in devices]
        return lax.ppermute(block, axes, route)

    def exchange(self, parts):
        return lax.all_to_all(parts, tuple(self.near), 0, 0, tiled=True)

    def pairs(self, inner, outer):
        axes = self.axes["height"]
        low = range(1, (1 << len(axes)) - 1, 2)
        route = [(i, i + 1) for i in low] + [(i + 1, i) for i in low]
        outer = lax.ppermute(outer, axes, route)
        return self.swap(inner, axes[-1]), outer

    def far_sums(self, total):
        for axis in self.far[:-1]:
            total = (total.astype(jnp.float32) + self.swap(total, axis).astype(jnp.float32)).astype(jnp.bfloat16)
        return total, self.swap(total, self.far[-1])


SIDES = ((0, 0), (0, 1), (1, 0), (1, 1))


def grant(mib):
    return pltpu.CompilerParams(vmem_limit_bytes=mib * 2**20)


def product(left, right):
    return jnp.dot(left, right, preferred_element_type=jnp.float32)


def product_nt(left, right):
    return lax.dot_general(left, right, (((1,), (1,)), ((), ())), preferred_element_type=jnp.float32)


def rows_at_once(rows_low, cols_low):
    return max(n for n in (1, 2, 4, 8) if rows_low % n == 0 and (n == 1 or 4 * n * cols_low <= 256))


def by_side(count, cols_low, dtype=jnp.bfloat16):
    size = 4 * count * cols_low
    to = lax.broadcasted_iota(jnp.int32, (size, size), 0)
    at = lax.broadcasted_iota(jnp.int32, (size, size), 1)
    q, rest = to % cols_low, to // cols_low
    p, side = rest % count, rest // count
    return (at == (p * 2 + side // 2) * 2 * cols_low + 2 * q + side % 2).astype(jnp.float32).astype(dtype)


def from_side(count, cols_low, dtype=jnp.bfloat16):
    size = 4 * count * cols_low
    at = lax.broadcasted_iota(jnp.int32, (size, size), 0)
    to = lax.broadcasted_iota(jnp.int32, (size, size), 1)
    q, rest = to % cols_low, to // cols_low
    p, side = rest % count, rest // count
    return (at == (p * 2 + side // 2) * 2 * cols_low + 2 * q + side % 2).astype(jnp.float32).astype(dtype)


def box(count, cols_low, dtype=jnp.bfloat16):
    size = 4 * count * cols_low
    to = lax.broadcasted_iota(jnp.int32, (size // 4, size), 0)
    at = lax.broadcasted_iota(jnp.int32, (size // 4, size), 1)
    p, q = at // (4 * cols_low), at % (2 * cols_low) // 2
    return (to == p * cols_low + q).astype(jnp.float32).astype(dtype)


def column(rows, cols_low, chan):
    return lax.broadcasted_iota(jnp.int32, (rows, chan), 0) % cols_low


def from_left(x, at):
    return jnp.where(at == 0, 0.0, pltpu.roll(x, 1, 0))


def from_right(x, at, last):
    return jnp.where(at == last, 0.0, pltpu.roll(x, x.shape[0] - 1, 0))


def sort_columns(source, target, cols_low):
    rows_low, chan = source.shape[0] // 2, source.shape[2]
    group = rows_at_once(rows_low, cols_low)
    span = group * cols_low
    order = by_side(group, cols_low)
    for n in range(rows_low // group):
        block = source[2 * group * n : 2 * group * (n + 1)].reshape(4 * span, chan)
        block = product(order, block).astype(jnp.bfloat16).reshape(4, span, chan)
        target[:, n * span : (n + 1) * span, :] = block


def tall(place_ref, low_ref, inner_ref, outer_ref):
    odd = place_ref[1] == 1
    up = jnp.where(odd, inner_ref[0], outer_ref[0])
    down = jnp.where(odd, outer_ref[0], inner_ref[0])
    return jnp.concatenate([up, low_ref[0], down], axis=0)


def spatial(low, ws_ref):
    rows_low, cols_low, chan = low.shape[0] - 2, low.shape[1], low.shape[2]
    count = rows_low * cols_low
    flat = low.reshape(-1, chan)
    rows = [[], []]
    for j in range(3):
        taps = [product(flat, ws_ref[i, j]).reshape(low.shape) for i in range(3)]
        even = taps[0][:rows_low] + (taps[1] + taps[2])[1 : rows_low + 1]
        odd = (taps[0] + taps[1])[1 : rows_low + 1] + taps[2][2:]
        rows[0].append(even.reshape(count, chan))
        rows[1].append(odd.reshape(count, chan))
    at = column(count, cols_low, chan)
    for first, second, third in rows:
        yield from_left(first, at) + (second + third)
        yield (first + second) + from_right(third, at, cols_low - 1)


def forward_kernel(place_ref, low_ref, inner_ref, outer_ref, ws_ref, act_ref, slope_ref):
    low = tall(place_ref, low_ref, inner_ref, outer_ref)
    for side, pre in enumerate(spatial(low, ws_ref)):
        sig = jax.nn.sigmoid(pre)
        act_ref[0, side] = (pre * sig).astype(jnp.bfloat16)
        slope_ref[0, side] = sig * (1.0 + pre * (1.0 - sig))


def act_kernel(low_ref, ws_ref, act_ref):
    for side, pre in enumerate(spatial(low_ref[0], ws_ref)):
        act_ref[0, side] = (pre * jax.nn.sigmoid(pre)).astype(jnp.bfloat16)


def add_sums(low, act, pg, cots, out_ref):
    rows_low, cols_low, half = low.shape[0] - 2, low.shape[1], low.shape[2]
    count = rows_low * cols_low
    sums = []
    wide = low.reshape(-1, half).astype(jnp.float32)
    at = column(wide.shape[0], cols_low, half)
    moved = [from_left(wide, at), wide, from_right(wide, at, cols_low - 1)]
    turned = {}
    for dc in range(3):
        view = moved[dc].astype(jnp.bfloat16).reshape(low.shape)
        for dr in range(3):
            turned[dr - 1, dc - 1] = view[dr : dr + rows_low].reshape(count, half).T
    for i in range(3):
        for j in range(3):
            left = jnp.concatenate([turned[(a + i - 1) // 2, (b + j - 1) // 2] for a, b in SIDES], axis=1)
            sums.append(product(left, pg))
    act = act.T
    for cot in cots:
        sums.append(product(act, cot))

    def each_piece(store):
        parts = out_ref.shape[0]
        size = half // parts
        for tap, value in enumerate(sums):
            for n in range(parts):
                store(n, slice(tap * size, (tap + 1) * size), value[n * size : (n + 1) * size])

    @pl.when(pl.program_id(0) == 0)
    def _():
        def store(n, rows, value):
            out_ref[n, rows, :] = value

        each_piece(store)

    @pl.when(pl.program_id(0) > 0)
    def _():
        def store(n, rows, value):
            out_ref[n, rows, :] += value

        each_piece(store)


def backward_kernel(place_ref, low_ref, inner_ref, outer_ref, act_ref, slope_ref, cot_ref, later_ref, wt_ref, pg_ref, ext_ref, out_ref):
    frame = pl.program_id(0)
    frames, _, count, chan = cot_ref.shape
    cols_low = low_ref.shape[2]

    @pl.when(frame == 0)
    def _():
        ext_ref[:frames] = cot_ref[...]
        for n in range(2):
            sort_columns(later_ref.at[n], ext_ref.at[frames + n], cols_low)

    pgs = []
    for side in range(4):
        act_grad = product_nt(ext_ref[frame, side], wt_ref[0])
        for k in (1, 2):
            act_grad = act_grad + product_nt(ext_ref[frame + k, side], wt_ref[k])
        pgs.append((act_grad * slope_ref[0, side]).astype(jnp.bfloat16))
        pg_ref[0, side] = pgs[side]
    low = tall(place_ref, low_ref, inner_ref, outer_ref)
    act = act_ref[0].reshape(4 * count, -1)
    cots = [ext_ref[frame + k].reshape(4 * count, chan) for k in range(3)]
    add_sums(low, act, jnp.concatenate(pgs, axis=0), cots, out_ref)


def half_kernel(place_ref, low_ref, inner_ref, outer_ref, act_ref, pg_ref, ext_ref, out_ref):
    frame = pl.program_id(0)
    _, _, count, chan = pg_ref.shape
    low = tall(place_ref, low_ref, inner_ref, outer_ref)
    act = act_ref[0].reshape(4 * count, -1)
    cots = [ext_ref[frame + k].reshape(4 * count, chan) for k in range(3)]
    add_sums(low, act, pg_ref[0].reshape(4 * count, chan), cots, out_ref)


def whole(shape):
    return pl.BlockSpec(shape, lambda f, *_: (0,) * len(shape))


def each(shape):
    return pl.BlockSpec((1,) + tuple(shape[1:]), lambda f, *_: (f,) + (0,) * (len(shape) - 1))


def half_of(shape):
    block = (1,) + tuple(shape[1:-1]) + (shape[-1] // 2,)
    return pl.BlockSpec(block, lambda f, side: (f,) + (0,) * (len(shape) - 2) + (side[0],))


SCALAR = pl.BlockSpec(memory_space=pltpu.SMEM)
UNREAD = pl.BlockSpec(memory_space=pl.ANY)


def like(shape, dtype):
    return jax.ShapeDtypeStruct(shape, dtype)


TOKEN = like((8, 128), jnp.float32)


def cost(units, mib):
    return pl.CostEstimate(flops=units * 2 * 2048 * 256 * 256, bytes_accessed=mib * 2**20, transcendentals=0)


def in_hbm(array):
    return pltpu.with_memory_space_constraint(array, pltpu.HBM)


FULL = pl.BlockSpec(memory_space=pltpu.VMEM)


def first_kernel(place_ref, low_ref, cot_ref, inner_ref, outer_ref, later_ref, sems):
    last = low_ref.shape[1] - 1
    odd = place_ref[1]
    copies = [
        pltpu.make_async_copy(cot_ref.at[0:2], later_ref, sems.at[0]),
        pltpu.make_async_copy(low_ref.at[:, pl.ds(last * (1 - odd), 1)], inner_ref, sems.at[1]),
        pltpu.make_async_copy(low_ref.at[:, pl.ds(last * odd, 1)], outer_ref, sems.at[2]),
    ]
    for copy in copies:
        copy.start()
    for copy in copies:
        copy.wait()


def first_messages(place, low, cot):
    row = like(low[:, :1].shape, low.dtype)
    return pl.pallas_call(
        first_kernel,
        in_specs=[SCALAR, UNREAD, UNREAD],
        out_specs=[FULL] * 3,
        out_shape=[row, row, like(cot[:2].shape, cot.dtype)],
        scratch_shapes=[pltpu.SemaphoreType.DMA((3,))],
        compiler_params=grant(4),
        name="first_messages",
    )(place, in_hbm(low), in_hbm(cot))


def load_kernel(low_hbm, cot_hbm, ws_hbm, wt_hbm, low_ref, ws_ref, wt_ref, side_ref, cot_ref, sems):
    frames, cols_low = low_ref.shape[0], low_ref.shape[2]
    copies = [pltpu.make_async_copy(cot_hbm.at[n], cot_ref.at[n], sems.at[n]) for n in range(frames)]
    pairs = ((low_hbm, low_ref), (ws_hbm, ws_ref), (wt_hbm, wt_ref))
    copies += [pltpu.make_async_copy(a, b, sems.at[frames + n]) for n, (a, b) in enumerate(pairs)]
    for copy in copies:
        copy.start()
    for n in range(frames):
        copies[n].wait()
        sort_columns(cot_ref.at[n], side_ref.at[n], cols_low)
    for copy in copies[frames:]:
        copy.wait()


def load(low, cot, ws, wt):
    frames, rows_low, cols_low, chan = low.shape
    return pl.pallas_call(
        load_kernel,
        in_specs=[UNREAD] * 4,
        out_specs=[FULL] * 4,
        out_shape=[like(low.shape, low.dtype), like(ws.shape, ws.dtype), like(wt.shape, wt.dtype),
                   like((frames, 4, rows_low * cols_low, chan), jnp.bfloat16)],
        scratch_shapes=[pltpu.VMEM(cot.shape, cot.dtype), pltpu.SemaphoreType.DMA((frames + 3,))],
        compiler_params=grant(12),
        cost_estimate=cost(2, 4),
        name="load",
    )(in_hbm(low), in_hbm(cot), in_hbm(ws), in_hbm(wt))


def nothing(*_):
    pass


def after(arrays, *before):
    return pl.pallas_call(
        nothing,
        in_specs=[UNREAD] * (len(arrays) + len(before)),
        out_specs=[UNREAD] * len(arrays),
        out_shape=[like(a.shape, a.dtype) for a in arrays],
        input_output_aliases={n: n for n in range(len(arrays))},
        compiler_params=grant(1),
        name="after",
    )(*arrays, *before)


def forward(place, low, inner, outer, ws):
    frames, rows_low, cols_low, chan = low.shape
    side = (frames, 4, rows_low * cols_low, chan)
    return pl.pallas_call(
        forward_kernel,
        grid=(frames,),
        in_specs=[SCALAR, each(low.shape), each(inner.shape), each(outer.shape), whole(ws.shape)],
        out_specs=[each(side)] * 2,
        out_shape=[like(side, jnp.bfloat16), like(side, jnp.float32)],
        compiler_params=grant(20),
        cost_estimate=cost(10, 8),
        name="forward",
    )(place, low, inner, outer, ws)


def edges_kernel(place_ref, low_ref, inner_ref, outer_ref, pg_ref, _, tall_ref, pg_inner, pg_outer):
    cols_low = low_ref.shape[2]
    first = low_ref.shape[0] - tall_ref.shape[0]
    for n in range(tall_ref.shape[0]):
        at = pl.ds(first + n, 1)
        tall_ref[n] = tall(place_ref, low_ref.at[at], inner_ref.at[at], outer_ref.at[at])
    odd = place_ref[1] == 1
    top, bottom = pg_ref[:, :2, :cols_low, :], pg_ref[:, 2:, -cols_low:, :]
    pg_inner[...] = jnp.where(odd, top, bottom)
    pg_outer[...] = jnp.where(odd, bottom, top)


def edges(place, low, inner, outer, pg, before):
    frames, rows_low, cols_low, chan = low.shape
    full = pl.BlockSpec(memory_space=pltpu.VMEM)
    rows = like((frames, 2, cols_low, chan), jnp.bfloat16)
    return pl.pallas_call(
        edges_kernel,
        in_specs=[SCALAR, full, full, full, full, UNREAD],
        out_specs=[full] * 3,
        out_shape=[like((2, rows_low + 2, cols_low, chan), jnp.bfloat16), rows, rows],
        compiler_params=grant(8),
        name="edges",
    )(place, low, inner, outer, pg, before)


def earlier_act(low, ws):
    frames, rows_tall, cols_low, chan = low.shape
    side = (frames, 4, (rows_tall - 2) * cols_low, chan)
    return pl.pallas_call(
        act_kernel,
        grid=(frames,),
        in_specs=[each(low.shape), whole(ws.shape)],
        out_specs=each(side),
        out_shape=like(side, jnp.bfloat16),
        compiler_params=grant(16),
        cost_estimate=cost(4, 3),
        name="earlier_act",
    )(low, ws)


def backward(place, parts, low, inner, outer, act, slope, cot, later, wt):
    frames, _, count, chan = act.shape
    ext = (frames + 2,) + act.shape[1:]
    piece = (parts, 12 * (chan // (2 * parts)), chan)
    return pl.pallas_call(
        backward_kernel,
        grid_spec=pltpu.PrefetchScalarGridSpec(
            num_scalar_prefetch=1,
            grid=(frames,),
            in_specs=[half_of(low.shape), half_of(inner.shape), half_of(outer.shape), half_of(act.shape),
                      each(slope.shape), whole(cot.shape), whole(later.shape), whole(wt.shape)],
            out_specs=[each(act.shape), whole(ext), whole(piece)],
        ),
        out_shape=[like(act.shape, jnp.bfloat16), like(ext, jnp.bfloat16), like(piece, jnp.float32)],
        compiler_params=grant(28),
        cost_estimate=cost(15, 10),
        name="backward",
    )(place, low, inner, outer, act, slope, cot, later, wt)


def half_grads(place, parts, low, inner, outer, act, pg, ext):
    frames, _, _, chan = act.shape
    piece = (parts, 12 * (chan // (2 * parts)), chan)
    return pl.pallas_call(
        half_kernel,
        grid_spec=pltpu.PrefetchScalarGridSpec(
            num_scalar_prefetch=1,
            grid=(frames,),
            in_specs=[half_of(low.shape), half_of(inner.shape), half_of(outer.shape), half_of(act.shape),
                      each(pg.shape), whole(ext.shape)],
            out_specs=whole(piece),
        ),
        out_shape=like(piece, jnp.float32),
        compiler_params=grant(24),
        cost_estimate=cost(10, 6),
        name="half_grads",
    )(place, low, inner, outer, act, pg, ext)


def section_kernel(act_ref, low_ref, wt_ref, _, out_ref, token_ref):
    token_ref[...] = jnp.zeros_like(token_ref)
    frame = pl.program_id(0)
    _, rows_low, cols_low, chan = low_ref.shape
    group = rows_at_once(rows_low, cols_low)
    span = group * cols_low
    order = from_side(group, cols_low)
    low = low_ref[0].reshape(-1, chan).astype(jnp.float32)
    mixed = []
    for side in range(4):
        total = low
        for k in range(3):
            total = total + product(act_ref[frame + 2 - k, side], wt_ref[k])
        mixed.append(total.astype(jnp.bfloat16))
    for n in range(rows_low // group):
        block = jnp.concatenate([m[n * span : (n + 1) * span] for m in mixed], axis=0)
        block = product(order, block).astype(jnp.bfloat16)
        out_ref[0, 2 * group * n : 2 * group * (n + 1)] = block.reshape(2 * group, 2 * cols_low, chan)


def section(act_ext, low, wt, before):
    frames, rows_low, cols_low, chan = low.shape
    out = (frames, 2 * rows_low, 2 * cols_low, chan)
    return pl.pallas_call(
        section_kernel,
        grid=(frames,),
        in_specs=[whole(act_ext.shape), each(low.shape), whole(wt.shape), UNREAD],
        out_specs=[each(out), whole(TOKEN.shape)],
        out_shape=[like(out, jnp.bfloat16), TOKEN],
        compiler_params=grant(16),
        cost_estimate=pl.CostEstimate(flops=2 * 2048 * chan * chan * 4, bytes_accessed=3 * 2**20, transcendentals=0),
        name="section",
    )(act_ext, low, wt, before)


def input_kernel(place_ref, pg_ref, inner_ref, outer_ref, cot_ref, ws_ref, _, out_ref, token_ref):
    token_ref[...] = jnp.zeros_like(token_ref)
    _, rows_low, cols_low, chan = out_ref.shape
    group = rows_at_once(rows_low, cols_low)
    span = group * cols_low
    boxes = box(group, cols_low)
    count = rows_low * cols_low
    total = jnp.concatenate(
        [product(boxes, cot_ref[0, 2 * group * n : 2 * group * (n + 1)].reshape(4 * span, chan))
         for n in range(rows_low // group)], axis=0)
    higher = (rows_low + 1, cols_low, chan)
    at = column(higher[0] * cols_low, cols_low, chan)
    own = [pg_ref[0, side].astype(jnp.float32) for side in range(4)]
    odd_place = place_ref[1] == 1
    inner = [inner_ref[0, b].astype(jnp.float32) for b in range(2)]
    outer = [outer_ref[0, b].astype(jnp.float32) for b in range(2)]
    above = [jnp.where(odd_place, inner[b], outer[b]) for b in range(2)]
    below = [jnp.where(odd_place, outer[b], inner[b]) for b in range(2)]
    even = [jnp.concatenate([own[b], below[b]], axis=0) for b in range(2)]
    odd = [jnp.concatenate([above[b], own[2 + b]], axis=0) for b in range(2)]
    for j in range(3):
        pair = []
        for first, second in (even, odd):
            if j == 0:
                value = second + from_right(first, at, cols_low - 1)
            elif j == 1:
                value = first + second
            else:
                value = first + from_left(second, at)
            pair.append(value.reshape(higher))
        top, low = pair
        for i, value in enumerate((low[1:] + top[1:], top[:-1] + low[1:], low[:-1] + top[:-1])):
            value = value.reshape(count, chan)
            high = value.astype(jnp.bfloat16)
            rest = (value - high.astype(jnp.float32)).astype(jnp.bfloat16)
            total = total + product_nt(high, ws_ref[i, j]) + product_nt(rest, ws_ref[i, j])
    out_ref[0] = total.astype(jnp.bfloat16).reshape(rows_low, cols_low, chan)


def input_grads(place, pg, inner, outer, cot, ws, before, low_shape):
    chan = low_shape[-1]
    return pl.pallas_call(
        input_kernel,
        grid=(low_shape[0],),
        in_specs=[SCALAR, each(pg.shape), each(inner.shape), each(outer.shape), each(cot.shape), whole(ws.shape), UNREAD],
        out_specs=[each(low_shape), whole(TOKEN.shape)],
        out_shape=[like(low_shape, jnp.bfloat16), TOKEN],
        compiler_params=grant(20),
        cost_estimate=pl.CostEstimate(flops=2 * 2048 * chan * chan * 6, bytes_accessed=4 * 2**20, transcendentals=0),
        name="input_grads",
    )(place, pg, inner, outer, cot, ws, before)


def put_kernel(place_ref, half_ref, *refs):
    spatial_ref, temporal_ref, wide, sems = refs[-4:]
    parts, rows, chan = half_ref.shape
    size, half = rows // 12, chan // 2
    for tap in range(12):
        for n in range(parts):
            wide[tap, n * size : (n + 1) * size, :] = half_ref[n, tap * size : (tap + 1) * size, :].astype(jnp.float32)
    to = pl.ds(pl.multiple_of(place_ref[0] * half, half), half)
    copies = []
    for tap in range(12):
        if tap < 9:
            target = spatial_ref.at[tap // 3, tap % 3, to]
        else:
            target = temporal_ref.at[tap - 9, to]
        copies.append(pltpu.make_async_copy(wide.at[tap], target, sems.at[tap]))
        copies[-1].start()
    for copy in copies:
        copy.wait()


def put(place, half, *done):
    chan = half.shape[-1]
    hbm = pl.BlockSpec(memory_space=pltpu.HBM)
    return pl.pallas_call(
        put_kernel,
        in_specs=[SCALAR, FULL] + [hbm] * len(done),
        out_specs=[hbm, hbm],
        out_shape=[like((3, 3, chan, chan), jnp.float32), like((3, chan, chan), jnp.float32)],
        input_output_aliases={2 + n: n for n in range(len(done))},
        scratch_shapes=[pltpu.VMEM((12, chan // 2, chan), jnp.float32), pltpu.SemaphoreType.DMA((12,))],
        compiler_params=grant(6),
        name="put",
    )(place, half, *done)


def add_kernel(mine_ref, theirs_ref, out_ref):
    out_ref[...] = (mine_ref[...] + theirs_ref[...]).astype(jnp.bfloat16)


def add_halves(mine, theirs):
    full = pl.BlockSpec(memory_space=pltpu.VMEM)
    return pl.pallas_call(
        add_kernel,
        in_specs=[full, full],
        out_specs=full,
        out_shape=like(mine.shape, jnp.bfloat16),
        compiler_params=grant(8),
        name="add_halves",
    )(mine, theirs)


def sum_kernel(got_ref, _, out_ref):
    total = got_ref[0].astype(jnp.float32)
    for n in range(1, got_ref.shape[0]):
        total = total + got_ref[n].astype(jnp.float32)
    out_ref[...] = total.astype(jnp.bfloat16)


def sum_parts(got, before):
    full = pl.BlockSpec(memory_space=pltpu.VMEM)
    return pl.pallas_call(
        sum_kernel,
        in_specs=[full, UNREAD],
        out_specs=full,
        out_shape=like(got.shape[1:], jnp.bfloat16),
        compiler_params=grant(4),
        name="sum_parts",
    )(got, before)


def spread_kernel(own_ref, theirs_ref, *refs):
    total = (own_ref[...].astype(jnp.float32) + theirs_ref[...].astype(jnp.float32)).astype(jnp.bfloat16)
    for n in range(refs[-1].shape[0]):
        refs[-1][n] = total


def spread(own, theirs, parts, *before):
    full = pl.BlockSpec(memory_space=pltpu.VMEM)
    return pl.pallas_call(
        spread_kernel,
        in_specs=[full, full] + [UNREAD] * len(before),
        out_specs=full,
        out_shape=like((parts,) + own.shape, jnp.bfloat16),
        compiler_params=grant(4),
        name="spread",
    )(own, theirs, *before)


def on_device(bits, low_frames, spatial_weight, temporal_weight, cotangent):
    low, cot = low_frames[0], cotangent[0]
    frames, rows_low, cols_low, chan = low.shape
    core = lax.axis_index(bits.core).astype(jnp.int32)
    odd = lax.axis_index(bits.axes["height"][-1]).astype(jnp.int32)
    mine, other = jnp.stack([core, odd]), jnp.stack([1 - core, odd])
    parts = 1 << len(bits.near)

    inner, outer, later = first_messages(mine, low, cot)
    later = bits.shift(later, "tm", -1)
    inner, outer = bits.pairs(inner, outer)
    low, ws, wt, cot_side = load(low, cot, spatial_weight, temporal_weight)
    act, slope = forward(mine, low, inner, outer, ws)
    pg, ext, theirs = backward(other, parts, low, inner, outer, act, slope, cot_side, later, wt)
    theirs = bits.swap(theirs, bits.core)
    own = half_grads(mine, parts, low, inner, outer, act, pg, ext)
    kept = add_halves(own, theirs)
    got = bits.exchange(kept)
    edge, pg_inner, pg_outer = edges(mine, low, inner, outer, pg, kept)
    earlier = earlier_act(bits.shift(edge, "tm", 1), ws)
    pg_inner, pg_outer = bits.pairs(pg_inner, pg_outer)
    total, far = bits.far_sums(sum_parts(got, earlier))
    section_out, section_done = section(jnp.concatenate([earlier, act], axis=0), low, wt, total)
    totals = spread(total, far, parts, section_done, pg_inner, pg_outer)
    input_grad, input_done = input_grads(mine, pg, pg_inner, pg_outer, cot, ws, totals, low.shape)
    half, = after([bits.exchange(totals)], input_done)
    theirs = bits.swap(half, bits.core)
    spatial_grad, temporal_grad = put(other, theirs, *put(mine, half))
    return section_out[None], input_grad[None], spatial_grad, temporal_grad


def solution(mesh):
    bits = Bits(mesh)
    block = P(*(bits.axes[name] for name in ("dp", "tm", "height")), None, None)
    return jax.shard_map(
        functools.partial(on_device, bits),
        mesh=bits.mesh,
        in_specs=(block, P(), P(), block),
        out_specs=(block, block, P(), P()),
        check_vma=False,
    )
```

```python
import functools

import jax
import jax.numpy as jnp
from jax import lax
from jax.experimental import pallas as pl
from jax.experimental.pallas import tpu as pltpu
from jax.sharding import Mesh
from jax.sharding import PartitionSpec as P


class Bits:
    def __init__(self, mesh):
        self.axes = {}
        for name in mesh.axis_names:
            count = mesh.shape[name].bit_length() - 1
            self.axes[name] = tuple(f"{name}{bit}" for bit in reversed(range(count)))
        names = [bit for bits in self.axes.values() for bit in bits]
        self.mesh = Mesh(mesh.devices.reshape([2] * len(names)), tuple(names))
        self.core = next((n for n in names if self.same_chip(n)), self.axes["tm"][-1])
        others = [[b for b in reversed(bits) if b != self.core] for bits in self.axes.values()]
        turns = [bits[turn] for turn in range(len(names)) for bits in others if turn < len(bits)]
        self.near = [n for n in names if n in turns[:4]]
        self.far = turns[4:]

    def same_chip(self, name):
        at = [1 if n == name else 0 for n in self.mesh.axis_names]
        here = self.mesh.devices[tuple([0] * len(at))]
        there = self.mesh.devices[tuple(at)]
        return tuple(getattr(here, "coords", (0,))) == tuple(getattr(there, "coords", (1,)))

    def swap(self, block, axis):
        return lax.ppermute(block, axis, [(0, 1), (1, 0)])

    def shift(self, block, name, distance):
        axes = self.axes[name]
        devices = range(1 << len(axes))
        route = [(i - distance, i) for i in devices if i - distance in devices]
        return lax.ppermute(block, axes, route)

    def exchange(self, parts):
        return lax.all_to_all(parts, tuple(self.near), 0, 0, tiled=True)

    def pairs(self, inner, outer):
        axes = self.axes["height"]
        low = range(1, (1 << len(axes)) - 1, 2)
        route = [(i, i + 1) for i in low] + [(i + 1, i) for i in low]
        outer = lax.ppermute(outer, axes, route)
        return self.swap(inner, axes[-1]), outer

    def far_sums(self, total):
        for axis in self.far:
            total = total.astype(jnp.float32) + self.swap(total, axis).astype(jnp.float32)
            total = lax.reduce_precision(total, 8, 7).astype(jnp.bfloat16)
        return total


SIDES = ((0, 0), (0, 1), (1, 0), (1, 1))


def grant(mib):
    return pltpu.CompilerParams(vmem_limit_bytes=mib * 2**20)


def product(left, right):
    return jnp.dot(left, right, preferred_element_type=jnp.float32)


def product_nt(left, right):
    return lax.dot_general(left, right, (((1,), (1,)), ((), ())), preferred_element_type=jnp.float32)


def rows_at_once(rows_low, cols_low):
    return max(n for n in (1, 2, 4, 8) if rows_low % n == 0 and (n == 1 or 4 * n * cols_low <= 256))


def by_side(count, cols_low, dtype=jnp.bfloat16):
    size = 4 * count * cols_low
    to = lax.broadcasted_iota(jnp.int32, (size, size), 0)
    at = lax.broadcasted_iota(jnp.int32, (size, size), 1)
    q, rest = to % cols_low, to // cols_low
    p, side = rest % count, rest // count
    return (at == (p * 2 + side // 2) * 2 * cols_low + 2 * q + side % 2).astype(jnp.float32).astype(dtype)


def from_side(count, cols_low, dtype=jnp.bfloat16):
    size = 4 * count * cols_low
    at = lax.broadcasted_iota(jnp.int32, (size, size), 0)
    to = lax.broadcasted_iota(jnp.int32, (size, size), 1)
    q, rest = to % cols_low, to // cols_low
    p, side = rest % count, rest // count
    return (at == (p * 2 + side // 2) * 2 * cols_low + 2 * q + side % 2).astype(jnp.float32).astype(dtype)


def box(count, cols_low, dtype=jnp.bfloat16):
    size = 4 * count * cols_low
    to = lax.broadcasted_iota(jnp.int32, (size // 4, size), 0)
    at = lax.broadcasted_iota(jnp.int32, (size // 4, size), 1)
    p, q = at // (4 * cols_low), at % (2 * cols_low) // 2
    return (to == p * cols_low + q).astype(jnp.float32).astype(dtype)


def column(rows, cols_low, chan):
    return lax.broadcasted_iota(jnp.int32, (rows, chan), 0) % cols_low


def from_left(x, at):
    return jnp.where(at == 0, 0.0, pltpu.roll(x, 1, 0))


def from_right(x, at, last):
    return jnp.where(at == last, 0.0, pltpu.roll(x, x.shape[0] - 1, 0))


def sort_columns(source, target, cols_low):
    rows_low, chan = source.shape[0] // 2, source.shape[2]
    group = rows_at_once(rows_low, cols_low)
    span = group * cols_low
    order = by_side(group, cols_low)
    for n in range(rows_low // group):
        block = source[2 * group * n : 2 * group * (n + 1)].reshape(4 * span, chan)
        block = product(order, block).astype(jnp.bfloat16).reshape(4, span, chan)
        target[:, n * span : (n + 1) * span, :] = block


def tall(place_ref, low_ref, inner_ref, outer_ref):
    odd = place_ref[1] == 1
    up = jnp.where(odd, inner_ref[0], outer_ref[0])
    down = jnp.where(odd, outer_ref[0], inner_ref[0])
    return jnp.concatenate([up, low_ref[0], down], axis=0)


def spatial(low, ws_ref):
    rows_low, cols_low, chan = low.shape[0] - 2, low.shape[1], low.shape[2]
    count = rows_low * cols_low
    flat = low.reshape(-1, chan)
    rows = [[], []]
    for j in range(3):
        taps = [product(flat, ws_ref[i, j]).reshape(low.shape) for i in range(3)]
        even = taps[0][:rows_low] + (taps[1] + taps[2])[1 : rows_low + 1]
        odd = (taps[0] + taps[1])[1 : rows_low + 1] + taps[2][2:]
        rows[0].append(even.reshape(count, chan))
        rows[1].append(odd.reshape(count, chan))
    at = column(count, cols_low, chan)
    for first, second, third in rows:
        yield from_left(first, at) + (second + third)
        yield (first + second) + from_right(third, at, cols_low - 1)


def forward_kernel(place_ref, low_ref, inner_ref, outer_ref, ws_ref, act_ref, slope_ref):
    low = tall(place_ref, low_ref, inner_ref, outer_ref)
    for side, pre in enumerate(spatial(low, ws_ref)):
        sig = jax.nn.sigmoid(pre)
        act_ref[0, side] = (pre * sig).astype(jnp.bfloat16)
        slope_ref[0, side] = sig * (1.0 + pre * (1.0 - sig))


def act_kernel(low_ref, ws_ref, act_ref):
    for side, pre in enumerate(spatial(low_ref[0], ws_ref)):
        act_ref[0, side] = (pre * jax.nn.sigmoid(pre)).astype(jnp.bfloat16)


def add_sums(low, act, pg, cots, out_ref):
    rows_low, cols_low, half = low.shape[0] - 2, low.shape[1], low.shape[2]
    count = rows_low * cols_low
    sums = []
    wide = low.reshape(-1, half).astype(jnp.float32)
    at = column(wide.shape[0], cols_low, half)
    moved = [from_left(wide, at), wide, from_right(wide, at, cols_low - 1)]
    turned = {}
    for dc in range(3):
        view = moved[dc].astype(jnp.bfloat16).reshape(low.shape)
        for dr in range(3):
            turned[dr - 1, dc - 1] = view[dr : dr + rows_low].reshape(count, half).T
    for i in range(3):
        for j in range(3):
            left = jnp.concatenate([turned[(a + i - 1) // 2, (b + j - 1) // 2] for a, b in SIDES], axis=1)
            sums.append(product(left, pg))
    act = act.T
    for cot in cots:
        sums.append(product(act, cot))

    @pl.when(pl.program_id(0) == 0)
    def _():
        for tap, value in enumerate(sums):
            out_ref[tap] = value

    @pl.when(pl.program_id(0) > 0)
    def _():
        for tap, value in enumerate(sums):
            out_ref[tap] += value


def backward_kernel(place_ref, low_ref, inner_ref, outer_ref, act_ref, slope_ref, cot_ref, later_ref, wt_ref, pg_ref, ext_ref, out_ref):
    frame = pl.program_id(0)
    frames, _, count, chan = cot_ref.shape
    cols_low = low_ref.shape[2]

    @pl.when(frame == 0)
    def _():
        ext_ref[:frames] = cot_ref[...]
        for n in range(2):
            sort_columns(later_ref.at[n], ext_ref.at[frames + n], cols_low)

    pgs = []
    for side in range(4):
        act_grad = product_nt(ext_ref[frame, side], wt_ref[0])
        for k in (1, 2):
            act_grad = act_grad + product_nt(ext_ref[frame + k, side], wt_ref[k])
        pgs.append((act_grad * slope_ref[0, side]).astype(jnp.bfloat16))
        pg_ref[0, side] = pgs[side]
    low = tall(place_ref, low_ref, inner_ref, outer_ref)
    act = act_ref[0].reshape(4 * count, -1)
    cots = [ext_ref[frame + k].reshape(4 * count, chan) for k in range(3)]
    add_sums(low, act, jnp.concatenate(pgs, axis=0), cots, out_ref)


def half_kernel(place_ref, low_ref, inner_ref, outer_ref, act_ref, pg_ref, ext_ref, out_ref):
    frame = pl.program_id(0)
    _, _, count, chan = pg_ref.shape
    low = tall(place_ref, low_ref, inner_ref, outer_ref)
    act = act_ref[0].reshape(4 * count, -1)
    cots = [ext_ref[frame + k].reshape(4 * count, chan) for k in range(3)]
    add_sums(low, act, pg_ref[0].reshape(4 * count, chan), cots, out_ref)


def whole(shape):
    return pl.BlockSpec(shape, lambda f, *_: (0,) * len(shape))


def each(shape):
    return pl.BlockSpec((1,) + tuple(shape[1:]), lambda f, *_: (f,) + (0,) * (len(shape) - 1))


def half_of(shape):
    block = (1,) + tuple(shape[1:-1]) + (shape[-1] // 2,)
    return pl.BlockSpec(block, lambda f, side: (f,) + (0,) * (len(shape) - 2) + (side[0],))


SCALAR = pl.BlockSpec(memory_space=pltpu.SMEM)
UNREAD = pl.BlockSpec(memory_space=pl.ANY)


def like(shape, dtype):
    return jax.ShapeDtypeStruct(shape, dtype)


TOKEN = like((8, 128), jnp.float32)


def cost(units, mib):
    return pl.CostEstimate(flops=units * 2 * 2048 * 256 * 256, bytes_accessed=mib * 2**20, transcendentals=0)


def in_hbm(array):
    return pltpu.with_memory_space_constraint(array, pltpu.HBM)


FULL = pl.BlockSpec(memory_space=pltpu.VMEM)


def first_kernel(place_ref, low_ref, cot_ref, inner_ref, outer_ref, later_ref, sems):
    last = low_ref.shape[1] - 1
    odd = place_ref[1]
    copies = [
        pltpu.make_async_copy(cot_ref.at[0:2], later_ref, sems.at[0]),
        pltpu.make_async_copy(low_ref.at[:, pl.ds(last * (1 - odd), 1)], inner_ref, sems.at[1]),
        pltpu.make_async_copy(low_ref.at[:, pl.ds(last * odd, 1)], outer_ref, sems.at[2]),
    ]
    for copy in copies:
        copy.start()
    for copy in copies:
        copy.wait()


def first_messages(place, low, cot):
    row = like(low[:, :1].shape, low.dtype)
    return pl.pallas_call(
        first_kernel,
        in_specs=[SCALAR, UNREAD, UNREAD],
        out_specs=[FULL] * 3,
        out_shape=[row, row, like(cot[:2].shape, cot.dtype)],
        scratch_shapes=[pltpu.SemaphoreType.DMA((3,))],
        compiler_params=grant(4),
        name="first_messages",
    )(place, in_hbm(low), in_hbm(cot))


def load_kernel(low_hbm, cot_hbm, ws_hbm, wt_hbm, low_ref, ws_ref, wt_ref, side_ref, cot_ref, sems):
    frames, cols_low = low_ref.shape[0], low_ref.shape[2]
    copies = [pltpu.make_async_copy(cot_hbm.at[n], cot_ref.at[n], sems.at[n]) for n in range(frames)]
    pairs = ((low_hbm, low_ref), (ws_hbm, ws_ref), (wt_hbm, wt_ref))
    copies += [pltpu.make_async_copy(a, b, sems.at[frames + n]) for n, (a, b) in enumerate(pairs)]
    for copy in copies:
        copy.start()
    for n in range(frames):
        copies[n].wait()
        sort_columns(cot_ref.at[n], side_ref.at[n], cols_low)
    for copy in copies[frames:]:
        copy.wait()


def load(low, cot, ws, wt):
    frames, rows_low, cols_low, chan = low.shape
    return pl.pallas_call(
        load_kernel,
        in_specs=[UNREAD] * 4,
        out_specs=[FULL] * 4,
        out_shape=[like(low.shape, low.dtype), like(ws.shape, ws.dtype), like(wt.shape, wt.dtype),
                   like((frames, 4, rows_low * cols_low, chan), jnp.bfloat16)],
        scratch_shapes=[pltpu.VMEM(cot.shape, cot.dtype), pltpu.SemaphoreType.DMA((frames + 3,))],
        compiler_params=grant(12),
        cost_estimate=cost(2, 4),
        name="load",
    )(in_hbm(low), in_hbm(cot), in_hbm(ws), in_hbm(wt))


def nothing(*_):
    pass


def after(arrays, *before):
    return pl.pallas_call(
        nothing,
        in_specs=[UNREAD] * (len(arrays) + len(before)),
        out_specs=[UNREAD] * len(arrays),
        out_shape=[like(a.shape, a.dtype) for a in arrays],
        input_output_aliases={n: n for n in range(len(arrays))},
        compiler_params=grant(1),
        name="after",
    )(*arrays, *before)


def forward(place, low, inner, outer, ws):
    frames, rows_low, cols_low, chan = low.shape
    side = (frames, 4, rows_low * cols_low, chan)
    return pl.pallas_call(
        forward_kernel,
        grid=(frames,),
        in_specs=[SCALAR, each(low.shape), each(inner.shape), each(outer.shape), whole(ws.shape)],
        out_specs=[each(side)] * 2,
        out_shape=[like(side, jnp.bfloat16), like(side, jnp.float32)],
        compiler_params=grant(20),
        cost_estimate=cost(10, 8),
        name="forward",
    )(place, low, inner, outer, ws)


def edges_kernel(place_ref, low_ref, inner_ref, outer_ref, pg_ref, _, tall_ref, pg_inner, pg_outer):
    cols_low = low_ref.shape[2]
    first = low_ref.shape[0] - tall_ref.shape[0]
    for n in range(tall_ref.shape[0]):
        at = pl.ds(first + n, 1)
        tall_ref[n] = tall(place_ref, low_ref.at[at], inner_ref.at[at], outer_ref.at[at])
    odd = place_ref[1] == 1
    top, bottom = pg_ref[:, :2, :cols_low, :], pg_ref[:, 2:, -cols_low:, :]
    pg_inner[...] = jnp.where(odd, top, bottom)
    pg_outer[...] = jnp.where(odd, bottom, top)


def edges(place, low, inner, outer, pg, before):
    frames, rows_low, cols_low, chan = low.shape
    full = pl.BlockSpec(memory_space=pltpu.VMEM)
    rows = like((frames, 2, cols_low, chan), jnp.bfloat16)
    return pl.pallas_call(
        edges_kernel,
        in_specs=[SCALAR, full, full, full, full, UNREAD],
        out_specs=[full] * 3,
        out_shape=[like((2, rows_low + 2, cols_low, chan), jnp.bfloat16), rows, rows],
        compiler_params=grant(8),
        name="edges",
    )(place, low, inner, outer, pg, before)


def earlier_act(low, ws):
    frames, rows_tall, cols_low, chan = low.shape
    side = (frames, 4, (rows_tall - 2) * cols_low, chan)
    return pl.pallas_call(
        act_kernel,
        grid=(frames,),
        in_specs=[each(low.shape), whole(ws.shape)],
        out_specs=each(side),
        out_shape=like(side, jnp.bfloat16),
        compiler_params=grant(16),
        cost_estimate=cost(4, 3),
        name="earlier_act",
    )(low, ws)


def backward(place, low, inner, outer, act, slope, cot, later, wt):
    frames, _, count, chan = act.shape
    ext = (frames + 2,) + act.shape[1:]
    half = (12, chan // 2, chan)
    return pl.pallas_call(
        backward_kernel,
        grid_spec=pltpu.PrefetchScalarGridSpec(
            num_scalar_prefetch=1,
            grid=(frames,),
            in_specs=[half_of(low.shape), half_of(inner.shape), half_of(outer.shape), half_of(act.shape),
                      each(slope.shape), whole(cot.shape), whole(later.shape), whole(wt.shape)],
            out_specs=[each(act.shape), whole(ext), whole(half)],
        ),
        out_shape=[like(act.shape, jnp.bfloat16), like(ext, jnp.bfloat16), like(half, jnp.float32)],
        compiler_params=grant(28),
        cost_estimate=cost(15, 10),
        name="backward",
    )(place, low, inner, outer, act, slope, cot, later, wt)


def half_grads(place, low, inner, outer, act, pg, ext):
    frames, _, _, chan = act.shape
    half = (12, chan // 2, chan)
    return pl.pallas_call(
        half_kernel,
        grid_spec=pltpu.PrefetchScalarGridSpec(
            num_scalar_prefetch=1,
            grid=(frames,),
            in_specs=[half_of(low.shape), half_of(inner.shape), half_of(outer.shape), half_of(act.shape),
                      each(pg.shape), whole(ext.shape)],
            out_specs=whole(half),
        ),
        out_shape=like(half, jnp.float32),
        compiler_params=grant(24),
        cost_estimate=cost(10, 6),
        name="half_grads",
    )(place, low, inner, outer, act, pg, ext)


def section_kernel(act_ref, low_ref, wt_ref, _, out_ref, token_ref):
    token_ref[...] = jnp.zeros_like(token_ref)
    frame = pl.program_id(0)
    _, rows_low, cols_low, chan = low_ref.shape
    group = rows_at_once(rows_low, cols_low)
    span = group * cols_low
    order = from_side(group, cols_low)
    low = low_ref[0].reshape(-1, chan).astype(jnp.float32)
    mixed = []
    for side in range(4):
        total = low
        for k in range(3):
            total = total + product(act_ref[frame + 2 - k, side], wt_ref[k])
        mixed.append(total.astype(jnp.bfloat16))
    for n in range(rows_low // group):
        block = jnp.concatenate([m[n * span : (n + 1) * span] for m in mixed], axis=0)
        block = product(order, block).astype(jnp.bfloat16)
        out_ref[0, 2 * group * n : 2 * group * (n + 1)] = block.reshape(2 * group, 2 * cols_low, chan)


def section(act_ext, low, wt, before):
    frames, rows_low, cols_low, chan = low.shape
    out = (frames, 2 * rows_low, 2 * cols_low, chan)
    return pl.pallas_call(
        section_kernel,
        grid=(frames,),
        in_specs=[whole(act_ext.shape), each(low.shape), whole(wt.shape), UNREAD],
        out_specs=[each(out), whole(TOKEN.shape)],
        out_shape=[like(out, jnp.bfloat16), TOKEN],
        compiler_params=grant(16),
        cost_estimate=pl.CostEstimate(flops=2 * 2048 * chan * chan * 4, bytes_accessed=3 * 2**20, transcendentals=0),
        name="section",
    )(act_ext, low, wt, before)


def input_kernel(place_ref, pg_ref, inner_ref, outer_ref, cot_ref, ws_ref, _, out_ref, token_ref):
    token_ref[...] = jnp.zeros_like(token_ref)
    _, rows_low, cols_low, chan = out_ref.shape
    group = rows_at_once(rows_low, cols_low)
    span = group * cols_low
    boxes = box(group, cols_low)
    count = rows_low * cols_low
    total = jnp.concatenate(
        [product(boxes, cot_ref[0, 2 * group * n : 2 * group * (n + 1)].reshape(4 * span, chan))
         for n in range(rows_low // group)], axis=0)
    higher = (rows_low + 1, cols_low, chan)
    at = column(higher[0] * cols_low, cols_low, chan)
    own = [pg_ref[0, side].astype(jnp.float32) for side in range(4)]
    odd_place = place_ref[1] == 1
    inner = [inner_ref[0, b].astype(jnp.float32) for b in range(2)]
    outer = [outer_ref[0, b].astype(jnp.float32) for b in range(2)]
    above = [jnp.where(odd_place, inner[b], outer[b]) for b in range(2)]
    below = [jnp.where(odd_place, outer[b], inner[b]) for b in range(2)]
    even = [jnp.concatenate([own[b], below[b]], axis=0) for b in range(2)]
    odd = [jnp.concatenate([above[b], own[2 + b]], axis=0) for b in range(2)]
    for j in range(3):
        pair = []
        for first, second in (even, odd):
            if j == 0:
                value = second + from_right(first, at, cols_low - 1)
            elif j == 1:
                value = first + second
            else:
                value = first + from_left(second, at)
            pair.append(value.reshape(higher))
        top, low = pair
        for i, value in enumerate((low[1:] + top[1:], top[:-1] + low[1:], low[:-1] + top[:-1])):
            value = value.reshape(count, chan)
            high = value.astype(jnp.bfloat16)
            rest = (value - high.astype(jnp.float32)).astype(jnp.bfloat16)
            total = total + product_nt(high, ws_ref[i, j]) + product_nt(rest, ws_ref[i, j])
    out_ref[0] = total.astype(jnp.bfloat16).reshape(rows_low, cols_low, chan)


def input_grads(place, pg, inner, outer, cot, ws, before, low_shape):
    chan = low_shape[-1]
    return pl.pallas_call(
        input_kernel,
        grid=(low_shape[0],),
        in_specs=[SCALAR, each(pg.shape), each(inner.shape), each(outer.shape), each(cot.shape), whole(ws.shape), UNREAD],
        out_specs=[each(low_shape), whole(TOKEN.shape)],
        out_shape=[like(low_shape, jnp.bfloat16), TOKEN],
        compiler_params=grant(20),
        cost_estimate=pl.CostEstimate(flops=2 * 2048 * chan * chan * 6, bytes_accessed=4 * 2**20, transcendentals=0),
        name="input_grads",
    )(place, pg, inner, outer, cot, ws, before)


def put_kernel(place_ref, half_ref, *refs):
    spatial_ref, temporal_ref, wide, sems = refs[-4:]
    taps, half, _ = half_ref.shape
    to = pl.ds(pl.multiple_of(place_ref[0] * half, half), half)
    copies = []
    for tap in range(taps):
        wide[tap] = half_ref[tap].astype(jnp.float32)
        if tap < 9:
            target = spatial_ref.at[tap // 3, tap % 3, to]
        else:
            target = temporal_ref.at[tap - 9, to]
        copies.append(pltpu.make_async_copy(wide.at[tap], target, sems.at[tap]))
        copies[-1].start()
    for copy in copies:
        copy.wait()


def put(place, half, *done):
    chan = half.shape[-1]
    hbm = pl.BlockSpec(memory_space=pltpu.HBM)
    return pl.pallas_call(
        put_kernel,
        in_specs=[SCALAR, FULL] + [hbm] * len(done),
        out_specs=[hbm, hbm],
        out_shape=[like((3, 3, chan, chan), jnp.float32), like((3, chan, chan), jnp.float32)],
        input_output_aliases={2 + n: n for n in range(len(done))},
        scratch_shapes=[pltpu.VMEM((12, chan // 2, chan), jnp.float32), pltpu.SemaphoreType.DMA((12,))],
        compiler_params=grant(6),
        name="put",
    )(place, half, *done)


def add_kernel(mine_ref, theirs_ref, out_ref):
    out_ref[...] = (mine_ref[...] + theirs_ref[...]).astype(jnp.bfloat16)


def add_halves(mine, theirs):
    full = pl.BlockSpec(memory_space=pltpu.VMEM)
    return pl.pallas_call(
        add_kernel,
        in_specs=[full, full],
        out_specs=full,
        out_shape=like(mine.shape, jnp.bfloat16),
        compiler_params=grant(8),
        name="add_halves",
    )(mine, theirs)


def sum_kernel(got_ref, _, out_ref):
    total = got_ref[0].astype(jnp.float32)
    for n in range(1, got_ref.shape[0]):
        total = total + got_ref[n].astype(jnp.float32)
    total = total.astype(jnp.bfloat16)
    for n in range(out_ref.shape[0]):
        out_ref[n] = total


def sum_parts(got, copies, before):
    return pl.pallas_call(
        sum_kernel,
        in_specs=[FULL, UNREAD],
        out_specs=FULL,
        out_shape=like((copies,) + got.shape[1:], jnp.bfloat16),
        compiler_params=grant(4),
        name="sum_parts",
    )(got, before)


def on_device(bits, low_frames, spatial_weight, temporal_weight, cotangent):
    low, cot = low_frames[0], cotangent[0]
    frames, rows_low, cols_low, chan = low.shape
    core = lax.axis_index(bits.core).astype(jnp.int32)
    odd = lax.axis_index(bits.axes["height"][-1]).astype(jnp.int32)
    mine, other = jnp.stack([core, odd]), jnp.stack([1 - core, odd])
    parts = 1 << len(bits.near)

    inner, outer, later = first_messages(mine, low, cot)
    later = bits.shift(later, "tm", -1)
    inner, outer = bits.pairs(inner, outer)
    low, ws, wt, cot_side = load(low, cot, spatial_weight, temporal_weight)
    act, slope = forward(mine, low, inner, outer, ws)
    pg, ext, theirs = backward(other, low, inner, outer, act, slope, cot_side, later, wt)
    theirs = bits.swap(theirs, bits.core)
    own = half_grads(mine, low, inner, outer, act, pg, ext)
    kept = add_halves(own, theirs)
    got = bits.exchange(kept.reshape(parts, -1, chan))
    edge, pg_inner, pg_outer = edges(mine, low, inner, outer, pg, kept)
    earlier = earlier_act(bits.shift(edge, "tm", 1), ws)
    pg_inner, pg_outer = bits.pairs(pg_inner, pg_outer)
    if bits.far:
        total = bits.far_sums(sum_parts(got, 1, earlier)[0])
        totals = jnp.broadcast_to(total, got.shape)
    else:
        totals = sum_parts(got, parts, earlier)
    section_out, section_done = section(jnp.concatenate([earlier, act], axis=0), low, wt, totals)
    input_grad, input_done = input_grads(mine, pg, pg_inner, pg_outer, cot, ws, totals, low.shape)
    half, = after([bits.exchange(totals).reshape(kept.shape)], section_done, input_done)
    theirs = bits.swap(half, bits.core)
    spatial_grad, temporal_grad = put(other, theirs, *put(mine, half))
    return section_out[None], input_grad[None], spatial_grad, temporal_grad


def solution(mesh):
    bits = Bits(mesh)
    block = P(*(bits.axes[name] for name in ("dp", "tm", "height")), None, None)
    return jax.shard_map(
        functools.partial(on_device, bits),
        mesh=bits.mesh,
        in_specs=(block, P(), P(), block),
        out_specs=(block, block, P(), P()),
        check_vma=False,
    )
```

```python
import functools

import jax
import jax.numpy as jnp
from jax import lax
from jax.experimental import pallas as pl
from jax.experimental.pallas import tpu as pltpu
from jax.sharding import Mesh
from jax.sharding import PartitionSpec as P


class Bits:
    def __init__(self, mesh):
        self.axes = {}
        for name in mesh.axis_names:
            count = mesh.shape[name].bit_length() - 1
            self.axes[name] = tuple(f"{name}{bit}" for bit in reversed(range(count)))
        names = [bit for bits in self.axes.values() for bit in bits]
        self.mesh = Mesh(mesh.devices.reshape([2] * len(names)), tuple(names))
        self.core = next((n for n in names if self.same_chip(n)), self.axes["tm"][-1])
        others = [[b for b in reversed(bits) if b != self.core] for bits in self.axes.values()]
        turns = [bits[turn] for turn in range(len(names)) for bits in others if turn < len(bits)]
        self.near = [n for n in names if n in turns[:3]]
        self.far = turns[3:]

    def same_chip(self, name):
        at = [1 if n == name else 0 for n in self.mesh.axis_names]
        here = self.mesh.devices[tuple([0] * len(at))]
        there = self.mesh.devices[tuple(at)]
        return tuple(getattr(here, "coords", (0,))) == tuple(getattr(there, "coords", (1,)))

    def swap(self, block, axis):
        return lax.ppermute(block, axis, [(0, 1), (1, 0)])

    def shift(self, block, name, distance):
        axes = self.axes[name]
        devices = range(1 << len(axes))
        route = [(i - distance, i) for i in devices if i - distance in devices]
        return lax.ppermute(block, axes, route)

    def exchange(self, parts):
        return lax.all_to_all(parts, tuple(self.near), 0, 0, tiled=True)

    def pairs(self, inner, outer):
        axes = self.axes["height"]
        low = range(1, (1 << len(axes)) - 1, 2)
        route = [(i, i + 1) for i in low] + [(i + 1, i) for i in low]
        outer = lax.ppermute(outer, axes, route)
        return self.swap(inner, axes[-1]), outer

    def far_sums(self, total):
        for axis in self.far[:-1]:
            total = total.astype(jnp.float32) + self.swap(total, axis).astype(jnp.float32)
            total = lax.reduce_precision(total, 8, 7).astype(jnp.bfloat16)
        return total, self.swap(total, self.far[-1])


SIDES = ((0, 0), (0, 1), (1, 0), (1, 1))


def grant(mib):
    return pltpu.CompilerParams(vmem_limit_bytes=mib * 2**20)


def product(left, right):
    return jnp.dot(left, right, preferred_element_type=jnp.float32)


def product_nt(left, right):
    return lax.dot_general(left, right, (((1,), (1,)), ((), ())), preferred_element_type=jnp.float32)


def rows_at_once(rows_low, cols_low):
    return max(n for n in (1, 2, 4, 8) if rows_low % n == 0 and (n == 1 or 4 * n * cols_low <= 256))


def by_side(count, cols_low, dtype=jnp.bfloat16):
    size = 4 * count * cols_low
    to = lax.broadcasted_iota(jnp.int32, (size, size), 0)
    at = lax.broadcasted_iota(jnp.int32, (size, size), 1)
    q, rest = to % cols_low, to // cols_low
    p, side = rest % count, rest // count
    return (at == (p * 2 + side // 2) * 2 * cols_low + 2 * q + side % 2).astype(jnp.float32).astype(dtype)


def from_side(count, cols_low, dtype=jnp.bfloat16):
    size = 4 * count * cols_low
    at = lax.broadcasted_iota(jnp.int32, (size, size), 0)
    to = lax.broadcasted_iota(jnp.int32, (size, size), 1)
    q, rest = to % cols_low, to // cols_low
    p, side = rest % count, rest // count
    return (at == (p * 2 + side // 2) * 2 * cols_low + 2 * q + side % 2).astype(jnp.float32).astype(dtype)


def box(count, cols_low, dtype=jnp.bfloat16):
    size = 4 * count * cols_low
    to = lax.broadcasted_iota(jnp.int32, (size // 4, size), 0)
    at = lax.broadcasted_iota(jnp.int32, (size // 4, size), 1)
    p, q = at // (4 * cols_low), at % (2 * cols_low) // 2
    return (to == p * cols_low + q).astype(jnp.float32).astype(dtype)


def column(rows, cols_low, chan):
    return lax.broadcasted_iota(jnp.int32, (rows, chan), 0) % cols_low


def from_left(x, at):
    return jnp.where(at == 0, 0.0, pltpu.roll(x, 1, 0))


def from_right(x, at, last):
    return jnp.where(at == last, 0.0, pltpu.roll(x, x.shape[0] - 1, 0))


def sort_columns(source, target, cols_low):
    rows_low, chan = source.shape[0] // 2, source.shape[2]
    group = rows_at_once(rows_low, cols_low)
    span = group * cols_low
    order = by_side(group, cols_low)
    for n in range(rows_low // group):
        block = source[2 * group * n : 2 * group * (n + 1)].reshape(4 * span, chan)
        block = product(order, block).astype(jnp.bfloat16).reshape(4, span, chan)
        target[:, n * span : (n + 1) * span, :] = block


def tall(place_ref, low_ref, inner_ref, outer_ref, frame, lanes=slice(None)):
    odd = place_ref[1] == 1
    inner, outer = inner_ref[frame, :, :, lanes], outer_ref[frame, :, :, lanes]
    up, down = jnp.where(odd, inner, outer), jnp.where(odd, outer, inner)
    return jnp.concatenate([up, low_ref[frame, :, :, lanes], down], axis=0)


def spatial(low, ws_ref):
    rows_low, cols_low, chan = low.shape[0] - 2, low.shape[1], low.shape[2]
    count = rows_low * cols_low
    flat = low.reshape(-1, chan)
    rows = [[], []]
    for j in range(3):
        taps = [product(flat, ws_ref[i, j]).reshape(low.shape) for i in range(3)]
        even = taps[0][:rows_low] + (taps[1] + taps[2])[1 : rows_low + 1]
        odd = (taps[0] + taps[1])[1 : rows_low + 1] + taps[2][2:]
        rows[0].append(even.reshape(count, chan))
        rows[1].append(odd.reshape(count, chan))
    at = column(count, cols_low, chan)
    for first, second, third in rows:
        yield from_left(first, at) + (second + third)
        yield (first + second) + from_right(third, at, cols_low - 1)


def forward_kernel(place_ref, low_ref, inner_ref, outer_ref, ws_ref, act_ref, slope_ref):
    for frame in range(low_ref.shape[0]):
        low = tall(place_ref, low_ref, inner_ref, outer_ref, frame)
        for side, pre in enumerate(spatial(low, ws_ref)):
            sig = jax.nn.sigmoid(pre)
            act_ref[frame, side] = (pre * sig).astype(jnp.bfloat16)
            slope_ref[frame, side] = sig * (1.0 + pre * (1.0 - sig))


def act_kernel(low_ref, ws_ref, act_ref):
    for side, pre in enumerate(spatial(low_ref[0], ws_ref)):
        act_ref[0, side] = (pre * jax.nn.sigmoid(pre)).astype(jnp.bfloat16)


def half_sums(place_ref, low_ref, inner_ref, outer_ref, act_ref, pg_ref, ext_ref, out_ref):
    frames, rows_low, cols_low, chan = low_ref.shape
    count, half = rows_low * cols_low, chan // 2
    lanes = pl.ds(pl.multiple_of(place_ref[0] * half, half), half)
    lefts = [[] for _ in range(9)]
    acts = []
    at = column((rows_low + 2) * cols_low, cols_low, half)
    for frame in range(frames):
        low = tall(place_ref, low_ref, inner_ref, outer_ref, frame, lanes)
        wide = low.reshape(-1, half).astype(jnp.float32)
        moved = [from_left(wide, at), wide, from_right(wide, at, cols_low - 1)]
        turned = {}
        for dc in range(3):
            view = moved[dc].astype(jnp.bfloat16).reshape(low.shape)
            for dr in range(3):
                turned[dr - 1, dc - 1] = view[dr : dr + rows_low].reshape(count, half).T
        for i in range(3):
            for j in range(3):
                lefts[3 * i + j] += [turned[(a + i - 1) // 2, (b + j - 1) // 2] for a, b in SIDES]
        acts.append(act_ref[frame, :, :, lanes].reshape(4 * count, half).T)
    pg = pg_ref[...].reshape(frames * 4 * count, chan)
    for tap, left in enumerate(lefts):
        out_ref[tap] = product(jnp.concatenate(left, axis=1), pg)
    act = jnp.concatenate(acts, axis=1)
    for k in range(3):
        out_ref[9 + k] = product(act, ext_ref[k : k + frames].reshape(frames * 4 * count, chan))


def backward_kernel(place_ref, low_ref, inner_ref, outer_ref, act_ref, slope_ref, cot_ref, later_ref, wt_ref, pg_ref, ext_ref, out_ref):
    frames, _, count, chan = cot_ref.shape
    ext_ref[:frames] = cot_ref[...]
    for n in range(2):
        sort_columns(later_ref.at[n], ext_ref.at[frames + n], low_ref.shape[2])
    for frame in range(frames):
        act_grad = product_nt(ext_ref[frame].reshape(4 * count, chan), wt_ref[0])
        for k in (1, 2):
            act_grad = act_grad + product_nt(ext_ref[frame + k].reshape(4 * count, chan), wt_ref[k])
        slope = slope_ref[frame].reshape(4 * count, chan)
        pg_ref[frame] = (act_grad * slope).astype(jnp.bfloat16).reshape(4, count, chan)
    half_sums(place_ref, low_ref, inner_ref, outer_ref, act_ref, pg_ref, ext_ref, out_ref)


def whole(shape):
    return pl.BlockSpec(shape, lambda f, *_: (0,) * len(shape))


def each(shape):
    return pl.BlockSpec((1,) + tuple(shape[1:]), lambda f, *_: (f,) + (0,) * (len(shape) - 1))


SCALAR = pl.BlockSpec(memory_space=pltpu.SMEM)
UNREAD = pl.BlockSpec(memory_space=pl.ANY)


def like(shape, dtype):
    return jax.ShapeDtypeStruct(shape, dtype)


TOKEN = like((8, 128), jnp.float32)


def cost(units, mib):
    return pl.CostEstimate(flops=units * 2 * 2048 * 256 * 256, bytes_accessed=mib * 2**20, transcendentals=0)


def in_hbm(array):
    return pltpu.with_memory_space_constraint(array, pltpu.HBM)


FULL = pl.BlockSpec(memory_space=pltpu.VMEM)


def first_kernel(place_ref, low_ref, cot_ref, inner_ref, outer_ref, later_ref, sems):
    last = low_ref.shape[1] - 1
    odd = place_ref[1]
    copies = [
        pltpu.make_async_copy(cot_ref.at[0:2], later_ref, sems.at[0]),
        pltpu.make_async_copy(low_ref.at[:, pl.ds(last * (1 - odd), 1)], inner_ref, sems.at[1]),
        pltpu.make_async_copy(low_ref.at[:, pl.ds(last * odd, 1)], outer_ref, sems.at[2]),
    ]
    for copy in copies:
        copy.start()
    for copy in copies:
        copy.wait()


def first_messages(place, low, cot):
    row = like(low[:, :1].shape, low.dtype)
    return pl.pallas_call(
        first_kernel,
        in_specs=[SCALAR, UNREAD, UNREAD],
        out_specs=[FULL] * 3,
        out_shape=[row, row, like(cot[:2].shape, cot.dtype)],
        scratch_shapes=[pltpu.SemaphoreType.DMA((3,))],
        compiler_params=grant(4),
        name="first_messages",
    )(place, in_hbm(low), in_hbm(cot))


def load_kernel(low_hbm, cot_hbm, ws_hbm, wt_hbm, low_ref, ws_ref, wt_ref, side_ref, cot_ref, sems):
    frames, cols_low = low_ref.shape[0], low_ref.shape[2]
    copies = [pltpu.make_async_copy(cot_hbm.at[n], cot_ref.at[n], sems.at[n]) for n in range(frames)]
    pairs = ((low_hbm, low_ref), (ws_hbm, ws_ref), (wt_hbm, wt_ref))
    copies += [pltpu.make_async_copy(a, b, sems.at[frames + n]) for n, (a, b) in enumerate(pairs)]
    for copy in copies:
        copy.start()
    for n in range(frames):
        copies[n].wait()
        sort_columns(cot_ref.at[n], side_ref.at[n], cols_low)
    for copy in copies[frames:]:
        copy.wait()


def load(low, cot, ws, wt):
    frames, rows_low, cols_low, chan = low.shape
    return pl.pallas_call(
        load_kernel,
        in_specs=[UNREAD] * 4,
        out_specs=[FULL] * 4,
        out_shape=[like(low.shape, low.dtype), like(ws.shape, ws.dtype), like(wt.shape, wt.dtype),
                   like((frames, 4, rows_low * cols_low, chan), jnp.bfloat16)],
        scratch_shapes=[pltpu.VMEM(cot.shape, cot.dtype), pltpu.SemaphoreType.DMA((frames + 3,))],
        compiler_params=grant(12),
        cost_estimate=cost(2, 4),
        name="load",
    )(in_hbm(low), in_hbm(cot), in_hbm(ws), in_hbm(wt))


def nothing(*_):
    pass


def after(arrays, *before):
    return pl.pallas_call(
        nothing,
        in_specs=[UNREAD] * (len(arrays) + len(before)),
        out_specs=[UNREAD] * len(arrays),
        out_shape=[like(a.shape, a.dtype) for a in arrays],
        input_output_aliases={n: n for n in range(len(arrays))},
        compiler_params=grant(1),
        name="after",
    )(*arrays, *before)


def forward(place, low, inner, outer, ws):
    frames, rows_low, cols_low, chan = low.shape
    side = (frames, 4, rows_low * cols_low, chan)
    return pl.pallas_call(
        forward_kernel,
        in_specs=[SCALAR] + [FULL] * 4,
        out_specs=[FULL] * 2,
        out_shape=[like(side, jnp.bfloat16), like(side, jnp.float32)],
        compiler_params=grant(20),
        cost_estimate=cost(10, 8),
        name="forward",
    )(place, low, inner, outer, ws)


def edges_kernel(place_ref, low_ref, inner_ref, outer_ref, pg_ref, _, tall_ref, pg_inner, pg_outer):
    cols_low = low_ref.shape[2]
    first = low_ref.shape[0] - tall_ref.shape[0]
    for n in range(tall_ref.shape[0]):
        tall_ref[n] = tall(place_ref, low_ref, inner_ref, outer_ref, first + n)
    odd = place_ref[1] == 1
    top, bottom = pg_ref[:, :2, :cols_low, :], pg_ref[:, 2:, -cols_low:, :]
    pg_inner[...] = jnp.where(odd, top, bottom)
    pg_outer[...] = jnp.where(odd, bottom, top)


def edges(place, low, inner, outer, pg, before):
    frames, rows_low, cols_low, chan = low.shape
    full = pl.BlockSpec(memory_space=pltpu.VMEM)
    rows = like((frames, 2, cols_low, chan), jnp.bfloat16)
    return pl.pallas_call(
        edges_kernel,
        in_specs=[SCALAR, full, full, full, full, UNREAD],
        out_specs=[full] * 3,
        out_shape=[like((2, rows_low + 2, cols_low, chan), jnp.bfloat16), rows, rows],
        compiler_params=grant(8),
        name="edges",
    )(place, low, inner, outer, pg, before)


def earlier_act(low, ws):
    frames, rows_tall, cols_low, chan = low.shape
    side = (frames, 4, (rows_tall - 2) * cols_low, chan)
    return pl.pallas_call(
        act_kernel,
        grid=(frames,),
        in_specs=[each(low.shape), whole(ws.shape)],
        out_specs=each(side),
        out_shape=like(side, jnp.bfloat16),
        compiler_params=grant(16),
        cost_estimate=cost(4, 3),
        name="earlier_act",
    )(low, ws)


def backward(place, low, inner, outer, act, slope, cot, later, wt):
    frames, _, _, chan = act.shape
    ext = (frames + 2,) + act.shape[1:]
    return pl.pallas_call(
        backward_kernel,
        in_specs=[SCALAR] + [FULL] * 8,
        out_specs=[FULL] * 3,
        out_shape=[like(act.shape, jnp.bfloat16), like(ext, jnp.bfloat16), like((12, chan // 2, chan), jnp.float32)],
        compiler_params=grant(24),
        cost_estimate=cost(15, 10),
        name="backward",
    )(place, low, inner, outer, act, slope, cot, later, wt)


def half_grads(place, low, inner, outer, act, pg, ext):
    chan = low.shape[-1]
    return pl.pallas_call(
        half_sums,
        in_specs=[SCALAR] + [FULL] * 6,
        out_specs=FULL,
        out_shape=like((12, chan // 2, chan), jnp.float32),
        compiler_params=grant(20),
        cost_estimate=cost(10, 6),
        name="half_grads",
    )(place, low, inner, outer, act, pg, ext)


def section_kernel(act_ref, low_ref, wt_ref, _, out_ref, token_ref):
    token_ref[...] = jnp.zeros_like(token_ref)
    frame = pl.program_id(0)
    _, rows_low, cols_low, chan = low_ref.shape
    group = rows_at_once(rows_low, cols_low)
    span = group * cols_low
    order = from_side(group, cols_low)
    low = low_ref[0].reshape(-1, chan).astype(jnp.float32)
    mixed = []
    for side in range(4):
        total = low
        for k in range(3):
            total = total + product(act_ref[frame + 2 - k, side], wt_ref[k])
        mixed.append(total.astype(jnp.bfloat16))
    for n in range(rows_low // group):
        block = jnp.concatenate([m[n * span : (n + 1) * span] for m in mixed], axis=0)
        block = product(order, block).astype(jnp.bfloat16)
        out_ref[0, 2 * group * n : 2 * group * (n + 1)] = block.reshape(2 * group, 2 * cols_low, chan)


def section(act_ext, low, wt, before):
    frames, rows_low, cols_low, chan = low.shape
    out = (frames, 2 * rows_low, 2 * cols_low, chan)
    return pl.pallas_call(
        section_kernel,
        grid=(frames,),
        in_specs=[whole(act_ext.shape), each(low.shape), whole(wt.shape), UNREAD],
        out_specs=[each(out), whole(TOKEN.shape)],
        out_shape=[like(out, jnp.bfloat16), TOKEN],
        compiler_params=grant(16),
        cost_estimate=pl.CostEstimate(flops=2 * 2048 * chan * chan * 4, bytes_accessed=3 * 2**20, transcendentals=0),
        name="section",
    )(act_ext, low, wt, before)


def input_kernel(place_ref, pg_ref, inner_ref, outer_ref, cot_ref, ws_ref, _, out_ref, token_ref):
    token_ref[...] = jnp.zeros_like(token_ref)
    _, rows_low, cols_low, chan = out_ref.shape
    group = rows_at_once(rows_low, cols_low)
    span = group * cols_low
    boxes = box(group, cols_low)
    count = rows_low * cols_low
    total = jnp.concatenate(
        [product(boxes, cot_ref[0, 2 * group * n : 2 * group * (n + 1)].reshape(4 * span, chan))
         for n in range(rows_low // group)], axis=0)
    higher = (rows_low + 1, cols_low, chan)
    at = column(higher[0] * cols_low, cols_low, chan)
    own = [pg_ref[0, side].astype(jnp.float32) for side in range(4)]
    odd_place = place_ref[1] == 1
    inner = [inner_ref[0, b].astype(jnp.float32) for b in range(2)]
    outer = [outer_ref[0, b].astype(jnp.float32) for b in range(2)]
    above = [jnp.where(odd_place, inner[b], outer[b]) for b in range(2)]
    below = [jnp.where(odd_place, outer[b], inner[b]) for b in range(2)]
    even = [jnp.concatenate([own[b], below[b]], axis=0) for b in range(2)]
    odd = [jnp.concatenate([above[b], own[2 + b]], axis=0) for b in range(2)]
    for j in range(3):
        pair = []
        for first, second in (even, odd):
            if j == 0:
                value = second + from_right(first, at, cols_low - 1)
            elif j == 1:
                value = first + second
            else:
                value = first + from_left(second, at)
            pair.append(value.reshape(higher))
        top, low = pair
        for i, value in enumerate((low[1:] + top[1:], top[:-1] + low[1:], low[:-1] + top[:-1])):
            value = value.reshape(count, chan)
            high = value.astype(jnp.bfloat16)
            rest = (value - high.astype(jnp.float32)).astype(jnp.bfloat16)
            total = total + product_nt(high, ws_ref[i, j]) + product_nt(rest, ws_ref[i, j])
    out_ref[0] = total.astype(jnp.bfloat16).reshape(rows_low, cols_low, chan)


def input_grads(place, pg, inner, outer, cot, ws, before, low_shape):
    chan = low_shape[-1]
    return pl.pallas_call(
        input_kernel,
        grid=(low_shape[0],),
        in_specs=[SCALAR, each(pg.shape), each(inner.shape), each(outer.shape), each(cot.shape), whole(ws.shape), UNREAD],
        out_specs=[each(low_shape), whole(TOKEN.shape)],
        out_shape=[like(low_shape, jnp.bfloat16), TOKEN],
        compiler_params=grant(20),
        cost_estimate=pl.CostEstimate(flops=2 * 2048 * chan * chan * 6, bytes_accessed=4 * 2**20, transcendentals=0),
        name="input_grads",
    )(place, pg, inner, outer, cot, ws, before)


def put_kernel(place_ref, half_ref, *refs):
    spatial_ref, temporal_ref, wide, sems = refs[-4:]
    taps, half, _ = half_ref.shape
    to = pl.ds(pl.multiple_of(place_ref[0] * half, half), half)
    copies = []
    for tap in range(taps):
        wide[tap] = half_ref[tap].astype(jnp.float32)
        if tap < 9:
            target = spatial_ref.at[tap // 3, tap % 3, to]
        else:
            target = temporal_ref.at[tap - 9, to]
        copies.append(pltpu.make_async_copy(wide.at[tap], target, sems.at[tap]))
        copies[-1].start()
    for copy in copies:
        copy.wait()


def put(place, half, *done):
    chan = half.shape[-1]
    hbm = pl.BlockSpec(memory_space=pltpu.HBM)
    return pl.pallas_call(
        put_kernel,
        in_specs=[SCALAR, FULL] + [hbm] * len(done),
        out_specs=[hbm, hbm],
        out_shape=[like((3, 3, chan, chan), jnp.float32), like((3, chan, chan), jnp.float32)],
        input_output_aliases={2 + n: n for n in range(len(done))},
        scratch_shapes=[pltpu.VMEM((12, chan // 2, chan), jnp.float32), pltpu.SemaphoreType.DMA((12,))],
        compiler_params=grant(6),
        name="put",
    )(place, half, *done)


def add_kernel(mine_ref, theirs_ref, out_ref):
    out_ref[...] = (mine_ref[...] + theirs_ref[...]).astype(jnp.bfloat16)


def add_halves(mine, theirs):
    full = pl.BlockSpec(memory_space=pltpu.VMEM)
    return pl.pallas_call(
        add_kernel,
        in_specs=[full, full],
        out_specs=full,
        out_shape=like(mine.shape, jnp.bfloat16),
        compiler_params=grant(8),
        name="add_halves",
    )(mine, theirs)


def sum_kernel(got_ref, _, out_ref):
    total = got_ref[0].astype(jnp.float32)
    for n in range(1, got_ref.shape[0]):
        total = total + got_ref[n].astype(jnp.float32)
    out_ref[...] = total.astype(jnp.bfloat16)


def sum_parts(got, before):
    return pl.pallas_call(
        sum_kernel,
        in_specs=[FULL, UNREAD],
        out_specs=FULL,
        out_shape=like(got.shape[1:], jnp.bfloat16),
        compiler_params=grant(4),
        name="sum_parts",
    )(got, before)


def spread_kernel(own_ref, theirs_ref, *refs):
    total = (own_ref[...].astype(jnp.float32) + theirs_ref[...].astype(jnp.float32)).astype(jnp.bfloat16)
    for n in range(refs[-1].shape[0]):
        refs[-1][n] = total


def spread(own, theirs, parts, *before):
    return pl.pallas_call(
        spread_kernel,
        in_specs=[FULL, FULL] + [UNREAD] * len(before),
        out_specs=FULL,
        out_shape=like((parts,) + own.shape, jnp.bfloat16),
        compiler_params=grant(4),
        name="spread",
    )(own, theirs, *before)


def on_device(bits, low_frames, spatial_weight, temporal_weight, cotangent):
    low, cot = low_frames[0], cotangent[0]
    frames, rows_low, cols_low, chan = low.shape
    core = lax.axis_index(bits.core).astype(jnp.int32)
    odd = lax.axis_index(bits.axes["height"][-1]).astype(jnp.int32)
    mine, other = jnp.stack([core, odd]), jnp.stack([1 - core, odd])
    parts = 1 << len(bits.near)

    inner, outer, later = first_messages(mine, low, cot)
    later = bits.shift(later, "tm", -1)
    inner, outer = bits.pairs(inner, outer)
    low, ws, wt, cot_side = load(low, cot, spatial_weight, temporal_weight)
    act, slope = forward(mine, low, inner, outer, ws)
    pg, ext, theirs = backward(other, low, inner, outer, act, slope, cot_side, later, wt)
    theirs = bits.swap(theirs, bits.core)
    own = half_grads(mine, low, inner, outer, act, pg, ext)
    kept = add_halves(own, theirs)
    got = bits.exchange(kept.reshape(parts, -1, chan))
    edge, pg_inner, pg_outer = edges(mine, low, inner, outer, pg, kept)
    earlier = earlier_act(bits.shift(edge, "tm", 1), ws)
    pg_inner, pg_outer = bits.pairs(pg_inner, pg_outer)
    total, far = bits.far_sums(sum_parts(got, earlier))
    section_out, section_done = section(jnp.concatenate([earlier, act], axis=0), low, wt, total)
    totals = spread(total, far, parts, section_done, pg_inner, pg_outer)
    input_grad, input_done = input_grads(mine, pg, pg_inner, pg_outer, cot, ws, totals, low.shape)
    half, = after([bits.exchange(totals).reshape(kept.shape)], input_done)
    theirs = bits.swap(half, bits.core)
    spatial_grad, temporal_grad = put(other, theirs, *put(mine, half))
    return section_out[None], input_grad[None], spatial_grad, temporal_grad


def solution(mesh):
    bits = Bits(mesh)
    block = P(*(bits.axes[name] for name in ("dp", "tm", "height")), None, None)
    return jax.shard_map(
        functools.partial(on_device, bits),
        mesh=bits.mesh,
        in_specs=(block, P(), P(), block),
        out_specs=(block, block, P(), P()),
        check_vma=False,
    )
```

```python
import functools

import jax
import jax.numpy as jnp
from jax import lax
from jax.experimental import pallas as pl
from jax.experimental.pallas import tpu as pltpu
from jax.sharding import Mesh
from jax.sharding import PartitionSpec as P


class Bits:
    def __init__(self, mesh):
        self.axes = {}
        for name in mesh.axis_names:
            count = mesh.shape[name].bit_length() - 1
            self.axes[name] = tuple(f"{name}{bit}" for bit in reversed(range(count)))
        names = [bit for bits in self.axes.values() for bit in bits]
        self.mesh = Mesh(mesh.devices.reshape([2] * len(names)), tuple(names))
        self.core = next((n for n in names if self.same_chip(n)), self.axes["tm"][-1])
        others = [[b for b in reversed(bits) if b != self.core] for bits in self.axes.values()]
        turns = [bits[turn] for turn in range(len(names)) for bits in others if turn < len(bits)]
        self.near = [n for n in names if n in turns[:3]]
        self.far = turns[3:]

    def same_chip(self, name):
        at = [1 if n == name else 0 for n in self.mesh.axis_names]
        here = self.mesh.devices[tuple([0] * len(at))]
        there = self.mesh.devices[tuple(at)]
        return tuple(getattr(here, "coords", (0,))) == tuple(getattr(there, "coords", (1,)))

    def swap(self, block, axis):
        return lax.ppermute(block, axis, [(0, 1), (1, 0)])

    def shift(self, block, name, distance):
        axes = self.axes[name]
        devices = range(1 << len(axes))
        route = [(i - distance, i) for i in devices if i - distance in devices]
        return lax.ppermute(block, axes, route)

    def send(self, block, mask):
        near = tuple(self.near)
        return lax.ppermute(block, near, [(n, n ^ mask) for n in range(1 << len(near))])

    def pairs(self, inner, outer):
        axes = self.axes["height"]
        low = range(1, (1 << len(axes)) - 1, 2)
        route = [(i, i + 1) for i in low] + [(i + 1, i) for i in low]
        outer = lax.ppermute(outer, axes, route)
        return self.swap(inner, axes[-1]), outer

    def far_sums(self, total):
        for axis in self.far[:-1]:
            total = total.astype(jnp.float32) + self.swap(total, axis).astype(jnp.float32)
            total = lax.reduce_precision(total, 8, 7).astype(jnp.bfloat16)
        return total, self.swap(total, self.far[-1])


SIDES = ((0, 0), (0, 1), (1, 0), (1, 1))


def grant(mib):
    return pltpu.CompilerParams(vmem_limit_bytes=mib * 2**20)


def product(left, right):
    return jnp.dot(left, right, preferred_element_type=jnp.float32)


def product_nt(left, right):
    return lax.dot_general(left, right, (((1,), (1,)), ((), ())), preferred_element_type=jnp.float32)


def rows_at_once(rows_low, cols_low):
    return max(n for n in (1, 2, 4, 8) if rows_low % n == 0 and (n == 1 or 4 * n * cols_low <= 256))


def by_side(count, cols_low, dtype=jnp.bfloat16):
    size = 4 * count * cols_low
    to = lax.broadcasted_iota(jnp.int32, (size, size), 0)
    at = lax.broadcasted_iota(jnp.int32, (size, size), 1)
    q, rest = to % cols_low, to // cols_low
    p, side = rest % count, rest // count
    return (at == (p * 2 + side // 2) * 2 * cols_low + 2 * q + side % 2).astype(jnp.float32).astype(dtype)


def from_side(count, cols_low, dtype=jnp.bfloat16):
    size = 4 * count * cols_low
    at = lax.broadcasted_iota(jnp.int32, (size, size), 0)
    to = lax.broadcasted_iota(jnp.int32, (size, size), 1)
    q, rest = to % cols_low, to // cols_low
    p, side = rest % count, rest // count
    return (at == (p * 2 + side // 2) * 2 * cols_low + 2 * q + side % 2).astype(jnp.float32).astype(dtype)


def box(count, cols_low, dtype=jnp.bfloat16):
    size = 4 * count * cols_low
    to = lax.broadcasted_iota(jnp.int32, (size // 4, size), 0)
    at = lax.broadcasted_iota(jnp.int32, (size // 4, size), 1)
    p, q = at // (4 * cols_low), at % (2 * cols_low) // 2
    return (to == p * cols_low + q).astype(jnp.float32).astype(dtype)


def column(rows, cols_low, chan):
    return lax.broadcasted_iota(jnp.int32, (rows, chan), 0) % cols_low


def from_left(x, at):
    return jnp.where(at == 0, 0.0, pltpu.roll(x, 1, 0))


def from_right(x, at, last):
    return jnp.where(at == last, 0.0, pltpu.roll(x, x.shape[0] - 1, 0))


def sort_columns(source, target, cols_low):
    rows_low, chan = source.shape[0] // 2, source.shape[2]
    group = rows_at_once(rows_low, cols_low)
    span = group * cols_low
    order = by_side(group, cols_low)
    for n in range(rows_low // group):
        block = source[2 * group * n : 2 * group * (n + 1)].reshape(4 * span, chan)
        block = product(order, block).astype(jnp.bfloat16).reshape(4, span, chan)
        target[:, n * span : (n + 1) * span, :] = block


def tall(place_ref, low_ref, inner_ref, outer_ref, frame, lanes=slice(None)):
    odd = place_ref[1] == 1
    inner, outer = inner_ref[frame, :, :, lanes], outer_ref[frame, :, :, lanes]
    up, down = jnp.where(odd, inner, outer), jnp.where(odd, outer, inner)
    return jnp.concatenate([up, low_ref[frame, :, :, lanes], down], axis=0)


def spatial(low, ws_ref):
    rows_low, cols_low, chan = low.shape[0] - 2, low.shape[1], low.shape[2]
    count = rows_low * cols_low
    flat = low.reshape(-1, chan)
    rows = [[], []]
    for j in range(3):
        taps = [product(flat, ws_ref[i, j]).reshape(low.shape) for i in range(3)]
        even = taps[0][:rows_low] + (taps[1] + taps[2])[1 : rows_low + 1]
        odd = (taps[0] + taps[1])[1 : rows_low + 1] + taps[2][2:]
        rows[0].append(even.reshape(count, chan))
        rows[1].append(odd.reshape(count, chan))
    at = column(count, cols_low, chan)
    for first, second, third in rows:
        yield from_left(first, at) + (second + third)
        yield (first + second) + from_right(third, at, cols_low - 1)


def forward_kernel(place_ref, low_ref, inner_ref, outer_ref, ws_ref, act_ref, slope_ref):
    for frame in range(low_ref.shape[0]):
        low = tall(place_ref, low_ref, inner_ref, outer_ref, frame)
        for side, pre in enumerate(spatial(low, ws_ref)):
            sig = jax.nn.sigmoid(pre)
            act_ref[frame, side] = (pre * sig).astype(jnp.bfloat16)
            slope_ref[frame, side] = sig * (1.0 + pre * (1.0 - sig))


def act_kernel(low_ref, ws_ref, act_ref):
    for side, pre in enumerate(spatial(low_ref[0], ws_ref)):
        act_ref[0, side] = (pre * jax.nn.sigmoid(pre)).astype(jnp.bfloat16)


def half_sums(place_ref, low_ref, inner_ref, outer_ref, act_ref, pg_ref, ext_ref, out_ref):
    frames, rows_low, cols_low, chan = low_ref.shape
    count, half = rows_low * cols_low, chan // 2
    lanes = pl.ds(pl.multiple_of(place_ref[0] * half, half), half)
    lefts = [[] for _ in range(9)]
    acts = []
    at = column((rows_low + 2) * cols_low, cols_low, half)
    for frame in range(frames):
        low = tall(place_ref, low_ref, inner_ref, outer_ref, frame, lanes)
        wide = low.reshape(-1, half).astype(jnp.float32)
        moved = [from_left(wide, at), wide, from_right(wide, at, cols_low - 1)]
        turned = {}
        for dc in range(3):
            view = moved[dc].astype(jnp.bfloat16).reshape(low.shape)
            for dr in range(3):
                turned[dr - 1, dc - 1] = view[dr : dr + rows_low].reshape(count, half).T
        for i in range(3):
            for j in range(3):
                lefts[3 * i + j] += [turned[(a + i - 1) // 2, (b + j - 1) // 2] for a, b in SIDES]
        acts.append(act_ref[frame, :, :, lanes].reshape(4 * count, half).T)
    pg = pg_ref[...].reshape(frames * 4 * count, chan)
    for tap, left in enumerate(lefts):
        out_ref[tap] = product(jnp.concatenate(left, axis=1), pg)
    act = jnp.concatenate(acts, axis=1)
    for k in range(3):
        out_ref[9 + k] = product(act, ext_ref[k : k + frames].reshape(frames * 4 * count, chan))


def backward_kernel(place_ref, low_ref, inner_ref, outer_ref, act_ref, slope_ref, cot_ref, later_ref, wt_ref, pg_ref, ext_ref, out_ref):
    frames, _, count, chan = cot_ref.shape
    ext_ref[:frames] = cot_ref[...]
    for n in range(2):
        sort_columns(later_ref.at[n], ext_ref.at[frames + n], low_ref.shape[2])
    for frame in range(frames):
        act_grad = product_nt(ext_ref[frame].reshape(4 * count, chan), wt_ref[0])
        for k in (1, 2):
            act_grad = act_grad + product_nt(ext_ref[frame + k].reshape(4 * count, chan), wt_ref[k])
        slope = slope_ref[frame].reshape(4 * count, chan)
        pg_ref[frame] = (act_grad * slope).astype(jnp.bfloat16).reshape(4, count, chan)
    half_sums(place_ref, low_ref, inner_ref, outer_ref, act_ref, pg_ref, ext_ref, out_ref)


def whole(shape):
    return pl.BlockSpec(shape, lambda f, *_: (0,) * len(shape))


def each(shape):
    return pl.BlockSpec((1,) + tuple(shape[1:]), lambda f, *_: (f,) + (0,) * (len(shape) - 1))


SCALAR = pl.BlockSpec(memory_space=pltpu.SMEM)
UNREAD = pl.BlockSpec(memory_space=pl.ANY)


def like(shape, dtype):
    return jax.ShapeDtypeStruct(shape, dtype)


TOKEN = like((8, 128), jnp.float32)


def cost(units, mib):
    return pl.CostEstimate(flops=units * 2 * 2048 * 256 * 256, bytes_accessed=mib * 2**20, transcendentals=0)


def in_hbm(array):
    return pltpu.with_memory_space_constraint(array, pltpu.HBM)


FULL = pl.BlockSpec(memory_space=pltpu.VMEM)


def first_kernel(place_ref, low_ref, cot_ref, inner_ref, outer_ref, later_ref, sems):
    last = low_ref.shape[1] - 1
    odd = place_ref[1]
    copies = [
        pltpu.make_async_copy(cot_ref.at[0:2], later_ref, sems.at[0]),
        pltpu.make_async_copy(low_ref.at[:, pl.ds(last * (1 - odd), 1)], inner_ref, sems.at[1]),
        pltpu.make_async_copy(low_ref.at[:, pl.ds(last * odd, 1)], outer_ref, sems.at[2]),
    ]
    for copy in copies:
        copy.start()
    for copy in copies:
        copy.wait()


def first_messages(place, low, cot):
    row = like(low[:, :1].shape, low.dtype)
    return pl.pallas_call(
        first_kernel,
        in_specs=[SCALAR, UNREAD, UNREAD],
        out_specs=[FULL] * 3,
        out_shape=[row, row, like(cot[:2].shape, cot.dtype)],
        scratch_shapes=[pltpu.SemaphoreType.DMA((3,))],
        compiler_params=grant(4),
        name="first_messages",
    )(place, in_hbm(low), in_hbm(cot))


def load_kernel(low_hbm, cot_hbm, ws_hbm, wt_hbm, low_ref, ws_ref, wt_ref, side_ref, cot_ref, sems):
    frames, cols_low = low_ref.shape[0], low_ref.shape[2]
    copies = [pltpu.make_async_copy(cot_hbm.at[n], cot_ref.at[n], sems.at[n]) for n in range(frames)]
    pairs = ((low_hbm, low_ref), (ws_hbm, ws_ref), (wt_hbm, wt_ref))
    copies += [pltpu.make_async_copy(a, b, sems.at[frames + n]) for n, (a, b) in enumerate(pairs)]
    for copy in copies:
        copy.start()
    for n in range(frames):
        copies[n].wait()
        sort_columns(cot_ref.at[n], side_ref.at[n], cols_low)
    for copy in copies[frames:]:
        copy.wait()


def load(low, cot, ws, wt):
    frames, rows_low, cols_low, chan = low.shape
    return pl.pallas_call(
        load_kernel,
        in_specs=[UNREAD] * 4,
        out_specs=[FULL] * 4,
        out_shape=[like(low.shape, low.dtype), like(ws.shape, ws.dtype), like(wt.shape, wt.dtype),
                   like((frames, 4, rows_low * cols_low, chan), jnp.bfloat16)],
        scratch_shapes=[pltpu.VMEM(cot.shape, cot.dtype), pltpu.SemaphoreType.DMA((frames + 3,))],
        compiler_params=grant(12),
        cost_estimate=cost(2, 4),
        name="load",
    )(in_hbm(low), in_hbm(cot), in_hbm(ws), in_hbm(wt))


def forward(place, low, inner, outer, ws):
    frames, rows_low, cols_low, chan = low.shape
    side = (frames, 4, rows_low * cols_low, chan)
    return pl.pallas_call(
        forward_kernel,
        in_specs=[SCALAR] + [FULL] * 4,
        out_specs=[FULL] * 2,
        out_shape=[like(side, jnp.bfloat16), like(side, jnp.float32)],
        compiler_params=grant(20),
        cost_estimate=cost(10, 8),
        name="forward",
    )(place, low, inner, outer, ws)


def edges_kernel(place_ref, low_ref, inner_ref, outer_ref, pg_ref, _, tall_ref, pg_inner, pg_outer):
    cols_low = low_ref.shape[2]
    first = low_ref.shape[0] - tall_ref.shape[0]
    for n in range(tall_ref.shape[0]):
        tall_ref[n] = tall(place_ref, low_ref, inner_ref, outer_ref, first + n)
    odd = place_ref[1] == 1
    top, bottom = pg_ref[:, :2, :cols_low, :], pg_ref[:, 2:, -cols_low:, :]
    pg_inner[...] = jnp.where(odd, top, bottom)
    pg_outer[...] = jnp.where(odd, bottom, top)


def edges(place, low, inner, outer, pg, before):
    frames, rows_low, cols_low, chan = low.shape
    full = pl.BlockSpec(memory_space=pltpu.VMEM)
    rows = like((frames, 2, cols_low, chan), jnp.bfloat16)
    return pl.pallas_call(
        edges_kernel,
        in_specs=[SCALAR, full, full, full, full, UNREAD],
        out_specs=[full] * 3,
        out_shape=[like((2, rows_low + 2, cols_low, chan), jnp.bfloat16), rows, rows],
        compiler_params=grant(8),
        name="edges",
    )(place, low, inner, outer, pg, before)


def earlier_act(low, ws):
    frames, rows_tall, cols_low, chan = low.shape
    side = (frames, 4, (rows_tall - 2) * cols_low, chan)
    return pl.pallas_call(
        act_kernel,
        grid=(frames,),
        in_specs=[each(low.shape), whole(ws.shape)],
        out_specs=each(side),
        out_shape=like(side, jnp.bfloat16),
        compiler_params=grant(16),
        cost_estimate=cost(4, 3),
        name="earlier_act",
    )(low, ws)


def backward(place, low, inner, outer, act, slope, cot, later, wt):
    frames, _, _, chan = act.shape
    ext = (frames + 2,) + act.shape[1:]
    return pl.pallas_call(
        backward_kernel,
        in_specs=[SCALAR] + [FULL] * 8,
        out_specs=[FULL] * 3,
        out_shape=[like(act.shape, jnp.bfloat16), like(ext, jnp.bfloat16), like((12, chan // 2, chan), jnp.float32)],
        compiler_params=grant(24),
        cost_estimate=cost(15, 10),
        name="backward",
    )(place, low, inner, outer, act, slope, cot, later, wt)


def half_grads(place, low, inner, outer, act, pg, ext):
    chan = low.shape[-1]
    return pl.pallas_call(
        half_sums,
        in_specs=[SCALAR] + [FULL] * 6,
        out_specs=FULL,
        out_shape=like((12, chan // 2, chan), jnp.float32),
        compiler_params=grant(20),
        cost_estimate=cost(10, 6),
        name="half_grads",
    )(place, low, inner, outer, act, pg, ext)


def section_kernel(act_ref, low_ref, wt_ref, _, out_ref, token_ref):
    token_ref[...] = jnp.zeros_like(token_ref)
    frame = pl.program_id(0)
    _, rows_low, cols_low, chan = low_ref.shape
    group = rows_at_once(rows_low, cols_low)
    span = group * cols_low
    order = from_side(group, cols_low)
    low = low_ref[0].reshape(-1, chan).astype(jnp.float32)
    mixed = []
    for side in range(4):
        total = low
        for k in range(3):
            total = total + product(act_ref[frame + 2 - k, side], wt_ref[k])
        mixed.append(total.astype(jnp.bfloat16))
    for n in range(rows_low // group):
        block = jnp.concatenate([m[n * span : (n + 1) * span] for m in mixed], axis=0)
        block = product(order, block).astype(jnp.bfloat16)
        out_ref[0, 2 * group * n : 2 * group * (n + 1)] = block.reshape(2 * group, 2 * cols_low, chan)


def section(act_ext, low, wt, before):
    frames, rows_low, cols_low, chan = low.shape
    out = (frames, 2 * rows_low, 2 * cols_low, chan)
    return pl.pallas_call(
        section_kernel,
        grid=(frames,),
        in_specs=[whole(act_ext.shape), each(low.shape), whole(wt.shape), UNREAD],
        out_specs=[each(out), whole(TOKEN.shape)],
        out_shape=[like(out, jnp.bfloat16), TOKEN],
        compiler_params=grant(16),
        cost_estimate=pl.CostEstimate(flops=2 * 2048 * chan * chan * 4, bytes_accessed=3 * 2**20, transcendentals=0),
        name="section",
    )(act_ext, low, wt, before)


def input_kernel(place_ref, pg_ref, inner_ref, outer_ref, cot_ref, ws_ref, _, out_ref, token_ref):
    token_ref[...] = jnp.zeros_like(token_ref)
    _, rows_low, cols_low, chan = out_ref.shape
    group = rows_at_once(rows_low, cols_low)
    span = group * cols_low
    boxes = box(group, cols_low)
    count = rows_low * cols_low
    total = jnp.concatenate(
        [product(boxes, cot_ref[0, 2 * group * n : 2 * group * (n + 1)].reshape(4 * span, chan))
         for n in range(rows_low // group)], axis=0)
    higher = (rows_low + 1, cols_low, chan)
    at = column(higher[0] * cols_low, cols_low, chan)
    own = [pg_ref[0, side].astype(jnp.float32) for side in range(4)]
    odd_place = place_ref[1] == 1
    inner = [inner_ref[0, b].astype(jnp.float32) for b in range(2)]
    outer = [outer_ref[0, b].astype(jnp.float32) for b in range(2)]
    above = [jnp.where(odd_place, inner[b], outer[b]) for b in range(2)]
    below = [jnp.where(odd_place, outer[b], inner[b]) for b in range(2)]
    even = [jnp.concatenate([own[b], below[b]], axis=0) for b in range(2)]
    odd = [jnp.concatenate([above[b], own[2 + b]], axis=0) for b in range(2)]
    for j in range(3):
        pair = []
        for first, second in (even, odd):
            if j == 0:
                value = second + from_right(first, at, cols_low - 1)
            elif j == 1:
                value = first + second
            else:
                value = first + from_left(second, at)
            pair.append(value.reshape(higher))
        top, low = pair
        for i, value in enumerate((low[1:] + top[1:], top[:-1] + low[1:], low[:-1] + top[:-1])):
            value = value.reshape(count, chan)
            high = value.astype(jnp.bfloat16)
            rest = (value - high.astype(jnp.float32)).astype(jnp.bfloat16)
            total = total + product_nt(high, ws_ref[i, j]) + product_nt(rest, ws_ref[i, j])
    out_ref[0] = total.astype(jnp.bfloat16).reshape(rows_low, cols_low, chan)


def input_grads(place, pg, inner, outer, cot, ws, before, low_shape):
    chan = low_shape[-1]
    return pl.pallas_call(
        input_kernel,
        grid=(low_shape[0],),
        in_specs=[SCALAR, each(pg.shape), each(inner.shape), each(outer.shape), each(cot.shape), whole(ws.shape), UNREAD],
        out_specs=[each(low_shape), whole(TOKEN.shape)],
        out_shape=[like(low_shape, jnp.bfloat16), TOKEN],
        compiler_params=grant(20),
        cost_estimate=pl.CostEstimate(flops=2 * 2048 * chan * chan * 6, bytes_accessed=4 * 2**20, transcendentals=0),
        name="input_grads",
    )(place, pg, inner, outer, cot, ws, before)


def put_kernel(place_ref, half_ref, *refs):
    spatial_ref, temporal_ref, wide, sems = refs[-4:]
    taps, half, _ = half_ref.shape
    to = pl.ds(pl.multiple_of(place_ref[0] * half, half), half)
    copies = []
    for tap in range(taps):
        wide[tap] = half_ref[tap].astype(jnp.float32)
        if tap < 9:
            target = spatial_ref.at[tap // 3, tap % 3, to]
        else:
            target = temporal_ref.at[tap - 9, to]
        copies.append(pltpu.make_async_copy(wide.at[tap], target, sems.at[tap]))
        copies[-1].start()
    for copy in copies:
        copy.wait()


def put(place, half, *done):
    chan = half.shape[-1]
    hbm = pl.BlockSpec(memory_space=pltpu.HBM)
    return pl.pallas_call(
        put_kernel,
        in_specs=[SCALAR, FULL] + [hbm] * len(done),
        out_specs=[hbm, hbm],
        out_shape=[like((3, 3, chan, chan), jnp.float32), like((3, chan, chan), jnp.float32)],
        input_output_aliases={2 + n: n for n in range(len(done))},
        scratch_shapes=[pltpu.VMEM((12, chan // 2, chan), jnp.float32), pltpu.SemaphoreType.DMA((12,))],
        compiler_params=grant(6),
        name="put",
    )(place, half, *done)


def add_kernel(place_ref, mine_ref, theirs_ref, *outs):
    rows = outs[0].shape[0]
    for n, out_ref in enumerate(outs):
        at = pl.ds(pl.multiple_of((place_ref[2] ^ n) * rows, rows), rows)
        out_ref[...] = (mine_ref[at] + theirs_ref[at]).astype(jnp.bfloat16)


def add_halves(place, parts, mine, theirs):
    rows, chan = mine.shape
    return pl.pallas_call(
        add_kernel,
        in_specs=[SCALAR, FULL, FULL],
        out_specs=[FULL] * parts,
        out_shape=[like((rows // parts, chan), jnp.bfloat16)] * parts,
        compiler_params=grant(6),
        name="add_halves",
    )(place, mine, theirs)


def sum_kernel(*refs):
    total = refs[0][...].astype(jnp.float32)
    for ref in refs[1:-2]:
        total = total + ref[...].astype(jnp.float32)
    refs[-1][...] = total.astype(jnp.bfloat16)


def sum_parts(parts, before):
    return pl.pallas_call(
        sum_kernel,
        in_specs=[FULL] * len(parts) + [UNREAD],
        out_specs=FULL,
        out_shape=like(parts[0].shape, jnp.bfloat16),
        compiler_params=grant(4),
        name="sum_parts",
    )(*parts, before)


def far_kernel(own_ref, theirs_ref, *refs):
    refs[-1][...] = (own_ref[...].astype(jnp.float32) + theirs_ref[...].astype(jnp.float32)).astype(jnp.bfloat16)


def add_far(own, theirs, *before):
    return pl.pallas_call(
        far_kernel,
        in_specs=[FULL, FULL] + [UNREAD] * len(before),
        out_specs=FULL,
        out_shape=like(own.shape, jnp.bfloat16),
        compiler_params=grant(2),
        name="add_far",
    )(own, theirs, *before)


def join_kernel(place_ref, *refs):
    out_ref = refs[-1]
    rows = refs[0].shape[0]
    for n, ref in enumerate(refs[:-2]):
        at = pl.ds(pl.multiple_of((place_ref[2] ^ n) * rows, rows), rows)
        out_ref[at] = ref[...]


def join(place, parts, before):
    rows, chan = parts[0].shape
    return pl.pallas_call(
        join_kernel,
        in_specs=[SCALAR] + [FULL] * len(parts) + [UNREAD],
        out_specs=FULL,
        out_shape=like((rows * len(parts), chan), jnp.bfloat16),
        compiler_params=grant(4),
        name="join",
    )(place, *parts, before)


def on_device(bits, low_frames, spatial_weight, temporal_weight, cotangent):
    low, cot = low_frames[0], cotangent[0]
    frames, rows_low, cols_low, chan = low.shape
    core = lax.axis_index(bits.core).astype(jnp.int32)
    odd = lax.axis_index(bits.axes["height"][-1]).astype(jnp.int32)
    code = lax.axis_index(tuple(bits.near)).astype(jnp.int32)
    mine, other = jnp.stack([core, odd, code]), jnp.stack([1 - core, odd, code])
    parts = 1 << len(bits.near)

    inner, outer, later = first_messages(mine, low, cot)
    later = bits.shift(later, "tm", -1)
    inner, outer = bits.pairs(inner, outer)
    low, ws, wt, cot_side = load(low, cot, spatial_weight, temporal_weight)
    act, slope = forward(mine, low, inner, outer, ws)
    pg, ext, theirs = backward(other, low, inner, outer, act, slope, cot_side, later, wt)
    theirs = bits.swap(theirs, bits.core)
    own = half_grads(mine, low, inner, outer, act, pg, ext)
    masks = range(1, parts)
    flat = (own.shape[0] * own.shape[1], chan)
    kept = add_halves(mine, parts, own.reshape(flat), theirs.reshape(flat))
    got = [kept[0]] + [bits.send(kept[n], n) for n in masks]
    edge, pg_inner, pg_outer = edges(mine, low, inner, outer, pg, kept[0])
    earlier = earlier_act(bits.shift(edge, "tm", 1), ws)
    pg_inner, pg_outer = bits.pairs(pg_inner, pg_outer)
    total, far = bits.far_sums(sum_parts(got, earlier))
    section_out, section_done = section(jnp.concatenate([earlier, act], axis=0), low, wt, total)
    total = add_far(total, far, section_done, pg_inner, pg_outer)
    input_grad, input_done = input_grads(mine, pg, pg_inner, pg_outer, cot, ws, total, low.shape)
    half = join(mine, [total] + [bits.send(total, n) for n in masks], input_done).reshape(own.shape)
    theirs = bits.swap(half, bits.core)
    spatial_grad, temporal_grad = put(other, theirs, *put(mine, half))
    return section_out[None], input_grad[None], spatial_grad, temporal_grad


def solution(mesh):
    bits = Bits(mesh)
    block = P(*(bits.axes[name] for name in ("dp", "tm", "height")), None, None)
    return jax.shard_map(
        functools.partial(on_device, bits),
        mesh=bits.mesh,
        in_specs=(block, P(), P(), block),
        out_specs=(block, block, P(), P()),
        check_vma=False,
    )
```

```python
import functools

import jax
import jax.numpy as jnp
from jax import lax
from jax.experimental import pallas as pl
from jax.experimental.pallas import tpu as pltpu
from jax.sharding import Mesh
from jax.sharding import PartitionSpec as P


class Bits:
    def __init__(self, mesh):
        self.axes = {}
        for name in mesh.axis_names:
            count = mesh.shape[name].bit_length() - 1
            self.axes[name] = tuple(f"{name}{bit}" for bit in reversed(range(count)))
        names = [bit for bits in self.axes.values() for bit in bits]
        self.mesh = Mesh(mesh.devices.reshape([2] * len(names)), tuple(names))
        self.core = next((n for n in names if self.same_chip(n)), self.axes["tm"][-1])
        others = [[b for b in reversed(bits) if b != self.core] for bits in self.axes.values()]
        turns = [bits[turn] for turn in range(len(names)) for bits in others if turn < len(bits)]
        self.near = [n for n in names if n in turns[:3]]
        self.far = turns[3:]

    def same_chip(self, name):
        at = [1 if n == name else 0 for n in self.mesh.axis_names]
        here = self.mesh.devices[tuple([0] * len(at))]
        there = self.mesh.devices[tuple(at)]
        return tuple(getattr(here, "coords", (0,))) == tuple(getattr(there, "coords", (1,)))

    def swap(self, block, axis):
        return lax.ppermute(block, axis, [(0, 1), (1, 0)])

    def shift(self, block, name, distance):
        axes = self.axes[name]
        devices = range(1 << len(axes))
        route = [(i - distance, i) for i in devices if i - distance in devices]
        return lax.ppermute(block, axes, route)

    def exchange(self, parts):
        return lax.all_to_all(parts, tuple(self.near), 0, 0, tiled=True)

    def send(self, block, mask):
        near = tuple(self.near)
        return lax.ppermute(block, near, [(n, n ^ mask) for n in range(1 << len(near))])

    def pairs(self, inner, outer):
        axes = self.axes["height"]
        low = range(1, (1 << len(axes)) - 1, 2)
        route = [(i, i + 1) for i in low] + [(i + 1, i) for i in low]
        outer = lax.ppermute(outer, axes, route)
        return self.swap(inner, axes[-1]), outer

    def far_sums(self, total):
        for axis in self.far[:-1]:
            total = total.astype(jnp.float32) + self.swap(total, axis).astype(jnp.float32)
            total = lax.reduce_precision(total, 8, 7).astype(jnp.bfloat16)
        return total, self.swap(total, self.far[-1])


SIDES = ((0, 0), (0, 1), (1, 0), (1, 1))


def grant(mib):
    return pltpu.CompilerParams(vmem_limit_bytes=mib * 2**20)


def product(left, right):
    return jnp.dot(left, right, preferred_element_type=jnp.float32)


def product_nt(left, right):
    return lax.dot_general(left, right, (((1,), (1,)), ((), ())), preferred_element_type=jnp.float32)


def rows_at_once(rows_low, cols_low):
    return max(n for n in (1, 2, 4, 8) if rows_low % n == 0 and (n == 1 or 4 * n * cols_low <= 256))


def by_side(count, cols_low, dtype=jnp.bfloat16):
    size = 4 * count * cols_low
    to = lax.broadcasted_iota(jnp.int32, (size, size), 0)
    at = lax.broadcasted_iota(jnp.int32, (size, size), 1)
    q, rest = to % cols_low, to // cols_low
    p, side = rest % count, rest // count
    return (at == (p * 2 + side // 2) * 2 * cols_low + 2 * q + side % 2).astype(jnp.float32).astype(dtype)


def from_side(count, cols_low, dtype=jnp.bfloat16):
    size = 4 * count * cols_low
    at = lax.broadcasted_iota(jnp.int32, (size, size), 0)
    to = lax.broadcasted_iota(jnp.int32, (size, size), 1)
    q, rest = to % cols_low, to // cols_low
    p, side = rest % count, rest // count
    return (at == (p * 2 + side // 2) * 2 * cols_low + 2 * q + side % 2).astype(jnp.float32).astype(dtype)


def box(count, cols_low, dtype=jnp.bfloat16):
    size = 4 * count * cols_low
    to = lax.broadcasted_iota(jnp.int32, (size // 4, size), 0)
    at = lax.broadcasted_iota(jnp.int32, (size // 4, size), 1)
    p, q = at // (4 * cols_low), at % (2 * cols_low) // 2
    return (to == p * cols_low + q).astype(jnp.float32).astype(dtype)


def column(rows, cols_low, chan):
    return lax.broadcasted_iota(jnp.int32, (rows, chan), 0) % cols_low


def from_left(x, at):
    return jnp.where(at == 0, 0.0, pltpu.roll(x, 1, 0))


def from_right(x, at, last):
    return jnp.where(at == last, 0.0, pltpu.roll(x, x.shape[0] - 1, 0))


def sort_columns(source, target, cols_low):
    rows_low, chan = source.shape[0] // 2, source.shape[2]
    group = rows_at_once(rows_low, cols_low)
    span = group * cols_low
    order = by_side(group, cols_low)
    for n in range(rows_low // group):
        block = source[2 * group * n : 2 * group * (n + 1)].reshape(4 * span, chan)
        block = product(order, block).astype(jnp.bfloat16).reshape(4, span, chan)
        target[:, n * span : (n + 1) * span, :] = block


def tall(place_ref, low_ref, inner_ref, outer_ref, frame, lanes=slice(None)):
    odd = place_ref[1] == 1
    inner, outer = inner_ref[frame, :, :, lanes], outer_ref[frame, :, :, lanes]
    up, down = jnp.where(odd, inner, outer), jnp.where(odd, outer, inner)
    return jnp.concatenate([up, low_ref[frame, :, :, lanes], down], axis=0)


def spatial(low, ws_ref):
    rows_low, cols_low, chan = low.shape[0] - 2, low.shape[1], low.shape[2]
    count = rows_low * cols_low
    flat = low.reshape(-1, chan)
    rows = [[], []]
    for j in range(3):
        taps = [product(flat, ws_ref[i, j]).reshape(low.shape) for i in range(3)]
        even = taps[0][:rows_low] + (taps[1] + taps[2])[1 : rows_low + 1]
        odd = (taps[0] + taps[1])[1 : rows_low + 1] + taps[2][2:]
        rows[0].append(even.reshape(count, chan))
        rows[1].append(odd.reshape(count, chan))
    at = column(count, cols_low, chan)
    for first, second, third in rows:
        yield from_left(first, at) + (second + third)
        yield (first + second) + from_right(third, at, cols_low - 1)


def forward_kernel(place_ref, low_ref, inner_ref, outer_ref, ws_ref, act_ref, slope_ref):
    for frame in range(low_ref.shape[0]):
        low = tall(place_ref, low_ref, inner_ref, outer_ref, frame)
        for side, pre in enumerate(spatial(low, ws_ref)):
            sig = jax.nn.sigmoid(pre)
            act_ref[frame, side] = (pre * sig).astype(jnp.bfloat16)
            slope_ref[frame, side] = sig * (1.0 + pre * (1.0 - sig))


def act_kernel(low_ref, ws_ref, _, act_ref):
    for side, pre in enumerate(spatial(low_ref[0], ws_ref)):
        act_ref[0, side] = (pre * jax.nn.sigmoid(pre)).astype(jnp.bfloat16)


def half_sums(place_ref, low_ref, inner_ref, outer_ref, act_ref, pg_ref, ext_ref, out_ref):
    frames, rows_low, cols_low, chan = low_ref.shape
    count, half = rows_low * cols_low, chan // 2
    lanes = pl.ds(pl.multiple_of(place_ref[0] * half, half), half)
    lefts = [[] for _ in range(9)]
    acts = []
    at = column((rows_low + 2) * cols_low, cols_low, half)
    for frame in range(frames):
        low = tall(place_ref, low_ref, inner_ref, outer_ref, frame, lanes)
        wide = low.reshape(-1, half).astype(jnp.float32)
        moved = [from_left(wide, at), wide, from_right(wide, at, cols_low - 1)]
        turned = {}
        for dc in range(3):
            view = moved[dc].astype(jnp.bfloat16).reshape(low.shape)
            for dr in range(3):
                turned[dr - 1, dc - 1] = view[dr : dr + rows_low].reshape(count, half).T
        for i in range(3):
            for j in range(3):
                lefts[3 * i + j] += [turned[(a + i - 1) // 2, (b + j - 1) // 2] for a, b in SIDES]
        acts.append(act_ref[frame, :, :, lanes].reshape(4 * count, half).T)
    pg = pg_ref[...].reshape(frames * 4 * count, chan)
    for tap, left in enumerate(lefts):
        out_ref[tap] = product(jnp.concatenate(left, axis=1), pg)
    act = jnp.concatenate(acts, axis=1)
    for k in range(3):
        out_ref[9 + k] = product(act, ext_ref[k : k + frames].reshape(frames * 4 * count, chan))


def backward_kernel(place_ref, low_ref, inner_ref, outer_ref, act_ref, slope_ref, cot_ref, later_ref, wt_ref, pg_ref, ext_ref, out_ref):
    frames, _, count, chan = cot_ref.shape
    ext_ref[:frames] = cot_ref[...]
    for n in range(2):
        sort_columns(later_ref.at[n], ext_ref.at[frames + n], low_ref.shape[2])
    for frame in range(frames):
        act_grad = product_nt(ext_ref[frame].reshape(4 * count, chan), wt_ref[0])
        for k in (1, 2):
            act_grad = act_grad + product_nt(ext_ref[frame + k].reshape(4 * count, chan), wt_ref[k])
        slope = slope_ref[frame].reshape(4 * count, chan)
        pg_ref[frame] = (act_grad * slope).astype(jnp.bfloat16).reshape(4, count, chan)
    half_sums(place_ref, low_ref, inner_ref, outer_ref, act_ref, pg_ref, ext_ref, out_ref)


def whole(shape):
    return pl.BlockSpec(shape, lambda f, *_: (0,) * len(shape))


def each(shape):
    return pl.BlockSpec((1,) + tuple(shape[1:]), lambda f, *_: (f,) + (0,) * (len(shape) - 1))


SCALAR = pl.BlockSpec(memory_space=pltpu.SMEM)
UNREAD = pl.BlockSpec(memory_space=pl.ANY)


def like(shape, dtype):
    return jax.ShapeDtypeStruct(shape, dtype)


TOKEN = like((8, 128), jnp.float32)


def cost(units, mib):
    return pl.CostEstimate(flops=units * 2 * 2048 * 256 * 256, bytes_accessed=mib * 2**20, transcendentals=0)


def in_hbm(array):
    return pltpu.with_memory_space_constraint(array, pltpu.HBM)


FULL = pl.BlockSpec(memory_space=pltpu.VMEM)


def first_kernel(place_ref, low_ref, cot_ref, inner_ref, outer_ref, later_ref, sems):
    last = low_ref.shape[1] - 1
    odd = place_ref[1]
    copies = [
        pltpu.make_async_copy(cot_ref.at[0:2], later_ref, sems.at[0]),
        pltpu.make_async_copy(low_ref.at[:, pl.ds(last * (1 - odd), 1)], inner_ref, sems.at[1]),
        pltpu.make_async_copy(low_ref.at[:, pl.ds(last * odd, 1)], outer_ref, sems.at[2]),
    ]
    for copy in copies:
        copy.start()
    for copy in copies:
        copy.wait()


def first_messages(place, low, cot):
    row = like(low[:, :1].shape, low.dtype)
    return pl.pallas_call(
        first_kernel,
        in_specs=[SCALAR, UNREAD, UNREAD],
        out_specs=[FULL] * 3,
        out_shape=[row, row, like(cot[:2].shape, cot.dtype)],
        scratch_shapes=[pltpu.SemaphoreType.DMA((3,))],
        compiler_params=grant(4),
        name="first_messages",
    )(place, in_hbm(low), in_hbm(cot))


def load_kernel(low_hbm, cot_hbm, ws_hbm, wt_hbm, low_ref, ws_ref, wt_ref, side_ref, cot_ref, sems):
    frames, cols_low = low_ref.shape[0], low_ref.shape[2]
    copies = [pltpu.make_async_copy(cot_hbm.at[n], cot_ref.at[n], sems.at[n]) for n in range(frames)]
    pairs = ((low_hbm, low_ref), (ws_hbm, ws_ref), (wt_hbm, wt_ref))
    copies += [pltpu.make_async_copy(a, b, sems.at[frames + n]) for n, (a, b) in enumerate(pairs)]
    for copy in copies:
        copy.start()
    for n in range(frames):
        copies[n].wait()
        sort_columns(cot_ref.at[n], side_ref.at[n], cols_low)
    for copy in copies[frames:]:
        copy.wait()


def load(low, cot, ws, wt):
    frames, rows_low, cols_low, chan = low.shape
    return pl.pallas_call(
        load_kernel,
        in_specs=[UNREAD] * 4,
        out_specs=[FULL] * 4,
        out_shape=[like(low.shape, low.dtype), like(ws.shape, ws.dtype), like(wt.shape, wt.dtype),
                   like((frames, 4, rows_low * cols_low, chan), jnp.bfloat16)],
        scratch_shapes=[pltpu.VMEM(cot.shape, cot.dtype), pltpu.SemaphoreType.DMA((frames + 3,))],
        compiler_params=grant(12),
        cost_estimate=cost(2, 4),
        name="load",
    )(in_hbm(low), in_hbm(cot), in_hbm(ws), in_hbm(wt))


def forward(place, low, inner, outer, ws):
    frames, rows_low, cols_low, chan = low.shape
    side = (frames, 4, rows_low * cols_low, chan)
    return pl.pallas_call(
        forward_kernel,
        in_specs=[SCALAR] + [FULL] * 4,
        out_specs=[FULL] * 2,
        out_shape=[like(side, jnp.bfloat16), like(side, jnp.float32)],
        compiler_params=grant(20),
        cost_estimate=cost(10, 8),
        name="forward",
    )(place, low, inner, outer, ws)


def edges_kernel(place_ref, low_ref, inner_ref, outer_ref, pg_ref, _, tall_ref, pg_inner, pg_outer):
    cols_low = low_ref.shape[2]
    first = low_ref.shape[0] - tall_ref.shape[0]
    for n in range(tall_ref.shape[0]):
        tall_ref[n] = tall(place_ref, low_ref, inner_ref, outer_ref, first + n)
    odd = place_ref[1] == 1
    top, bottom = pg_ref[:, :2, :cols_low, :], pg_ref[:, 2:, -cols_low:, :]
    pg_inner[...] = jnp.where(odd, top, bottom)
    pg_outer[...] = jnp.where(odd, bottom, top)


def edges(place, low, inner, outer, pg, before):
    frames, rows_low, cols_low, chan = low.shape
    full = pl.BlockSpec(memory_space=pltpu.VMEM)
    rows = like((frames, 2, cols_low, chan), jnp.bfloat16)
    return pl.pallas_call(
        edges_kernel,
        in_specs=[SCALAR, full, full, full, full, UNREAD],
        out_specs=[full] * 3,
        out_shape=[like((2, rows_low + 2, cols_low, chan), jnp.bfloat16), rows, rows],
        compiler_params=grant(8),
        name="edges",
    )(place, low, inner, outer, pg, before)


def earlier_act(low, ws, before):
    frames, rows_tall, cols_low, chan = low.shape
    side = (frames, 4, (rows_tall - 2) * cols_low, chan)
    return pl.pallas_call(
        act_kernel,
        grid=(frames,),
        in_specs=[each(low.shape), whole(ws.shape), UNREAD],
        out_specs=each(side),
        out_shape=like(side, jnp.bfloat16),
        compiler_params=grant(16),
        cost_estimate=cost(4, 3),
        name="earlier_act",
    )(low, ws, before)


def backward(place, low, inner, outer, act, slope, cot, later, wt):
    frames, _, _, chan = act.shape
    ext = (frames + 2,) + act.shape[1:]
    return pl.pallas_call(
        backward_kernel,
        in_specs=[SCALAR] + [FULL] * 8,
        out_specs=[FULL] * 3,
        out_shape=[like(act.shape, jnp.bfloat16), like(ext, jnp.bfloat16), like((12, chan // 2, chan), jnp.float32)],
        compiler_params=grant(24),
        cost_estimate=cost(15, 10),
        name="backward",
    )(place, low, inner, outer, act, slope, cot, later, wt)


def half_grads(place, low, inner, outer, act, pg, ext):
    chan = low.shape[-1]
    return pl.pallas_call(
        half_sums,
        in_specs=[SCALAR] + [FULL] * 6,
        out_specs=FULL,
        out_shape=like((12, chan // 2, chan), jnp.float32),
        compiler_params=grant(20),
        cost_estimate=cost(10, 6),
        name="half_grads",
    )(place, low, inner, outer, act, pg, ext)


def section_kernel(act_ref, low_ref, wt_ref, _, out_ref, token_ref):
    token_ref[...] = jnp.zeros_like(token_ref)
    frame = pl.program_id(0)
    _, rows_low, cols_low, chan = low_ref.shape
    group = rows_at_once(rows_low, cols_low)
    span = group * cols_low
    order = from_side(group, cols_low)
    low = low_ref[0].reshape(-1, chan).astype(jnp.float32)
    mixed = []
    for side in range(4):
        total = low
        for k in range(3):
            total = total + product(act_ref[frame + 2 - k, side], wt_ref[k])
        mixed.append(total.astype(jnp.bfloat16))
    for n in range(rows_low // group):
        block = jnp.concatenate([m[n * span : (n + 1) * span] for m in mixed], axis=0)
        block = product(order, block).astype(jnp.bfloat16)
        out_ref[0, 2 * group * n : 2 * group * (n + 1)] = block.reshape(2 * group, 2 * cols_low, chan)


def section(act_ext, low, wt, before):
    frames, rows_low, cols_low, chan = low.shape
    out = (frames, 2 * rows_low, 2 * cols_low, chan)
    return pl.pallas_call(
        section_kernel,
        grid=(frames,),
        in_specs=[whole(act_ext.shape), each(low.shape), whole(wt.shape), UNREAD],
        out_specs=[each(out), whole(TOKEN.shape)],
        out_shape=[like(out, jnp.bfloat16), TOKEN],
        compiler_params=grant(16),
        cost_estimate=pl.CostEstimate(flops=2 * 2048 * chan * chan * 4, bytes_accessed=3 * 2**20, transcendentals=0),
        name="section",
    )(act_ext, low, wt, before)


def input_kernel(place_ref, pg_ref, inner_ref, outer_ref, cot_ref, ws_ref, _, out_ref, token_ref):
    token_ref[...] = jnp.zeros_like(token_ref)
    _, rows_low, cols_low, chan = out_ref.shape
    group = rows_at_once(rows_low, cols_low)
    span = group * cols_low
    boxes = box(group, cols_low)
    count = rows_low * cols_low
    total = jnp.concatenate(
        [product(boxes, cot_ref[0, 2 * group * n : 2 * group * (n + 1)].reshape(4 * span, chan))
         for n in range(rows_low // group)], axis=0)
    higher = (rows_low + 1, cols_low, chan)
    at = column(higher[0] * cols_low, cols_low, chan)
    own = [pg_ref[0, side].astype(jnp.float32) for side in range(4)]
    odd_place = place_ref[1] == 1
    inner = [inner_ref[0, b].astype(jnp.float32) for b in range(2)]
    outer = [outer_ref[0, b].astype(jnp.float32) for b in range(2)]
    above = [jnp.where(odd_place, inner[b], outer[b]) for b in range(2)]
    below = [jnp.where(odd_place, outer[b], inner[b]) for b in range(2)]
    even = [jnp.concatenate([own[b], below[b]], axis=0) for b in range(2)]
    odd = [jnp.concatenate([above[b], own[2 + b]], axis=0) for b in range(2)]
    for j in range(3):
        pair = []
        for first, second in (even, odd):
            if j == 0:
                value = second + from_right(first, at, cols_low - 1)
            elif j == 1:
                value = first + second
            else:
                value = first + from_left(second, at)
            pair.append(value.reshape(higher))
        top, low = pair
        for i, value in enumerate((low[1:] + top[1:], top[:-1] + low[1:], low[:-1] + top[:-1])):
            value = value.reshape(count, chan)
            high = value.astype(jnp.bfloat16)
            rest = (value - high.astype(jnp.float32)).astype(jnp.bfloat16)
            total = total + product_nt(high, ws_ref[i, j]) + product_nt(rest, ws_ref[i, j])
    out_ref[0] = total.astype(jnp.bfloat16).reshape(rows_low, cols_low, chan)


def input_grads(place, pg, inner, outer, cot, ws, before, low_shape):
    chan = low_shape[-1]
    return pl.pallas_call(
        input_kernel,
        grid=(low_shape[0],),
        in_specs=[SCALAR, each(pg.shape), each(inner.shape), each(outer.shape), each(cot.shape), whole(ws.shape), UNREAD],
        out_specs=[each(low_shape), whole(TOKEN.shape)],
        out_shape=[like(low_shape, jnp.bfloat16), TOKEN],
        compiler_params=grant(20),
        cost_estimate=pl.CostEstimate(flops=2 * 2048 * chan * chan * 6, bytes_accessed=4 * 2**20, transcendentals=0),
        name="input_grads",
    )(place, pg, inner, outer, cot, ws, before)


def put_kernel(place_ref, half_ref, *refs):
    spatial_ref, temporal_ref, wide, sems = refs[-4:]
    taps, half, _ = half_ref.shape
    to = pl.ds(pl.multiple_of(place_ref[0] * half, half), half)
    copies = []
    for tap in range(taps):
        wide[tap] = half_ref[tap].astype(jnp.float32)
        if tap < 9:
            target = spatial_ref.at[tap // 3, tap % 3, to]
        else:
            target = temporal_ref.at[tap - 9, to]
        copies.append(pltpu.make_async_copy(wide.at[tap], target, sems.at[tap]))
        copies[-1].start()
    for copy in copies:
        copy.wait()


def put(place, half, *done):
    chan = half.shape[-1]
    hbm = pl.BlockSpec(memory_space=pltpu.HBM)
    return pl.pallas_call(
        put_kernel,
        in_specs=[SCALAR, FULL] + [hbm] * len(done),
        out_specs=[hbm, hbm],
        out_shape=[like((3, 3, chan, chan), jnp.float32), like((3, chan, chan), jnp.float32)],
        input_output_aliases={2 + n: n for n in range(len(done))},
        scratch_shapes=[pltpu.VMEM((12, chan // 2, chan), jnp.float32), pltpu.SemaphoreType.DMA((12,))],
        compiler_params=grant(6),
        name="put",
    )(place, half, *done)


def add_kernel(mine_ref, theirs_ref, out_ref):
    out_ref[...] = (mine_ref[...] + theirs_ref[...]).astype(jnp.bfloat16)


def add_halves(mine, theirs):
    return pl.pallas_call(
        add_kernel,
        in_specs=[FULL, FULL],
        out_specs=FULL,
        out_shape=like(mine.shape, jnp.bfloat16),
        compiler_params=grant(6),
        name="add_halves",
    )(mine, theirs)


def sum_kernel(got_ref, _, out_ref):
    total = got_ref[0].astype(jnp.float32)
    for n in range(1, got_ref.shape[0]):
        total = total + got_ref[n].astype(jnp.float32)
    out_ref[...] = total.astype(jnp.bfloat16)


def sum_parts(got, before):
    return pl.pallas_call(
        sum_kernel,
        in_specs=[FULL, UNREAD],
        out_specs=FULL,
        out_shape=like(got.shape[1:], jnp.bfloat16),
        compiler_params=grant(4),
        name="sum_parts",
    )(got, before)


def far_kernel(own_ref, theirs_ref, *refs):
    refs[-1][...] = (own_ref[...].astype(jnp.float32) + theirs_ref[...].astype(jnp.float32)).astype(jnp.bfloat16)


def add_far(own, theirs, *before):
    return pl.pallas_call(
        far_kernel,
        in_specs=[FULL, FULL] + [UNREAD] * len(before),
        out_specs=FULL,
        out_shape=like(own.shape, jnp.bfloat16),
        compiler_params=grant(2),
        name="add_far",
    )(own, theirs, *before)


def join_kernel(place_ref, *refs):
    out_ref = refs[-1]
    rows = refs[0].shape[0]
    for n, ref in enumerate(refs[:-1]):
        at = pl.ds(pl.multiple_of((place_ref[2] ^ n) * rows, rows), rows)
        out_ref[at] = ref[...]


def join(place, parts):
    rows, chan = parts[0].shape
    return pl.pallas_call(
        join_kernel,
        in_specs=[SCALAR] + [FULL] * len(parts),
        out_specs=FULL,
        out_shape=like((rows * len(parts), chan), jnp.bfloat16),
        compiler_params=grant(4),
        name="join",
    )(place, *parts)


def on_device(bits, low_frames, spatial_weight, temporal_weight, cotangent):
    low, cot = low_frames[0], cotangent[0]
    frames, rows_low, cols_low, chan = low.shape
    core = lax.axis_index(bits.core).astype(jnp.int32)
    odd = lax.axis_index(bits.axes["height"][-1]).astype(jnp.int32)
    code = lax.axis_index(tuple(bits.near)).astype(jnp.int32)
    mine, other = jnp.stack([core, odd, code]), jnp.stack([1 - core, odd, code])
    parts = 1 << len(bits.near)

    inner, outer, later = first_messages(mine, low, cot)
    later = bits.shift(later, "tm", -1)
    inner, outer = bits.pairs(inner, outer)
    low, ws, wt, cot_side = load(low, cot, spatial_weight, temporal_weight)
    act, slope = forward(mine, low, inner, outer, ws)
    pg, ext, theirs = backward(other, low, inner, outer, act, slope, cot_side, later, wt)
    theirs = bits.swap(theirs, bits.core)
    own = half_grads(mine, low, inner, outer, act, pg, ext)
    kept = add_halves(own, theirs)
    got = bits.exchange(kept.reshape(parts, -1, chan))

    edge, pg_inner, pg_outer = edges(mine, low, inner, outer, pg, kept)
    pg_inner, pg_outer = bits.pairs(pg_inner, pg_outer)
    input_grad, input_done = input_grads(mine, pg, pg_inner, pg_outer, cot, ws, kept, low.shape)
    edge = bits.shift(edge, "tm", 1)
    total, far = bits.far_sums(sum_parts(got, input_done))
    earlier = earlier_act(edge, ws, total)
    section_out, section_done = section(jnp.concatenate([earlier, act], axis=0), low, wt, total)
    total = add_far(total, far, section_done)
    half = join(mine, [total] + [bits.send(total, n) for n in range(1, parts)]).reshape(own.shape)
    theirs = bits.swap(half, bits.core)
    spatial_grad, temporal_grad = put(other, theirs, *put(mine, half))
    return section_out[None], input_grad[None], spatial_grad, temporal_grad


def solution(mesh):
    bits = Bits(mesh)
    block = P(*(bits.axes[name] for name in ("dp", "tm", "height")), None, None)
    return jax.shard_map(
        functools.partial(on_device, bits),
        mesh=bits.mesh,
        in_specs=(block, P(), P(), block),
        out_specs=(block, block, P(), P()),
        check_vma=False,
    )
```

```python
import functools

import jax
import jax.numpy as jnp
from jax import lax
from jax.experimental import pallas as pl
from jax.experimental.pallas import tpu as pltpu
from jax.sharding import Mesh
from jax.sharding import PartitionSpec as P


class Bits:
    def __init__(self, mesh):
        self.axes = {}
        for name in mesh.axis_names:
            count = mesh.shape[name].bit_length() - 1
            self.axes[name] = tuple(f"{name}{bit}" for bit in reversed(range(count)))
        names = [bit for bits in self.axes.values() for bit in bits]
        self.mesh = Mesh(mesh.devices.reshape([2] * len(names)), tuple(names))
        self.core = next((n for n in names if self.same_chip(n)), self.axes["tm"][-1])
        others = [[b for b in reversed(bits) if b != self.core] for bits in self.axes.values()]
        turns = [bits[turn] for turn in range(len(names)) for bits in others if turn < len(bits)]
        self.near = [n for n in names if n in turns[:3]]
        self.far = turns[3:]

    def same_chip(self, name):
        at = [1 if n == name else 0 for n in self.mesh.axis_names]
        here = self.mesh.devices[tuple([0] * len(at))]
        there = self.mesh.devices[tuple(at)]
        return tuple(getattr(here, "coords", (0,))) == tuple(getattr(there, "coords", (1,)))

    def swap(self, block, axis):
        return lax.ppermute(block, axis, [(0, 1), (1, 0)])

    def shift(self, block, name, distance):
        axes = self.axes[name]
        devices = range(1 << len(axes))
        route = [(i - distance, i) for i in devices if i - distance in devices]
        return lax.ppermute(block, axes, route)

    def exchange(self, parts):
        return lax.all_to_all(parts, tuple(self.near), 0, 0, tiled=True)

    def pairs(self, inner, outer):
        axes = self.axes["height"]
        low = range(1, (1 << len(axes)) - 1, 2)
        route = [(i, i + 1) for i in low] + [(i + 1, i) for i in low]
        outer = lax.ppermute(outer, axes, route)
        return self.swap(inner, axes[-1]), outer

    def far_sums(self, total):
        for axis in self.far[:-1]:
            total = total.astype(jnp.float32) + self.swap(total, axis).astype(jnp.float32)
            total = lax.reduce_precision(total, 8, 7).astype(jnp.bfloat16)
        return total, self.swap(total, self.far[-1])


SIDES = ((0, 0), (0, 1), (1, 0), (1, 1))


def grant(mib):
    return pltpu.CompilerParams(vmem_limit_bytes=mib * 2**20)


def product(left, right):
    return jnp.dot(left, right, preferred_element_type=jnp.float32)


def product_nt(left, right):
    return lax.dot_general(left, right, (((1,), (1,)), ((), ())), preferred_element_type=jnp.float32)


def rows_at_once(rows_low, cols_low):
    return max(n for n in (1, 2, 4, 8) if rows_low % n == 0 and (n == 1 or 4 * n * cols_low <= 256))


def by_side(count, cols_low, dtype=jnp.bfloat16):
    size = 4 * count * cols_low
    to = lax.broadcasted_iota(jnp.int32, (size, size), 0)
    at = lax.broadcasted_iota(jnp.int32, (size, size), 1)
    q, rest = to % cols_low, to // cols_low
    p, side = rest % count, rest // count
    return (at == (p * 2 + side // 2) * 2 * cols_low + 2 * q + side % 2).astype(jnp.float32).astype(dtype)


def from_side(count, cols_low, dtype=jnp.bfloat16):
    size = 4 * count * cols_low
    at = lax.broadcasted_iota(jnp.int32, (size, size), 0)
    to = lax.broadcasted_iota(jnp.int32, (size, size), 1)
    q, rest = to % cols_low, to // cols_low
    p, side = rest % count, rest // count
    return (at == (p * 2 + side // 2) * 2 * cols_low + 2 * q + side % 2).astype(jnp.float32).astype(dtype)


def column(rows, cols_low, chan):
    return lax.broadcasted_iota(jnp.int32, (rows, chan), 0) % cols_low


def from_left(x, at):
    return jnp.where(at == 0, 0.0, pltpu.roll(x, 1, 0))


def from_right(x, at, last):
    return jnp.where(at == last, 0.0, pltpu.roll(x, x.shape[0] - 1, 0))


def sort_columns(source, target, cols_low):
    rows_low, chan = source.shape[0] // 2, source.shape[2]
    group = rows_at_once(rows_low, cols_low)
    span = group * cols_low
    order = by_side(group, cols_low)
    for n in range(rows_low // group):
        block = source[2 * group * n : 2 * group * (n + 1)].reshape(4 * span, chan)
        block = product(order, block).astype(jnp.bfloat16).reshape(4, span, chan)
        target[:, n * span : (n + 1) * span, :] = block


def tall(place_ref, low_ref, inner_ref, outer_ref, frame, lanes=slice(None)):
    odd = place_ref[1] == 1
    inner, outer = inner_ref[frame, :, :, lanes], outer_ref[frame, :, :, lanes]
    up, down = jnp.where(odd, inner, outer), jnp.where(odd, outer, inner)
    return jnp.concatenate([up, low_ref[frame, :, :, lanes], down], axis=0)


def spatial(low, ws_ref):
    rows_low, cols_low, chan = low.shape[0] - 2, low.shape[1], low.shape[2]
    count = rows_low * cols_low
    flat = low.reshape(-1, chan)
    rows = [[], []]
    for j in range(3):
        taps = [product(flat, ws_ref[i, j]).reshape(low.shape) for i in range(3)]
        even = taps[0][:rows_low] + (taps[1] + taps[2])[1 : rows_low + 1]
        odd = (taps[0] + taps[1])[1 : rows_low + 1] + taps[2][2:]
        rows[0].append(even.reshape(count, chan))
        rows[1].append(odd.reshape(count, chan))
    at = column(count, cols_low, chan)
    for first, second, third in rows:
        yield from_left(first, at) + (second + third)
        yield (first + second) + from_right(third, at, cols_low - 1)


def forward_kernel(place_ref, low_ref, inner_ref, outer_ref, ws_ref, act_ref, slope_ref):
    for frame in range(low_ref.shape[0]):
        low = tall(place_ref, low_ref, inner_ref, outer_ref, frame)
        for side, pre in enumerate(spatial(low, ws_ref)):
            sig = jax.nn.sigmoid(pre)
            act_ref[frame, side] = (pre * sig).astype(jnp.bfloat16)
            slope_ref[frame, side] = sig * (1.0 + pre * (1.0 - sig))


def act_kernel(low_ref, ws_ref, _, act_ref):
    for frame in range(low_ref.shape[0]):
        for side, pre in enumerate(spatial(low_ref[frame], ws_ref)):
            act_ref[frame, side] = (pre * jax.nn.sigmoid(pre)).astype(jnp.bfloat16)


def half_sums(place_ref, low_ref, inner_ref, outer_ref, act_ref, pg_ref, ext_ref, out_ref):
    frames, rows_low, cols_low, chan = low_ref.shape
    count, half = rows_low * cols_low, chan // 2
    lanes = pl.ds(pl.multiple_of(place_ref[0] * half, half), half)
    lefts = [[] for _ in range(9)]
    acts = []
    at = column((rows_low + 2) * cols_low, cols_low, half)
    for frame in range(frames):
        low = tall(place_ref, low_ref, inner_ref, outer_ref, frame, lanes)
        wide = low.reshape(-1, half).astype(jnp.float32)
        moved = [from_left(wide, at), wide, from_right(wide, at, cols_low - 1)]
        turned = {}
        for dc in range(3):
            view = moved[dc].astype(jnp.bfloat16).reshape(low.shape)
            for dr in range(3):
                turned[dr - 1, dc - 1] = view[dr : dr + rows_low].reshape(count, half).T
        for i in range(3):
            for j in range(3):
                lefts[3 * i + j] += [turned[(a + i - 1) // 2, (b + j - 1) // 2] for a, b in SIDES]
        acts.append(act_ref[frame, :, :, lanes].reshape(4 * count, half).T)
    pg = pg_ref[...].reshape(frames * 4 * count, chan)
    for tap, left in enumerate(lefts):
        out_ref[tap] = product(jnp.concatenate(left, axis=1), pg)
    act = jnp.concatenate(acts, axis=1)
    for k in range(3):
        out_ref[9 + k] = product(act, ext_ref[k : k + frames].reshape(frames * 4 * count, chan))


def backward_kernel(place_ref, low_ref, inner_ref, outer_ref, act_ref, slope_ref, cot_ref, later_ref, wt_ref, pg_ref, ext_ref, out_ref):
    frames, _, count, chan = cot_ref.shape
    ext_ref[:frames] = cot_ref[...]
    for n in range(2):
        sort_columns(later_ref.at[n], ext_ref.at[frames + n], low_ref.shape[2])
    for frame in range(frames):
        act_grad = product_nt(ext_ref[frame].reshape(4 * count, chan), wt_ref[0])
        for k in (1, 2):
            act_grad = act_grad + product_nt(ext_ref[frame + k].reshape(4 * count, chan), wt_ref[k])
        slope = slope_ref[frame].reshape(4 * count, chan)
        pg_ref[frame] = (act_grad * slope).astype(jnp.bfloat16).reshape(4, count, chan)
    half_sums(place_ref, low_ref, inner_ref, outer_ref, act_ref, pg_ref, ext_ref, out_ref)


SCALAR = pl.BlockSpec(memory_space=pltpu.SMEM)
UNREAD = pl.BlockSpec(memory_space=pl.ANY)


def like(shape, dtype):
    return jax.ShapeDtypeStruct(shape, dtype)


TOKEN = like((8, 128), jnp.float32)


def cost(units, mib):
    return pl.CostEstimate(flops=units * 2 * 2048 * 256 * 256, bytes_accessed=mib * 2**20, transcendentals=0)


def in_hbm(array):
    return pltpu.with_memory_space_constraint(array, pltpu.HBM)


FULL = pl.BlockSpec(memory_space=pltpu.VMEM)


def first_kernel(place_ref, low_ref, cot_ref, inner_ref, outer_ref, later_ref, sems):
    last = low_ref.shape[1] - 1
    odd = place_ref[1]
    copies = [
        (low_ref.at[:, pl.ds(last * (1 - odd), 1)], inner_ref),
        (low_ref.at[:, pl.ds(last * odd, 1)], outer_ref),
    ]
    copies += [(cot_ref.at[n, r], later_ref.at[n, r]) for n in range(2) for r in range(cot_ref.shape[1])]
    copies = [pltpu.make_async_copy(a, b, sems.at[n]) for n, (a, b) in enumerate(copies)]
    for copy in copies:
        copy.start()
    for copy in copies:
        copy.wait()


def first_messages(place, low, cot):
    row = like(low[:, :1].shape, low.dtype)
    return pl.pallas_call(
        first_kernel,
        in_specs=[SCALAR, UNREAD, UNREAD],
        out_specs=[FULL] * 3,
        out_shape=[row, row, like(cot[:2].shape, cot.dtype)],
        scratch_shapes=[pltpu.SemaphoreType.DMA((2 + 2 * cot.shape[1],))],
        compiler_params=grant(4),
        name="first_messages",
    )(place, in_hbm(low), in_hbm(cot))


def load_kernel(low_hbm, cot_hbm, ws_hbm, wt_hbm, low_ref, ws_ref, wt_ref, side_ref, cot_ref, sems):
    frames, cols_low = low_ref.shape[0], low_ref.shape[2]
    copies = [pltpu.make_async_copy(cot_hbm.at[n], cot_ref.at[n], sems.at[n]) for n in range(frames)]
    pairs = [(low_hbm, low_ref)] + [(wt_hbm.at[k], wt_ref.at[k]) for k in range(3)]
    pairs += [(ws_hbm.at[i, j], ws_ref.at[i, j]) for i in range(3) for j in range(3)]
    copies += [pltpu.make_async_copy(a, b, sems.at[frames + n]) for n, (a, b) in enumerate(pairs)]
    for copy in copies:
        copy.start()
    for n in range(frames):
        copies[n].wait()
        sort_columns(cot_ref.at[n], side_ref.at[n], cols_low)
    for copy in copies[frames:]:
        copy.wait()


def load(low, cot, ws, wt):
    frames, rows_low, cols_low, chan = low.shape
    return pl.pallas_call(
        load_kernel,
        in_specs=[UNREAD] * 4,
        out_specs=[FULL] * 4,
        out_shape=[like(low.shape, low.dtype), like(ws.shape, ws.dtype), like(wt.shape, wt.dtype),
                   like((frames, 4, rows_low * cols_low, chan), jnp.bfloat16)],
        scratch_shapes=[pltpu.VMEM(cot.shape, cot.dtype), pltpu.SemaphoreType.DMA((frames + 13,))],
        compiler_params=grant(12),
        cost_estimate=cost(2, 4),
        name="load",
    )(in_hbm(low), in_hbm(cot), in_hbm(ws), in_hbm(wt))


def forward(place, low, inner, outer, ws):
    frames, rows_low, cols_low, chan = low.shape
    side = (frames, 4, rows_low * cols_low, chan)
    return pl.pallas_call(
        forward_kernel,
        in_specs=[SCALAR] + [FULL] * 4,
        out_specs=[FULL] * 2,
        out_shape=[like(side, jnp.bfloat16), like(side, jnp.float32)],
        compiler_params=grant(20),
        cost_estimate=cost(10, 8),
        name="forward",
    )(place, low, inner, outer, ws)


def edges_kernel(place_ref, low_ref, inner_ref, outer_ref, pg_ref, _, tall_ref, pg_inner, pg_outer):
    cols_low = low_ref.shape[2]
    first = low_ref.shape[0] - tall_ref.shape[0]
    for n in range(tall_ref.shape[0]):
        tall_ref[n] = tall(place_ref, low_ref, inner_ref, outer_ref, first + n)
    odd = place_ref[1] == 1
    top, bottom = pg_ref[:, :2, :cols_low, :], pg_ref[:, 2:, -cols_low:, :]
    pg_inner[...] = jnp.where(odd, top, bottom)
    pg_outer[...] = jnp.where(odd, bottom, top)


def edges(place, low, inner, outer, pg, before):
    frames, rows_low, cols_low, chan = low.shape
    full = pl.BlockSpec(memory_space=pltpu.VMEM)
    rows = like((frames, 2, cols_low, chan), jnp.bfloat16)
    return pl.pallas_call(
        edges_kernel,
        in_specs=[SCALAR, full, full, full, full, UNREAD],
        out_specs=[full] * 3,
        out_shape=[like((2, rows_low + 2, cols_low, chan), jnp.bfloat16), rows, rows],
        compiler_params=grant(8),
        name="edges",
    )(place, low, inner, outer, pg, before)


def earlier_act(low, ws, before):
    frames, rows_tall, cols_low, chan = low.shape
    return pl.pallas_call(
        act_kernel,
        in_specs=[FULL, FULL, UNREAD],
        out_specs=FULL,
        out_shape=like((frames, 4, (rows_tall - 2) * cols_low, chan), jnp.bfloat16),
        compiler_params=grant(10),
        cost_estimate=cost(4, 3),
        name="earlier_act",
    )(low, ws, before)


def backward(place, low, inner, outer, act, slope, cot, later, wt):
    frames, _, _, chan = act.shape
    ext = (frames + 2,) + act.shape[1:]
    return pl.pallas_call(
        backward_kernel,
        in_specs=[SCALAR] + [FULL] * 8,
        out_specs=[FULL] * 3,
        out_shape=[like(act.shape, jnp.bfloat16), like(ext, jnp.bfloat16), like((12, chan // 2, chan), jnp.float32)],
        compiler_params=grant(24),
        cost_estimate=cost(15, 10),
        name="backward",
    )(place, low, inner, outer, act, slope, cot, later, wt)


def half_grads(place, low, inner, outer, act, pg, ext):
    chan = low.shape[-1]
    return pl.pallas_call(
        half_sums,
        in_specs=[SCALAR] + [FULL] * 6,
        out_specs=FULL,
        out_shape=like((12, chan // 2, chan), jnp.float32),
        compiler_params=grant(20),
        cost_estimate=cost(10, 6),
        name="half_grads",
    )(place, low, inner, outer, act, pg, ext)


def section_kernel(earlier_ref, act_ref, low_ref, wt_ref, _, out_ref, token_ref, held, sems):
    frames, rows_low, cols_low, chan = low_ref.shape
    group = rows_at_once(rows_low, cols_low)
    span, count = group * cols_low, rows_low * cols_low
    order = from_side(group, cols_low)
    token_ref[...] = jnp.zeros_like(token_ref)
    copies = []
    for frame in range(frames):
        total = jnp.concatenate([low_ref[frame].reshape(count, chan).astype(jnp.float32)] * 4, axis=0)
        for k in range(3):
            act = act_ref[frame - k] if frame >= k else earlier_ref[frame - k + 2]
            total = total + product(act.reshape(4 * count, chan), wt_ref[k])
        mixed = total.astype(jnp.bfloat16).reshape(4, count, chan)
        for n in range(rows_low // group):
            block = mixed[:, n * span : (n + 1) * span].reshape(4 * span, chan)
            block = product(order, block).astype(jnp.bfloat16)
            held[frame, 2 * group * n : 2 * group * (n + 1)] = block.reshape(2 * group, 2 * cols_low, chan)
        copies.append(pltpu.make_async_copy(held.at[frame], out_ref.at[frame], sems.at[frame]))
        copies[-1].start()
    for copy in copies:
        copy.wait()


HBM = pl.BlockSpec(memory_space=pltpu.HBM)


def section(earlier, act, low, wt, before):
    frames, rows_low, cols_low, chan = low.shape
    out = (frames, 2 * rows_low, 2 * cols_low, chan)
    return pl.pallas_call(
        section_kernel,
        in_specs=[FULL] * 4 + [UNREAD],
        out_specs=[HBM, FULL],
        out_shape=[like(out, jnp.bfloat16), TOKEN],
        scratch_shapes=[pltpu.VMEM(out, jnp.bfloat16), pltpu.SemaphoreType.DMA((frames,))],
        compiler_params=grant(10),
        cost_estimate=cost(4, 3),
        name="section",
    )(earlier, act, low, wt, before)


def split(value):
    high = value.astype(jnp.bfloat16)
    return high, (value - high.astype(jnp.float32)).astype(jnp.bfloat16)


def column_pair(first, second, j, at, last):
    if j == 0:
        return second + from_right(first, at, last)
    if j == 1:
        return first + second
    return first + from_left(second, at)


def input_kernel(pg_ref, ext_ref, ws_ref, _, out_ref):
    frames, _, count, chan = pg_ref.shape
    cols_low = out_ref.shape[2]
    rows_low = count // cols_low
    at = column(count, cols_low, chan)
    for frame in range(frames):
        total = sum(ext_ref[frame, side].astype(jnp.float32) for side in range(4))
        own = [pg_ref[frame, side].astype(jnp.float32) for side in range(4)]
        zero = jnp.zeros((1, cols_low, chan), jnp.float32)
        for j in range(3):
            even = column_pair(own[0], own[1], j, at, cols_low - 1).reshape(rows_low, cols_low, chan)
            odd = column_pair(own[2], own[3], j, at, cols_low - 1).reshape(rows_low, cols_low, chan)
            below = jnp.concatenate([even[1:], zero], axis=0)
            above = jnp.concatenate([zero, odd[:-1]], axis=0)
            for i, value in enumerate((odd + below, even + odd, above + even)):
                for part in split(value.reshape(count, chan)):
                    total = total + product_nt(part, ws_ref[i, j])
        out_ref[frame] = total.reshape(rows_low, cols_low, chan)


def input_own(pg, ext, ws, before, low_shape):
    return pl.pallas_call(
        input_kernel,
        in_specs=[FULL] * 3 + [UNREAD],
        out_specs=FULL,
        out_shape=like(low_shape, jnp.float32),
        compiler_params=grant(10),
        cost_estimate=cost(6, 4),
        name="input_own",
    )(pg, ext, ws, before)


def input_edge_kernel(place_ref, own_ref, inner_ref, outer_ref, ws_ref, out_ref, token_ref, held, sem):
    frames, rows_low, cols_low, chan = own_ref.shape
    token_ref[...] = jnp.zeros_like(token_ref)
    odd_place = place_ref[1] == 1
    flat = (frames * cols_low, chan)
    at = column(flat[0], cols_low, chan)
    inner = [inner_ref[:, b].reshape(flat).astype(jnp.float32) for b in range(2)]
    outer = [outer_ref[:, b].reshape(flat).astype(jnp.float32) for b in range(2)]
    above = [jnp.where(odd_place, inner[b], outer[b]) for b in range(2)]
    below = [jnp.where(odd_place, outer[b], inner[b]) for b in range(2)]
    terms = []
    for (first, second), i in ((above, 2), (below, 0)):
        total = jnp.zeros(flat, jnp.float32)
        for j in range(3):
            for part in split(column_pair(first, second, j, at, cols_low - 1)):
                total = total + product_nt(part, ws_ref[i, j])
        terms.append(total.reshape(frames, cols_low, chan))
    for row in range(rows_low):
        value = own_ref[:, row]
        if row == 0:
            value = value + terms[0]
        if row == rows_low - 1:
            value = value + terms[1]
        held[:, row] = value.astype(jnp.bfloat16)
    copy = pltpu.make_async_copy(held, out_ref, sem)
    copy.start()
    copy.wait()


def input_grads(place, own, inner, outer, ws):
    return pl.pallas_call(
        input_edge_kernel,
        in_specs=[SCALAR] + [FULL] * 4,
        out_specs=[HBM, FULL],
        out_shape=[like(own.shape, jnp.bfloat16), TOKEN],
        scratch_shapes=[pltpu.VMEM(own.shape, jnp.bfloat16), pltpu.SemaphoreType.DMA],
        compiler_params=grant(6),
        cost_estimate=cost(1, 1),
        name="input_edge",
    )(place, own, inner, outer, ws)


def put_kernel(place_ref, half_ref, *refs):
    spatial_ref, temporal_ref, wide, sems = refs[-4:]
    taps, half, _ = half_ref.shape
    to = pl.ds(pl.multiple_of(place_ref[0] * half, half), half)
    copies = []
    for tap in range(taps):
        wide[tap] = half_ref[tap].astype(jnp.float32)
        if tap < 9:
            target = spatial_ref.at[tap // 3, tap % 3, to]
        else:
            target = temporal_ref.at[tap - 9, to]
        copies.append(pltpu.make_async_copy(wide.at[tap], target, sems.at[tap]))
        copies[-1].start()
    for copy in copies:
        copy.wait()


def put(place, half, *done):
    chan = half.shape[-1]
    return pl.pallas_call(
        put_kernel,
        in_specs=[SCALAR, FULL] + [HBM] * len(done),
        out_specs=[HBM, HBM],
        out_shape=[like((3, 3, chan, chan), jnp.float32), like((3, chan, chan), jnp.float32)],
        input_output_aliases={2 + n: n for n in range(len(done))},
        scratch_shapes=[pltpu.VMEM((12, chan // 2, chan), jnp.float32), pltpu.SemaphoreType.DMA((12,))],
        compiler_params=grant(6),
        name="put",
    )(place, half, *done)


def add_kernel(mine_ref, theirs_ref, out_ref):
    out_ref[...] = (mine_ref[...] + theirs_ref[...]).astype(jnp.bfloat16)


def add_halves(mine, theirs):
    full = pl.BlockSpec(memory_space=pltpu.VMEM)
    return pl.pallas_call(
        add_kernel,
        in_specs=[full, full],
        out_specs=full,
        out_shape=like(mine.shape, jnp.bfloat16),
        compiler_params=grant(8),
        name="add_halves",
    )(mine, theirs)


def sum_kernel(got_ref, _, out_ref):
    total = got_ref[0].astype(jnp.float32)
    for n in range(1, got_ref.shape[0]):
        total = total + got_ref[n].astype(jnp.float32)
    out_ref[...] = total.astype(jnp.bfloat16)


def sum_parts(got, before):
    return pl.pallas_call(
        sum_kernel,
        in_specs=[FULL, UNREAD],
        out_specs=FULL,
        out_shape=like(got.shape[1:], jnp.bfloat16),
        compiler_params=grant(4),
        name="sum_parts",
    )(got, before)


def spread_kernel(own_ref, theirs_ref, *refs):
    total = (own_ref[...].astype(jnp.float32) + theirs_ref[...].astype(jnp.float32)).astype(jnp.bfloat16)
    for n in range(refs[-1].shape[0]):
        refs[-1][n] = total


def spread(own, theirs, parts, *before):
    return pl.pallas_call(
        spread_kernel,
        in_specs=[FULL, FULL] + [UNREAD] * len(before),
        out_specs=FULL,
        out_shape=like((parts,) + own.shape, jnp.bfloat16),
        compiler_params=grant(4),
        name="spread",
    )(own, theirs, *before)


def on_device(bits, low_frames, spatial_weight, temporal_weight, cotangent):
    low, cot = low_frames[0], cotangent[0]
    frames, rows_low, cols_low, chan = low.shape
    core = lax.axis_index(bits.core).astype(jnp.int32)
    odd = lax.axis_index(bits.axes["height"][-1]).astype(jnp.int32)
    mine, other = jnp.stack([core, odd]), jnp.stack([1 - core, odd])
    parts = 1 << len(bits.near)

    inner, outer, later = first_messages(mine, low, cot)
    later = bits.shift(later, "tm", -1)
    inner, outer = bits.pairs(inner, outer)
    low, ws, wt, cot_side = load(low, cot, spatial_weight, temporal_weight)
    act, slope = forward(mine, low, inner, outer, ws)
    pg, ext, theirs = backward(other, low, inner, outer, act, slope, cot_side, later, wt)
    theirs = bits.swap(theirs, bits.core)
    own = half_grads(mine, low, inner, outer, act, pg, ext)
    kept = add_halves(own, theirs)
    got = bits.exchange(kept.reshape(parts, -1, chan))
    edge, pg_inner, pg_outer = edges(mine, low, inner, outer, pg, kept)
    edge = bits.shift(edge, "tm", 1)
    pg_inner, pg_outer = bits.pairs(pg_inner, pg_outer)
    own_part = input_own(pg, ext, ws, kept, low.shape)
    total, far = bits.far_sums(sum_parts(got, own_part))
    earlier = earlier_act(edge, ws, total)
    section_out, section_done = section(earlier, act, low, wt, total)
    input_grad, input_done = input_grads(mine, own_part, pg_inner, pg_outer, ws)
    totals = spread(total, far, parts, section_done, input_done)
    half = bits.exchange(totals).reshape(kept.shape)
    theirs = bits.swap(half, bits.core)
    spatial_grad, temporal_grad = put(other, theirs, *put(mine, half))
    return section_out[None], input_grad[None], spatial_grad, temporal_grad


def solution(mesh):
    bits = Bits(mesh)
    block = P(*(bits.axes[name] for name in ("dp", "tm", "height")), None, None)
    return jax.shard_map(
        functools.partial(on_device, bits),
        mesh=bits.mesh,
        in_specs=(block, P(), P(), block),
        out_specs=(block, block, P(), P()),
        check_vma=False,
    )
```

```python
import functools

import jax
import jax.numpy as jnp
import numpy as np
from jax import lax
from jax.experimental import pallas as pl
from jax.experimental.pallas import tpu as pltpu
from jax.sharding import Mesh
from jax.sharding import PartitionSpec as P


class Bits:
    def __init__(self, mesh):
        self.axes = {}
        for name in mesh.axis_names:
            count = mesh.shape[name].bit_length() - 1
            self.axes[name] = tuple(f"{name}{bit}" for bit in reversed(range(count)))
        names = [bit for bits in self.axes.values() for bit in bits]
        self.mesh = Mesh(mesh.devices.reshape([2] * len(names)), tuple(names))
        self.core = next((n for n in names if self.same_chip(n)), self.axes["tm"][-1])
        others = [[b for b in reversed(bits) if b != self.core] for bits in self.axes.values()]
        turns = [bits[turn] for turn in range(len(names)) for bits in others if turn < len(bits)]
        self.near = [n for n in names if n in turns[:3]]
        self.far = turns[3:]

    def same_chip(self, name):
        at = [1 if n == name else 0 for n in self.mesh.axis_names]
        here = self.mesh.devices[tuple([0] * len(at))]
        there = self.mesh.devices[tuple(at)]
        return tuple(getattr(here, "coords", (0,))) == tuple(getattr(there, "coords", (1,)))

    def swap(self, block, axis):
        return lax.ppermute(block, axis, [(0, 1), (1, 0)])

    def shift(self, block, name, distance):
        axes = self.axes[name]
        devices = range(1 << len(axes))
        route = [(i - distance, i) for i in devices if i - distance in devices]
        return lax.ppermute(block, axes, route)

    def exchange(self, parts):
        return lax.all_to_all(parts, tuple(self.near), 0, 0, tiled=True)

    def pairs(self, inner, outer):
        axes = self.axes["height"]
        low = range(1, (1 << len(axes)) - 1, 2)
        route = [(i, i + 1) for i in low] + [(i + 1, i) for i in low]
        outer = lax.ppermute(outer, axes, route)
        return self.swap(inner, axes[-1]), outer

    def far_sums(self, total):
        for axis in self.far[:-1]:
            total = total.astype(jnp.float32) + self.swap(total, axis).astype(jnp.float32)
            total = lax.reduce_precision(total, 8, 7).astype(jnp.bfloat16)
        return total, self.swap(total, self.far[-1])


SIDES = ((0, 0), (0, 1), (1, 0), (1, 1))


def grant(mib):
    return pltpu.CompilerParams(vmem_limit_bytes=mib * 2**20)


def product(left, right):
    return jnp.dot(left, right, preferred_element_type=jnp.float32)


def product_nt(left, right):
    return lax.dot_general(left, right, (((1,), (1,)), ((), ())), preferred_element_type=jnp.float32)


def rows_at_once(rows_low, cols_low):
    return max(n for n in (1, 2, 4, 8) if rows_low % n == 0 and (n == 1 or 4 * n * cols_low <= 256))


def side_order(rows_low, cols_low):
    count = rows_at_once(rows_low, cols_low)
    size = 4 * count * cols_low
    at = np.arange(size).reshape(count, 2, cols_low, 2).transpose(1, 3, 0, 2).reshape(-1)
    return (at[:, None] == np.arange(size)[None, :]).astype(np.float32)


def column(rows, cols_low, chan):
    return lax.broadcasted_iota(jnp.int32, (rows // cols_low, cols_low, chan), 1).reshape(rows, chan)


def from_left(x, at):
    return jnp.where(at == 0, 0.0, pltpu.roll(x, 1, 0))


def from_right(x, at, last):
    return jnp.where(at == last, 0.0, pltpu.roll(x, x.shape[0] - 1, 0))


def sort_columns(source, target, cols_low, order):
    rows_low, chan = source.shape[0] // 2, source.shape[2]
    group = rows_at_once(rows_low, cols_low)
    span = group * cols_low
    for n in range(rows_low // group):
        block = source[2 * group * n : 2 * group * (n + 1)].reshape(4 * span, chan)
        block = product(order, block).astype(jnp.bfloat16).reshape(4, span, chan)
        target[:, n * span : (n + 1) * span, :] = block


def tall(place_ref, low_ref, inner_ref, outer_ref, frame, lanes=slice(None)):
    odd = place_ref[1] == 1
    inner, outer = inner_ref[frame, :, :, lanes], outer_ref[frame, :, :, lanes]
    up, down = jnp.where(odd, inner, outer), jnp.where(odd, outer, inner)
    return jnp.concatenate([up, low_ref[frame, :, :, lanes], down], axis=0)


def spatial(low, ws_ref):
    rows_low, cols_low, chan = low.shape[0] - 2, low.shape[1], low.shape[2]
    count = rows_low * cols_low
    flat = low.reshape(-1, chan)
    rows = [[], []]
    for j in range(3):
        taps = [product(flat, ws_ref[i, j]).reshape(low.shape) for i in range(3)]
        even = taps[0][:rows_low] + (taps[1] + taps[2])[1 : rows_low + 1]
        odd = (taps[0] + taps[1])[1 : rows_low + 1] + taps[2][2:]
        rows[0].append(even.reshape(count, chan))
        rows[1].append(odd.reshape(count, chan))
    at = column(count, cols_low, chan)
    for first, second, third in rows:
        yield from_left(first, at) + (second + third)
        yield (first + second) + from_right(third, at, cols_low - 1)


def forward_kernel(place_ref, low_ref, inner_ref, outer_ref, ws_ref, act_ref, slope_ref):
    for frame in range(low_ref.shape[0]):
        low = tall(place_ref, low_ref, inner_ref, outer_ref, frame)
        for side, pre in enumerate(spatial(low, ws_ref)):
            sig = jax.nn.sigmoid(pre)
            act_ref[frame, side] = (pre * sig).astype(jnp.bfloat16)
            slope_ref[frame, side] = sig * (1.0 + pre * (1.0 - sig))


def act_kernel(low_ref, ws_ref, _, act_ref):
    for side, pre in enumerate(spatial(low_ref[0], ws_ref)):
        act_ref[0, side] = (pre * jax.nn.sigmoid(pre)).astype(jnp.bfloat16)


def half_sums(place_ref, low_ref, inner_ref, outer_ref, act_ref, pg_ref, ext_ref, out_ref):
    frames, rows_low, cols_low, chan = low_ref.shape
    count, half = rows_low * cols_low, chan // 2
    lanes = pl.ds(pl.multiple_of(place_ref[0] * half, half), half)
    lefts = [[] for _ in range(9)]
    acts = []
    at = column((rows_low + 2) * cols_low, cols_low, half)
    for frame in range(frames):
        low = tall(place_ref, low_ref, inner_ref, outer_ref, frame, lanes)
        wide = low.reshape(-1, half).astype(jnp.float32)
        moved = [from_left(wide, at), wide, from_right(wide, at, cols_low - 1)]
        turned = {}
        for dc in range(3):
            view = moved[dc].astype(jnp.bfloat16).reshape(low.shape)
            for dr in range(3):
                turned[dr - 1, dc - 1] = view[dr : dr + rows_low].reshape(count, half).T
        for i in range(3):
            for j in range(3):
                lefts[3 * i + j] += [turned[(a + i - 1) // 2, (b + j - 1) // 2] for a, b in SIDES]
        acts.append(act_ref[frame, :, :, lanes].reshape(4 * count, half).T)
    pg = pg_ref[...].reshape(frames * 4 * count, chan)
    left = jnp.concatenate([jnp.concatenate(left, axis=1) for left in lefts], axis=0)
    out_ref[:9] = product(left, pg).reshape(9, half, chan)
    act = jnp.concatenate(acts, axis=1)
    for k in range(3):
        out_ref[9 + k] = product(act, ext_ref[k : k + frames].reshape(frames * 4 * count, chan))


def backward_kernel(place_ref, low_ref, inner_ref, outer_ref, act_ref, slope_ref, cot_ref, later_ref, turned_ref, sort_ref, pg_ref, ext_ref, out_ref):
    frames, _, count, chan = cot_ref.shape
    ext_ref[:frames] = cot_ref[...]
    for n in range(2):
        sort_columns(later_ref.at[n], ext_ref.at[frames + n], low_ref.shape[2], sort_ref[...])
    for frame in range(frames):
        cots = [ext_ref[frame + k].reshape(4 * count, chan) for k in range(3)]
        act_grad = product(jnp.concatenate(cots, axis=1), turned_ref[...])
        slope = slope_ref[frame].reshape(4 * count, chan)
        pg_ref[frame] = (act_grad * slope).astype(jnp.bfloat16).reshape(4, count, chan)
    half_sums(place_ref, low_ref, inner_ref, outer_ref, act_ref, pg_ref, ext_ref, out_ref)


SCALAR = pl.BlockSpec(memory_space=pltpu.SMEM)
UNREAD = pl.BlockSpec(memory_space=pl.ANY)


def like(shape, dtype):
    return jax.ShapeDtypeStruct(shape, dtype)


TOKEN = like((8, 128), jnp.float32)


def cost(units, mib):
    return pl.CostEstimate(flops=units * 2 * 2048 * 256 * 256, bytes_accessed=mib * 2**20, transcendentals=0)


def in_hbm(array):
    return pltpu.with_memory_space_constraint(array, pltpu.HBM)


FULL = pl.BlockSpec(memory_space=pltpu.VMEM)


def first_kernel(place_ref, low_ref, cot_ref, inner_ref, outer_ref, later_ref, sems):
    last = low_ref.shape[1] - 1
    odd = place_ref[1]
    copies = [
        (low_ref.at[:, pl.ds(last * (1 - odd), 1)], inner_ref),
        (low_ref.at[:, pl.ds(last * odd, 1)], outer_ref),
    ]
    copies += [(cot_ref.at[n, r], later_ref.at[n, r]) for n in range(2) for r in range(cot_ref.shape[1])]
    copies = [pltpu.make_async_copy(a, b, sems.at[n]) for n, (a, b) in enumerate(copies)]
    for copy in copies:
        copy.start()
    for copy in copies:
        copy.wait()


def first_messages(place, low, cot):
    row = like(low[:, :1].shape, low.dtype)
    return pl.pallas_call(
        first_kernel,
        in_specs=[SCALAR, UNREAD, UNREAD],
        out_specs=[FULL] * 3,
        out_shape=[row, row, like(cot[:2].shape, cot.dtype)],
        scratch_shapes=[pltpu.SemaphoreType.DMA((2 + 2 * cot.shape[1],))],
        compiler_params=grant(4),
        name="first_messages",
    )(place, in_hbm(low), in_hbm(cot))


def load_kernel(low_hbm, cot_hbm, ws_hbm, wt_hbm, sort_hbm,
                low_ref, ws_ref, wt_ref, sort_ref, merge_ref, turned_ref, side_ref, cot_ref, wide_ref, sems):
    frames, cols_low, chan = low_ref.shape[0], low_ref.shape[2], low_ref.shape[3]
    pairs = [(sort_hbm, wide_ref)] + [(cot_hbm.at[n], cot_ref.at[n]) for n in range(frames)]
    pairs += [(wt_hbm.at[k], wt_ref.at[k]) for k in range(3)] + [(low_hbm, low_ref)]
    pairs += [(ws_hbm.at[i, j], ws_ref.at[i, j]) for i in range(3) for j in range(3)]
    copies = [pltpu.make_async_copy(a, b, sems.at[n]) for n, (a, b) in enumerate(pairs)]
    for copy in copies:
        copy.start()
    copies[0].wait()
    sort_ref[...] = wide_ref[...].astype(jnp.bfloat16)
    merge_ref[...] = wide_ref[...].T.astype(jnp.bfloat16)
    for n in range(frames):
        copies[1 + n].wait()
        sort_columns(cot_ref.at[n], side_ref.at[n], cols_low, sort_ref[...])
    for k in range(3):
        copies[1 + frames + k].wait()
        turned_ref[k * chan : (k + 1) * chan] = wt_ref[k].T
    for copy in copies[4 + frames :]:
        copy.wait()


def load(low, cot, ws, wt):
    frames, rows_low, cols_low, chan = low.shape
    sort = jnp.asarray(side_order(rows_low, cols_low))
    order = like(sort.shape, jnp.bfloat16)
    shapes = [low, ws, wt, order, order, like((3 * chan, chan), wt.dtype),
              like((frames, 4, rows_low * cols_low, chan), jnp.bfloat16)]
    return pl.pallas_call(
        load_kernel,
        in_specs=[UNREAD] * 5,
        out_specs=[FULL] * 7,
        out_shape=[like(a.shape, a.dtype) for a in shapes],
        scratch_shapes=[pltpu.VMEM(cot.shape, cot.dtype), pltpu.VMEM(sort.shape, sort.dtype),
                        pltpu.SemaphoreType.DMA((frames + 14,))],
        compiler_params=grant(14),
        cost_estimate=cost(2, 4),
        name="load",
    )(*[in_hbm(a) for a in (low, cot, ws, wt, sort)])


def forward(place, low, inner, outer, ws):
    frames, rows_low, cols_low, chan = low.shape
    side = (frames, 4, rows_low * cols_low, chan)
    return pl.pallas_call(
        forward_kernel,
        in_specs=[SCALAR] + [FULL] * 4,
        out_specs=[FULL] * 2,
        out_shape=[like(side, jnp.bfloat16), like(side, jnp.float32)],
        compiler_params=grant(20),
        cost_estimate=cost(10, 8),
        name="forward",
    )(place, low, inner, outer, ws)


def edges_kernel(place_ref, low_ref, inner_ref, outer_ref, pg_ref, _, tall_ref, pg_inner, pg_outer):
    cols_low = low_ref.shape[2]
    first = low_ref.shape[0] - tall_ref.shape[0]
    for n in range(tall_ref.shape[0]):
        tall_ref[n] = tall(place_ref, low_ref, inner_ref, outer_ref, first + n)
    odd = place_ref[1] == 1
    top, bottom = pg_ref[:, :2, :cols_low, :], pg_ref[:, 2:, -cols_low:, :]
    pg_inner[...] = jnp.where(odd, top, bottom)
    pg_outer[...] = jnp.where(odd, bottom, top)


def edges(place, low, inner, outer, pg, before):
    frames, rows_low, cols_low, chan = low.shape
    full = pl.BlockSpec(memory_space=pltpu.VMEM)
    rows = like((frames, 2, cols_low, chan), jnp.bfloat16)
    return pl.pallas_call(
        edges_kernel,
        in_specs=[SCALAR, full, full, full, full, UNREAD],
        out_specs=[full] * 3,
        out_shape=[like((2, rows_low + 2, cols_low, chan), jnp.bfloat16), rows, rows],
        compiler_params=grant(8),
        name="edges",
    )(place, low, inner, outer, pg, before)


def earlier_act(low, ws, before):
    frames, rows_tall, cols_low, chan = low.shape
    side = (frames, 4, (rows_tall - 2) * cols_low, chan)
    return pl.pallas_call(
        act_kernel,
        grid=(frames,),
        in_specs=[pl.BlockSpec((1,) + low.shape[1:], lambda f: (f, 0, 0, 0)), FULL, UNREAD],
        out_specs=pl.BlockSpec((1,) + side[1:], lambda f: (f, 0, 0, 0)),
        out_shape=like(side, jnp.bfloat16),
        compiler_params=grant(10),
        cost_estimate=cost(4, 3),
        name="earlier_act",
    )(low, ws, before)


def backward(place, low, inner, outer, act, slope, cot, later, turned, sort):
    frames, _, _, chan = act.shape
    ext = (frames + 2,) + act.shape[1:]
    return pl.pallas_call(
        backward_kernel,
        in_specs=[SCALAR] + [FULL] * 9,
        out_specs=[FULL] * 3,
        out_shape=[like(act.shape, jnp.bfloat16), like(ext, jnp.bfloat16), like((12, chan // 2, chan), jnp.float32)],
        compiler_params=grant(24),
        cost_estimate=cost(15, 10),
        name="backward",
    )(place, low, inner, outer, act, slope, cot, later, turned, sort)


def half_grads(place, low, inner, outer, act, pg, ext):
    chan = low.shape[-1]
    return pl.pallas_call(
        half_sums,
        in_specs=[SCALAR] + [FULL] * 6,
        out_specs=FULL,
        out_shape=like((12, chan // 2, chan), jnp.float32),
        compiler_params=grant(20),
        cost_estimate=cost(10, 6),
        name="half_grads",
    )(place, low, inner, outer, act, pg, ext)


def section_kernel(earlier_ref, act_ref, low_ref, wt_ref, merge_ref, _, out_ref, token_ref, held, sems):
    frames, rows_low, cols_low, chan = low_ref.shape
    group = rows_at_once(rows_low, cols_low)
    span, count = group * cols_low, rows_low * cols_low
    order = merge_ref[...]
    wt = wt_ref[...].reshape(3 * chan, chan)
    token_ref[...] = jnp.zeros_like(token_ref)
    copies = []
    for frame in range(frames):
        total = jnp.concatenate([low_ref[frame].reshape(count, chan).astype(jnp.float32)] * 4, axis=0)
        acts = [act_ref[frame - k] if frame >= k else earlier_ref[frame - k + 2] for k in range(3)]
        acts = jnp.concatenate([act.reshape(4 * count, chan) for act in acts], axis=1)
        total = total + product(acts, wt)
        mixed = total.astype(jnp.bfloat16).reshape(4, count, chan)
        for n in range(rows_low // group):
            block = mixed[:, n * span : (n + 1) * span].reshape(4 * span, chan)
            block = product(order, block).astype(jnp.bfloat16)
            held[frame, 2 * group * n : 2 * group * (n + 1)] = block.reshape(2 * group, 2 * cols_low, chan)
        copies.append(pltpu.make_async_copy(held.at[frame], out_ref.at[frame], sems.at[frame]))
        copies[-1].start()
    for copy in copies:
        copy.wait()


HBM = pl.BlockSpec(memory_space=pltpu.HBM)


def section(earlier, act, low, wt, merge, before):
    frames, rows_low, cols_low, chan = low.shape
    out = (frames, 2 * rows_low, 2 * cols_low, chan)
    return pl.pallas_call(
        section_kernel,
        in_specs=[FULL] * 5 + [UNREAD],
        out_specs=[HBM, FULL],
        out_shape=[like(out, jnp.bfloat16), TOKEN],
        scratch_shapes=[pltpu.VMEM(out, jnp.bfloat16), pltpu.SemaphoreType.DMA((frames,))],
        compiler_params=grant(10),
        cost_estimate=cost(4, 3),
        name="section",
    )(earlier, act, low, wt, merge, before)


def split(value):
    high = value.astype(jnp.bfloat16)
    return high, (value - high.astype(jnp.float32)).astype(jnp.bfloat16)


def column_pair(first, second, j, at, last):
    if j == 0:
        return second + from_right(first, at, last)
    if j == 1:
        return first + second
    return first + from_left(second, at)


def input_kernel(pg_ref, ext_ref, ws_ref, _, out_ref):
    frames, _, count, chan = pg_ref.shape
    cols_low = out_ref.shape[2]
    rows_low = count // cols_low
    at = column(count, cols_low, chan)
    turned = jnp.concatenate([ws_ref[i, j].T for j in range(3) for i in range(3)], axis=0)
    for frame in range(frames):
        total = sum(ext_ref[frame, side].astype(jnp.float32) for side in range(4))
        own = [pg_ref[frame, side].astype(jnp.float32) for side in range(4)]
        zero = jnp.zeros((1, cols_low, chan), jnp.float32)
        parts = []
        for j in range(3):
            even = column_pair(own[0], own[1], j, at, cols_low - 1).reshape(rows_low, cols_low, chan)
            odd = column_pair(own[2], own[3], j, at, cols_low - 1).reshape(rows_low, cols_low, chan)
            below = jnp.concatenate([even[1:], zero], axis=0)
            above = jnp.concatenate([zero, odd[:-1]], axis=0)
            for value in (odd + below, even + odd, above + even):
                parts.append(jnp.concatenate(split(value.reshape(count, chan)), axis=0))
        sums = product(jnp.concatenate(parts, axis=1), turned)
        total = total + (sums[:count] + sums[count:])
        out_ref[frame] = total.reshape(rows_low, cols_low, chan)


def input_own(pg, ext, ws, before, low_shape):
    return pl.pallas_call(
        input_kernel,
        in_specs=[FULL] * 3 + [UNREAD],
        out_specs=FULL,
        out_shape=like(low_shape, jnp.float32),
        compiler_params=grant(16),
        cost_estimate=cost(6, 4),
        name="input_own",
    )(pg, ext, ws, before)


def input_edge_kernel(place_ref, own_ref, inner_ref, outer_ref, ws_ref, _, out_ref, token_ref, held, sem):
    frames, rows_low, cols_low, chan = own_ref.shape
    token_ref[...] = jnp.zeros_like(token_ref)
    odd_place = place_ref[1] == 1
    flat = (frames * cols_low, chan)
    at = column(flat[0], cols_low, chan)
    inner = [inner_ref[:, b].reshape(flat).astype(jnp.float32) for b in range(2)]
    outer = [outer_ref[:, b].reshape(flat).astype(jnp.float32) for b in range(2)]
    above = [jnp.where(odd_place, inner[b], outer[b]) for b in range(2)]
    below = [jnp.where(odd_place, outer[b], inner[b]) for b in range(2)]
    terms = []
    for (first, second), i in ((above, 2), (below, 0)):
        total = jnp.zeros(flat, jnp.float32)
        for j in range(3):
            for part in split(column_pair(first, second, j, at, cols_low - 1)):
                total = total + product_nt(part, ws_ref[i, j])
        terms.append(total.reshape(frames, cols_low, chan))
    for row in range(rows_low):
        value = own_ref[:, row]
        if row == 0:
            value = value + terms[0]
        if row == rows_low - 1:
            value = value + terms[1]
        held[:, row] = value.astype(jnp.bfloat16)
    copy = pltpu.make_async_copy(held, out_ref, sem)
    copy.start()
    copy.wait()


def input_grads(place, own, inner, outer, ws, before):
    return pl.pallas_call(
        input_edge_kernel,
        in_specs=[SCALAR] + [FULL] * 4 + [UNREAD],
        out_specs=[HBM, FULL],
        out_shape=[like(own.shape, jnp.bfloat16), TOKEN],
        scratch_shapes=[pltpu.VMEM(own.shape, jnp.bfloat16), pltpu.SemaphoreType.DMA],
        compiler_params=grant(6),
        cost_estimate=cost(1, 1),
        name="input_edge",
    )(place, own, inner, outer, ws, before)


def put_kernel(place_ref, half_ref, *refs):
    spatial_ref, temporal_ref, wide, sems = refs[-4:]
    taps, half, _ = half_ref.shape
    to = pl.ds(pl.multiple_of(place_ref[0] * half, half), half)
    copies = []
    for tap in range(taps):
        wide[tap] = half_ref[tap].astype(jnp.float32)
        if tap < 9:
            target = spatial_ref.at[tap // 3, tap % 3, to]
        else:
            target = temporal_ref.at[tap - 9, to]
        copies.append(pltpu.make_async_copy(wide.at[tap], target, sems.at[tap]))
        copies[-1].start()
    for copy in copies:
        copy.wait()


def put(place, half, *done):
    chan = half.shape[-1]
    return pl.pallas_call(
        put_kernel,
        in_specs=[SCALAR, FULL] + [HBM] * len(done),
        out_specs=[HBM, HBM],
        out_shape=[like((3, 3, chan, chan), jnp.float32), like((3, chan, chan), jnp.float32)],
        input_output_aliases={2 + n: n for n in range(len(done))},
        scratch_shapes=[pltpu.VMEM((12, chan // 2, chan), jnp.float32), pltpu.SemaphoreType.DMA((12,))],
        compiler_params=grant(6),
        name="put",
    )(place, half, *done)


def add_kernel(mine_ref, theirs_ref, out_ref):
    out_ref[...] = (mine_ref[...] + theirs_ref[...]).astype(jnp.bfloat16)


def add_halves(mine, theirs):
    full = pl.BlockSpec(memory_space=pltpu.VMEM)
    return pl.pallas_call(
        add_kernel,
        in_specs=[full, full],
        out_specs=full,
        out_shape=like(mine.shape, jnp.bfloat16),
        compiler_params=grant(8),
        name="add_halves",
    )(mine, theirs)


def sum_kernel(got_ref, _, out_ref):
    total = got_ref[0].astype(jnp.float32)
    for n in range(1, got_ref.shape[0]):
        total = total + got_ref[n].astype(jnp.float32)
    out_ref[...] = total.astype(jnp.bfloat16)


def sum_parts(got, before):
    return pl.pallas_call(
        sum_kernel,
        in_specs=[FULL, UNREAD],
        out_specs=FULL,
        out_shape=like(got.shape[1:], jnp.bfloat16),
        compiler_params=grant(4),
        name="sum_parts",
    )(got, before)


def spread_kernel(own_ref, theirs_ref, *refs):
    total = (own_ref[...].astype(jnp.float32) + theirs_ref[...].astype(jnp.float32)).astype(jnp.bfloat16)
    for n in range(refs[-1].shape[0]):
        refs[-1][n] = total


def spread(own, theirs, parts, *before):
    return pl.pallas_call(
        spread_kernel,
        in_specs=[FULL, FULL] + [UNREAD] * len(before),
        out_specs=FULL,
        out_shape=like((parts,) + own.shape, jnp.bfloat16),
        compiler_params=grant(4),
        name="spread",
    )(own, theirs, *before)


def on_device(bits, low_frames, spatial_weight, temporal_weight, cotangent):
    low, cot = low_frames[0], cotangent[0]
    frames, rows_low, cols_low, chan = low.shape
    core = lax.axis_index(bits.core).astype(jnp.int32)
    odd = lax.axis_index(bits.axes["height"][-1]).astype(jnp.int32)
    mine, other = jnp.stack([core, odd]), jnp.stack([1 - core, odd])
    parts = 1 << len(bits.near)

    inner, outer, later = first_messages(mine, low, cot)
    later = bits.shift(later, "tm", -1)
    inner, outer = bits.pairs(inner, outer)
    low, ws, wt, sort, merge, turned, cot_side = load(low, cot, spatial_weight, temporal_weight)
    act, slope = forward(mine, low, inner, outer, ws)
    pg, ext, theirs = backward(other, low, inner, outer, act, slope, cot_side, later, turned, sort)
    theirs = bits.swap(theirs, bits.core)
    own = half_grads(mine, low, inner, outer, act, pg, ext)
    kept = add_halves(own, theirs)
    got = bits.exchange(kept.reshape(parts, -1, chan))
    edge, pg_inner, pg_outer = edges(mine, low, inner, outer, pg, kept)
    edge = bits.shift(edge, "tm", 1)
    pg_inner, pg_outer = bits.pairs(pg_inner, pg_outer)
    own_part = input_own(pg, ext, ws, kept, low.shape)
    total, far = bits.far_sums(sum_parts(got, own_part))
    earlier = earlier_act(edge, ws, total)
    section_out, section_done = section(earlier, act, low, wt, merge, total)
    input_grad, input_done = input_grads(mine, own_part, pg_inner, pg_outer, ws, total)
    totals = spread(total, far, parts, section_done, input_done)
    half = bits.exchange(totals).reshape(kept.shape)
    theirs = bits.swap(half, bits.core)
    spatial_grad, temporal_grad = put(other, theirs, *put(mine, half))
    return section_out[None], input_grad[None], spatial_grad, temporal_grad


def solution(mesh):
    bits = Bits(mesh)
    block = P(*(bits.axes[name] for name in ("dp", "tm", "height")), None, None)
    return jax.shard_map(
        functools.partial(on_device, bits),
        mesh=bits.mesh,
        in_specs=(block, P(), P(), block),
        out_specs=(block, block, P(), P()),
        check_vma=False,
    )
```

```python
import functools

import jax
import jax.numpy as jnp
import numpy as np
from jax import lax
from jax.experimental import pallas as pl
from jax.experimental.pallas import tpu as pltpu
from jax.sharding import Mesh
from jax.sharding import PartitionSpec as P


class Bits:
    def __init__(self, mesh):
        self.axes = {}
        for name in mesh.axis_names:
            count = mesh.shape[name].bit_length() - 1
            self.axes[name] = tuple(f"{name}{bit}" for bit in reversed(range(count)))
        names = [bit for bits in self.axes.values() for bit in bits]
        self.mesh = Mesh(mesh.devices.reshape([2] * len(names)), tuple(names))
        self.core = next((n for n in names if self.same_chip(n)), self.axes["tm"][-1])
        others = [[b for b in reversed(bits) if b != self.core] for bits in self.axes.values()]
        turns = [bits[turn] for turn in range(len(names)) for bits in others if turn < len(bits)]
        self.near = [n for n in names if n in turns[:3]]
        self.far = turns[3:]

    def same_chip(self, name):
        at = [1 if n == name else 0 for n in self.mesh.axis_names]
        here = self.mesh.devices[tuple([0] * len(at))]
        there = self.mesh.devices[tuple(at)]
        return tuple(getattr(here, "coords", (0,))) == tuple(getattr(there, "coords", (1,)))

    def swap(self, block, axis):
        return lax.ppermute(block, axis, [(0, 1), (1, 0)])

    def shift(self, block, name, distance):
        axes = self.axes[name]
        devices = range(1 << len(axes))
        route = [(i - distance, i) for i in devices if i - distance in devices]
        return lax.ppermute(block, axes, route)

    def exchange(self, parts):
        return lax.all_to_all(parts, tuple(self.near), 0, 0, tiled=True)

    def pairs(self, inner, outer):
        axes = self.axes["height"]
        low = range(1, (1 << len(axes)) - 1, 2)
        route = [(i, i + 1) for i in low] + [(i + 1, i) for i in low]
        outer = lax.ppermute(outer, axes, route)
        return self.swap(inner, axes[-1]), outer

    def far_sums(self, total):
        for axis in self.far[:-1]:
            total = total.astype(jnp.float32) + self.swap(total, axis).astype(jnp.float32)
            total = lax.reduce_precision(total, 8, 7).astype(jnp.bfloat16)
        return total, self.swap(total, self.far[-1])


SIDES = ((0, 0), (0, 1), (1, 0), (1, 1))


def grant(mib):
    return pltpu.CompilerParams(vmem_limit_bytes=mib * 2**20)


def product(left, right):
    return jnp.dot(left, right, preferred_element_type=jnp.float32)


def product_nt(left, right):
    return lax.dot_general(left, right, (((1,), (1,)), ((), ())), preferred_element_type=jnp.float32)


def rows_at_once(rows_low, cols_low):
    return max(n for n in (1, 2, 4, 8) if rows_low % n == 0 and (n == 1 or 4 * n * cols_low <= 256))


def side_order(rows_low, cols_low):
    count = rows_at_once(rows_low, cols_low)
    size = 4 * count * cols_low
    at = np.arange(size).reshape(count, 2, cols_low, 2).transpose(1, 3, 0, 2).reshape(-1)
    return (at[:, None] == np.arange(size)[None, :]).astype(np.float32)


def column(rows, cols_low, chan):
    return lax.broadcasted_iota(jnp.int32, (rows // cols_low, cols_low, chan), 1).reshape(rows, chan)


def from_left(x, at):
    return jnp.where(at == 0, 0.0, pltpu.roll(x, 1, 0))


def from_right(x, at, last):
    return jnp.where(at == last, 0.0, pltpu.roll(x, x.shape[0] - 1, 0))


def sort_columns(source, target, cols_low, order):
    rows_low, chan = source.shape[0] // 2, source.shape[2]
    group = rows_at_once(rows_low, cols_low)
    span = group * cols_low
    for n in range(rows_low // group):
        block = source[2 * group * n : 2 * group * (n + 1)].reshape(4 * span, chan)
        block = product(order, block).astype(jnp.bfloat16).reshape(4, span, chan)
        target[:, n * span : (n + 1) * span, :] = block


def tall(place_ref, low_ref, inner_ref, outer_ref, frame, lanes=slice(None)):
    odd = place_ref[1] == 1
    inner, outer = inner_ref[frame, :, :, lanes], outer_ref[frame, :, :, lanes]
    up, down = jnp.where(odd, inner, outer), jnp.where(odd, outer, inner)
    return jnp.concatenate([up, low_ref[frame, :, :, lanes], down], axis=0)


def spatial(low, ws_ref):
    rows_low, cols_low, chan = low.shape[0] - 2, low.shape[1], low.shape[2]
    count = rows_low * cols_low
    flat = low.reshape(-1, chan)
    rows = [[], []]
    for j in range(3):
        taps = [product(flat, ws_ref[i, j]).reshape(low.shape) for i in range(3)]
        even = taps[0][:rows_low] + (taps[1] + taps[2])[1 : rows_low + 1]
        odd = (taps[0] + taps[1])[1 : rows_low + 1] + taps[2][2:]
        rows[0].append(even.reshape(count, chan))
        rows[1].append(odd.reshape(count, chan))
    at = column(count, cols_low, chan)
    for first, second, third in rows:
        yield from_left(first, at) + (second + third)
        yield (first + second) + from_right(third, at, cols_low - 1)


def forward_kernel(place_ref, low_ref, inner_ref, outer_ref, ws_ref, act_ref, slope_ref):
    for frame in range(low_ref.shape[0]):
        low = tall(place_ref, low_ref, inner_ref, outer_ref, frame)
        for side, pre in enumerate(spatial(low, ws_ref)):
            sig = jax.nn.sigmoid(pre)
            act_ref[frame, side] = (pre * sig).astype(jnp.bfloat16)
            slope_ref[frame, side] = sig * (1.0 + pre * (1.0 - sig))


def half_sums(place_ref, low_ref, inner_ref, outer_ref, act_ref, pg_ref, ext_ref, out_ref):
    frames, rows_low, cols_low, chan = low_ref.shape
    count, half = rows_low * cols_low, chan // 2
    lanes = pl.ds(pl.multiple_of(place_ref[0] * half, half), half)
    lefts = [[] for _ in range(9)]
    acts = []
    at = column((rows_low + 2) * cols_low, cols_low, half)
    for frame in range(frames):
        low = tall(place_ref, low_ref, inner_ref, outer_ref, frame, lanes)
        wide = low.reshape(-1, half).astype(jnp.float32)
        moved = [from_left(wide, at), wide, from_right(wide, at, cols_low - 1)]
        turned = {}
        for dc in range(3):
            view = moved[dc].astype(jnp.bfloat16).reshape(low.shape)
            for dr in range(3):
                turned[dr - 1, dc - 1] = view[dr : dr + rows_low].reshape(count, half).T
        for i in range(3):
            for j in range(3):
                lefts[3 * i + j] += [turned[(a + i - 1) // 2, (b + j - 1) // 2] for a, b in SIDES]
        acts.append(act_ref[frame, :, :, lanes].reshape(4 * count, half).T)
    pg = pg_ref[...].reshape(frames * 4 * count, chan)
    left = jnp.concatenate([jnp.concatenate(left, axis=1) for left in lefts], axis=0)
    out_ref[:9] = product(left, pg).reshape(9, half, chan)
    act = jnp.concatenate(acts, axis=1)
    for k in range(3):
        out_ref[9 + k] = product(act, ext_ref[k : k + frames].reshape(frames * 4 * count, chan))


def backward_kernel(place_ref, low_ref, inner_ref, outer_ref, act_ref, slope_ref, cot_ref, later_ref, turned_ref, sort_ref, pg_ref, ext_ref, out_ref):
    frames, _, count, chan = cot_ref.shape
    ext_ref[:frames] = cot_ref[...]
    for n in range(2):
        sort_columns(later_ref.at[n], ext_ref.at[frames + n], low_ref.shape[2], sort_ref[...])
    for frame in range(frames):
        cots = [ext_ref[frame + k].reshape(4 * count, chan) for k in range(3)]
        act_grad = product(jnp.concatenate(cots, axis=1), turned_ref[...])
        slope = slope_ref[frame].reshape(4 * count, chan)
        pg_ref[frame] = (act_grad * slope).astype(jnp.bfloat16).reshape(4, count, chan)
    half_sums(place_ref, low_ref, inner_ref, outer_ref, act_ref, pg_ref, ext_ref, out_ref)


SCALAR = pl.BlockSpec(memory_space=pltpu.SMEM)
UNREAD = pl.BlockSpec(memory_space=pl.ANY)


def like(shape, dtype):
    return jax.ShapeDtypeStruct(shape, dtype)


TOKEN = like((8, 128), jnp.float32)


def cost(units, mib):
    return pl.CostEstimate(flops=units * 2 * 2048 * 256 * 256, bytes_accessed=mib * 2**20, transcendentals=0)


def in_hbm(array):
    return pltpu.with_memory_space_constraint(array, pltpu.HBM)


FULL = pl.BlockSpec(memory_space=pltpu.VMEM)


def first_kernel(place_ref, low_ref, cot_ref, inner_ref, outer_ref, later_ref, sems):
    last = low_ref.shape[1] - 1
    odd = place_ref[1]
    copies = [
        (low_ref.at[:, pl.ds(last * (1 - odd), 1)], inner_ref),
        (low_ref.at[:, pl.ds(last * odd, 1)], outer_ref),
    ]
    copies += [(cot_ref.at[n, r], later_ref.at[n, r]) for n in range(2) for r in range(cot_ref.shape[1])]
    copies = [pltpu.make_async_copy(a, b, sems.at[n]) for n, (a, b) in enumerate(copies)]
    for copy in copies:
        copy.start()
    for copy in copies:
        copy.wait()


def first_messages(place, low, cot):
    row = like(low[:, :1].shape, low.dtype)
    return pl.pallas_call(
        first_kernel,
        in_specs=[SCALAR, UNREAD, UNREAD],
        out_specs=[FULL] * 3,
        out_shape=[row, row, like(cot[:2].shape, cot.dtype)],
        scratch_shapes=[pltpu.SemaphoreType.DMA((2 + 2 * cot.shape[1],))],
        compiler_params=grant(4),
        name="first_messages",
    )(place, in_hbm(low), in_hbm(cot))


def load_kernel(low_hbm, cot_hbm, ws_hbm, wt_hbm, sort_hbm,
                low_ref, ws_ref, wt_ref, sort_ref, merge_ref, turned_ref, side_ref, cot_ref, wide_ref, sems):
    frames, cols_low, chan = low_ref.shape[0], low_ref.shape[2], low_ref.shape[3]
    pairs = [(sort_hbm, wide_ref)] + [(cot_hbm.at[n], cot_ref.at[n]) for n in range(frames)]
    pairs += [(wt_hbm.at[k], wt_ref.at[k]) for k in range(3)] + [(low_hbm, low_ref)]
    pairs += [(ws_hbm.at[i, j], ws_ref.at[i, j]) for i in range(3) for j in range(3)]
    copies = [pltpu.make_async_copy(a, b, sems.at[n]) for n, (a, b) in enumerate(pairs)]
    for copy in copies:
        copy.start()
    copies[0].wait()
    sort_ref[...] = wide_ref[...].astype(jnp.bfloat16)
    merge_ref[...] = wide_ref[...].T.astype(jnp.bfloat16)
    for n in range(frames):
        copies[1 + n].wait()
        sort_columns(cot_ref.at[n], side_ref.at[n], cols_low, sort_ref[...])
    for k in range(3):
        copies[1 + frames + k].wait()
        turned_ref[k * chan : (k + 1) * chan] = wt_ref[k].T
    for copy in copies[4 + frames :]:
        copy.wait()


def load(low, cot, ws, wt):
    frames, rows_low, cols_low, chan = low.shape
    sort = jnp.asarray(side_order(rows_low, cols_low))
    order = like(sort.shape, jnp.bfloat16)
    shapes = [low, ws, wt, order, order, like((3 * chan, chan), wt.dtype),
              like((frames, 4, rows_low * cols_low, chan), jnp.bfloat16)]
    return pl.pallas_call(
        load_kernel,
        in_specs=[UNREAD] * 5,
        out_specs=[FULL] * 7,
        out_shape=[like(a.shape, a.dtype) for a in shapes],
        scratch_shapes=[pltpu.VMEM(cot.shape, cot.dtype), pltpu.VMEM(sort.shape, sort.dtype),
                        pltpu.SemaphoreType.DMA((frames + 14,))],
        compiler_params=grant(14),
        cost_estimate=cost(2, 4),
        name="load",
    )(*[in_hbm(a) for a in (low, cot, ws, wt, sort)])


def forward(place, low, inner, outer, ws):
    frames, rows_low, cols_low, chan = low.shape
    side = (frames, 4, rows_low * cols_low, chan)
    return pl.pallas_call(
        forward_kernel,
        in_specs=[SCALAR] + [FULL] * 4,
        out_specs=[FULL] * 2,
        out_shape=[like(side, jnp.bfloat16), like(side, jnp.float32)],
        compiler_params=grant(20),
        cost_estimate=cost(10, 8),
        name="forward",
    )(place, low, inner, outer, ws)


def edges_kernel(place_ref, low_ref, inner_ref, outer_ref, pg_ref, _, tall_ref, pg_inner, pg_outer):
    cols_low = low_ref.shape[2]
    first = low_ref.shape[0] - tall_ref.shape[0]
    for n in range(tall_ref.shape[0]):
        tall_ref[n] = tall(place_ref, low_ref, inner_ref, outer_ref, first + n)
    odd = place_ref[1] == 1
    top, bottom = pg_ref[:, :2, :cols_low, :], pg_ref[:, 2:, -cols_low:, :]
    pg_inner[...] = jnp.where(odd, top, bottom)
    pg_outer[...] = jnp.where(odd, bottom, top)


def edges(place, low, inner, outer, pg, before):
    frames, rows_low, cols_low, chan = low.shape
    full = pl.BlockSpec(memory_space=pltpu.VMEM)
    rows = like((frames, 2, cols_low, chan), jnp.bfloat16)
    return pl.pallas_call(
        edges_kernel,
        in_specs=[SCALAR, full, full, full, full, UNREAD],
        out_specs=[full] * 3,
        out_shape=[like((2, rows_low + 2, cols_low, chan), jnp.bfloat16), rows, rows],
        compiler_params=grant(8),
        name="edges",
    )(place, low, inner, outer, pg, before)


def backward(place, low, inner, outer, act, slope, cot, later, turned, sort):
    frames, _, _, chan = act.shape
    ext = (frames + 2,) + act.shape[1:]
    return pl.pallas_call(
        backward_kernel,
        in_specs=[SCALAR] + [FULL] * 9,
        out_specs=[FULL] * 3,
        out_shape=[like(act.shape, jnp.bfloat16), like(ext, jnp.bfloat16), like((12, chan // 2, chan), jnp.float32)],
        compiler_params=grant(24),
        cost_estimate=cost(15, 10),
        name="backward",
    )(place, low, inner, outer, act, slope, cot, later, turned, sort)


def half_grads(place, low, inner, outer, act, pg, ext):
    chan = low.shape[-1]
    return pl.pallas_call(
        half_sums,
        in_specs=[SCALAR] + [FULL] * 6,
        out_specs=FULL,
        out_shape=like((12, chan // 2, chan), jnp.float32),
        compiler_params=grant(20),
        cost_estimate=cost(10, 6),
        name="half_grads",
    )(place, low, inner, outer, act, pg, ext)


HBM = pl.BlockSpec(memory_space=pltpu.HBM)


def split(value):
    high = value.astype(jnp.bfloat16)
    return high, (value - high.astype(jnp.float32)).astype(jnp.bfloat16)


def column_pair(first, second, j, at, last):
    if j == 0:
        return second + from_right(first, at, last)
    if j == 1:
        return first + second
    return first + from_left(second, at)


def input_kernel(pg_ref, ext_ref, ws_ref, _, out_ref):
    frames, _, count, chan = pg_ref.shape
    cols_low = out_ref.shape[2]
    rows_low = count // cols_low
    at = column(count, cols_low, chan)
    turned = jnp.concatenate([ws_ref[i, j].T for j in range(3) for i in range(3)], axis=0)
    for frame in range(frames):
        total = sum(ext_ref[frame, side].astype(jnp.float32) for side in range(4))
        own = [pg_ref[frame, side].astype(jnp.float32) for side in range(4)]
        zero = jnp.zeros((1, cols_low, chan), jnp.float32)
        parts = []
        for j in range(3):
            even = column_pair(own[0], own[1], j, at, cols_low - 1).reshape(rows_low, cols_low, chan)
            odd = column_pair(own[2], own[3], j, at, cols_low - 1).reshape(rows_low, cols_low, chan)
            below = jnp.concatenate([even[1:], zero], axis=0)
            above = jnp.concatenate([zero, odd[:-1]], axis=0)
            for value in (odd + below, even + odd, above + even):
                parts.append(jnp.concatenate(split(value.reshape(count, chan)), axis=0))
        sums = product(jnp.concatenate(parts, axis=1), turned)
        total = total + (sums[:count] + sums[count:])
        out_ref[frame] = total.reshape(rows_low, cols_low, chan)


def input_own(pg, ext, ws, before, low_shape):
    return pl.pallas_call(
        input_kernel,
        in_specs=[FULL] * 3 + [UNREAD],
        out_specs=FULL,
        out_shape=like(low_shape, jnp.float32),
        compiler_params=grant(16),
        cost_estimate=cost(6, 4),
        name="input_own",
    )(pg, ext, ws, before)


def finish_kernel(place_ref, edge_hbm, inner_hbm, outer_hbm, act_ref, low_ref, own_ref, ws_ref, wt_ref, merge_ref, _,
                  section_ref, input_ref, token_ref, edge_ref, inner_ref, outer_ref, earlier, held, input_held, sems):
    frames, rows_low, cols_low, chan = low_ref.shape
    group = rows_at_once(rows_low, cols_low)
    span, count = group * cols_low, rows_low * cols_low
    arrivals = [pltpu.make_async_copy(a, b, sems.at[n]) for n, (a, b) in enumerate(
        ((edge_hbm, edge_ref), (inner_hbm, inner_ref), (outer_hbm, outer_ref)))]
    for copy in arrivals:
        copy.start()
    token_ref[...] = jnp.zeros_like(token_ref)
    wt = wt_ref[...].reshape(3 * chan, chan)
    leaving = []

    def section_frame(frame):
        acts = [act_ref[frame - k] if frame >= k else earlier[frame - k + 2] for k in range(3)]
        acts = jnp.concatenate([act.reshape(4 * count, chan) for act in acts], axis=1)
        low = low_ref[frame].reshape(1, count, chan).astype(jnp.float32)
        mixed = (product(acts, wt).reshape(4, count, chan) + low).astype(jnp.bfloat16)
        for n in range(rows_low // group):
            block = mixed[:, n * span : (n + 1) * span].reshape(4 * span, chan)
            block = product(merge_ref[...], block).astype(jnp.bfloat16)
            held[frame, 2 * group * n : 2 * group * (n + 1)] = block.reshape(2 * group, 2 * cols_low, chan)
        leaving.append(pltpu.make_async_copy(held.at[frame], section_ref.at[frame], sems.at[4 + frame]))
        leaving[-1].start()

    for frame in range(2, frames):
        section_frame(frame)

    for copy in arrivals[1:]:
        copy.wait()
    odd_place = place_ref[1] == 1
    flat = (frames * cols_low, chan)
    at = column(flat[0], cols_low, chan)
    inner = [inner_ref[:, b].reshape(flat).astype(jnp.float32) for b in range(2)]
    outer = [outer_ref[:, b].reshape(flat).astype(jnp.float32) for b in range(2)]
    above = [jnp.where(odd_place, inner[b], outer[b]) for b in range(2)]
    below = [jnp.where(odd_place, outer[b], inner[b]) for b in range(2)]
    terms = []
    for (first, second), i in ((above, 2), (below, 0)):
        total = jnp.zeros(flat, jnp.float32)
        for j in range(3):
            parts = jnp.concatenate(split(column_pair(first, second, j, at, cols_low - 1)), axis=0)
            sums = product_nt(parts, ws_ref[i, j])
            total = total + (sums[: flat[0]] + sums[flat[0] :])
        terms.append(total.reshape(frames, cols_low, chan))
    for row in range(rows_low):
        value = own_ref[:, row]
        if row == 0:
            value = value + terms[0]
        if row == rows_low - 1:
            value = value + terms[1]
        input_held[:, row] = value.astype(jnp.bfloat16)
    leaving.append(pltpu.make_async_copy(input_held, input_ref, sems.at[3]))
    leaving[-1].start()

    arrivals[0].wait()
    for frame in range(2):
        for side, pre in enumerate(spatial(edge_ref[frame], ws_ref)):
            earlier[frame, side] = (pre * jax.nn.sigmoid(pre)).astype(jnp.bfloat16)
    for frame in reversed(range(2)):
        section_frame(frame)
    for copy in leaving:
        copy.wait()


def finish(place, edge, inner, outer, act, low, own, ws, wt, merge, before):
    frames, rows_low, cols_low, chan = low.shape
    out = (frames, 2 * rows_low, 2 * cols_low, chan)
    arrivals = [edge, inner, outer]
    return pl.pallas_call(
        finish_kernel,
        in_specs=[SCALAR] + [HBM] * 3 + [FULL] * 6 + [UNREAD],
        out_specs=[HBM, HBM, FULL],
        out_shape=[like(out, jnp.bfloat16), like(low.shape, jnp.bfloat16), TOKEN],
        scratch_shapes=[pltpu.VMEM(a.shape, a.dtype) for a in arrivals]
        + [pltpu.VMEM((2,) + act.shape[1:], act.dtype), pltpu.VMEM(out, jnp.bfloat16),
           pltpu.VMEM(low.shape, jnp.bfloat16), pltpu.SemaphoreType.DMA((4 + frames,))],
        compiler_params=grant(14),
        cost_estimate=cost(8, 4),
        name="finish",
    )(place, *arrivals, act, low, own, ws, wt, merge, before)


def put_kernel(place_ref, half_ref, *refs):
    spatial_ref, temporal_ref, wide, sems = refs[-4:]
    taps, half, _ = half_ref.shape
    to = pl.ds(pl.multiple_of(place_ref[0] * half, half), half)
    copies = []
    for tap in range(taps):
        wide[tap] = half_ref[tap].astype(jnp.float32)
        if tap < 9:
            target = spatial_ref.at[tap // 3, tap % 3, to]
        else:
            target = temporal_ref.at[tap - 9, to]
        copies.append(pltpu.make_async_copy(wide.at[tap], target, sems.at[tap]))
        copies[-1].start()
    for copy in copies:
        copy.wait()


def put(place, half, *done):
    chan = half.shape[-1]
    return pl.pallas_call(
        put_kernel,
        in_specs=[SCALAR, FULL] + [HBM] * len(done),
        out_specs=[HBM, HBM],
        out_shape=[like((3, 3, chan, chan), jnp.float32), like((3, chan, chan), jnp.float32)],
        input_output_aliases={2 + n: n for n in range(len(done))},
        scratch_shapes=[pltpu.VMEM((12, chan // 2, chan), jnp.float32), pltpu.SemaphoreType.DMA((12,))],
        compiler_params=grant(6),
        name="put",
    )(place, half, *done)


def add_kernel(mine_ref, theirs_ref, out_ref):
    out_ref[...] = (mine_ref[...] + theirs_ref[...]).astype(jnp.bfloat16)


def add_halves(mine, theirs):
    full = pl.BlockSpec(memory_space=pltpu.VMEM)
    return pl.pallas_call(
        add_kernel,
        in_specs=[full, full],
        out_specs=full,
        out_shape=like(mine.shape, jnp.bfloat16),
        compiler_params=grant(8),
        name="add_halves",
    )(mine, theirs)


def sum_kernel(got_ref, _, out_ref):
    total = got_ref[0].astype(jnp.float32)
    for n in range(1, got_ref.shape[0]):
        total = total + got_ref[n].astype(jnp.float32)
    out_ref[...] = total.astype(jnp.bfloat16)


def sum_parts(got, before):
    return pl.pallas_call(
        sum_kernel,
        in_specs=[FULL, UNREAD],
        out_specs=FULL,
        out_shape=like(got.shape[1:], jnp.bfloat16),
        compiler_params=grant(4),
        name="sum_parts",
    )(got, before)


def spread_kernel(own_ref, theirs_ref, *refs):
    total = (own_ref[...].astype(jnp.float32) + theirs_ref[...].astype(jnp.float32)).astype(jnp.bfloat16)
    for n in range(refs[-1].shape[0]):
        refs[-1][n] = total


def spread(own, theirs, parts, *before):
    return pl.pallas_call(
        spread_kernel,
        in_specs=[FULL, FULL] + [UNREAD] * len(before),
        out_specs=FULL,
        out_shape=like((parts,) + own.shape, jnp.bfloat16),
        compiler_params=grant(4),
        name="spread",
    )(own, theirs, *before)


def on_device(bits, low_frames, spatial_weight, temporal_weight, cotangent):
    low, cot = low_frames[0], cotangent[0]
    frames, rows_low, cols_low, chan = low.shape
    core = lax.axis_index(bits.core).astype(jnp.int32)
    odd = lax.axis_index(bits.axes["height"][-1]).astype(jnp.int32)
    mine, other = jnp.stack([core, odd]), jnp.stack([1 - core, odd])
    parts = 1 << len(bits.near)

    inner, outer, later = first_messages(mine, low, cot)
    later = bits.shift(later, "tm", -1)
    inner, outer = bits.pairs(inner, outer)
    low, ws, wt, sort, merge, turned, cot_side = load(low, cot, spatial_weight, temporal_weight)
    act, slope = forward(mine, low, inner, outer, ws)
    pg, ext, theirs = backward(other, low, inner, outer, act, slope, cot_side, later, turned, sort)
    theirs = bits.swap(theirs, bits.core)
    own = half_grads(mine, low, inner, outer, act, pg, ext)
    kept = add_halves(own, theirs)
    got = bits.exchange(kept.reshape(parts, -1, chan))
    edge, pg_inner, pg_outer = edges(mine, low, inner, outer, pg, kept)
    edge = bits.shift(edge, "tm", 1)
    pg_inner, pg_outer = bits.pairs(pg_inner, pg_outer)
    own_part = input_own(pg, ext, ws, kept, low.shape)
    total, far = bits.far_sums(sum_parts(got, own_part))
    section_out, input_grad, done = finish(
        mine, edge, pg_inner, pg_outer, act, low, own_part, ws, wt, merge, total
    )
    totals = spread(total, far, parts, done)
    half = bits.exchange(totals).reshape(kept.shape)
    theirs = bits.swap(half, bits.core)
    spatial_grad, temporal_grad = put(other, theirs, *put(mine, half))
    return section_out[None], input_grad[None], spatial_grad, temporal_grad


def solution(mesh):
    bits = Bits(mesh)
    block = P(*(bits.axes[name] for name in ("dp", "tm", "height")), None, None)
    return jax.shard_map(
        functools.partial(on_device, bits),
        mesh=bits.mesh,
        in_specs=(block, P(), P(), block),
        out_specs=(block, block, P(), P()),
        check_vma=False,
    )
```

```python
import functools

import jax
import jax.numpy as jnp
import numpy as np
from jax import lax
from jax.experimental import pallas as pl
from jax.experimental.pallas import tpu as pltpu
from jax.sharding import Mesh
from jax.sharding import PartitionSpec as P


class Bits:
    def __init__(self, mesh):
        self.axes = {}
        for name in mesh.axis_names:
            count = mesh.shape[name].bit_length() - 1
            self.axes[name] = tuple(f"{name}{bit}" for bit in reversed(range(count)))
        names = [bit for bits in self.axes.values() for bit in bits]
        self.mesh = Mesh(mesh.devices.reshape([2] * len(names)), tuple(names))
        self.core = next((n for n in names if self.same_chip(n)), self.axes["tm"][-1])
        others = [[b for b in reversed(bits) if b != self.core] for bits in self.axes.values()]
        turns = [bits[turn] for turn in range(len(names)) for bits in others if turn < len(bits)]
        self.near = [n for n in names if n in turns[:3]]
        self.far = turns[3:]

    def same_chip(self, name):
        at = [1 if n == name else 0 for n in self.mesh.axis_names]
        here = self.mesh.devices[tuple([0] * len(at))]
        there = self.mesh.devices[tuple(at)]
        return tuple(getattr(here, "coords", (0,))) == tuple(getattr(there, "coords", (1,)))

    def swap(self, block, axis):
        return lax.ppermute(block, axis, [(0, 1), (1, 0)])

    def shift(self, block, name, distance):
        axes = self.axes[name]
        devices = range(1 << len(axes))
        route = [(i - distance, i) for i in devices if i - distance in devices]
        return lax.ppermute(block, axes, route)

    def exchange(self, parts):
        return lax.all_to_all(parts, tuple(self.near), 0, 0, tiled=True)

    def pairs(self, inner, outer):
        axes = self.axes["height"]
        low = range(1, (1 << len(axes)) - 1, 2)
        route = [(i, i + 1) for i in low] + [(i + 1, i) for i in low]
        outer = lax.ppermute(outer, axes, route)
        return self.swap(inner, axes[-1]), outer

    def far_sums(self, total):
        for axis in self.far[:-1]:
            total = total.astype(jnp.float32) + self.swap(total, axis).astype(jnp.float32)
            total = lax.reduce_precision(total, 8, 7).astype(jnp.bfloat16)
        return total, self.swap(total, self.far[-1])


SIDES = ((0, 0), (0, 1), (1, 0), (1, 1))


def grant(mib):
    return pltpu.CompilerParams(vmem_limit_bytes=mib * 2**20)


def product(left, right):
    return jnp.dot(left, right, preferred_element_type=jnp.float32)


def product_nt(left, right):
    return lax.dot_general(left, right, (((1,), (1,)), ((), ())), preferred_element_type=jnp.float32)


def rows_at_once(rows_low, cols_low):
    return max(n for n in (1, 2, 4, 8) if rows_low % n == 0 and (n == 1 or 4 * n * cols_low <= 256))


def side_order(rows_low, cols_low):
    count = rows_at_once(rows_low, cols_low)
    size = 4 * count * cols_low
    at = np.arange(size).reshape(count, 2, cols_low, 2).transpose(1, 3, 0, 2).reshape(-1)
    return (at[:, None] == np.arange(size)[None, :]).astype(np.float32)


def column(rows, cols_low, chan):
    return lax.broadcasted_iota(jnp.int32, (rows // cols_low, cols_low, chan), 1).reshape(rows, chan)


def from_left(x, at):
    return jnp.where(at == 0, 0.0, pltpu.roll(x, 1, 0))


def from_right(x, at, last):
    return jnp.where(at == last, 0.0, pltpu.roll(x, x.shape[0] - 1, 0))


def sort_columns(source, target, cols_low, order):
    rows_low, chan = source.shape[0] // 2, source.shape[2]
    group = rows_at_once(rows_low, cols_low)
    span = group * cols_low
    for n in range(rows_low // group):
        block = source[2 * group * n : 2 * group * (n + 1)].reshape(4 * span, chan)
        block = product(order, block).astype(jnp.bfloat16).reshape(4, span, chan)
        target[:, n * span : (n + 1) * span, :] = block


def tall(place_ref, low_ref, inner_ref, outer_ref, frame, lanes=slice(None)):
    odd = place_ref[1] == 1
    inner, outer = inner_ref[frame, :, :, lanes], outer_ref[frame, :, :, lanes]
    up, down = jnp.where(odd, inner, outer), jnp.where(odd, outer, inner)
    return jnp.concatenate([up, low_ref[frame, :, :, lanes], down], axis=0)


def spatial(low, ws_ref):
    rows_low, cols_low, chan = low.shape[0] - 2, low.shape[1], low.shape[2]
    count = rows_low * cols_low
    flat = low.reshape(-1, chan)
    rows = [[], []]
    for j in range(3):
        taps = [product(flat, ws_ref[i, j]).reshape(low.shape) for i in range(3)]
        even = taps[0][:rows_low] + (taps[1] + taps[2])[1 : rows_low + 1]
        odd = (taps[0] + taps[1])[1 : rows_low + 1] + taps[2][2:]
        rows[0].append(even.reshape(count, chan))
        rows[1].append(odd.reshape(count, chan))
    at = column(count, cols_low, chan)
    for first, second, third in rows:
        yield from_left(first, at) + (second + third)
        yield (first + second) + from_right(third, at, cols_low - 1)


def forward_kernel(place_ref, low_ref, inner_ref, outer_ref, ws_ref, act_ref, slope_ref):
    for frame in range(low_ref.shape[0]):
        low = tall(place_ref, low_ref, inner_ref, outer_ref, frame)
        for side, pre in enumerate(spatial(low, ws_ref)):
            sig = jax.nn.sigmoid(pre)
            act_ref[frame, side] = (pre * sig).astype(jnp.bfloat16)
            slope_ref[frame, side] = sig * (1.0 + pre * (1.0 - sig))


def half_sums(place_ref, low_ref, inner_ref, outer_ref, act_ref, pg_ref, ext_ref, out_ref):
    frames, rows_low, cols_low, chan = low_ref.shape
    count, half = rows_low * cols_low, chan // 2
    lanes = pl.ds(pl.multiple_of(place_ref[0] * half, half), half)
    lefts = [[] for _ in range(9)]
    acts = []
    at = column((rows_low + 2) * cols_low, cols_low, half)
    for frame in range(frames):
        low = tall(place_ref, low_ref, inner_ref, outer_ref, frame, lanes)
        wide = low.reshape(-1, half).astype(jnp.float32)
        moved = [from_left(wide, at), wide, from_right(wide, at, cols_low - 1)]
        turned = {}
        for dc in range(3):
            view = moved[dc].astype(jnp.bfloat16).reshape(low.shape)
            for dr in range(3):
                turned[dr - 1, dc - 1] = view[dr : dr + rows_low].reshape(count, half).T
        for i in range(3):
            for j in range(3):
                lefts[3 * i + j] += [turned[(a + i - 1) // 2, (b + j - 1) // 2] for a, b in SIDES]
        acts.append(act_ref[frame, :, :, lanes].reshape(4 * count, half).T)
    pg = pg_ref[...].reshape(frames * 4 * count, chan)
    left = jnp.concatenate([jnp.concatenate(left, axis=1) for left in lefts], axis=0)
    out_ref[:9] = product(left, pg).reshape(9, half, chan)
    act = jnp.concatenate(acts, axis=1)
    for k in range(3):
        out_ref[9 + k] = product(act, ext_ref[k : k + frames].reshape(frames * 4 * count, chan))


def backward_kernel(place_ref, low_ref, inner_ref, outer_ref, act_ref, slope_ref, cot_ref, later_ref, turned_ref, sort_ref,
                    pg_ref, ext_ref, out_ref, act_out, pg_out, box_out, box_ref, sems):
    frames, _, count, chan = cot_ref.shape
    copies = [pltpu.make_async_copy(act_ref, act_out, sems.at[0])]
    copies[0].start()
    ext_ref[:frames] = cot_ref[...]
    for n in range(2):
        sort_columns(later_ref.at[n], ext_ref.at[frames + n], low_ref.shape[2], sort_ref[...])
    for frame in range(frames):
        cots = [ext_ref[frame + k].reshape(4 * count, chan) for k in range(3)]
        act_grad = product(jnp.concatenate(cots, axis=1), turned_ref[...])
        slope = slope_ref[frame].reshape(4 * count, chan)
        pg_ref[frame] = (act_grad * slope).astype(jnp.bfloat16).reshape(4, count, chan)
        box_ref[frame] = sum(cot_ref[frame, side].astype(jnp.float32) for side in range(4))
        copies.append(pltpu.make_async_copy(pg_ref.at[frame], pg_out.at[frame], sems.at[1 + frame]))
        copies[-1].start()
    copies.append(pltpu.make_async_copy(box_ref, box_out, sems.at[1 + frames]))
    copies[-1].start()
    half_sums(place_ref, low_ref, inner_ref, outer_ref, act_ref, pg_ref, ext_ref, out_ref)
    for copy in copies:
        copy.wait()


SCALAR = pl.BlockSpec(memory_space=pltpu.SMEM)
UNREAD = pl.BlockSpec(memory_space=pl.ANY)


def like(shape, dtype):
    return jax.ShapeDtypeStruct(shape, dtype)


TOKEN = like((8, 128), jnp.float32)


def cost(units, mib):
    return pl.CostEstimate(flops=units * 2 * 2048 * 256 * 256, bytes_accessed=mib * 2**20, transcendentals=0)


def in_hbm(array):
    return pltpu.with_memory_space_constraint(array, pltpu.HBM)


FULL = pl.BlockSpec(memory_space=pltpu.VMEM)
HBM = pl.BlockSpec(memory_space=pltpu.HBM)


def first_kernel(place_ref, low_ref, cot_ref, inner_ref, outer_ref, later_ref, sems):
    last = low_ref.shape[1] - 1
    odd = place_ref[1]
    copies = [
        (low_ref.at[:, pl.ds(last * (1 - odd), 1)], inner_ref),
        (low_ref.at[:, pl.ds(last * odd, 1)], outer_ref),
    ]
    copies += [(cot_ref.at[n, r], later_ref.at[n, r]) for n in range(2) for r in range(cot_ref.shape[1])]
    copies = [pltpu.make_async_copy(a, b, sems.at[n]) for n, (a, b) in enumerate(copies)]
    for copy in copies:
        copy.start()
    for copy in copies:
        copy.wait()


def first_messages(place, low, cot):
    row = like(low[:, :1].shape, low.dtype)
    return pl.pallas_call(
        first_kernel,
        in_specs=[SCALAR, UNREAD, UNREAD],
        out_specs=[FULL] * 3,
        out_shape=[row, row, like(cot[:2].shape, cot.dtype)],
        scratch_shapes=[pltpu.SemaphoreType.DMA((2 + 2 * cot.shape[1],))],
        compiler_params=grant(4),
        name="first_messages",
    )(place, in_hbm(low), in_hbm(cot))


def load_kernel(low_hbm, cot_hbm, ws_hbm, wt_hbm, sort_hbm,
                low_ref, ws_ref, sort_ref, turned_ref, side_ref, cot_ref, wide_ref, wt_ref, sems):
    frames, cols_low, chan = low_ref.shape[0], low_ref.shape[2], low_ref.shape[3]
    pairs = [(sort_hbm, wide_ref)] + [(cot_hbm.at[n], cot_ref.at[n]) for n in range(frames)]
    pairs += [(wt_hbm.at[k], wt_ref.at[k]) for k in range(3)] + [(low_hbm, low_ref)]
    pairs += [(ws_hbm.at[i, j], ws_ref.at[i, j]) for i in range(3) for j in range(3)]
    copies = [pltpu.make_async_copy(a, b, sems.at[n]) for n, (a, b) in enumerate(pairs)]
    for copy in copies:
        copy.start()
    copies[0].wait()
    sort_ref[...] = wide_ref[...].astype(jnp.bfloat16)
    for n in range(frames):
        copies[1 + n].wait()
        sort_columns(cot_ref.at[n], side_ref.at[n], cols_low, sort_ref[...])
    for k in range(3):
        copies[1 + frames + k].wait()
        turned_ref[k * chan : (k + 1) * chan] = wt_ref[k].T
    for copy in copies[4 + frames :]:
        copy.wait()


def load(low, cot, ws, wt, sort):
    frames, rows_low, cols_low, chan = low.shape
    order = like(sort.shape, jnp.bfloat16)
    shapes = [low, ws, order, like((3 * chan, chan), wt.dtype),
              like((frames, 4, rows_low * cols_low, chan), jnp.bfloat16)]
    return pl.pallas_call(
        load_kernel,
        in_specs=[UNREAD] * 5,
        out_specs=[FULL] * 5,
        out_shape=[like(a.shape, a.dtype) for a in shapes],
        scratch_shapes=[pltpu.VMEM(cot.shape, cot.dtype), pltpu.VMEM(sort.shape, sort.dtype), pltpu.VMEM(wt.shape, wt.dtype),
                        pltpu.SemaphoreType.DMA((frames + 14,))],
        compiler_params=grant(14),
        cost_estimate=cost(2, 4),
        name="load",
    )(*[in_hbm(a) for a in (low, cot, ws, wt, sort)])


def forward(place, low, inner, outer, ws):
    frames, rows_low, cols_low, chan = low.shape
    side = (frames, 4, rows_low * cols_low, chan)
    return pl.pallas_call(
        forward_kernel,
        in_specs=[SCALAR] + [FULL] * 4,
        out_specs=[FULL] * 2,
        out_shape=[like(side, jnp.bfloat16), like(side, jnp.float32)],
        compiler_params=grant(20),
        cost_estimate=cost(10, 8),
        name="forward",
    )(place, low, inner, outer, ws)


def edges_kernel(place_ref, low_hbm, inner_ref, outer_ref, pg_hbm, _, tall_ref, pg_inner, pg_outer, low_ref, rows_ref, sems):
    cols_low = low_ref.shape[2]
    frames, first = low_hbm.shape[0], low_hbm.shape[0] - 2
    copies = [
        pltpu.make_async_copy(low_hbm.at[first:], low_ref, sems.at[0]),
        pltpu.make_async_copy(pg_hbm.at[:, 0:2, 0:cols_low], rows_ref.at[0], sems.at[1]),
        pltpu.make_async_copy(pg_hbm.at[:, 2:4, pg_hbm.shape[2] - cols_low :], rows_ref.at[1], sems.at[2]),
    ]
    for copy in copies:
        copy.start()
    for copy in copies:
        copy.wait()
    odd = place_ref[1] == 1
    for n in range(2):
        inner, outer = inner_ref[first + n], outer_ref[first + n]
        up, down = jnp.where(odd, inner, outer), jnp.where(odd, outer, inner)
        tall_ref[n] = jnp.concatenate([up, low_ref[n], down], axis=0)
    pg_inner[...] = jnp.where(odd, rows_ref[0], rows_ref[1])
    pg_outer[...] = jnp.where(odd, rows_ref[1], rows_ref[0])


def edges(place, low, inner, outer, pg, before):
    frames, rows_low, cols_low, chan = low.shape
    rows = like((frames, 2, cols_low, chan), jnp.bfloat16)
    return pl.pallas_call(
        edges_kernel,
        in_specs=[SCALAR, HBM, FULL, FULL, HBM, UNREAD],
        out_specs=[FULL] * 3,
        out_shape=[like((2, rows_low + 2, cols_low, chan), jnp.bfloat16), rows, rows],
        scratch_shapes=[pltpu.VMEM((2,) + low.shape[1:], low.dtype), pltpu.VMEM((2,) + rows.shape, rows.dtype),
                        pltpu.SemaphoreType.DMA((3,))],
        compiler_params=grant(4),
        name="edges",
    )(place, in_hbm(low), inner, outer, in_hbm(pg), before)


def backward(place, low, inner, outer, act, slope, cot, later, turned, sort):
    frames, _, count, chan = act.shape
    ext = (frames + 2,) + act.shape[1:]
    box = (frames, count, chan)
    return pl.pallas_call(
        backward_kernel,
        in_specs=[SCALAR] + [FULL] * 9,
        out_specs=[FULL] * 3 + [HBM] * 3,
        out_shape=[like(act.shape, jnp.bfloat16), like(ext, jnp.bfloat16), like((12, chan // 2, chan), jnp.float32),
                   like(act.shape, jnp.bfloat16), like(act.shape, jnp.bfloat16), like(box, jnp.float32)],
        scratch_shapes=[pltpu.VMEM(box, jnp.float32), pltpu.SemaphoreType.DMA((frames + 2,))],
        compiler_params=grant(26),
        cost_estimate=cost(15, 10),
        name="backward",
    )(place, low, inner, outer, act, slope, cot, later, turned, sort)


def half_grads(place, low, inner, outer, act, pg, ext):
    chan = low.shape[-1]
    return pl.pallas_call(
        half_sums,
        in_specs=[SCALAR] + [FULL] * 6,
        out_specs=FULL,
        out_shape=like((12, chan // 2, chan), jnp.float32),
        compiler_params=grant(20),
        cost_estimate=cost(10, 6),
        name="half_grads",
    )(place, low, inner, outer, act, pg, ext)


def split(value):
    high = value.astype(jnp.bfloat16)
    return high, (value - high.astype(jnp.float32)).astype(jnp.bfloat16)


def column_pair(first, second, j, at, last):
    if j == 0:
        return second + from_right(first, at, last)
    if j == 1:
        return first + second
    return first + from_left(second, at)


def section_frame(acts, low, wt, merge, held):
    rows_low, cols_low, chan = low.shape
    group = rows_at_once(rows_low, cols_low)
    span, count = group * cols_low, rows_low * cols_low
    acts = jnp.concatenate([act.reshape(4 * count, chan) for act in acts], axis=1)
    mixed = product(acts, wt.reshape(3 * chan, chan)).reshape(4, count, chan)
    mixed = (mixed + low.reshape(1, count, chan).astype(jnp.float32)).astype(jnp.bfloat16)
    for n in range(rows_low // group):
        block = mixed[:, n * span : (n + 1) * span].reshape(4 * span, chan)
        block = product(merge, block).astype(jnp.bfloat16)
        held[2 * group * n : 2 * group * (n + 1)] = block.reshape(2 * group, 2 * cols_low, chan)


def middle_kernel(pg_hbm, act_hbm, box_hbm, low_hbm, ws_hbm, wt_hbm, sort_hbm, _,
                  out_ref, section_ref, ws_ref, wt_ref, merge_ref, act_ref, low_ref,
                  pg_ref, box_ref, wide_ref, held, sems):
    frames, rows_low, cols_low, chan = low_ref.shape
    count = rows_low * cols_low
    pairs = [(pg_hbm.at[0], pg_ref.at[0])]
    pairs += [(ws_hbm.at[i, j], ws_ref.at[i, j]) for i in range(3) for j in range(3)]
    pairs += [(box_hbm, box_ref)] + [(pg_hbm.at[n], pg_ref.at[n]) for n in range(1, frames)]
    pairs += [(sort_hbm, wide_ref), (act_hbm, act_ref), (wt_hbm, wt_ref), (low_hbm, low_ref)]
    copies = [pltpu.make_async_copy(a, b, sems.at[n]) for n, (a, b) in enumerate(pairs)]
    for copy in copies:
        copy.start()
    for copy in copies[:11]:
        copy.wait()
    at = column(count, cols_low, chan)
    turned = jnp.concatenate([ws_ref[i, j].T for j in range(3) for i in range(3)], axis=0)
    for frame in range(frames):
        if frame:
            copies[10 + frame].wait()
        own = [pg_ref[frame, side].astype(jnp.float32) for side in range(4)]
        zero = jnp.zeros((1, cols_low, chan), jnp.float32)
        parts = []
        for j in range(3):
            even = column_pair(own[0], own[1], j, at, cols_low - 1).reshape(rows_low, cols_low, chan)
            odd = column_pair(own[2], own[3], j, at, cols_low - 1).reshape(rows_low, cols_low, chan)
            below = jnp.concatenate([even[1:], zero], axis=0)
            above = jnp.concatenate([zero, odd[:-1]], axis=0)
            for value in (odd + below, even + odd, above + even):
                parts.append(jnp.concatenate(split(value.reshape(count, chan)), axis=0))
        sums = product(jnp.concatenate(parts, axis=1), turned)
        out_ref[frame] = (box_ref[frame] + (sums[:count] + sums[count:])).reshape(rows_low, cols_low, chan)
    for copy in copies[10 + frames :]:
        copy.wait()
    merge_ref[...] = wide_ref[...].T.astype(jnp.bfloat16)
    leaving = []
    for frame in range(3, frames):
        acts = [act_ref[frame - k] for k in range(3)]
        section_frame(acts, low_ref[frame], wt_ref[...], merge_ref[...], held.at[frame - 3])
        leaving.append(pltpu.make_async_copy(held.at[frame - 3], section_ref.at[frame], sems.at[frame]))
        leaving[-1].start()
    for copy in leaving:
        copy.wait()


def middle(pg, act, box, low, ws, wt, sort, before):
    frames, rows_low, cols_low, chan = low.shape
    out = (frames, 2 * rows_low, 2 * cols_low, chan)
    order = like(sort.shape, jnp.bfloat16)
    operands = [like(a.shape, a.dtype) for a in (ws, wt, order, act, low)]
    return pl.pallas_call(
        middle_kernel,
        in_specs=[HBM] * 7 + [UNREAD],
        out_specs=[FULL, HBM] + [FULL] * 5,
        out_shape=[like(low.shape, jnp.float32), like(out, jnp.bfloat16)] + operands,
        scratch_shapes=[pltpu.VMEM(pg.shape, pg.dtype), pltpu.VMEM(box.shape, box.dtype),
                        pltpu.VMEM(sort.shape, sort.dtype), pltpu.VMEM((frames - 3,) + out[1:], jnp.bfloat16),
                        pltpu.SemaphoreType.DMA((14 + frames,))],
        compiler_params=grant(20),
        cost_estimate=cost(8, 5),
        name="middle",
    )(*[in_hbm(a) for a in (pg, act, box, low, ws, wt, sort)], before)


def finish_kernel(place_ref, edge_hbm, inner_hbm, outer_hbm, act_ref, low_ref, own_ref, ws_ref, wt_ref, merge_ref, _, __,
                  section_ref, input_ref, token_ref, edge_ref, inner_ref, outer_ref, earlier, held, input_held, sems):
    frames, rows_low, cols_low, chan = low_ref.shape
    arrivals = [pltpu.make_async_copy(a, b, sems.at[n]) for n, (a, b) in enumerate(
        ((edge_hbm, edge_ref), (inner_hbm, inner_ref), (outer_hbm, outer_ref)))]
    for copy in arrivals:
        copy.start()
    token_ref[...] = jnp.zeros_like(token_ref)
    leaving = []

    def put_frame(frame):
        acts = [act_ref[frame - k] if frame >= k else earlier[frame - k + 2] for k in range(3)]
        section_frame(acts, low_ref[frame], wt_ref[...], merge_ref[...], held.at[frame])
        leaving.append(pltpu.make_async_copy(held.at[frame], section_ref.at[frame], sems.at[4 + frame]))
        leaving[-1].start()

    put_frame(2)
    for copy in arrivals[1:]:
        copy.wait()
    odd_place = place_ref[1] == 1
    flat = (frames * cols_low, chan)
    at = column(flat[0], cols_low, chan)
    inner = [inner_ref[:, b].reshape(flat).astype(jnp.float32) for b in range(2)]
    outer = [outer_ref[:, b].reshape(flat).astype(jnp.float32) for b in range(2)]
    above = [jnp.where(odd_place, inner[b], outer[b]) for b in range(2)]
    below = [jnp.where(odd_place, outer[b], inner[b]) for b in range(2)]
    terms = []
    for (first, second), i in ((above, 2), (below, 0)):
        total = jnp.zeros(flat, jnp.float32)
        for j in range(3):
            parts = jnp.concatenate(split(column_pair(first, second, j, at, cols_low - 1)), axis=0)
            sums = product_nt(parts, ws_ref[i, j])
            total = total + (sums[: flat[0]] + sums[flat[0] :])
        terms.append(total.reshape(frames, cols_low, chan))
    for row in range(rows_low):
        value = own_ref[:, row]
        if row == 0:
            value = value + terms[0]
        if row == rows_low - 1:
            value = value + terms[1]
        input_held[:, row] = value.astype(jnp.bfloat16)
    leaving.append(pltpu.make_async_copy(input_held, input_ref, sems.at[3]))
    leaving[-1].start()

    arrivals[0].wait()
    for frame in range(2):
        for side, pre in enumerate(spatial(edge_ref[frame], ws_ref)):
            earlier[frame, side] = (pre * jax.nn.sigmoid(pre)).astype(jnp.bfloat16)
    for frame in reversed(range(2)):
        put_frame(frame)
    for copy in leaving:
        copy.wait()


def finish(place, edge, inner, outer, act, low, own, ws, wt, merge, begun, before):
    frames, rows_low, cols_low, chan = low.shape
    out = begun.shape
    arrivals = [edge, inner, outer]
    return pl.pallas_call(
        finish_kernel,
        in_specs=[SCALAR] + [HBM] * 3 + [FULL] * 6 + [HBM, UNREAD],
        out_specs=[HBM, HBM, FULL],
        input_output_aliases={10: 0},
        out_shape=[like(out, jnp.bfloat16), like(low.shape, jnp.bfloat16), TOKEN],
        scratch_shapes=[pltpu.VMEM(a.shape, a.dtype) for a in arrivals]
        + [pltpu.VMEM((2,) + act.shape[1:], act.dtype), pltpu.VMEM((3,) + out[1:], jnp.bfloat16),
           pltpu.VMEM(low.shape, jnp.bfloat16), pltpu.SemaphoreType.DMA((7,))],
        compiler_params=grant(14),
        cost_estimate=cost(8, 4),
        name="finish",
    )(place, *arrivals, act, low, own, ws, wt, merge, begun, before)


def put_kernel(place_ref, half_ref, *refs):
    spatial_ref, temporal_ref, wide, sems = refs[-4:]
    taps, half, _ = half_ref.shape
    to = pl.ds(pl.multiple_of(place_ref[0] * half, half), half)
    copies = []
    for tap in range(taps):
        wide[tap] = half_ref[tap].astype(jnp.float32)
        if tap < 9:
            target = spatial_ref.at[tap // 3, tap % 3, to]
        else:
            target = temporal_ref.at[tap - 9, to]
        copies.append(pltpu.make_async_copy(wide.at[tap], target, sems.at[tap]))
        copies[-1].start()
    for copy in copies:
        copy.wait()


def put(place, half, *done):
    chan = half.shape[-1]
    return pl.pallas_call(
        put_kernel,
        in_specs=[SCALAR, FULL] + [HBM] * len(done),
        out_specs=[HBM, HBM],
        out_shape=[like((3, 3, chan, chan), jnp.float32), like((3, chan, chan), jnp.float32)],
        input_output_aliases={2 + n: n for n in range(len(done))},
        scratch_shapes=[pltpu.VMEM((12, chan // 2, chan), jnp.float32), pltpu.SemaphoreType.DMA((12,))],
        compiler_params=grant(6),
        name="put",
    )(place, half, *done)


def add_kernel(mine_ref, theirs_ref, out_ref):
    out_ref[...] = (mine_ref[...] + theirs_ref[...]).astype(jnp.bfloat16)


def add_halves(mine, theirs):
    full = pl.BlockSpec(memory_space=pltpu.VMEM)
    return pl.pallas_call(
        add_kernel,
        in_specs=[full, full],
        out_specs=full,
        out_shape=like(mine.shape, jnp.bfloat16),
        compiler_params=grant(8),
        name="add_halves",
    )(mine, theirs)


def sum_kernel(got_ref, _, out_ref):
    total = got_ref[0].astype(jnp.float32)
    for n in range(1, got_ref.shape[0]):
        total = total + got_ref[n].astype(jnp.float32)
    out_ref[...] = total.astype(jnp.bfloat16)


def sum_parts(got, before):
    return pl.pallas_call(
        sum_kernel,
        in_specs=[FULL, UNREAD],
        out_specs=FULL,
        out_shape=like(got.shape[1:], jnp.bfloat16),
        compiler_params=grant(4),
        name="sum_parts",
    )(got, before)


def spread_kernel(own_ref, theirs_ref, *refs):
    total = (own_ref[...].astype(jnp.float32) + theirs_ref[...].astype(jnp.float32)).astype(jnp.bfloat16)
    for n in range(refs[-1].shape[0]):
        refs[-1][n] = total


def spread(own, theirs, parts, *before):
    return pl.pallas_call(
        spread_kernel,
        in_specs=[FULL, FULL] + [UNREAD] * len(before),
        out_specs=FULL,
        out_shape=like((parts,) + own.shape, jnp.bfloat16),
        compiler_params=grant(4),
        name="spread",
    )(own, theirs, *before)


def on_device(bits, low_frames, spatial_weight, temporal_weight, cotangent):
    low, cot = low_frames[0], cotangent[0]
    frames, rows_low, cols_low, chan = low.shape
    core = lax.axis_index(bits.core).astype(jnp.int32)
    odd = lax.axis_index(bits.axes["height"][-1]).astype(jnp.int32)
    mine, other = jnp.stack([core, odd]), jnp.stack([1 - core, odd])
    parts = 1 << len(bits.near)

    inner, outer, later = first_messages(mine, low, cot)
    later = bits.shift(later, "tm", -1)
    inner, outer = bits.pairs(inner, outer)
    order = jnp.asarray(side_order(rows_low, cols_low))
    low_in, ws, sort, turned, cot_side = load(low, cot, spatial_weight, temporal_weight, order)
    act, slope = forward(mine, low_in, inner, outer, ws)
    pg, ext, theirs, act_out, pg_out, box = backward(
        other, low_in, inner, outer, act, slope, cot_side, later, turned, sort
    )
    theirs = bits.swap(theirs, bits.core)
    own = half_grads(mine, low_in, inner, outer, act, pg, ext)
    kept = add_halves(own, theirs)
    got = bits.exchange(kept.reshape(parts, -1, chan))
    edge, pg_inner, pg_outer = edges(mine, low, inner, outer, pg_out, kept)
    edge = bits.shift(edge, "tm", 1)
    pg_inner, pg_outer = bits.pairs(pg_inner, pg_outer)
    own_part, begun, ws, wt, merge, act, low_in = middle(
        pg_out, act_out, box, low, spatial_weight, temporal_weight, order, kept
    )
    total, far = bits.far_sums(sum_parts(got, own_part))
    section_out, input_grad, done = finish(
        mine, edge, pg_inner, pg_outer, act, low_in, own_part, ws, wt, merge, begun, total
    )
    totals = spread(total, far, parts, done)
    half = bits.exchange(totals).reshape(kept.shape)
    theirs = bits.swap(half, bits.core)
    spatial_grad, temporal_grad = put(other, theirs, *put(mine, half))
    return section_out[None], input_grad[None], spatial_grad, temporal_grad


def solution(mesh):
    bits = Bits(mesh)
    block = P(*(bits.axes[name] for name in ("dp", "tm", "height")), None, None)
    return jax.shard_map(
        functools.partial(on_device, bits),
        mesh=bits.mesh,
        in_specs=(block, P(), P(), block),
        out_specs=(block, block, P(), P()),
        check_vma=False,
    )
```

```python
import functools

import jax
import jax.numpy as jnp
import numpy as np
from jax import lax
from jax.experimental import pallas as pl
from jax.experimental.pallas import tpu as pltpu
from jax.sharding import Mesh
from jax.sharding import PartitionSpec as P


class Bits:
    def __init__(self, mesh):
        self.axes = {}
        for name in mesh.axis_names:
            count = mesh.shape[name].bit_length() - 1
            self.axes[name] = tuple(f"{name}{bit}" for bit in reversed(range(count)))
        names = [bit for bits in self.axes.values() for bit in bits]
        self.mesh = Mesh(mesh.devices.reshape([2] * len(names)), tuple(names))
        self.core = next((n for n in names if self.same_chip(n)), self.axes["tm"][-1])
        others = [[b for b in reversed(bits) if b != self.core] for bits in self.axes.values()]
        turns = [bits[turn] for turn in range(len(names)) for bits in others if turn < len(bits)]
        self.near = [n for n in names if n in turns[:3]]
        self.far = turns[3:]

    def same_chip(self, name):
        at = [1 if n == name else 0 for n in self.mesh.axis_names]
        here = self.mesh.devices[tuple([0] * len(at))]
        there = self.mesh.devices[tuple(at)]
        return tuple(getattr(here, "coords", (0,))) == tuple(getattr(there, "coords", (1,)))

    def swap(self, block, axis):
        return lax.ppermute(block, axis, [(0, 1), (1, 0)])

    def shift(self, block, name, distance):
        axes = self.axes[name]
        devices = range(1 << len(axes))
        route = [(i - distance, i) for i in devices if i - distance in devices]
        return lax.ppermute(block, axes, route)

    def exchange(self, parts):
        return lax.all_to_all(parts, tuple(self.near), 0, 0, tiled=True)

    def pairs(self, inner, outer):
        axes = self.axes["height"]
        low = range(1, (1 << len(axes)) - 1, 2)
        route = [(i, i + 1) for i in low] + [(i + 1, i) for i in low]
        outer = lax.ppermute(outer, axes, route)
        return self.swap(inner, axes[-1]), outer

    def far_sums(self, total):
        for axis in self.far[:-1]:
            total = total.astype(jnp.float32) + self.swap(total, axis).astype(jnp.float32)
            total = lax.reduce_precision(total, 8, 7).astype(jnp.bfloat16)
        return total, self.swap(total, self.far[-1])


SIDES = ((0, 0), (0, 1), (1, 0), (1, 1))


def grant(mib):
    return pltpu.CompilerParams(vmem_limit_bytes=mib * 2**20)


def product(left, right):
    return jnp.dot(left, right, preferred_element_type=jnp.float32)


def product_nt(left, right):
    return lax.dot_general(left, right, (((1,), (1,)), ((), ())), preferred_element_type=jnp.float32)


def rows_at_once(rows_low, cols_low):
    return max(n for n in (1, 2, 4, 8) if rows_low % n == 0 and (n == 1 or 4 * n * cols_low <= 256))


def side_order(rows_low, cols_low):
    count = rows_at_once(rows_low, cols_low)
    size = 4 * count * cols_low
    at = np.arange(size).reshape(count, 2, cols_low, 2).transpose(1, 3, 0, 2).reshape(-1)
    return (at[:, None] == np.arange(size)[None, :]).astype(np.float32)


def column(rows, cols_low, chan):
    return lax.broadcasted_iota(jnp.int32, (rows // cols_low, cols_low, chan), 1).reshape(rows, chan)


def from_left(x, at):
    return jnp.where(at == 0, 0.0, pltpu.roll(x, 1, 0))


def from_right(x, at, last):
    return jnp.where(at == last, 0.0, pltpu.roll(x, x.shape[0] - 1, 0))


def sort_columns(source, target, cols_low, order):
    rows_low, chan = source.shape[0] // 2, source.shape[2]
    group = rows_at_once(rows_low, cols_low)
    span = group * cols_low
    for n in range(rows_low // group):
        block = source[2 * group * n : 2 * group * (n + 1)].reshape(4 * span, chan)
        block = product(order, block).astype(jnp.bfloat16).reshape(4, span, chan)
        target[:, n * span : (n + 1) * span, :] = block


def tall(place_ref, low_ref, inner_ref, outer_ref, frame, lanes=slice(None)):
    odd = place_ref[1] == 1
    inner, outer = inner_ref[frame, :, :, lanes], outer_ref[frame, :, :, lanes]
    up, down = jnp.where(odd, inner, outer), jnp.where(odd, outer, inner)
    return jnp.concatenate([up, low_ref[frame, :, :, lanes], down], axis=0)


def spatial(low, ws_ref):
    rows_low, cols_low, chan = low.shape[0] - 2, low.shape[1], low.shape[2]
    count = rows_low * cols_low
    flat = low.reshape(-1, chan)
    rows = [[], []]
    for j in range(3):
        taps = [product(flat, ws_ref[i, j]).reshape(low.shape) for i in range(3)]
        even = taps[0][:rows_low] + (taps[1] + taps[2])[1 : rows_low + 1]
        odd = (taps[0] + taps[1])[1 : rows_low + 1] + taps[2][2:]
        rows[0].append(even.reshape(count, chan))
        rows[1].append(odd.reshape(count, chan))
    at = column(count, cols_low, chan)
    for first, second, third in rows:
        yield from_left(first, at) + (second + third)
        yield (first + second) + from_right(third, at, cols_low - 1)


def forward_kernel(place_ref, low_ref, inner_ref, outer_ref, ws_ref, act_ref, slope_ref):
    for frame in range(low_ref.shape[0]):
        low = tall(place_ref, low_ref, inner_ref, outer_ref, frame)
        for side, pre in enumerate(spatial(low, ws_ref)):
            sig = jax.nn.sigmoid(pre)
            act_ref[frame, side] = (pre * sig).astype(jnp.bfloat16)
            slope_ref[frame, side] = sig * (1.0 + pre * (1.0 - sig))


def half_sums(place_ref, low_ref, inner_ref, outer_ref, act_ref, pg_ref, ext_ref, out_ref):
    frames, rows_low, cols_low, chan = low_ref.shape
    count, half = rows_low * cols_low, chan // 2
    lanes = pl.ds(pl.multiple_of(place_ref[0] * half, half), half)
    lefts = [[] for _ in range(9)]
    acts = []
    at = column((rows_low + 2) * cols_low, cols_low, half)
    for frame in range(frames):
        low = tall(place_ref, low_ref, inner_ref, outer_ref, frame, lanes)
        wide = low.reshape(-1, half).astype(jnp.float32)
        moved = [from_left(wide, at), wide, from_right(wide, at, cols_low - 1)]
        turned = {}
        for dc in range(3):
            view = moved[dc].astype(jnp.bfloat16).reshape(low.shape)
            for dr in range(3):
                turned[dr - 1, dc - 1] = view[dr : dr + rows_low].reshape(count, half).T
        for i in range(3):
            for j in range(3):
                lefts[3 * i + j] += [turned[(a + i - 1) // 2, (b + j - 1) // 2] for a, b in SIDES]
        acts.append(act_ref[frame, :, :, lanes].reshape(4 * count, half).T)
    pg = pg_ref[...].reshape(frames * 4 * count, chan)
    left = jnp.concatenate([jnp.concatenate(left, axis=1) for left in lefts], axis=0)
    out_ref[:9] = product(left, pg).reshape(9, half, chan)
    act = jnp.concatenate(acts, axis=1)
    for k in range(3):
        out_ref[9 + k] = product(act, ext_ref[k : k + frames].reshape(frames * 4 * count, chan))


def backward_kernel(place_ref, low_ref, inner_ref, outer_ref, act_ref, slope_ref, cot_ref, later_ref, turned_ref, sort_ref,
                    pg_ref, ext_ref, out_ref, box_ref):
    frames, _, count, chan = cot_ref.shape
    ext_ref[:frames] = cot_ref[...]
    for n in range(2):
        sort_columns(later_ref.at[n], ext_ref.at[frames + n], low_ref.shape[2], sort_ref[...])
    for frame in range(frames):
        cots = [ext_ref[frame + k].reshape(4 * count, chan) for k in range(3)]
        act_grad = product(jnp.concatenate(cots, axis=1), turned_ref[...])
        slope = slope_ref[frame].reshape(4 * count, chan)
        pg_ref[frame] = (act_grad * slope).astype(jnp.bfloat16).reshape(4, count, chan)
        box_ref[frame] = sum(cot_ref[frame, side].astype(jnp.float32) for side in range(4))
    half_sums(place_ref, low_ref, inner_ref, outer_ref, act_ref, pg_ref, ext_ref, out_ref)


SCALAR = pl.BlockSpec(memory_space=pltpu.SMEM)
UNREAD = pl.BlockSpec(memory_space=pl.ANY)


def like(shape, dtype):
    return jax.ShapeDtypeStruct(shape, dtype)


TOKEN = like((8, 128), jnp.float32)


def cost(units, mib):
    return pl.CostEstimate(flops=units * 2 * 2048 * 256 * 256, bytes_accessed=mib * 2**20, transcendentals=0)


def in_hbm(array):
    return pltpu.with_memory_space_constraint(array, pltpu.HBM)


FULL = pl.BlockSpec(memory_space=pltpu.VMEM)


def first_kernel(place_ref, low_ref, cot_ref, inner_ref, outer_ref, later_ref, sems):
    last = low_ref.shape[1] - 1
    odd = place_ref[1]
    copies = [
        (low_ref.at[:, pl.ds(last * (1 - odd), 1)], inner_ref),
        (low_ref.at[:, pl.ds(last * odd, 1)], outer_ref),
    ]
    copies += [(cot_ref.at[n, r], later_ref.at[n, r]) for n in range(2) for r in range(cot_ref.shape[1])]
    copies = [pltpu.make_async_copy(a, b, sems.at[n]) for n, (a, b) in enumerate(copies)]
    for copy in copies:
        copy.start()
    for copy in copies:
        copy.wait()


def first_messages(place, low, cot):
    row = like(low[:, :1].shape, low.dtype)
    return pl.pallas_call(
        first_kernel,
        in_specs=[SCALAR, UNREAD, UNREAD],
        out_specs=[FULL] * 3,
        out_shape=[row, row, like(cot[:2].shape, cot.dtype)],
        scratch_shapes=[pltpu.SemaphoreType.DMA((2 + 2 * cot.shape[1],))],
        compiler_params=grant(4),
        name="first_messages",
    )(place, in_hbm(low), in_hbm(cot))


def load_kernel(low_hbm, cot_hbm, ws_hbm, wt_hbm, sort_hbm,
                low_ref, ws_ref, sort_ref, turned_ref, side_ref, cot_ref, wide_ref, wt_ref, sems):
    frames, cols_low, chan = low_ref.shape[0], low_ref.shape[2], low_ref.shape[3]
    pairs = [(sort_hbm, wide_ref)] + [(cot_hbm.at[n], cot_ref.at[n]) for n in range(frames)]
    pairs += [(wt_hbm.at[k], wt_ref.at[k]) for k in range(3)] + [(low_hbm, low_ref)]
    pairs += [(ws_hbm.at[i, j], ws_ref.at[i, j]) for i in range(3) for j in range(3)]
    copies = [pltpu.make_async_copy(a, b, sems.at[n]) for n, (a, b) in enumerate(pairs)]
    for copy in copies:
        copy.start()
    copies[0].wait()
    sort_ref[...] = wide_ref[...].astype(jnp.bfloat16)
    for n in range(frames):
        copies[1 + n].wait()
        sort_columns(cot_ref.at[n], side_ref.at[n], cols_low, sort_ref[...])
    for k in range(3):
        copies[1 + frames + k].wait()
        turned_ref[k * chan : (k + 1) * chan] = wt_ref[k].T
    for copy in copies[4 + frames :]:
        copy.wait()


def load(low, cot, ws, wt, sort):
    frames, rows_low, cols_low, chan = low.shape
    order = like(sort.shape, jnp.bfloat16)
    shapes = [low, ws, order, like((3 * chan, chan), wt.dtype),
              like((frames, 4, rows_low * cols_low, chan), jnp.bfloat16)]
    return pl.pallas_call(
        load_kernel,
        in_specs=[UNREAD] * 5,
        out_specs=[FULL] * 5,
        out_shape=[like(a.shape, a.dtype) for a in shapes],
        scratch_shapes=[pltpu.VMEM(cot.shape, cot.dtype), pltpu.VMEM(sort.shape, sort.dtype), pltpu.VMEM(wt.shape, wt.dtype),
                        pltpu.SemaphoreType.DMA((frames + 14,))],
        compiler_params=grant(14),
        cost_estimate=cost(2, 4),
        name="load",
    )(*[in_hbm(a) for a in (low, cot, ws, wt, sort)])


def forward(place, low, inner, outer, ws):
    frames, rows_low, cols_low, chan = low.shape
    side = (frames, 4, rows_low * cols_low, chan)
    return pl.pallas_call(
        forward_kernel,
        in_specs=[SCALAR] + [FULL] * 4,
        out_specs=[FULL] * 2,
        out_shape=[like(side, jnp.bfloat16), like(side, jnp.float32)],
        compiler_params=grant(20),
        cost_estimate=cost(10, 8),
        name="forward",
    )(place, low, inner, outer, ws)


def edges_kernel(place_ref, low_ref, inner_ref, outer_ref, pg_ref, _, tall_ref, pg_inner, pg_outer):
    cols_low = low_ref.shape[2]
    first = low_ref.shape[0] - tall_ref.shape[0]
    for n in range(tall_ref.shape[0]):
        tall_ref[n] = tall(place_ref, low_ref, inner_ref, outer_ref, first + n)
    odd = place_ref[1] == 1
    top, bottom = pg_ref[:, :2, :cols_low, :], pg_ref[:, 2:, -cols_low:, :]
    pg_inner[...] = jnp.where(odd, top, bottom)
    pg_outer[...] = jnp.where(odd, bottom, top)


def edges(place, low, inner, outer, pg, before):
    frames, rows_low, cols_low, chan = low.shape
    full = pl.BlockSpec(memory_space=pltpu.VMEM)
    rows = like((frames, 2, cols_low, chan), jnp.bfloat16)
    return pl.pallas_call(
        edges_kernel,
        in_specs=[SCALAR, full, full, full, full, UNREAD],
        out_specs=[full] * 3,
        out_shape=[like((2, rows_low + 2, cols_low, chan), jnp.bfloat16), rows, rows],
        compiler_params=grant(8),
        name="edges",
    )(place, low, inner, outer, pg, before)


def backward(place, low, inner, outer, act, slope, cot, later, turned, sort):
    frames, _, count, chan = act.shape
    ext = (frames + 2,) + act.shape[1:]
    return pl.pallas_call(
        backward_kernel,
        in_specs=[SCALAR] + [FULL] * 9,
        out_specs=[FULL] * 4,
        out_shape=[like(act.shape, jnp.bfloat16), like(ext, jnp.bfloat16), like((12, chan // 2, chan), jnp.float32),
                   like((frames, count, chan), jnp.float32)],
        compiler_params=grant(24),
        cost_estimate=cost(15, 10),
        name="backward",
    )(place, low, inner, outer, act, slope, cot, later, turned, sort)


def half_grads(place, low, inner, outer, act, pg, ext):
    chan = low.shape[-1]
    return pl.pallas_call(
        half_sums,
        in_specs=[SCALAR] + [FULL] * 6,
        out_specs=FULL,
        out_shape=like((12, chan // 2, chan), jnp.float32),
        compiler_params=grant(20),
        cost_estimate=cost(10, 6),
        name="half_grads",
    )(place, low, inner, outer, act, pg, ext)


HBM = pl.BlockSpec(memory_space=pltpu.HBM)


def split(value):
    high = value.astype(jnp.bfloat16)
    return high, (value - high.astype(jnp.float32)).astype(jnp.bfloat16)


def column_pair(first, second, j, at, last):
    if j == 0:
        return second + from_right(first, at, last)
    if j == 1:
        return first + second
    return first + from_left(second, at)


def input_kernel(pg_ref, box_ref, ws_ref, _, out_ref):
    frames, _, count, chan = pg_ref.shape
    cols_low = out_ref.shape[2]
    rows_low = count // cols_low
    at = column(count, cols_low, chan)
    turned = jnp.concatenate([ws_ref[i, j].T for j in range(3) for i in range(3)], axis=0)
    for frame in range(frames):
        own = [pg_ref[frame, side].astype(jnp.float32) for side in range(4)]
        zero = jnp.zeros((1, cols_low, chan), jnp.float32)
        parts = []
        for j in range(3):
            even = column_pair(own[0], own[1], j, at, cols_low - 1).reshape(rows_low, cols_low, chan)
            odd = column_pair(own[2], own[3], j, at, cols_low - 1).reshape(rows_low, cols_low, chan)
            below = jnp.concatenate([even[1:], zero], axis=0)
            above = jnp.concatenate([zero, odd[:-1]], axis=0)
            for value in (odd + below, even + odd, above + even):
                parts.append(jnp.concatenate(split(value.reshape(count, chan)), axis=0))
        sums = product(jnp.concatenate(parts, axis=1), turned)
        total = box_ref[frame] + (sums[:count] + sums[count:])
        out_ref[frame] = total.reshape(rows_low, cols_low, chan)


def input_own(pg, box, ws, before, low_shape):
    return pl.pallas_call(
        input_kernel,
        in_specs=[FULL] * 3 + [UNREAD],
        out_specs=FULL,
        out_shape=like(low_shape, jnp.float32),
        compiler_params=grant(16),
        cost_estimate=cost(6, 4),
        name="input_own",
    )(pg, box, ws, before)


def finish_kernel(place_ref, own_ref, inner_hbm, outer_hbm, ws_hbm, edge_hbm, act_hbm, wt_hbm, sort_hbm, low_hbm, _,
                  section_ref, input_ref, token_ref,
                  inner_ref, outer_ref, ws_ref, edge_ref, act_ref, wt_ref, wide_ref, low_ref, earlier, held, input_held, sems):
    frames, rows_low, cols_low, chan = low_ref.shape
    group = rows_at_once(rows_low, cols_low)
    span, count = group * cols_low, rows_low * cols_low
    pairs = [(inner_hbm, inner_ref), (outer_hbm, outer_ref)]
    pairs += [(ws_hbm.at[i, j], ws_ref.at[i, j]) for i in (2, 0, 1) for j in range(3)]
    pairs += [(edge_hbm, edge_ref), (wt_hbm, wt_ref)]
    pairs += [(act_hbm.at[n], act_ref.at[n]) for n in range(frames)] + [(sort_hbm, wide_ref), (low_hbm, low_ref)]
    copies = [pltpu.make_async_copy(a, b, sems.at[n]) for n, (a, b) in enumerate(pairs)]
    for copy in copies:
        copy.start()
    token_ref[...] = jnp.zeros_like(token_ref)

    for copy in copies[:8]:
        copy.wait()
    odd_place = place_ref[1] == 1
    flat = (frames * cols_low, chan)
    at = column(flat[0], cols_low, chan)
    inner = [inner_ref[:, b].reshape(flat).astype(jnp.float32) for b in range(2)]
    outer = [outer_ref[:, b].reshape(flat).astype(jnp.float32) for b in range(2)]
    above = [jnp.where(odd_place, inner[b], outer[b]) for b in range(2)]
    below = [jnp.where(odd_place, outer[b], inner[b]) for b in range(2)]
    terms = []
    for (first, second), i in ((above, 2), (below, 0)):
        total = jnp.zeros(flat, jnp.float32)
        for j in range(3):
            parts = jnp.concatenate(split(column_pair(first, second, j, at, cols_low - 1)), axis=0)
            sums = product_nt(parts, ws_ref[i, j])
            total = total + (sums[: flat[0]] + sums[flat[0] :])
        terms.append(total.reshape(frames, cols_low, chan))
    for row in range(rows_low):
        value = own_ref[:, row]
        if row == 0:
            value = value + terms[0]
        if row == rows_low - 1:
            value = value + terms[1]
        input_held[:, row] = value.astype(jnp.bfloat16)
    leaving = [pltpu.make_async_copy(input_held, input_ref, sems.at[len(copies)])]
    leaving[0].start()

    for copy in copies[8:12]:
        copy.wait()
    for frame in range(2):
        for side, pre in enumerate(spatial(edge_ref[frame], ws_ref)):
            earlier[frame, side] = (pre * jax.nn.sigmoid(pre)).astype(jnp.bfloat16)
    for copy in copies[12:]:
        copy.wait()
    merge = wide_ref[...].T.astype(jnp.bfloat16)
    wt = wt_ref[...].reshape(3 * chan, chan)
    for frame in range(frames):
        acts = [act_ref[frame - k] if frame >= k else earlier[frame - k + 2] for k in range(3)]
        acts = jnp.concatenate([act.reshape(4 * count, chan) for act in acts], axis=1)
        low = low_ref[frame].reshape(1, count, chan).astype(jnp.float32)
        mixed = (product(acts, wt).reshape(4, count, chan) + low).astype(jnp.bfloat16)
        for n in range(rows_low // group):
            block = mixed[:, n * span : (n + 1) * span].reshape(4 * span, chan)
            block = product(merge, block).astype(jnp.bfloat16)
            held[frame, 2 * group * n : 2 * group * (n + 1)] = block.reshape(2 * group, 2 * cols_low, chan)
        leaving.append(pltpu.make_async_copy(held.at[frame], section_ref.at[frame], sems.at[len(copies) + 1 + frame]))
        leaving[-1].start()
    for copy in leaving:
        copy.wait()


def finish(place, own, inner, outer, ws, edge, act, wt, sort, low, before):
    frames, rows_low, cols_low, chan = low.shape
    out = (frames, 2 * rows_low, 2 * cols_low, chan)
    fetched = [inner, outer, ws, edge, act, wt, sort, low]
    return pl.pallas_call(
        finish_kernel,
        in_specs=[SCALAR, FULL] + [HBM] * 8 + [UNREAD],
        out_specs=[HBM, HBM, FULL],
        out_shape=[like(out, jnp.bfloat16), like(low.shape, jnp.bfloat16), TOKEN],
        scratch_shapes=[pltpu.VMEM(a.shape, a.dtype) for a in fetched]
        + [pltpu.VMEM((2,) + act.shape[1:], act.dtype), pltpu.VMEM(out, jnp.bfloat16),
           pltpu.VMEM(low.shape, jnp.bfloat16), pltpu.SemaphoreType.DMA((16 + 2 * frames,))],
        compiler_params=grant(16),
        cost_estimate=cost(8, 4),
        name="finish",
    )(place, own, inner, outer, in_hbm(ws), edge, *[in_hbm(a) for a in (act, wt, sort, low)], before)


def put_kernel(place_ref, half_ref, *refs):
    spatial_ref, temporal_ref, wide, sems = refs[-4:]
    taps, half, _ = half_ref.shape
    to = pl.ds(pl.multiple_of(place_ref[0] * half, half), half)
    copies = []
    for tap in range(taps):
        wide[tap] = half_ref[tap].astype(jnp.float32)
        if tap < 9:
            target = spatial_ref.at[tap // 3, tap % 3, to]
        else:
            target = temporal_ref.at[tap - 9, to]
        copies.append(pltpu.make_async_copy(wide.at[tap], target, sems.at[tap]))
        copies[-1].start()
    for copy in copies:
        copy.wait()


def put(place, half, *done):
    chan = half.shape[-1]
    return pl.pallas_call(
        put_kernel,
        in_specs=[SCALAR, FULL] + [HBM] * len(done),
        out_specs=[HBM, HBM],
        out_shape=[like((3, 3, chan, chan), jnp.float32), like((3, chan, chan), jnp.float32)],
        input_output_aliases={2 + n: n for n in range(len(done))},
        scratch_shapes=[pltpu.VMEM((12, chan // 2, chan), jnp.float32), pltpu.SemaphoreType.DMA((12,))],
        compiler_params=grant(6),
        name="put",
    )(place, half, *done)


def add_kernel(mine_ref, theirs_ref, out_ref):
    out_ref[...] = (mine_ref[...] + theirs_ref[...]).astype(jnp.bfloat16)


def add_halves(mine, theirs):
    full = pl.BlockSpec(memory_space=pltpu.VMEM)
    return pl.pallas_call(
        add_kernel,
        in_specs=[full, full],
        out_specs=full,
        out_shape=like(mine.shape, jnp.bfloat16),
        compiler_params=grant(8),
        name="add_halves",
    )(mine, theirs)


def sum_kernel(got_ref, _, out_ref):
    total = got_ref[0].astype(jnp.float32)
    for n in range(1, got_ref.shape[0]):
        total = total + got_ref[n].astype(jnp.float32)
    out_ref[...] = total.astype(jnp.bfloat16)


def sum_parts(got, before):
    return pl.pallas_call(
        sum_kernel,
        in_specs=[FULL, UNREAD],
        out_specs=FULL,
        out_shape=like(got.shape[1:], jnp.bfloat16),
        compiler_params=grant(4),
        name="sum_parts",
    )(got, before)


def spread_kernel(own_ref, theirs_ref, *refs):
    total = (own_ref[...].astype(jnp.float32) + theirs_ref[...].astype(jnp.float32)).astype(jnp.bfloat16)
    for n in range(refs[-1].shape[0]):
        refs[-1][n] = total


def spread(own, theirs, parts, *before):
    return pl.pallas_call(
        spread_kernel,
        in_specs=[FULL, FULL] + [UNREAD] * len(before),
        out_specs=FULL,
        out_shape=like((parts,) + own.shape, jnp.bfloat16),
        compiler_params=grant(4),
        name="spread",
    )(own, theirs, *before)


def on_device(bits, low_frames, spatial_weight, temporal_weight, cotangent):
    low, cot = low_frames[0], cotangent[0]
    frames, rows_low, cols_low, chan = low.shape
    core = lax.axis_index(bits.core).astype(jnp.int32)
    odd = lax.axis_index(bits.axes["height"][-1]).astype(jnp.int32)
    mine, other = jnp.stack([core, odd]), jnp.stack([1 - core, odd])
    parts = 1 << len(bits.near)

    inner, outer, later = first_messages(mine, low, cot)
    later = bits.shift(later, "tm", -1)
    inner, outer = bits.pairs(inner, outer)
    order = jnp.asarray(side_order(rows_low, cols_low))
    low_in, ws, sort, turned, cot_side = load(low, cot, spatial_weight, temporal_weight, order)
    act, slope = forward(mine, low_in, inner, outer, ws)
    pg, ext, theirs, box = backward(
        other, low_in, inner, outer, act, slope, cot_side, later, turned, sort
    )
    theirs = bits.swap(theirs, bits.core)
    own = half_grads(mine, low_in, inner, outer, act, pg, ext)
    kept = add_halves(own, theirs)
    got = bits.exchange(kept.reshape(parts, -1, chan))
    edge, pg_inner, pg_outer = edges(mine, low_in, inner, outer, pg, kept)
    edge = bits.shift(edge, "tm", 1)
    pg_inner, pg_outer = bits.pairs(pg_inner, pg_outer)
    own_part = input_own(pg, box, ws, kept, low.shape)
    total, far = bits.far_sums(sum_parts(got, own_part))
    section_out, input_grad, done = finish(
        mine, own_part, pg_inner, pg_outer, spatial_weight, edge, act, temporal_weight, order, low, total
    )
    totals = spread(total, far, parts, done)
    half = bits.exchange(totals).reshape(kept.shape)
    theirs = bits.swap(half, bits.core)
    spatial_grad, temporal_grad = put(other, theirs, *put(mine, half))
    return section_out[None], input_grad[None], spatial_grad, temporal_grad


def solution(mesh):
    bits = Bits(mesh)
    block = P(*(bits.axes[name] for name in ("dp", "tm", "height")), None, None)
    return jax.shard_map(
        functools.partial(on_device, bits),
        mesh=bits.mesh,
        in_specs=(block, P(), P(), block),
        out_specs=(block, block, P(), P()),
        check_vma=False,
    )
```

```python
import functools

import jax
import jax.numpy as jnp
import numpy as np
from jax import lax
from jax.experimental import pallas as pl
from jax.experimental.pallas import tpu as pltpu
from jax.sharding import Mesh
from jax.sharding import PartitionSpec as P


class Bits:
    def __init__(self, mesh):
        self.axes = {}
        for name in mesh.axis_names:
            count = mesh.shape[name].bit_length() - 1
            self.axes[name] = tuple(f"{name}{bit}" for bit in reversed(range(count)))
        names = [bit for bits in self.axes.values() for bit in bits]
        self.mesh = Mesh(mesh.devices.reshape([2] * len(names)), tuple(names))
        self.core = next((n for n in names if self.same_chip(n)), self.axes["tm"][-1])
        others = [[b for b in reversed(bits) if b != self.core] for bits in self.axes.values()]
        turns = [bits[turn] for turn in range(len(names)) for bits in others if turn < len(bits)]
        self.near = [n for n in names if n in turns[:3]]
        self.far = turns[3:]

    def same_chip(self, name):
        at = [1 if n == name else 0 for n in self.mesh.axis_names]
        here = self.mesh.devices[tuple([0] * len(at))]
        there = self.mesh.devices[tuple(at)]
        return tuple(getattr(here, "coords", (0,))) == tuple(getattr(there, "coords", (1,)))

    def swap(self, block, axis):
        return lax.ppermute(block, axis, [(0, 1), (1, 0)])

    def shift(self, block, name, distance):
        axes = self.axes[name]
        devices = range(1 << len(axes))
        route = [(i - distance, i) for i in devices if i - distance in devices]
        return lax.ppermute(block, axes, route)

    def exchange(self, parts):
        return lax.all_to_all(parts, tuple(self.near), 0, 0, tiled=True)

    def pairs(self, inner, outer, inner_made_first=False):
        axes = self.axes["height"]
        low = range(1, (1 << len(axes)) - 1, 2)
        route = [(i, i + 1) for i in low] + [(i + 1, i) for i in low]
        if inner_made_first:
            inner = self.swap(inner, axes[-1])
            return inner, lax.ppermute(outer, axes, route)
        outer = lax.ppermute(outer, axes, route)
        return self.swap(inner, axes[-1]), outer

    def far_sums(self, total):
        for axis in self.far[:-1]:
            total = total.astype(jnp.float32) + self.swap(total, axis).astype(jnp.float32)
            total = lax.reduce_precision(total, 8, 7).astype(jnp.bfloat16)
        return total, self.swap(total, self.far[-1])


SIDES = ((0, 0), (0, 1), (1, 0), (1, 1))


def grant(mib):
    return pltpu.CompilerParams(vmem_limit_bytes=mib * 2**20)


def product(left, right):
    return jnp.dot(left, right, preferred_element_type=jnp.float32)


def product_nt(left, right):
    return lax.dot_general(left, right, (((1,), (1,)), ((), ())), preferred_element_type=jnp.float32)


def rows_at_once(rows_low, cols_low):
    return max(n for n in (1, 2, 4, 8) if rows_low % n == 0 and (n == 1 or 4 * n * cols_low <= 256))


def side_order(rows_low, cols_low):
    count = rows_at_once(rows_low, cols_low)
    size = 4 * count * cols_low
    at = np.arange(size).reshape(count, 2, cols_low, 2).transpose(1, 3, 0, 2).reshape(-1)
    return (at[:, None] == np.arange(size)[None, :]).astype(np.float32)


def column(rows, cols_low, chan):
    return lax.broadcasted_iota(jnp.int32, (rows // cols_low, cols_low, chan), 1).reshape(rows, chan)


def from_left(x, at):
    return jnp.where(at == 0, 0.0, pltpu.roll(x, 1, 0))


def from_right(x, at, last):
    return jnp.where(at == last, 0.0, pltpu.roll(x, x.shape[0] - 1, 0))


def sort_columns(source, target, cols_low, order):
    rows_low, chan = source.shape[0] // 2, source.shape[2]
    group = rows_at_once(rows_low, cols_low)
    span = group * cols_low
    for n in range(rows_low // group):
        block = source[2 * group * n : 2 * group * (n + 1)].reshape(4 * span, chan)
        block = product(order, block).astype(jnp.bfloat16).reshape(4, span, chan)
        target[:, n * span : (n + 1) * span, :] = block


def tall(place_ref, low_ref, inner_ref, outer_ref, frame, lanes=slice(None)):
    odd = place_ref[1] == 1
    inner, outer = inner_ref[frame, :, :, lanes], outer_ref[frame, :, :, lanes]
    up, down = jnp.where(odd, inner, outer), jnp.where(odd, outer, inner)
    return jnp.concatenate([up, low_ref[frame, :, :, lanes], down], axis=0)


def spatial(low, ws_ref):
    rows_low, cols_low, chan = low.shape[0] - 2, low.shape[1], low.shape[2]
    count = rows_low * cols_low
    flat = low.reshape(-1, chan)
    rows = [[], []]
    for j in range(3):
        taps = [product(flat, ws_ref[i, j]).reshape(low.shape) for i in range(3)]
        even = taps[0][:rows_low] + (taps[1] + taps[2])[1 : rows_low + 1]
        odd = (taps[0] + taps[1])[1 : rows_low + 1] + taps[2][2:]
        rows[0].append(even.reshape(count, chan))
        rows[1].append(odd.reshape(count, chan))
    at = column(count, cols_low, chan)
    for first, second, third in rows:
        yield from_left(first, at) + (second + third)
        yield (first + second) + from_right(third, at, cols_low - 1)


def forward_kernel(place_ref, low_ref, inner_ref, outer_ref, ws_ref, act_ref, slope_ref):
    for frame in range(low_ref.shape[0]):
        low = tall(place_ref, low_ref, inner_ref, outer_ref, frame)
        for side, pre in enumerate(spatial(low, ws_ref)):
            sig = jax.nn.sigmoid(pre)
            act_ref[frame, side] = (pre * sig).astype(jnp.bfloat16)
            slope_ref[frame, side] = sig * (1.0 + pre * (1.0 - sig))


def half_sums(place_ref, low_ref, inner_ref, outer_ref, act_ref, pg_ref, ext_ref, out_ref):
    frames, rows_low, cols_low, chan = low_ref.shape
    count, half = rows_low * cols_low, chan // 2
    lanes = pl.ds(pl.multiple_of(place_ref[0] * half, half), half)
    lefts = [[] for _ in range(9)]
    acts = []
    at = column((rows_low + 2) * cols_low, cols_low, half)
    for frame in range(frames):
        low = tall(place_ref, low_ref, inner_ref, outer_ref, frame, lanes)
        wide = low.reshape(-1, half).astype(jnp.float32)
        moved = [from_left(wide, at), wide, from_right(wide, at, cols_low - 1)]
        turned = {}
        for dc in range(3):
            view = moved[dc].astype(jnp.bfloat16).reshape(low.shape)
            for dr in range(3):
                turned[dr - 1, dc - 1] = view[dr : dr + rows_low].reshape(count, half).T
        for i in range(3):
            for j in range(3):
                lefts[3 * i + j] += [turned[(a + i - 1) // 2, (b + j - 1) // 2] for a, b in SIDES]
        acts.append(act_ref[frame, :, :, lanes].reshape(4 * count, half).T)
    pg = pg_ref[...].reshape(frames * 4 * count, chan)
    left = jnp.concatenate([jnp.concatenate(left, axis=1) for left in lefts], axis=0)
    out_ref[:9] = product(left, pg).reshape(9, half, chan)
    act = jnp.concatenate(acts, axis=1)
    for k in range(3):
        out_ref[9 + k] = product(act, ext_ref[k : k + frames].reshape(frames * 4 * count, chan))


def half_kernel(place_ref, low_ref, inner_ref, outer_ref, act_ref, pg_ref, ext_ref, out_ref, act_out, sem):
    copy = pltpu.make_async_copy(act_ref, act_out, sem)
    copy.start()
    half_sums(place_ref, low_ref, inner_ref, outer_ref, act_ref, pg_ref, ext_ref, out_ref)
    copy.wait()


def backward_kernel(place_ref, low_ref, inner_ref, outer_ref, act_ref, slope_ref, cot_ref, later_ref, turned_ref, sort_ref,
                    pg_ref, ext_ref, out_ref, box_ref):
    frames, _, count, chan = cot_ref.shape
    ext_ref[:frames] = cot_ref[...]
    for n in range(2):
        sort_columns(later_ref.at[n], ext_ref.at[frames + n], low_ref.shape[2], sort_ref[...])
    for frame in range(frames):
        cots = [ext_ref[frame + k].reshape(4 * count, chan) for k in range(3)]
        act_grad = product(jnp.concatenate(cots, axis=1), turned_ref[...])
        slope = slope_ref[frame].reshape(4 * count, chan)
        pg_ref[frame] = (act_grad * slope).astype(jnp.bfloat16).reshape(4, count, chan)
        box_ref[frame] = sum(cot_ref[frame, side].astype(jnp.float32) for side in range(4))
    half_sums(place_ref, low_ref, inner_ref, outer_ref, act_ref, pg_ref, ext_ref, out_ref)


SCALAR = pl.BlockSpec(memory_space=pltpu.SMEM)
UNREAD = pl.BlockSpec(memory_space=pl.ANY)


def like(shape, dtype):
    return jax.ShapeDtypeStruct(shape, dtype)


TOKEN = like((8, 128), jnp.float32)


def cost(units, mib):
    return pl.CostEstimate(flops=units * 2 * 2048 * 256 * 256, bytes_accessed=mib * 2**20, transcendentals=0)


def in_hbm(array):
    return pltpu.with_memory_space_constraint(array, pltpu.HBM)


FULL = pl.BlockSpec(memory_space=pltpu.VMEM)


def first_kernel(place_ref, low_ref, cot_ref, inner_ref, outer_ref, later_ref, sems):
    last = low_ref.shape[1] - 1
    odd = place_ref[1]
    copies = [
        (low_ref.at[:, pl.ds(last * (1 - odd), 1)], inner_ref),
        (low_ref.at[:, pl.ds(last * odd, 1)], outer_ref),
    ]
    copies += [(cot_ref.at[n, r], later_ref.at[n, r]) for n in range(2) for r in range(cot_ref.shape[1])]
    copies = [pltpu.make_async_copy(a, b, sems.at[n]) for n, (a, b) in enumerate(copies)]
    for copy in copies:
        copy.start()
    for copy in copies:
        copy.wait()


def first_messages(place, low, cot):
    row = like(low[:, :1].shape, low.dtype)
    return pl.pallas_call(
        first_kernel,
        in_specs=[SCALAR, UNREAD, UNREAD],
        out_specs=[FULL] * 3,
        out_shape=[row, row, like(cot[:2].shape, cot.dtype)],
        scratch_shapes=[pltpu.SemaphoreType.DMA((2 + 2 * cot.shape[1],))],
        compiler_params=grant(4),
        name="first_messages",
    )(place, in_hbm(low), in_hbm(cot))


def load_kernel(low_hbm, cot_hbm, ws_hbm, wt_hbm, sort_hbm,
                low_ref, ws_ref, sort_ref, turned_ref, side_ref, cot_ref, wide_ref, wt_ref, sems):
    frames, cols_low, chan = low_ref.shape[0], low_ref.shape[2], low_ref.shape[3]
    pairs = [(sort_hbm, wide_ref)] + [(cot_hbm.at[n], cot_ref.at[n]) for n in range(frames)]
    pairs += [(wt_hbm.at[k], wt_ref.at[k]) for k in range(3)] + [(low_hbm, low_ref)]
    pairs += [(ws_hbm.at[i, j], ws_ref.at[i, j]) for i in range(3) for j in range(3)]
    copies = [pltpu.make_async_copy(a, b, sems.at[n]) for n, (a, b) in enumerate(pairs)]
    for copy in copies:
        copy.start()
    copies[0].wait()
    sort_ref[...] = wide_ref[...].astype(jnp.bfloat16)
    for n in range(frames):
        copies[1 + n].wait()
        sort_columns(cot_ref.at[n], side_ref.at[n], cols_low, sort_ref[...])
    for k in range(3):
        copies[1 + frames + k].wait()
        turned_ref[k * chan : (k + 1) * chan] = wt_ref[k].T
    for copy in copies[4 + frames :]:
        copy.wait()


def load(low, cot, ws, wt, sort):
    frames, rows_low, cols_low, chan = low.shape
    order = like(sort.shape, jnp.bfloat16)
    shapes = [low, ws, order, like((3 * chan, chan), wt.dtype),
              like((frames, 4, rows_low * cols_low, chan), jnp.bfloat16)]
    return pl.pallas_call(
        load_kernel,
        in_specs=[UNREAD] * 5,
        out_specs=[FULL] * 5,
        out_shape=[like(a.shape, a.dtype) for a in shapes],
        scratch_shapes=[pltpu.VMEM(cot.shape, cot.dtype), pltpu.VMEM(sort.shape, sort.dtype), pltpu.VMEM(wt.shape, wt.dtype),
                        pltpu.SemaphoreType.DMA((frames + 14,))],
        compiler_params=grant(14),
        cost_estimate=cost(2, 4),
        name="load",
    )(*[in_hbm(a) for a in (low, cot, ws, wt, sort)])


def forward(place, low, inner, outer, ws):
    frames, rows_low, cols_low, chan = low.shape
    side = (frames, 4, rows_low * cols_low, chan)
    return pl.pallas_call(
        forward_kernel,
        in_specs=[SCALAR] + [FULL] * 4,
        out_specs=[FULL] * 2,
        out_shape=[like(side, jnp.bfloat16), like(side, jnp.float32)],
        compiler_params=grant(20),
        cost_estimate=cost(10, 8),
        name="forward",
    )(place, low, inner, outer, ws)


def edges_kernel(place_ref, low_ref, inner_ref, outer_ref, pg_ref, _, tall_ref, pg_inner, pg_outer):
    cols_low = low_ref.shape[2]
    first = low_ref.shape[0] - tall_ref.shape[0]
    for n in range(tall_ref.shape[0]):
        tall_ref[n] = tall(place_ref, low_ref, inner_ref, outer_ref, first + n)
    odd = place_ref[1] == 1
    top, bottom = pg_ref[:, :2, :cols_low, :], pg_ref[:, 2:, -cols_low:, :]
    pg_inner[...] = jnp.where(odd, top, bottom)
    pg_outer[...] = jnp.where(odd, bottom, top)


def edges(place, low, inner, outer, pg, before):
    frames, rows_low, cols_low, chan = low.shape
    full = pl.BlockSpec(memory_space=pltpu.VMEM)
    rows = like((frames, 2, cols_low, chan), jnp.bfloat16)
    return pl.pallas_call(
        edges_kernel,
        in_specs=[SCALAR, full, full, full, full, UNREAD],
        out_specs=[full] * 3,
        out_shape=[like((2, rows_low + 2, cols_low, chan), jnp.bfloat16), rows, rows],
        compiler_params=grant(8),
        name="edges",
    )(place, low, inner, outer, pg, before)


def backward(place, low, inner, outer, act, slope, cot, later, turned, sort):
    frames, _, count, chan = act.shape
    ext = (frames + 2,) + act.shape[1:]
    return pl.pallas_call(
        backward_kernel,
        in_specs=[SCALAR] + [FULL] * 9,
        out_specs=[FULL] * 4,
        out_shape=[like(act.shape, jnp.bfloat16), like(ext, jnp.bfloat16), like((12, chan // 2, chan), jnp.float32),
                   like((frames, count, chan), jnp.float32)],
        compiler_params=grant(24),
        cost_estimate=cost(15, 10),
        name="backward",
    )(place, low, inner, outer, act, slope, cot, later, turned, sort)


def half_grads(place, low, inner, outer, act, pg, ext):
    chan = low.shape[-1]
    return pl.pallas_call(
        half_kernel,
        in_specs=[SCALAR] + [FULL] * 6,
        out_specs=[FULL, HBM],
        out_shape=[like((12, chan // 2, chan), jnp.float32), like(act.shape, act.dtype)],
        scratch_shapes=[pltpu.SemaphoreType.DMA],
        compiler_params=grant(20),
        cost_estimate=cost(10, 6),
        name="half_grads",
    )(place, low, inner, outer, act, pg, ext)


HBM = pl.BlockSpec(memory_space=pltpu.HBM)


def split(value):
    high = value.astype(jnp.bfloat16)
    return high, (value - high.astype(jnp.float32)).astype(jnp.bfloat16)


def column_pair(first, second, j, at, last):
    if j == 0:
        return second + from_right(first, at, last)
    if j == 1:
        return first + second
    return first + from_left(second, at)


def input_kernel(pg_ref, box_ref, ws_ref, _, out_ref):
    frames, _, count, chan = pg_ref.shape
    cols_low = out_ref.shape[2]
    rows_low = count // cols_low
    at = column(count, cols_low, chan)
    turned = jnp.concatenate([ws_ref[i, j].T for j in range(3) for i in range(3)], axis=0)
    for frame in range(frames):
        own = [pg_ref[frame, side].astype(jnp.float32) for side in range(4)]
        zero = jnp.zeros((1, cols_low, chan), jnp.float32)
        parts = []
        for j in range(3):
            even = column_pair(own[0], own[1], j, at, cols_low - 1).reshape(rows_low, cols_low, chan)
            odd = column_pair(own[2], own[3], j, at, cols_low - 1).reshape(rows_low, cols_low, chan)
            below = jnp.concatenate([even[1:], zero], axis=0)
            above = jnp.concatenate([zero, odd[:-1]], axis=0)
            for value in (odd + below, even + odd, above + even):
                parts.append(jnp.concatenate(split(value.reshape(count, chan)), axis=0))
        sums = product(jnp.concatenate(parts, axis=1), turned)
        total = box_ref[frame] + (sums[:count] + sums[count:])
        out_ref[frame] = total.reshape(rows_low, cols_low, chan)


def input_own(pg, box, ws, before, low_shape):
    return pl.pallas_call(
        input_kernel,
        in_specs=[FULL] * 3 + [UNREAD],
        out_specs=FULL,
        out_shape=like(low_shape, jnp.float32),
        compiler_params=grant(16),
        cost_estimate=cost(6, 4),
        name="input_own",
    )(pg, box, ws, before)


def finish_kernel(place_ref, own_ref, inner_hbm, outer_hbm, ws_hbm, edge_hbm, act_hbm, wt_hbm, sort_hbm, low_hbm, _,
                  section_ref, input_ref, token_ref,
                  inner_ref, outer_ref, ws_ref, edge_ref, act_ref, wt_ref, wide_ref, low_ref, earlier, held, input_held, sems):
    frames, rows_low, cols_low, chan = low_ref.shape
    group = rows_at_once(rows_low, cols_low)
    span, count = group * cols_low, rows_low * cols_low
    pairs = [(inner_hbm, inner_ref), (outer_hbm, outer_ref)]
    pairs += [(ws_hbm.at[i, j], ws_ref.at[i, j]) for i in (2, 0, 1) for j in range(3)]
    pairs += [(edge_hbm, edge_ref), (wt_hbm, wt_ref)]
    pairs += [(act_hbm.at[n], act_ref.at[n]) for n in range(frames)] + [(sort_hbm, wide_ref), (low_hbm, low_ref)]
    copies = [pltpu.make_async_copy(a, b, sems.at[n]) for n, (a, b) in enumerate(pairs)]
    for copy in copies:
        copy.start()
    token_ref[...] = jnp.zeros_like(token_ref)

    for copy in copies[:8]:
        copy.wait()
    odd_place = place_ref[1] == 1
    flat = (frames * cols_low, chan)
    at = column(flat[0], cols_low, chan)
    inner = [inner_ref[:, b].reshape(flat).astype(jnp.float32) for b in range(2)]
    outer = [outer_ref[:, b].reshape(flat).astype(jnp.float32) for b in range(2)]
    above = [jnp.where(odd_place, inner[b], outer[b]) for b in range(2)]
    below = [jnp.where(odd_place, outer[b], inner[b]) for b in range(2)]
    terms = []
    for (first, second), i in ((above, 2), (below, 0)):
        total = jnp.zeros(flat, jnp.float32)
        for j in range(3):
            parts = jnp.concatenate(split(column_pair(first, second, j, at, cols_low - 1)), axis=0)
            sums = product_nt(parts, ws_ref[i, j])
            total = total + (sums[: flat[0]] + sums[flat[0] :])
        terms.append(total.reshape(frames, cols_low, chan))
    for row in range(rows_low):
        value = own_ref[:, row]
        if row == 0:
            value = value + terms[0]
        if row == rows_low - 1:
            value = value + terms[1]
        input_held[:, row] = value.astype(jnp.bfloat16)
    leaving = [pltpu.make_async_copy(input_held, input_ref, sems.at[len(copies)])]
    leaving[0].start()

    for copy in copies[8:12]:
        copy.wait()
    for frame in range(2):
        for side, pre in enumerate(spatial(edge_ref[frame], ws_ref)):
            earlier[frame, side] = (pre * jax.nn.sigmoid(pre)).astype(jnp.bfloat16)
    for copy in copies[12:]:
        copy.wait()
    merge = wide_ref[...].T.astype(jnp.bfloat16)
    wt = wt_ref[...].reshape(3 * chan, chan)
    for frame in range(frames):
        acts = [act_ref[frame - k] if frame >= k else earlier[frame - k + 2] for k in range(3)]
        acts = jnp.concatenate([act.reshape(4 * count, chan) for act in acts], axis=1)
        low = low_ref[frame].reshape(1, count, chan).astype(jnp.float32)
        mixed = (product(acts, wt).reshape(4, count, chan) + low).astype(jnp.bfloat16)
        for n in range(rows_low // group):
            block = mixed[:, n * span : (n + 1) * span].reshape(4 * span, chan)
            block = product(merge, block).astype(jnp.bfloat16)
            held[frame, 2 * group * n : 2 * group * (n + 1)] = block.reshape(2 * group, 2 * cols_low, chan)
        leaving.append(pltpu.make_async_copy(held.at[frame], section_ref.at[frame], sems.at[len(copies) + 1 + frame]))
        leaving[-1].start()
    for copy in leaving:
        copy.wait()


def finish(place, own, inner, outer, ws, edge, act, wt, sort, low, before):
    frames, rows_low, cols_low, chan = low.shape
    out = (frames, 2 * rows_low, 2 * cols_low, chan)
    fetched = [inner, outer, ws, edge, act, wt, sort, low]
    return pl.pallas_call(
        finish_kernel,
        in_specs=[SCALAR, FULL] + [HBM] * 8 + [UNREAD],
        out_specs=[HBM, HBM, FULL],
        out_shape=[like(out, jnp.bfloat16), like(low.shape, jnp.bfloat16), TOKEN],
        scratch_shapes=[pltpu.VMEM(a.shape, a.dtype) for a in fetched]
        + [pltpu.VMEM((2,) + act.shape[1:], act.dtype), pltpu.VMEM(out, jnp.bfloat16),
           pltpu.VMEM(low.shape, jnp.bfloat16), pltpu.SemaphoreType.DMA((16 + 2 * frames,))],
        compiler_params=grant(16),
        cost_estimate=cost(8, 4),
        name="finish",
    )(place, own, inner, outer, in_hbm(ws), edge, *[in_hbm(a) for a in (act, wt, sort, low)], before)


def put_kernel(place_ref, half_ref, *refs):
    spatial_ref, temporal_ref, wide, sems = refs[-4:]
    taps, half, _ = half_ref.shape
    to = pl.ds(pl.multiple_of(place_ref[0] * half, half), half)
    copies = []
    for tap in range(taps):
        wide[tap] = half_ref[tap].astype(jnp.float32)
        if tap < 9:
            target = spatial_ref.at[tap // 3, tap % 3, to]
        else:
            target = temporal_ref.at[tap - 9, to]
        copies.append(pltpu.make_async_copy(wide.at[tap], target, sems.at[tap]))
        copies[-1].start()
    for copy in copies:
        copy.wait()


def put(place, half, *done):
    chan = half.shape[-1]
    return pl.pallas_call(
        put_kernel,
        in_specs=[SCALAR, FULL] + [HBM] * len(done),
        out_specs=[HBM, HBM],
        out_shape=[like((3, 3, chan, chan), jnp.float32), like((3, chan, chan), jnp.float32)],
        input_output_aliases={2 + n: n for n in range(len(done))},
        scratch_shapes=[pltpu.VMEM((12, chan // 2, chan), jnp.float32), pltpu.SemaphoreType.DMA((12,))],
        compiler_params=grant(6),
        name="put",
    )(place, half, *done)


def add_kernel(mine_ref, theirs_ref, out_ref):
    out_ref[...] = (mine_ref[...] + theirs_ref[...]).astype(jnp.bfloat16)


def add_halves(mine, theirs):
    full = pl.BlockSpec(memory_space=pltpu.VMEM)
    return pl.pallas_call(
        add_kernel,
        in_specs=[full, full],
        out_specs=full,
        out_shape=like(mine.shape, jnp.bfloat16),
        compiler_params=grant(8),
        name="add_halves",
    )(mine, theirs)


def sum_kernel(got_ref, _, out_ref):
    total = got_ref[0].astype(jnp.float32)
    for n in range(1, got_ref.shape[0]):
        total = total + got_ref[n].astype(jnp.float32)
    out_ref[...] = total.astype(jnp.bfloat16)


def sum_parts(got, before):
    return pl.pallas_call(
        sum_kernel,
        in_specs=[FULL, UNREAD],
        out_specs=FULL,
        out_shape=like(got.shape[1:], jnp.bfloat16),
        compiler_params=grant(4),
        name="sum_parts",
    )(got, before)


def spread_kernel(own_ref, theirs_ref, *refs):
    total = (own_ref[...].astype(jnp.float32) + theirs_ref[...].astype(jnp.float32)).astype(jnp.bfloat16)
    for n in range(refs[-1].shape[0]):
        refs[-1][n] = total


def spread(own, theirs, parts, *before):
    return pl.pallas_call(
        spread_kernel,
        in_specs=[FULL, FULL] + [UNREAD] * len(before),
        out_specs=FULL,
        out_shape=like((parts,) + own.shape, jnp.bfloat16),
        compiler_params=grant(4),
        name="spread",
    )(own, theirs, *before)


def on_device(bits, low_frames, spatial_weight, temporal_weight, cotangent):
    low, cot = low_frames[0], cotangent[0]
    frames, rows_low, cols_low, chan = low.shape
    core = lax.axis_index(bits.core).astype(jnp.int32)
    odd = lax.axis_index(bits.axes["height"][-1]).astype(jnp.int32)
    mine, other = jnp.stack([core, odd]), jnp.stack([1 - core, odd])
    parts = 1 << len(bits.near)

    inner, outer, later = first_messages(mine, low, cot)
    later = bits.shift(later, "tm", -1)
    inner, outer = bits.pairs(inner, outer, True)
    order = jnp.asarray(side_order(rows_low, cols_low))
    low_in, ws, sort, turned, cot_side = load(low, cot, spatial_weight, temporal_weight, order)
    act, slope = forward(mine, low_in, inner, outer, ws)
    pg, ext, theirs, box = backward(
        other, low_in, inner, outer, act, slope, cot_side, later, turned, sort
    )
    theirs = bits.swap(theirs, bits.core)
    own, act = half_grads(mine, low_in, inner, outer, act, pg, ext)
    kept = add_halves(own, theirs)
    got = bits.exchange(kept.reshape(parts, -1, chan))
    edge, pg_inner, pg_outer = edges(mine, low_in, inner, outer, pg, kept)
    edge = bits.shift(edge, "tm", 1)
    pg_inner, pg_outer = bits.pairs(pg_inner, pg_outer)
    own_part = input_own(pg, box, ws, kept, low.shape)
    total, far = bits.far_sums(sum_parts(got, own_part))
    section_out, input_grad, done = finish(
        mine, own_part, pg_inner, pg_outer, spatial_weight, edge, act, temporal_weight, order, low, total
    )
    totals = spread(total, far, parts, done)
    half = bits.exchange(totals).reshape(kept.shape)
    theirs = bits.swap(half, bits.core)
    spatial_grad, temporal_grad = put(other, theirs, *put(mine, half))
    return section_out[None], input_grad[None], spatial_grad, temporal_grad


def solution(mesh):
    bits = Bits(mesh)
    block = P(*(bits.axes[name] for name in ("dp", "tm", "height")), None, None)
    return jax.shard_map(
        functools.partial(on_device, bits),
        mesh=bits.mesh,
        in_specs=(block, P(), P(), block),
        out_specs=(block, block, P(), P()),
        check_vma=False,
    )
```

```python
import functools

import jax
import jax.numpy as jnp
import numpy as np
from jax import lax
from jax.experimental import pallas as pl
from jax.experimental.pallas import tpu as pltpu
from jax.sharding import Mesh
from jax.sharding import PartitionSpec as P


class Bits:
    def __init__(self, mesh):
        self.axes = {}
        for name in mesh.axis_names:
            count = mesh.shape[name].bit_length() - 1
            self.axes[name] = tuple(f"{name}{bit}" for bit in reversed(range(count)))
        names = [bit for bits in self.axes.values() for bit in bits]
        self.mesh = Mesh(mesh.devices.reshape([2] * len(names)), tuple(names))
        self.core = next((n for n in names if self.same_chip(n)), self.axes["tm"][-1])
        others = [[b for b in reversed(bits) if b != self.core] for bits in self.axes.values()]
        turns = [bits[turn] for turn in range(len(names)) for bits in others if turn < len(bits)]
        self.near = [n for n in names if n in turns[:3]]
        self.far = turns[3:]

    def same_chip(self, name):
        at = [1 if n == name else 0 for n in self.mesh.axis_names]
        here = self.mesh.devices[tuple([0] * len(at))]
        there = self.mesh.devices[tuple(at)]
        return tuple(getattr(here, "coords", (0,))) == tuple(getattr(there, "coords", (1,)))

    def swap(self, block, axis):
        return lax.ppermute(block, axis, [(0, 1), (1, 0)])

    def shift(self, block, name, distance):
        axes = self.axes[name]
        devices = range(1 << len(axes))
        route = [(i - distance, i) for i in devices if i - distance in devices]
        return lax.ppermute(block, axes, route)

    def exchange(self, parts):
        return lax.all_to_all(parts, tuple(self.near), 0, 0, tiled=True)

    def pairs(self, inner, outer):
        axes = self.axes["height"]
        low = range(1, (1 << len(axes)) - 1, 2)
        route = [(i, i + 1) for i in low] + [(i + 1, i) for i in low]
        outer = lax.ppermute(outer, axes, route)
        return self.swap(inner, axes[-1]), outer

    def far_sums(self, total):
        for axis in self.far[:-1]:
            total = total.astype(jnp.float32) + self.swap(total, axis).astype(jnp.float32)
            total = lax.reduce_precision(total, 8, 7).astype(jnp.bfloat16)
        return total, self.swap(total, self.far[-1])


SIDES = ((0, 0), (0, 1), (1, 0), (1, 1))


def grant(mib):
    return pltpu.CompilerParams(vmem_limit_bytes=mib * 2**20)


def product(left, right):
    return jnp.dot(left, right, preferred_element_type=jnp.float32)


def product_nt(left, right):
    return lax.dot_general(left, right, (((1,), (1,)), ((), ())), preferred_element_type=jnp.float32)


def rows_at_once(rows_low, cols_low):
    return max(n for n in (1, 2, 4, 8) if rows_low % n == 0 and (n == 1 or 4 * n * cols_low <= 256))


def side_order(rows_low, cols_low):
    count = rows_at_once(rows_low, cols_low)
    size = 4 * count * cols_low
    at = np.arange(size).reshape(count, 2, cols_low, 2).transpose(1, 3, 0, 2).reshape(-1)
    return (at[:, None] == np.arange(size)[None, :]).astype(np.float32)


def column(rows, cols_low, chan):
    return lax.broadcasted_iota(jnp.int32, (rows // cols_low, cols_low, chan), 1).reshape(rows, chan)


def from_left(x, at):
    return jnp.where(at == 0, 0.0, pltpu.roll(x, 1, 0))


def from_right(x, at, last):
    return jnp.where(at == last, 0.0, pltpu.roll(x, x.shape[0] - 1, 0))


def sort_columns(source, target, cols_low, order):
    rows_low, chan = source.shape[0] // 2, source.shape[2]
    group = rows_at_once(rows_low, cols_low)
    span = group * cols_low
    for n in range(rows_low // group):
        block = source[2 * group * n : 2 * group * (n + 1)].reshape(4 * span, chan)
        block = product(order, block).astype(jnp.bfloat16).reshape(4, span, chan)
        target[:, n * span : (n + 1) * span, :] = block


def tall(place_ref, low_ref, inner_ref, outer_ref, frame, lanes=slice(None)):
    odd = place_ref[1] == 1
    inner, outer = inner_ref[frame, :, :, lanes], outer_ref[frame, :, :, lanes]
    up, down = jnp.where(odd, inner, outer), jnp.where(odd, outer, inner)
    return jnp.concatenate([up, low_ref[frame, :, :, lanes], down], axis=0)


def spatial(low, ws_ref):
    rows_low, cols_low, chan = low.shape[0] - 2, low.shape[1], low.shape[2]
    count = rows_low * cols_low
    flat = low.reshape(-1, chan)
    rows = [[], []]
    for j in range(3):
        taps = [product(flat, ws_ref[i, j]).reshape(low.shape) for i in range(3)]
        even = taps[0][:rows_low] + (taps[1] + taps[2])[1 : rows_low + 1]
        odd = (taps[0] + taps[1])[1 : rows_low + 1] + taps[2][2:]
        rows[0].append(even.reshape(count, chan))
        rows[1].append(odd.reshape(count, chan))
    at = column(count, cols_low, chan)
    for first, second, third in rows:
        yield from_left(first, at) + (second + third)
        yield (first + second) + from_right(third, at, cols_low - 1)


def forward_kernel(place_ref, low_ref, inner_ref, outer_ref, ws_ref, act_ref, slope_ref):
    for frame in range(low_ref.shape[0]):
        low = tall(place_ref, low_ref, inner_ref, outer_ref, frame)
        for side, pre in enumerate(spatial(low, ws_ref)):
            sig = jax.nn.sigmoid(pre)
            act_ref[frame, side] = (pre * sig).astype(jnp.bfloat16)
            slope_ref[frame, side] = sig * (1.0 + pre * (1.0 - sig))


def half_sums(place_ref, low_ref, inner_ref, outer_ref, act_ref, pg_ref, ext_ref, out_ref):
    frames, rows_low, cols_low, chan = low_ref.shape
    count, half = rows_low * cols_low, chan // 2
    lanes = pl.ds(pl.multiple_of(place_ref[0] * half, half), half)
    lefts = [[] for _ in range(9)]
    acts = []
    at = column((rows_low + 2) * cols_low, cols_low, half)
    for frame in range(frames):
        low = tall(place_ref, low_ref, inner_ref, outer_ref, frame, lanes)
        wide = low.reshape(-1, half).astype(jnp.float32)
        moved = [from_left(wide, at), wide, from_right(wide, at, cols_low - 1)]
        turned = {}
        for dc in range(3):
            view = moved[dc].astype(jnp.bfloat16).reshape(low.shape)
            for dr in range(3):
                turned[dr - 1, dc - 1] = view[dr : dr + rows_low].reshape(count, half).T
        for i in range(3):
            for j in range(3):
                lefts[3 * i + j] += [turned[(a + i - 1) // 2, (b + j - 1) // 2] for a, b in SIDES]
        acts.append(act_ref[frame, :, :, lanes].reshape(4 * count, half).T)
    pg = pg_ref[...].reshape(frames * 4 * count, chan)
    left = jnp.concatenate([jnp.concatenate(left, axis=1) for left in lefts], axis=0)
    out_ref[:9] = product(left, pg).reshape(9, half, chan)
    act = jnp.concatenate(acts, axis=1)
    for k in range(3):
        out_ref[9 + k] = product(act, ext_ref[k : k + frames].reshape(frames * 4 * count, chan))


def half_kernel(place_ref, low_ref, inner_ref, outer_ref, act_ref, pg_ref, ext_ref, out_ref, act_out, sem):
    copy = pltpu.make_async_copy(act_ref, act_out, sem)
    copy.start()
    half_sums(place_ref, low_ref, inner_ref, outer_ref, act_ref, pg_ref, ext_ref, out_ref)
    copy.wait()


def backward_kernel(place_ref, low_ref, inner_ref, outer_ref, act_ref, slope_ref, cot_ref, later_ref, turned_ref, sort_ref,
                    pg_ref, ext_ref, out_ref, box_ref):
    frames, _, count, chan = cot_ref.shape
    ext_ref[:frames] = cot_ref[...]
    for n in range(2):
        sort_columns(later_ref.at[n], ext_ref.at[frames + n], low_ref.shape[2], sort_ref[...])
    for frame in range(frames):
        cots = [ext_ref[frame + k].reshape(4 * count, chan) for k in range(3)]
        act_grad = product(jnp.concatenate(cots, axis=1), turned_ref[...])
        slope = slope_ref[frame].reshape(4 * count, chan)
        pg_ref[frame] = (act_grad * slope).astype(jnp.bfloat16).reshape(4, count, chan)
        box_ref[frame] = sum(cot_ref[frame, side].astype(jnp.float32) for side in range(4))
    half_sums(place_ref, low_ref, inner_ref, outer_ref, act_ref, pg_ref, ext_ref, out_ref)


SCALAR = pl.BlockSpec(memory_space=pltpu.SMEM)
UNREAD = pl.BlockSpec(memory_space=pl.ANY)


def like(shape, dtype):
    return jax.ShapeDtypeStruct(shape, dtype)


TOKEN = like((8, 128), jnp.float32)


def cost(units, mib):
    return pl.CostEstimate(flops=units * 2 * 2048 * 256 * 256, bytes_accessed=mib * 2**20, transcendentals=0)


def in_hbm(array):
    return pltpu.with_memory_space_constraint(array, pltpu.HBM)


FULL = pl.BlockSpec(memory_space=pltpu.VMEM)


def first_kernel(place_ref, low_ref, cot_ref, inner_ref, outer_ref, later_ref, sems):
    last = low_ref.shape[1] - 1
    odd = place_ref[1]
    copies = [
        (low_ref.at[:, pl.ds(last * (1 - odd), 1)], inner_ref),
        (low_ref.at[:, pl.ds(last * odd, 1)], outer_ref),
    ]
    copies += [(cot_ref.at[n, r], later_ref.at[n, r]) for n in range(2) for r in range(cot_ref.shape[1])]
    copies = [pltpu.make_async_copy(a, b, sems.at[n]) for n, (a, b) in enumerate(copies)]
    for copy in copies:
        copy.start()
    for copy in copies:
        copy.wait()


def first_messages(place, low, cot):
    row = like(low[:, :1].shape, low.dtype)
    return pl.pallas_call(
        first_kernel,
        in_specs=[SCALAR, UNREAD, UNREAD],
        out_specs=[FULL] * 3,
        out_shape=[row, row, like(cot[:2].shape, cot.dtype)],
        scratch_shapes=[pltpu.SemaphoreType.DMA((2 + 2 * cot.shape[1],))],
        compiler_params=grant(4),
        name="first_messages",
    )(place, in_hbm(low), in_hbm(cot))


def load_kernel(low_hbm, cot_hbm, ws_hbm, wt_hbm, sort_hbm,
                low_ref, ws_ref, sort_ref, turned_ref, side_ref, cot_ref, wide_ref, wt_ref, sems):
    frames, cols_low, chan = low_ref.shape[0], low_ref.shape[2], low_ref.shape[3]
    pairs = [(sort_hbm, wide_ref)] + [(cot_hbm.at[n], cot_ref.at[n]) for n in range(frames)]
    pairs += [(wt_hbm.at[k], wt_ref.at[k]) for k in range(3)] + [(low_hbm, low_ref)]
    pairs += [(ws_hbm.at[i, j], ws_ref.at[i, j]) for i in range(3) for j in range(3)]
    copies = [pltpu.make_async_copy(a, b, sems.at[n]) for n, (a, b) in enumerate(pairs)]
    for copy in copies:
        copy.start()
    copies[0].wait()
    sort_ref[...] = wide_ref[...].astype(jnp.bfloat16)
    for n in range(frames):
        copies[1 + n].wait()
        sort_columns(cot_ref.at[n], side_ref.at[n], cols_low, sort_ref[...])
    for k in range(3):
        copies[1 + frames + k].wait()
        turned_ref[k * chan : (k + 1) * chan] = wt_ref[k].T
    for copy in copies[4 + frames :]:
        copy.wait()


def load(low, cot, ws, wt, sort):
    frames, rows_low, cols_low, chan = low.shape
    order = like(sort.shape, jnp.bfloat16)
    shapes = [low, ws, order, like((3 * chan, chan), wt.dtype),
              like((frames, 4, rows_low * cols_low, chan), jnp.bfloat16)]
    return pl.pallas_call(
        load_kernel,
        in_specs=[UNREAD] * 5,
        out_specs=[FULL] * 5,
        out_shape=[like(a.shape, a.dtype) for a in shapes],
        scratch_shapes=[pltpu.VMEM(cot.shape, cot.dtype), pltpu.VMEM(sort.shape, sort.dtype), pltpu.VMEM(wt.shape, wt.dtype),
                        pltpu.SemaphoreType.DMA((frames + 14,))],
        compiler_params=grant(14),
        cost_estimate=cost(2, 4),
        name="load",
    )(*[in_hbm(a) for a in (low, cot, ws, wt, sort)])


def forward(place, low, inner, outer, ws):
    frames, rows_low, cols_low, chan = low.shape
    side = (frames, 4, rows_low * cols_low, chan)
    return pl.pallas_call(
        forward_kernel,
        in_specs=[SCALAR] + [FULL] * 4,
        out_specs=[FULL] * 2,
        out_shape=[like(side, jnp.bfloat16), like(side, jnp.float32)],
        compiler_params=grant(20),
        cost_estimate=cost(10, 8),
        name="forward",
    )(place, low, inner, outer, ws)


def edges_kernel(place_ref, low_ref, inner_ref, outer_ref, pg_ref, _, tall_ref, pg_inner, pg_outer):
    cols_low = low_ref.shape[2]
    first = low_ref.shape[0] - tall_ref.shape[0]
    for n in range(tall_ref.shape[0]):
        tall_ref[n] = tall(place_ref, low_ref, inner_ref, outer_ref, first + n)
    odd = place_ref[1] == 1
    top, bottom = pg_ref[:, :2, :cols_low, :], pg_ref[:, 2:, -cols_low:, :]
    pg_inner[...] = jnp.where(odd, top, bottom)
    pg_outer[...] = jnp.where(odd, bottom, top)


def edges(place, low, inner, outer, pg, before):
    frames, rows_low, cols_low, chan = low.shape
    full = pl.BlockSpec(memory_space=pltpu.VMEM)
    rows = like((frames, 2, cols_low, chan), jnp.bfloat16)
    return pl.pallas_call(
        edges_kernel,
        in_specs=[SCALAR, full, full, full, full, UNREAD],
        out_specs=[full] * 3,
        out_shape=[like((2, rows_low + 2, cols_low, chan), jnp.bfloat16), rows, rows],
        compiler_params=grant(8),
        name="edges",
    )(place, low, inner, outer, pg, before)


def backward(place, low, inner, outer, act, slope, cot, later, turned, sort):
    frames, _, count, chan = act.shape
    ext = (frames + 2,) + act.shape[1:]
    return pl.pallas_call(
        backward_kernel,
        in_specs=[SCALAR] + [FULL] * 9,
        out_specs=[FULL] * 4,
        out_shape=[like(act.shape, jnp.bfloat16), like(ext, jnp.bfloat16), like((12, chan // 2, chan), jnp.float32),
                   like((frames, count, chan), jnp.float32)],
        compiler_params=grant(24),
        cost_estimate=cost(15, 10),
        name="backward",
    )(place, low, inner, outer, act, slope, cot, later, turned, sort)


def half_grads(place, low, inner, outer, act, pg, ext):
    chan = low.shape[-1]
    return pl.pallas_call(
        half_kernel,
        in_specs=[SCALAR] + [FULL] * 6,
        out_specs=[FULL, HBM],
        out_shape=[like((12, chan // 2, chan), jnp.float32), pltpu.HBM(act.shape, act.dtype)],
        scratch_shapes=[pltpu.SemaphoreType.DMA],
        compiler_params=grant(20),
        cost_estimate=cost(10, 6),
        name="half_grads",
    )(place, low, inner, outer, act, pg, ext)


HBM = pl.BlockSpec(memory_space=pltpu.HBM)


def split(value):
    high = value.astype(jnp.bfloat16)
    return high, (value - high.astype(jnp.float32)).astype(jnp.bfloat16)


def column_pair(first, second, j, at, last):
    if j == 0:
        return second + from_right(first, at, last)
    if j == 1:
        return first + second
    return first + from_left(second, at)


def input_kernel(pg_ref, box_ref, ws_ref, _, out_ref):
    frames, _, count, chan = pg_ref.shape
    cols_low = out_ref.shape[2]
    rows_low = count // cols_low
    at = column(count, cols_low, chan)
    turned = jnp.concatenate([ws_ref[i, j].T for j in range(3) for i in range(3)], axis=0)
    for frame in range(frames):
        own = [pg_ref[frame, side].astype(jnp.float32) for side in range(4)]
        zero = jnp.zeros((1, cols_low, chan), jnp.float32)
        parts = []
        for j in range(3):
            even = column_pair(own[0], own[1], j, at, cols_low - 1).reshape(rows_low, cols_low, chan)
            odd = column_pair(own[2], own[3], j, at, cols_low - 1).reshape(rows_low, cols_low, chan)
            below = jnp.concatenate([even[1:], zero], axis=0)
            above = jnp.concatenate([zero, odd[:-1]], axis=0)
            for value in (odd + below, even + odd, above + even):
                parts.append(jnp.concatenate(split(value.reshape(count, chan)), axis=0))
        sums = product(jnp.concatenate(parts, axis=1), turned)
        total = box_ref[frame] + (sums[:count] + sums[count:])
        out_ref[frame] = total.reshape(rows_low, cols_low, chan)


def input_own(pg, box, ws, before, low_shape):
    return pl.pallas_call(
        input_kernel,
        in_specs=[FULL] * 3 + [UNREAD],
        out_specs=FULL,
        out_shape=like(low_shape, jnp.float32),
        compiler_params=grant(16),
        cost_estimate=cost(6, 4),
        name="input_own",
    )(pg, box, ws, before)


def finish_kernel(place_ref, own_ref, ws_ref, inner_hbm, outer_hbm, edge_hbm, act_hbm, wt_hbm, sort_hbm, low_hbm, _,
                  section_ref, input_ref, token_ref,
                  inner_ref, outer_ref, edge_ref, act_ref, wt_ref, wide_ref, low_ref, earlier, held, input_held, sems):
    frames, rows_low, cols_low, chan = low_ref.shape
    group = rows_at_once(rows_low, cols_low)
    span, count = group * cols_low, rows_low * cols_low
    pairs = [(inner_hbm, inner_ref), (outer_hbm, outer_ref)]
    pairs += [(edge_hbm, edge_ref), (wt_hbm, wt_ref)]
    pairs += [(act_hbm.at[n], act_ref.at[n]) for n in range(frames)] + [(sort_hbm, wide_ref), (low_hbm, low_ref)]
    copies = [pltpu.make_async_copy(a, b, sems.at[n]) for n, (a, b) in enumerate(pairs)]
    for copy in copies:
        copy.start()
    token_ref[...] = jnp.zeros_like(token_ref)

    for copy in copies[:2]:
        copy.wait()
    odd_place = place_ref[1] == 1
    flat = (frames * cols_low, chan)
    at = column(flat[0], cols_low, chan)
    inner = [inner_ref[:, b].reshape(flat).astype(jnp.float32) for b in range(2)]
    outer = [outer_ref[:, b].reshape(flat).astype(jnp.float32) for b in range(2)]
    above = [jnp.where(odd_place, inner[b], outer[b]) for b in range(2)]
    below = [jnp.where(odd_place, outer[b], inner[b]) for b in range(2)]
    terms = []
    for (first, second), i in ((above, 2), (below, 0)):
        total = jnp.zeros(flat, jnp.float32)
        for j in range(3):
            parts = jnp.concatenate(split(column_pair(first, second, j, at, cols_low - 1)), axis=0)
            sums = product_nt(parts, ws_ref[i, j])
            total = total + (sums[: flat[0]] + sums[flat[0] :])
        terms.append(total.reshape(frames, cols_low, chan))
    for row in range(rows_low):
        value = own_ref[:, row]
        if row == 0:
            value = value + terms[0]
        if row == rows_low - 1:
            value = value + terms[1]
        input_held[:, row] = value.astype(jnp.bfloat16)
    leaving = [pltpu.make_async_copy(input_held, input_ref, sems.at[len(copies)])]
    leaving[0].start()

    for copy in copies[2:3]:
        copy.wait()
    for frame in range(2):
        for side, pre in enumerate(spatial(edge_ref[frame], ws_ref)):
            earlier[frame, side] = (pre * jax.nn.sigmoid(pre)).astype(jnp.bfloat16)
    for copy in copies[3:]:
        copy.wait()
    merge = wide_ref[...].T.astype(jnp.bfloat16)
    wt = wt_ref[...].reshape(3 * chan, chan)
    for frame in range(frames):
        acts = [act_ref[frame - k] if frame >= k else earlier[frame - k + 2] for k in range(3)]
        acts = jnp.concatenate([act.reshape(4 * count, chan) for act in acts], axis=1)
        low = low_ref[frame].reshape(1, count, chan).astype(jnp.float32)
        mixed = (product(acts, wt).reshape(4, count, chan) + low).astype(jnp.bfloat16)
        for n in range(rows_low // group):
            block = mixed[:, n * span : (n + 1) * span].reshape(4 * span, chan)
            block = product(merge, block).astype(jnp.bfloat16)
            held[frame, 2 * group * n : 2 * group * (n + 1)] = block.reshape(2 * group, 2 * cols_low, chan)
        leaving.append(pltpu.make_async_copy(held.at[frame], section_ref.at[frame], sems.at[len(copies) + 1 + frame]))
        leaving[-1].start()
    for copy in leaving:
        copy.wait()


def finish(place, own, ws, inner, outer, edge, act, wt, sort, low, before):
    frames, rows_low, cols_low, chan = low.shape
    out = (frames, 2 * rows_low, 2 * cols_low, chan)
    fetched = [inner, outer, edge, act, wt, sort, low]
    return pl.pallas_call(
        finish_kernel,
        in_specs=[SCALAR, FULL, FULL] + [HBM] * 7 + [UNREAD],
        out_specs=[HBM, HBM, FULL],
        out_shape=[like(out, jnp.bfloat16), like(low.shape, jnp.bfloat16), TOKEN],
        scratch_shapes=[pltpu.VMEM(a.shape, a.dtype) for a in fetched]
        + [pltpu.VMEM((2,) + act.shape[1:], act.dtype), pltpu.VMEM(out, jnp.bfloat16),
           pltpu.VMEM(low.shape, jnp.bfloat16), pltpu.SemaphoreType.DMA((7 + 2 * frames,))],
        compiler_params=grant(16),
        cost_estimate=cost(8, 4),
        name="finish",
    )(place, own, ws, inner, outer, edge, *[in_hbm(a) for a in (act, wt, sort, low)], before)


def put_kernel(place_ref, half_ref, *refs):
    spatial_ref, temporal_ref, wide, sems = refs[-4:]
    taps, half, _ = half_ref.shape
    to = pl.ds(pl.multiple_of(place_ref[0] * half, half), half)
    copies = []
    for tap in range(taps):
        wide[tap] = half_ref[tap].astype(jnp.float32)
        if tap < 9:
            target = spatial_ref.at[tap // 3, tap % 3, to]
        else:
            target = temporal_ref.at[tap - 9, to]
        copies.append(pltpu.make_async_copy(wide.at[tap], target, sems.at[tap]))
        copies[-1].start()
    for copy in copies:
        copy.wait()


def put(place, half, *done):
    chan = half.shape[-1]
    return pl.pallas_call(
        put_kernel,
        in_specs=[SCALAR, FULL] + [HBM] * len(done),
        out_specs=[HBM, HBM],
        out_shape=[like((3, 3, chan, chan), jnp.float32), like((3, chan, chan), jnp.float32)],
        input_output_aliases={2 + n: n for n in range(len(done))},
        scratch_shapes=[pltpu.VMEM((12, chan // 2, chan), jnp.float32), pltpu.SemaphoreType.DMA((12,))],
        compiler_params=grant(6),
        name="put",
    )(place, half, *done)


def add_kernel(mine_ref, theirs_ref, out_ref):
    out_ref[...] = (mine_ref[...] + theirs_ref[...]).astype(jnp.bfloat16)


def add_halves(mine, theirs):
    full = pl.BlockSpec(memory_space=pltpu.VMEM)
    return pl.pallas_call(
        add_kernel,
        in_specs=[full, full],
        out_specs=full,
        out_shape=like(mine.shape, jnp.bfloat16),
        compiler_params=grant(8),
        name="add_halves",
    )(mine, theirs)


def sum_kernel(got_ref, _, out_ref):
    total = got_ref[0].astype(jnp.float32)
    for n in range(1, got_ref.shape[0]):
        total = total + got_ref[n].astype(jnp.float32)
    out_ref[...] = total.astype(jnp.bfloat16)


def sum_parts(got, before):
    return pl.pallas_call(
        sum_kernel,
        in_specs=[FULL, UNREAD],
        out_specs=FULL,
        out_shape=like(got.shape[1:], jnp.bfloat16),
        compiler_params=grant(4),
        name="sum_parts",
    )(got, before)


def spread_kernel(own_ref, theirs_ref, *refs):
    total = (own_ref[...].astype(jnp.float32) + theirs_ref[...].astype(jnp.float32)).astype(jnp.bfloat16)
    for n in range(refs[-1].shape[0]):
        refs[-1][n] = total


def spread(own, theirs, parts, *before):
    return pl.pallas_call(
        spread_kernel,
        in_specs=[FULL, FULL] + [UNREAD] * len(before),
        out_specs=FULL,
        out_shape=like((parts,) + own.shape, jnp.bfloat16),
        compiler_params=grant(4),
        name="spread",
    )(own, theirs, *before)


def on_device(bits, low_frames, spatial_weight, temporal_weight, cotangent):
    low, cot = low_frames[0], cotangent[0]
    frames, rows_low, cols_low, chan = low.shape
    core = lax.axis_index(bits.core).astype(jnp.int32)
    odd = lax.axis_index(bits.axes["height"][-1]).astype(jnp.int32)
    mine, other = jnp.stack([core, odd]), jnp.stack([1 - core, odd])
    parts = 1 << len(bits.near)

    inner, outer, later = first_messages(mine, low, cot)
    later = bits.shift(later, "tm", -1)
    inner, outer = bits.pairs(inner, outer)
    order = jnp.asarray(side_order(rows_low, cols_low))
    low_in, ws, sort, turned, cot_side = load(low, cot, spatial_weight, temporal_weight, order)
    act, slope = forward(mine, low_in, inner, outer, ws)
    pg, ext, theirs, box = backward(
        other, low_in, inner, outer, act, slope, cot_side, later, turned, sort
    )
    theirs = bits.swap(theirs, bits.core)
    own, act = half_grads(mine, low_in, inner, outer, act, pg, ext)
    kept = add_halves(own, theirs)
    got = bits.exchange(kept.reshape(parts, -1, chan))
    edge, pg_inner, pg_outer = edges(mine, low_in, inner, outer, pg, kept)
    edge = bits.shift(edge, "tm", 1)
    pg_inner, pg_outer = bits.pairs(pg_inner, pg_outer)
    own_part = input_own(pg, box, ws, kept, low.shape)
    total, far = bits.far_sums(sum_parts(got, own_part))
    section_out, input_grad, done = finish(
        mine, own_part, ws, pg_inner, pg_outer, edge, act, temporal_weight, order, low, total
    )
    totals = spread(total, far, parts, done)
    half = bits.exchange(totals).reshape(kept.shape)
    theirs = bits.swap(half, bits.core)
    spatial_grad, temporal_grad = put(other, theirs, *put(mine, half))
    return section_out[None], input_grad[None], spatial_grad, temporal_grad


def solution(mesh):
    bits = Bits(mesh)
    block = P(*(bits.axes[name] for name in ("dp", "tm", "height")), None, None)
    return jax.shard_map(
        functools.partial(on_device, bits),
        mesh=bits.mesh,
        in_specs=(block, P(), P(), block),
        out_specs=(block, block, P(), P()),
        check_vma=False,
    )
```

```python
import functools

import jax
import jax.numpy as jnp
import numpy as np
from jax import lax
from jax.experimental import pallas as pl
from jax.experimental.pallas import tpu as pltpu
from jax.sharding import Mesh
from jax.sharding import PartitionSpec as P


class Bits:
    def __init__(self, mesh):
        self.axes = {}
        for name in mesh.axis_names:
            count = mesh.shape[name].bit_length() - 1
            self.axes[name] = tuple(f"{name}{bit}" for bit in reversed(range(count)))
        names = [bit for bits in self.axes.values() for bit in bits]
        self.mesh = Mesh(mesh.devices.reshape([2] * len(names)), tuple(names))
        self.core = next((n for n in names if self.same_chip(n)), self.axes["tm"][-1])
        others = [[b for b in reversed(bits) if b != self.core] for bits in self.axes.values()]
        turns = [bits[turn] for turn in range(len(names)) for bits in others if turn < len(bits)]
        self.near = [n for n in names if n in turns[:3]]
        self.far = turns[3:]

    def same_chip(self, name):
        at = [1 if n == name else 0 for n in self.mesh.axis_names]
        here = self.mesh.devices[tuple([0] * len(at))]
        there = self.mesh.devices[tuple(at)]
        return tuple(getattr(here, "coords", (0,))) == tuple(getattr(there, "coords", (1,)))

    def swap(self, block, axis):
        return lax.ppermute(block, axis, [(0, 1), (1, 0)])

    def shift(self, block, name, distance):
        axes = self.axes[name]
        devices = range(1 << len(axes))
        route = [(i - distance, i) for i in devices if i - distance in devices]
        return lax.ppermute(block, axes, route)

    def exchange(self, parts):
        return lax.all_to_all(parts, tuple(self.near), 0, 0, tiled=True)

    def pairs(self, inner, outer):
        axes = self.axes["height"]
        low = range(1, (1 << len(axes)) - 1, 2)
        route = [(i, i + 1) for i in low] + [(i + 1, i) for i in low]
        outer = lax.ppermute(outer, axes, route)
        return self.swap(inner, axes[-1]), outer

    def far_sums(self, total):
        for axis in self.far[:-1]:
            total = total.astype(jnp.float32) + self.swap(total, axis).astype(jnp.float32)
            total = lax.reduce_precision(total, 8, 7).astype(jnp.bfloat16)
        return total, self.swap(total, self.far[-1])


SIDES = ((0, 0), (0, 1), (1, 0), (1, 1))


def grant(mib):
    return pltpu.CompilerParams(vmem_limit_bytes=mib * 2**20)


def product(left, right):
    return jnp.dot(left, right, preferred_element_type=jnp.float32)


def product_nt(left, right):
    return lax.dot_general(left, right, (((1,), (1,)), ((), ())), preferred_element_type=jnp.float32)


def rows_at_once(rows_low, cols_low):
    return max(n for n in (1, 2, 4, 8) if rows_low % n == 0 and (n == 1 or 4 * n * cols_low <= 256))


def side_order(rows_low, cols_low):
    count = rows_at_once(rows_low, cols_low)
    size = 4 * count * cols_low
    at = np.arange(size).reshape(count, 2, cols_low, 2).transpose(1, 3, 0, 2).reshape(-1)
    return (at[:, None] == np.arange(size)[None, :]).astype(np.float32)


def column(rows, cols_low, chan):
    return lax.broadcasted_iota(jnp.int32, (rows // cols_low, cols_low, chan), 1).reshape(rows, chan)


def from_left(x, at):
    return jnp.where(at == 0, 0.0, pltpu.roll(x, 1, 0))


def from_right(x, at, last):
    return jnp.where(at == last, 0.0, pltpu.roll(x, x.shape[0] - 1, 0))


def sort_columns(source, target, cols_low, order):
    rows_low, chan = source.shape[0] // 2, source.shape[2]
    group = rows_at_once(rows_low, cols_low)
    span = group * cols_low
    for n in range(rows_low // group):
        block = source[2 * group * n : 2 * group * (n + 1)].reshape(4 * span, chan)
        block = product(order, block).astype(jnp.bfloat16).reshape(4, span, chan)
        target[:, n * span : (n + 1) * span, :] = block


def tall(place_ref, low_ref, inner_ref, outer_ref, frame, lanes=slice(None)):
    odd = place_ref[1] == 1
    inner, outer = inner_ref[frame, :, :, lanes], outer_ref[frame, :, :, lanes]
    up, down = jnp.where(odd, inner, outer), jnp.where(odd, outer, inner)
    return jnp.concatenate([up, low_ref[frame, :, :, lanes], down], axis=0)


def spatial(low, ws_ref):
    rows_low, cols_low, chan = low.shape[0] - 2, low.shape[1], low.shape[2]
    count = rows_low * cols_low
    flat = low.reshape(-1, chan)
    rows = [[], []]
    for j in range(3):
        taps = [product(flat, ws_ref[i, j]).reshape(low.shape) for i in range(3)]
        even = taps[0][:rows_low] + (taps[1] + taps[2])[1 : rows_low + 1]
        odd = (taps[0] + taps[1])[1 : rows_low + 1] + taps[2][2:]
        rows[0].append(even.reshape(count, chan))
        rows[1].append(odd.reshape(count, chan))
    at = column(count, cols_low, chan)
    for first, second, third in rows:
        yield from_left(first, at) + (second + third)
        yield (first + second) + from_right(third, at, cols_low - 1)


def forward_kernel(place_ref, low_ref, inner_ref, outer_ref, ws_ref, act_ref, slope_ref):
    for frame in range(low_ref.shape[0]):
        low = tall(place_ref, low_ref, inner_ref, outer_ref, frame)
        for side, pre in enumerate(spatial(low, ws_ref)):
            sig = jax.nn.sigmoid(pre)
            act_ref[frame, side] = (pre * sig).astype(jnp.bfloat16)
            slope_ref[frame, side] = sig * (1.0 + pre * (1.0 - sig))


def half_sums(place_ref, low_ref, inner_ref, outer_ref, act_ref, pg_ref, ext_ref, out_ref):
    frames, rows_low, cols_low, chan = low_ref.shape
    count, half = rows_low * cols_low, chan // 2
    lanes = pl.ds(pl.multiple_of(place_ref[0] * half, half), half)
    lefts = [[] for _ in range(9)]
    acts = []
    at = column((rows_low + 2) * cols_low, cols_low, half)
    for frame in range(frames):
        low = tall(place_ref, low_ref, inner_ref, outer_ref, frame, lanes)
        wide = low.reshape(-1, half).astype(jnp.float32)
        moved = [from_left(wide, at), wide, from_right(wide, at, cols_low - 1)]
        turned = {}
        for dc in range(3):
            view = moved[dc].astype(jnp.bfloat16).reshape(low.shape)
            for dr in range(3):
                turned[dr - 1, dc - 1] = view[dr : dr + rows_low].reshape(count, half).T
        for i in range(3):
            for j in range(3):
                lefts[3 * i + j] += [turned[(a + i - 1) // 2, (b + j - 1) // 2] for a, b in SIDES]
        acts.append(act_ref[frame, :, :, lanes].reshape(4 * count, half).T)
    pg = pg_ref[...].reshape(frames * 4 * count, chan)
    left = jnp.concatenate([jnp.concatenate(left, axis=1) for left in lefts], axis=0)
    out_ref[:9] = product(left, pg).reshape(9, half, chan)
    act = jnp.concatenate(acts, axis=1)
    for k in range(3):
        out_ref[9 + k] = product(act, ext_ref[k : k + frames].reshape(frames * 4 * count, chan))


def half_kernel(place_ref, low_ref, inner_ref, outer_ref, act_ref, pg_ref, ext_ref, out_ref, act_out, box_out, box_ref, sems):
    copies = [pltpu.make_async_copy(act_ref, act_out, sems.at[0]), pltpu.make_async_copy(box_ref, box_out, sems.at[1])]
    copies[0].start()
    for frame in range(box_ref.shape[0]):
        box_ref[frame] = sum(ext_ref[frame, side].astype(jnp.float32) for side in range(4))
    copies[1].start()
    half_sums(place_ref, low_ref, inner_ref, outer_ref, act_ref, pg_ref, ext_ref, out_ref)
    for copy in copies:
        copy.wait()


def backward_kernel(place_ref, low_ref, inner_ref, outer_ref, act_ref, slope_ref, cot_ref, later_ref, turned_ref, sort_ref,
                    pg_ref, ext_ref, out_ref):
    frames, _, count, chan = cot_ref.shape
    ext_ref[:frames] = cot_ref[...]
    for n in range(2):
        sort_columns(later_ref.at[n], ext_ref.at[frames + n], low_ref.shape[2], sort_ref[...])
    for frame in range(frames):
        cots = [ext_ref[frame + k].reshape(4 * count, chan) for k in range(3)]
        act_grad = product(jnp.concatenate(cots, axis=1), turned_ref[...])
        slope = slope_ref[frame].reshape(4 * count, chan)
        pg_ref[frame] = (act_grad * slope).astype(jnp.bfloat16).reshape(4, count, chan)
    half_sums(place_ref, low_ref, inner_ref, outer_ref, act_ref, pg_ref, ext_ref, out_ref)


SCALAR = pl.BlockSpec(memory_space=pltpu.SMEM)
UNREAD = pl.BlockSpec(memory_space=pl.ANY)


def like(shape, dtype):
    return jax.ShapeDtypeStruct(shape, dtype)


TOKEN = like((8, 128), jnp.float32)


def cost(units, mib):
    return pl.CostEstimate(flops=units * 2 * 2048 * 256 * 256, bytes_accessed=mib * 2**20, transcendentals=0)


def in_hbm(array):
    return pltpu.with_memory_space_constraint(array, pltpu.HBM)


FULL = pl.BlockSpec(memory_space=pltpu.VMEM)


def first_kernel(place_ref, low_ref, cot_ref, inner_ref, outer_ref, later_ref, sems):
    last = low_ref.shape[1] - 1
    odd = place_ref[1]
    copies = [
        (low_ref.at[:, pl.ds(last * (1 - odd), 1)], inner_ref),
        (low_ref.at[:, pl.ds(last * odd, 1)], outer_ref),
    ]
    copies += [(cot_ref.at[n, r], later_ref.at[n, r]) for n in range(2) for r in range(cot_ref.shape[1])]
    copies = [pltpu.make_async_copy(a, b, sems.at[n]) for n, (a, b) in enumerate(copies)]
    for copy in copies:
        copy.start()
    for copy in copies:
        copy.wait()


def first_messages(place, low, cot):
    row = like(low[:, :1].shape, low.dtype)
    return pl.pallas_call(
        first_kernel,
        in_specs=[SCALAR, UNREAD, UNREAD],
        out_specs=[FULL] * 3,
        out_shape=[row, row, like(cot[:2].shape, cot.dtype)],
        scratch_shapes=[pltpu.SemaphoreType.DMA((2 + 2 * cot.shape[1],))],
        compiler_params=grant(4),
        name="first_messages",
    )(place, in_hbm(low), in_hbm(cot))


def load_kernel(low_hbm, cot_hbm, ws_hbm, wt_hbm, sort_hbm,
                low_ref, ws_ref, wt_ref, sort_ref, turned_ref, side_ref, cot_ref, wide_ref, sems):
    frames, cols_low, chan = low_ref.shape[0], low_ref.shape[2], low_ref.shape[3]
    pairs = [(sort_hbm, wide_ref)] + [(cot_hbm.at[n], cot_ref.at[n]) for n in range(frames)]
    pairs += [(wt_hbm.at[k], wt_ref.at[k]) for k in range(3)] + [(low_hbm, low_ref)]
    pairs += [(ws_hbm.at[i, j], ws_ref.at[i, j]) for i in range(3) for j in range(3)]
    copies = [pltpu.make_async_copy(a, b, sems.at[n]) for n, (a, b) in enumerate(pairs)]
    for copy in copies:
        copy.start()
    copies[0].wait()
    sort_ref[...] = wide_ref[...].astype(jnp.bfloat16)
    for n in range(frames):
        copies[1 + n].wait()
        sort_columns(cot_ref.at[n], side_ref.at[n], cols_low, sort_ref[...])
    for k in range(3):
        copies[1 + frames + k].wait()
        turned_ref[k * chan : (k + 1) * chan] = wt_ref[k].T
    for copy in copies[4 + frames :]:
        copy.wait()


def load(low, cot, ws, wt, sort):
    frames, rows_low, cols_low, chan = low.shape
    order = like(sort.shape, jnp.bfloat16)
    shapes = [low, ws, wt, order, like((3 * chan, chan), wt.dtype),
              like((frames, 4, rows_low * cols_low, chan), jnp.bfloat16)]
    return pl.pallas_call(
        load_kernel,
        in_specs=[UNREAD] * 5,
        out_specs=[FULL] * 6,
        out_shape=[like(a.shape, a.dtype) for a in shapes],
        scratch_shapes=[pltpu.VMEM(cot.shape, cot.dtype), pltpu.VMEM(sort.shape, sort.dtype),
                        pltpu.SemaphoreType.DMA((frames + 14,))],
        compiler_params=grant(14),
        cost_estimate=cost(2, 4),
        name="load",
    )(*[in_hbm(a) for a in (low, cot, ws, wt, sort)])


def forward(place, low, inner, outer, ws):
    frames, rows_low, cols_low, chan = low.shape
    side = (frames, 4, rows_low * cols_low, chan)
    return pl.pallas_call(
        forward_kernel,
        in_specs=[SCALAR] + [FULL] * 4,
        out_specs=[FULL] * 2,
        out_shape=[like(side, jnp.bfloat16), like(side, jnp.float32)],
        compiler_params=grant(20),
        cost_estimate=cost(10, 8),
        name="forward",
    )(place, low, inner, outer, ws)


def edges_kernel(place_ref, low_ref, inner_ref, outer_ref, pg_ref, _, tall_ref, pg_inner, pg_outer):
    cols_low = low_ref.shape[2]
    first = low_ref.shape[0] - tall_ref.shape[0]
    for n in range(tall_ref.shape[0]):
        tall_ref[n] = tall(place_ref, low_ref, inner_ref, outer_ref, first + n)
    odd = place_ref[1] == 1
    top, bottom = pg_ref[:, :2, :cols_low, :], pg_ref[:, 2:, -cols_low:, :]
    pg_inner[...] = jnp.where(odd, top, bottom)
    pg_outer[...] = jnp.where(odd, bottom, top)


def edges(place, low, inner, outer, pg, before):
    frames, rows_low, cols_low, chan = low.shape
    full = pl.BlockSpec(memory_space=pltpu.VMEM)
    rows = like((frames, 2, cols_low, chan), jnp.bfloat16)
    return pl.pallas_call(
        edges_kernel,
        in_specs=[SCALAR, full, full, full, full, UNREAD],
        out_specs=[full] * 3,
        out_shape=[like((2, rows_low + 2, cols_low, chan), jnp.bfloat16), rows, rows],
        compiler_params=grant(8),
        name="edges",
    )(place, low, inner, outer, pg, before)


def backward(place, low, inner, outer, act, slope, cot, later, turned, sort):
    frames, _, count, chan = act.shape
    ext = (frames + 2,) + act.shape[1:]
    return pl.pallas_call(
        backward_kernel,
        in_specs=[SCALAR] + [FULL] * 9,
        out_specs=[FULL] * 3,
        out_shape=[like(act.shape, jnp.bfloat16), like(ext, jnp.bfloat16), like((12, chan // 2, chan), jnp.float32)],
        compiler_params=grant(24),
        cost_estimate=cost(15, 10),
        name="backward",
    )(place, low, inner, outer, act, slope, cot, later, turned, sort)


def half_grads(place, low, inner, outer, act, pg, ext):
    frames, _, count, chan = act.shape
    box = (frames, count, chan)
    return pl.pallas_call(
        half_kernel,
        in_specs=[SCALAR] + [FULL] * 6,
        out_specs=[FULL, HBM, HBM],
        out_shape=[like((12, chan // 2, chan), jnp.float32), pltpu.HBM(act.shape, act.dtype), pltpu.HBM(box, jnp.float32)],
        scratch_shapes=[pltpu.VMEM(box, jnp.float32), pltpu.SemaphoreType.DMA((2,))],
        compiler_params=grant(20),
        cost_estimate=cost(10, 6),
        name="half_grads",
    )(place, low, inner, outer, act, pg, ext)


HBM = pl.BlockSpec(memory_space=pltpu.HBM)


def split(value):
    high = value.astype(jnp.bfloat16)
    return high, (value - high.astype(jnp.float32)).astype(jnp.bfloat16)


def column_pair(first, second, j, at, last):
    if j == 0:
        return second + from_right(first, at, last)
    if j == 1:
        return first + second
    return first + from_left(second, at)


def input_kernel(pg_ref, box_hbm, ws_ref, _, out_ref, box_ref, sem):
    frames, _, count, chan = pg_ref.shape
    cols_low = out_ref.shape[2]
    rows_low = count // cols_low
    at = column(count, cols_low, chan)
    copy = pltpu.make_async_copy(box_hbm, box_ref, sem)
    copy.start()
    turned = jnp.concatenate([ws_ref[i, j].T for j in range(3) for i in range(3)], axis=0)
    for frame in range(frames):
        own = [pg_ref[frame, side].astype(jnp.float32) for side in range(4)]
        zero = jnp.zeros((1, cols_low, chan), jnp.float32)
        parts = []
        for j in range(3):
            even = column_pair(own[0], own[1], j, at, cols_low - 1).reshape(rows_low, cols_low, chan)
            odd = column_pair(own[2], own[3], j, at, cols_low - 1).reshape(rows_low, cols_low, chan)
            below = jnp.concatenate([even[1:], zero], axis=0)
            above = jnp.concatenate([zero, odd[:-1]], axis=0)
            for value in (odd + below, even + odd, above + even):
                parts.append(jnp.concatenate(split(value.reshape(count, chan)), axis=0))
        sums = product(jnp.concatenate(parts, axis=1), turned)
        if frame == 0:
            copy.wait()
        total = box_ref[frame] + (sums[:count] + sums[count:])
        out_ref[frame] = total.reshape(rows_low, cols_low, chan)


def input_own(pg, box, ws, before, low_shape):
    return pl.pallas_call(
        input_kernel,
        in_specs=[FULL, HBM, FULL, UNREAD],
        out_specs=FULL,
        out_shape=like(low_shape, jnp.float32),
        scratch_shapes=[pltpu.VMEM(box.shape, box.dtype), pltpu.SemaphoreType.DMA],
        compiler_params=grant(16),
        cost_estimate=cost(6, 4),
        name="input_own",
    )(pg, in_hbm(box), ws, before)


def finish_kernel(place_ref, own_ref, ws_ref, wt_ref, sort_ref, low_ref, inner_hbm, outer_hbm, edge_hbm, act_hbm, _,
                  section_ref, input_ref, token_ref,
                  inner_ref, outer_ref, edge_ref, act_ref, earlier, held, input_held, sems):
    frames, rows_low, cols_low, chan = low_ref.shape
    group = rows_at_once(rows_low, cols_low)
    span, count = group * cols_low, rows_low * cols_low
    pairs = [(inner_hbm, inner_ref), (outer_hbm, outer_ref)]
    pairs += [(edge_hbm, edge_ref)]
    pairs += [(act_hbm.at[n], act_ref.at[n]) for n in range(frames)]
    copies = [pltpu.make_async_copy(a, b, sems.at[n]) for n, (a, b) in enumerate(pairs)]
    for copy in copies:
        copy.start()
    token_ref[...] = jnp.zeros_like(token_ref)

    for copy in copies[:2]:
        copy.wait()
    odd_place = place_ref[1] == 1
    flat = (frames * cols_low, chan)
    at = column(flat[0], cols_low, chan)
    inner = [inner_ref[:, b].reshape(flat).astype(jnp.float32) for b in range(2)]
    outer = [outer_ref[:, b].reshape(flat).astype(jnp.float32) for b in range(2)]
    above = [jnp.where(odd_place, inner[b], outer[b]) for b in range(2)]
    below = [jnp.where(odd_place, outer[b], inner[b]) for b in range(2)]
    terms = []
    for (first, second), i in ((above, 2), (below, 0)):
        total = jnp.zeros(flat, jnp.float32)
        for j in range(3):
            parts = jnp.concatenate(split(column_pair(first, second, j, at, cols_low - 1)), axis=0)
            sums = product_nt(parts, ws_ref[i, j])
            total = total + (sums[: flat[0]] + sums[flat[0] :])
        terms.append(total.reshape(frames, cols_low, chan))
    for row in range(rows_low):
        value = own_ref[:, row]
        if row == 0:
            value = value + terms[0]
        if row == rows_low - 1:
            value = value + terms[1]
        input_held[:, row] = value.astype(jnp.bfloat16)
    leaving = [pltpu.make_async_copy(input_held, input_ref, sems.at[len(copies)])]
    leaving[0].start()

    for copy in copies[2:3]:
        copy.wait()
    for frame in range(2):
        for side, pre in enumerate(spatial(edge_ref[frame], ws_ref)):
            earlier[frame, side] = (pre * jax.nn.sigmoid(pre)).astype(jnp.bfloat16)
    for copy in copies[3:]:
        copy.wait()
    merge = sort_ref[...].T
    wt = wt_ref[...].reshape(3 * chan, chan)
    for frame in range(frames):
        acts = [act_ref[frame - k] if frame >= k else earlier[frame - k + 2] for k in range(3)]
        acts = jnp.concatenate([act.reshape(4 * count, chan) for act in acts], axis=1)
        low = low_ref[frame].reshape(1, count, chan).astype(jnp.float32)
        mixed = (product(acts, wt).reshape(4, count, chan) + low).astype(jnp.bfloat16)
        for n in range(rows_low // group):
            block = mixed[:, n * span : (n + 1) * span].reshape(4 * span, chan)
            block = product(merge, block).astype(jnp.bfloat16)
            held[frame, 2 * group * n : 2 * group * (n + 1)] = block.reshape(2 * group, 2 * cols_low, chan)
        leaving.append(pltpu.make_async_copy(held.at[frame], section_ref.at[frame], sems.at[len(copies) + 1 + frame]))
        leaving[-1].start()
    for copy in leaving:
        copy.wait()


def finish(place, own, ws, wt, sort, low, inner, outer, edge, act, before):
    frames, rows_low, cols_low, chan = low.shape
    out = (frames, 2 * rows_low, 2 * cols_low, chan)
    fetched = [inner, outer, edge, act]
    return pl.pallas_call(
        finish_kernel,
        in_specs=[SCALAR] + [FULL] * 5 + [HBM] * 4 + [UNREAD],
        out_specs=[HBM, HBM, FULL],
        out_shape=[like(out, jnp.bfloat16), like(low.shape, jnp.bfloat16), TOKEN],
        scratch_shapes=[pltpu.VMEM(a.shape, a.dtype) for a in fetched]
        + [pltpu.VMEM((2,) + act.shape[1:], act.dtype), pltpu.VMEM(out, jnp.bfloat16),
           pltpu.VMEM(low.shape, jnp.bfloat16), pltpu.SemaphoreType.DMA((7 + 2 * frames,))],
        compiler_params=grant(16),
        cost_estimate=cost(8, 4),
        name="finish",
    )(place, own, ws, wt, sort, low, inner, outer, edge, in_hbm(act), before)


def put_kernel(place_ref, half_ref, *refs):
    spatial_ref, temporal_ref, wide, sems = refs[-4:]
    taps, half, _ = half_ref.shape
    to = pl.ds(pl.multiple_of(place_ref[0] * half, half), half)
    copies = []
    for tap in range(taps):
        wide[tap] = half_ref[tap].astype(jnp.float32)
        if tap < 9:
            target = spatial_ref.at[tap // 3, tap % 3, to]
        else:
            target = temporal_ref.at[tap - 9, to]
        copies.append(pltpu.make_async_copy(wide.at[tap], target, sems.at[tap]))
        copies[-1].start()
    for copy in copies:
        copy.wait()


def put(place, half, *done):
    chan = half.shape[-1]
    return pl.pallas_call(
        put_kernel,
        in_specs=[SCALAR, FULL] + [HBM] * len(done),
        out_specs=[HBM, HBM],
        out_shape=[like((3, 3, chan, chan), jnp.float32), like((3, chan, chan), jnp.float32)],
        input_output_aliases={2 + n: n for n in range(len(done))},
        scratch_shapes=[pltpu.VMEM((12, chan // 2, chan), jnp.float32), pltpu.SemaphoreType.DMA((12,))],
        compiler_params=grant(6),
        name="put",
    )(place, half, *done)


def add_kernel(mine_ref, theirs_ref, out_ref):
    out_ref[...] = (mine_ref[...] + theirs_ref[...]).astype(jnp.bfloat16)


def add_halves(mine, theirs):
    full = pl.BlockSpec(memory_space=pltpu.VMEM)
    return pl.pallas_call(
        add_kernel,
        in_specs=[full, full],
        out_specs=full,
        out_shape=like(mine.shape, jnp.bfloat16),
        compiler_params=grant(8),
        name="add_halves",
    )(mine, theirs)


def sum_kernel(got_ref, _, out_ref):
    total = got_ref[0].astype(jnp.float32)
    for n in range(1, got_ref.shape[0]):
        total = total + got_ref[n].astype(jnp.float32)
    out_ref[...] = total.astype(jnp.bfloat16)


def sum_parts(got, before):
    return pl.pallas_call(
        sum_kernel,
        in_specs=[FULL, UNREAD],
        out_specs=FULL,
        out_shape=like(got.shape[1:], jnp.bfloat16),
        compiler_params=grant(4),
        name="sum_parts",
    )(got, before)


def spread_kernel(own_ref, theirs_ref, *refs):
    total = (own_ref[...].astype(jnp.float32) + theirs_ref[...].astype(jnp.float32)).astype(jnp.bfloat16)
    for n in range(refs[-1].shape[0]):
        refs[-1][n] = total


def spread(own, theirs, parts, *before):
    return pl.pallas_call(
        spread_kernel,
        in_specs=[FULL, FULL] + [UNREAD] * len(before),
        out_specs=FULL,
        out_shape=like((parts,) + own.shape, jnp.bfloat16),
        compiler_params=grant(4),
        name="spread",
    )(own, theirs, *before)


def on_device(bits, low_frames, spatial_weight, temporal_weight, cotangent):
    low, cot = low_frames[0], cotangent[0]
    frames, rows_low, cols_low, chan = low.shape
    core = lax.axis_index(bits.core).astype(jnp.int32)
    odd = lax.axis_index(bits.axes["height"][-1]).astype(jnp.int32)
    mine, other = jnp.stack([core, odd]), jnp.stack([1 - core, odd])
    parts = 1 << len(bits.near)

    inner, outer, later = first_messages(mine, low, cot)
    later = bits.shift(later, "tm", -1)
    inner, outer = bits.pairs(inner, outer)
    order = jnp.asarray(side_order(rows_low, cols_low))
    low, ws, wt, sort, turned, cot_side = load(low, cot, spatial_weight, temporal_weight, order)
    act, slope = forward(mine, low, inner, outer, ws)
    pg, ext, theirs = backward(
        other, low, inner, outer, act, slope, cot_side, later, turned, sort
    )
    theirs = bits.swap(theirs, bits.core)
    own, act, box = half_grads(mine, low, inner, outer, act, pg, ext)
    kept = add_halves(own, theirs)
    got = bits.exchange(kept.reshape(parts, -1, chan))
    edge, pg_inner, pg_outer = edges(mine, low, inner, outer, pg, kept)
    edge = bits.shift(edge, "tm", 1)
    pg_inner, pg_outer = bits.pairs(pg_inner, pg_outer)
    own_part = input_own(pg, box, ws, kept, low.shape)
    total, far = bits.far_sums(sum_parts(got, own_part))
    section_out, input_grad, done = finish(
        mine, own_part, ws, wt, sort, low, pg_inner, pg_outer, edge, act, total
    )
    totals = spread(total, far, parts, done)
    half = bits.exchange(totals).reshape(kept.shape)
    theirs = bits.swap(half, bits.core)
    spatial_grad, temporal_grad = put(other, theirs, *put(mine, half))
    return section_out[None], input_grad[None], spatial_grad, temporal_grad


def solution(mesh):
    bits = Bits(mesh)
    block = P(*(bits.axes[name] for name in ("dp", "tm", "height")), None, None)
    return jax.shard_map(
        functools.partial(on_device, bits),
        mesh=bits.mesh,
        in_specs=(block, P(), P(), block),
        out_specs=(block, block, P(), P()),
        check_vma=False,
    )
```

```python
import functools

import jax
import jax.numpy as jnp
import numpy as np
from jax import lax
from jax.experimental import pallas as pl
from jax.experimental.pallas import tpu as pltpu
from jax.sharding import Mesh
from jax.sharding import PartitionSpec as P


class Bits:
    def __init__(self, mesh):
        self.axes = {}
        for name in mesh.axis_names:
            count = mesh.shape[name].bit_length() - 1
            self.axes[name] = tuple(f"{name}{bit}" for bit in reversed(range(count)))
        names = [bit for bits in self.axes.values() for bit in bits]
        self.mesh = Mesh(mesh.devices.reshape([2] * len(names)), tuple(names))
        self.core = next((n for n in names if self.same_chip(n)), self.axes["tm"][-1])
        others = [[b for b in reversed(bits) if b != self.core] for bits in self.axes.values()]
        turns = [bits[turn] for turn in range(len(names)) for bits in others if turn < len(bits)]
        self.near = [n for n in names if n in turns[:3]]
        self.far = turns[3:]

    def same_chip(self, name):
        at = [1 if n == name else 0 for n in self.mesh.axis_names]
        here = self.mesh.devices[tuple([0] * len(at))]
        there = self.mesh.devices[tuple(at)]
        return tuple(getattr(here, "coords", (0,))) == tuple(getattr(there, "coords", (1,)))

    def swap(self, block, axis):
        return lax.ppermute(block, axis, [(0, 1), (1, 0)])

    def shift(self, block, name, distance):
        axes = self.axes[name]
        devices = range(1 << len(axes))
        route = [(i - distance, i) for i in devices if i - distance in devices]
        return lax.ppermute(block, axes, route)

    def exchange(self, parts):
        return lax.all_to_all(parts, tuple(self.near), 0, 0, tiled=True)

    def pairs(self, inner, outer):
        axes = self.axes["height"]
        low = range(1, (1 << len(axes)) - 1, 2)
        route = [(i, i + 1) for i in low] + [(i + 1, i) for i in low]
        outer = lax.ppermute(outer, axes, route)
        return self.swap(inner, axes[-1]), outer

    def far_sums(self, total):
        for axis in self.far[:-1]:
            total = total.astype(jnp.float32) + self.swap(total, axis).astype(jnp.float32)
            total = lax.reduce_precision(total, 8, 7).astype(jnp.bfloat16)
        return total, self.swap(total, self.far[-1])


SIDES = ((0, 0), (0, 1), (1, 0), (1, 1))


def grant(mib):
    return pltpu.CompilerParams(vmem_limit_bytes=mib * 2**20)


def product(left, right):
    return jnp.dot(left, right, preferred_element_type=jnp.float32)


def product_nt(left, right):
    return lax.dot_general(left, right, (((1,), (1,)), ((), ())), preferred_element_type=jnp.float32)


def rows_at_once(rows_low, cols_low):
    return max(n for n in (1, 2, 4, 8) if rows_low % n == 0 and (n == 1 or 4 * n * cols_low <= 256))


def side_order(rows_low, cols_low):
    count = rows_at_once(rows_low, cols_low)
    size = 4 * count * cols_low
    at = np.arange(size).reshape(count, 2, cols_low, 2).transpose(1, 3, 0, 2).reshape(-1)
    return (at[:, None] == np.arange(size)[None, :]).astype(np.float32)


def column(rows, cols_low, chan):
    return lax.broadcasted_iota(jnp.int32, (rows // cols_low, cols_low, chan), 1).reshape(rows, chan)


def from_left(x, at):
    return jnp.where(at == 0, 0.0, pltpu.roll(x, 1, 0))


def from_right(x, at, last):
    return jnp.where(at == last, 0.0, pltpu.roll(x, x.shape[0] - 1, 0))


def sort_columns(source, target, cols_low, order):
    rows_low, chan = source.shape[0] // 2, source.shape[2]
    group = rows_at_once(rows_low, cols_low)
    span = group * cols_low
    for n in range(rows_low // group):
        block = source[2 * group * n : 2 * group * (n + 1)].reshape(4 * span, chan)
        block = product(order, block).astype(jnp.bfloat16).reshape(4, span, chan)
        target[:, n * span : (n + 1) * span, :] = block


def tall(place_ref, low_ref, inner_ref, outer_ref, frame, lanes=slice(None)):
    odd = place_ref[1] == 1
    inner, outer = inner_ref[frame, :, :, lanes], outer_ref[frame, :, :, lanes]
    up, down = jnp.where(odd, inner, outer), jnp.where(odd, outer, inner)
    return jnp.concatenate([up, low_ref[frame, :, :, lanes], down], axis=0)


def spatial(low, ws_ref):
    rows_low, cols_low, chan = low.shape[0] - 2, low.shape[1], low.shape[2]
    count = rows_low * cols_low
    flat = low.reshape(-1, chan)
    rows = [[], []]
    for j in range(3):
        taps = [product(flat, ws_ref[i, j]).reshape(low.shape) for i in range(3)]
        even = taps[0][:rows_low] + (taps[1] + taps[2])[1 : rows_low + 1]
        odd = (taps[0] + taps[1])[1 : rows_low + 1] + taps[2][2:]
        rows[0].append(even.reshape(count, chan))
        rows[1].append(odd.reshape(count, chan))
    at = column(count, cols_low, chan)
    for first, second, third in rows:
        yield from_left(first, at) + (second + third)
        yield (first + second) + from_right(third, at, cols_low - 1)


def forward_kernel(place_ref, low_ref, inner_ref, outer_ref, ws_ref, act_ref, slope_ref):
    for frame in range(low_ref.shape[0]):
        low = tall(place_ref, low_ref, inner_ref, outer_ref, frame)
        for side, pre in enumerate(spatial(low, ws_ref)):
            sig = jax.nn.sigmoid(pre)
            act_ref[frame, side] = (pre * sig).astype(jnp.bfloat16)
            slope_ref[frame, side] = sig * (1.0 + pre * (1.0 - sig))


def half_sums(place_ref, low_ref, inner_ref, outer_ref, act_ref, pg_ref, ext_ref, out_ref):
    frames, rows_low, cols_low, chan = low_ref.shape
    count, half = rows_low * cols_low, chan // 2
    lanes = pl.ds(pl.multiple_of(place_ref[0] * half, half), half)
    lefts = [[] for _ in range(9)]
    acts = []
    at = column((rows_low + 2) * cols_low, cols_low, half)
    for frame in range(frames):
        low = tall(place_ref, low_ref, inner_ref, outer_ref, frame, lanes)
        wide = low.reshape(-1, half).astype(jnp.float32)
        moved = [from_left(wide, at), wide, from_right(wide, at, cols_low - 1)]
        turned = {}
        for dc in range(3):
            view = moved[dc].astype(jnp.bfloat16).reshape(low.shape)
            for dr in range(3):
                turned[dr - 1, dc - 1] = view[dr : dr + rows_low].reshape(count, half).T
        for i in range(3):
            for j in range(3):
                lefts[3 * i + j] += [turned[(a + i - 1) // 2, (b + j - 1) // 2] for a, b in SIDES]
        acts.append(act_ref[frame, :, :, lanes].reshape(4 * count, half).T)
    pg = pg_ref[...].reshape(frames * 4 * count, chan)
    left = jnp.concatenate([jnp.concatenate(left, axis=1) for left in lefts], axis=0)
    out_ref[:9] = product(left, pg).reshape(9, half, chan)
    act = jnp.concatenate(acts, axis=1)
    for k in range(3):
        out_ref[9 + k] = product(act, ext_ref[k : k + frames].reshape(frames * 4 * count, chan))


def half_kernel(place_ref, low_ref, inner_ref, outer_ref, act_ref, pg_ref, ext_ref, out_ref, act_out, sem):
    copy = pltpu.make_async_copy(act_ref, act_out, sem)
    copy.start()
    half_sums(place_ref, low_ref, inner_ref, outer_ref, act_ref, pg_ref, ext_ref, out_ref)
    copy.wait()


def backward_kernel(place_ref, low_ref, inner_ref, outer_ref, act_ref, slope_ref, cot_ref, later_ref, turned_ref, sort_ref,
                    pg_ref, ext_ref, out_ref):
    frames, _, count, chan = cot_ref.shape
    ext_ref[:frames] = cot_ref[...]
    for n in range(2):
        sort_columns(later_ref.at[n], ext_ref.at[frames + n], low_ref.shape[2], sort_ref[...])
    for frame in range(frames):
        cots = [ext_ref[frame + k].reshape(4 * count, chan) for k in range(3)]
        act_grad = product(jnp.concatenate(cots, axis=1), turned_ref[...])
        slope = slope_ref[frame].reshape(4 * count, chan)
        pg_ref[frame] = (act_grad * slope).astype(jnp.bfloat16).reshape(4, count, chan)
    half_sums(place_ref, low_ref, inner_ref, outer_ref, act_ref, pg_ref, ext_ref, out_ref)


SCALAR = pl.BlockSpec(memory_space=pltpu.SMEM)
UNREAD = pl.BlockSpec(memory_space=pl.ANY)


def like(shape, dtype):
    return jax.ShapeDtypeStruct(shape, dtype)


TOKEN = like((8, 128), jnp.float32)


def cost(units, mib):
    return pl.CostEstimate(flops=units * 2 * 2048 * 256 * 256, bytes_accessed=mib * 2**20, transcendentals=0)


def in_hbm(array):
    return pltpu.with_memory_space_constraint(array, pltpu.HBM)


FULL = pl.BlockSpec(memory_space=pltpu.VMEM)


def first_kernel(place_ref, low_ref, cot_ref, inner_ref, outer_ref, later_ref, sems):
    last = low_ref.shape[1] - 1
    odd = place_ref[1]
    copies = [
        (low_ref.at[:, pl.ds(last * (1 - odd), 1)], inner_ref),
        (low_ref.at[:, pl.ds(last * odd, 1)], outer_ref),
    ]
    copies += [(cot_ref.at[n, r], later_ref.at[n, r]) for n in range(2) for r in range(cot_ref.shape[1])]
    copies = [pltpu.make_async_copy(a, b, sems.at[n]) for n, (a, b) in enumerate(copies)]
    for copy in copies:
        copy.start()
    for copy in copies:
        copy.wait()


def first_messages(place, low, cot):
    row = like(low[:, :1].shape, low.dtype)
    return pl.pallas_call(
        first_kernel,
        in_specs=[SCALAR, UNREAD, UNREAD],
        out_specs=[FULL] * 3,
        out_shape=[row, row, like(cot[:2].shape, cot.dtype)],
        scratch_shapes=[pltpu.SemaphoreType.DMA((2 + 2 * cot.shape[1],))],
        compiler_params=grant(4),
        name="first_messages",
    )(place, in_hbm(low), in_hbm(cot))


def load_kernel(low_hbm, cot_hbm, ws_hbm, wt_hbm, sort_hbm,
                low_ref, ws_ref, sort_ref, turned_ref, side_ref, cot_ref, wide_ref, wt_ref, sems):
    frames, cols_low, chan = low_ref.shape[0], low_ref.shape[2], low_ref.shape[3]
    pairs = [(sort_hbm, wide_ref)] + [(cot_hbm.at[n], cot_ref.at[n]) for n in range(frames)]
    pairs += [(wt_hbm.at[k], wt_ref.at[k]) for k in range(3)] + [(low_hbm, low_ref)]
    pairs += [(ws_hbm.at[i, j], ws_ref.at[i, j]) for i in range(3) for j in range(3)]
    copies = [pltpu.make_async_copy(a, b, sems.at[n]) for n, (a, b) in enumerate(pairs)]
    for copy in copies:
        copy.start()
    copies[0].wait()
    sort_ref[...] = wide_ref[...].astype(jnp.bfloat16)
    for n in range(frames):
        copies[1 + n].wait()
        sort_columns(cot_ref.at[n], side_ref.at[n], cols_low, sort_ref[...])
    for k in range(3):
        copies[1 + frames + k].wait()
        turned_ref[k * chan : (k + 1) * chan] = wt_ref[k].T
    for copy in copies[4 + frames :]:
        copy.wait()


def load(low, cot, ws, wt, sort):
    frames, rows_low, cols_low, chan = low.shape
    order = like(sort.shape, jnp.bfloat16)
    shapes = [low, ws, order, like((3 * chan, chan), wt.dtype),
              like((frames, 4, rows_low * cols_low, chan), jnp.bfloat16)]
    return pl.pallas_call(
        load_kernel,
        in_specs=[UNREAD] * 5,
        out_specs=[FULL] * 5,
        out_shape=[like(a.shape, a.dtype) for a in shapes],
        scratch_shapes=[pltpu.VMEM(cot.shape, cot.dtype), pltpu.VMEM(sort.shape, sort.dtype), pltpu.VMEM(wt.shape, wt.dtype),
                        pltpu.SemaphoreType.DMA((frames + 14,))],
        compiler_params=grant(14),
        cost_estimate=cost(2, 4),
        name="load",
    )(*[in_hbm(a) for a in (low, cot, ws, wt, sort)])


def forward(place, low, inner, outer, ws):
    frames, rows_low, cols_low, chan = low.shape
    side = (frames, 4, rows_low * cols_low, chan)
    return pl.pallas_call(
        forward_kernel,
        in_specs=[SCALAR] + [FULL] * 4,
        out_specs=[FULL] * 2,
        out_shape=[like(side, jnp.bfloat16), like(side, jnp.float32)],
        compiler_params=grant(20),
        cost_estimate=cost(10, 8),
        name="forward",
    )(place, low, inner, outer, ws)


def edges_kernel(place_ref, low_ref, inner_ref, outer_ref, pg_ref, _, tall_ref, pg_inner, pg_outer):
    cols_low = low_ref.shape[2]
    first = low_ref.shape[0] - tall_ref.shape[0]
    for n in range(tall_ref.shape[0]):
        tall_ref[n] = tall(place_ref, low_ref, inner_ref, outer_ref, first + n)
    odd = place_ref[1] == 1
    top, bottom = pg_ref[:, :2, :cols_low, :], pg_ref[:, 2:, -cols_low:, :]
    pg_inner[...] = jnp.where(odd, top, bottom)
    pg_outer[...] = jnp.where(odd, bottom, top)


def edges(place, low, inner, outer, pg, before):
    frames, rows_low, cols_low, chan = low.shape
    full = pl.BlockSpec(memory_space=pltpu.VMEM)
    rows = like((frames, 2, cols_low, chan), jnp.bfloat16)
    return pl.pallas_call(
        edges_kernel,
        in_specs=[SCALAR, full, full, full, full, UNREAD],
        out_specs=[full] * 3,
        out_shape=[like((2, rows_low + 2, cols_low, chan), jnp.bfloat16), rows, rows],
        compiler_params=grant(8),
        name="edges",
    )(place, low, inner, outer, pg, before)


def backward(place, low, inner, outer, act, slope, cot, later, turned, sort):
    frames, _, count, chan = act.shape
    ext = (frames + 2,) + act.shape[1:]
    return pl.pallas_call(
        backward_kernel,
        in_specs=[SCALAR] + [FULL] * 9,
        out_specs=[FULL] * 3,
        out_shape=[like(act.shape, jnp.bfloat16), like(ext, jnp.bfloat16), like((12, chan // 2, chan), jnp.float32)],
        compiler_params=grant(24),
        cost_estimate=cost(15, 10),
        name="backward",
    )(place, low, inner, outer, act, slope, cot, later, turned, sort)


def half_grads(place, low, inner, outer, act, pg, ext):
    chan = low.shape[-1]
    return pl.pallas_call(
        half_kernel,
        in_specs=[SCALAR] + [FULL] * 6,
        out_specs=[FULL, HBM],
        out_shape=[like((12, chan // 2, chan), jnp.float32), pltpu.HBM(act.shape, act.dtype)],
        scratch_shapes=[pltpu.SemaphoreType.DMA],
        compiler_params=grant(20),
        cost_estimate=cost(10, 6),
        name="half_grads",
    )(place, low, inner, outer, act, pg, ext)


HBM = pl.BlockSpec(memory_space=pltpu.HBM)


def split(value):
    high = value.astype(jnp.bfloat16)
    return high, (value - high.astype(jnp.float32)).astype(jnp.bfloat16)


def column_pair(first, second, j, at, last):
    if j == 0:
        return second + from_right(first, at, last)
    if j == 1:
        return first + second
    return first + from_left(second, at)


def input_kernel(pg_ref, ext_hbm, ws_ref, _, out_ref, cot_ref, sems):
    frames, _, count, chan = pg_ref.shape
    cols_low = out_ref.shape[2]
    rows_low = count // cols_low
    at = column(count, cols_low, chan)
    copies = [pltpu.make_async_copy(ext_hbm.at[n], cot_ref.at[n], sems.at[n]) for n in range(frames)]
    for copy in copies:
        copy.start()
    turned = jnp.concatenate([ws_ref[i, j].T for j in range(3) for i in range(3)], axis=0)
    for frame in range(frames):
        own = [pg_ref[frame, side].astype(jnp.float32) for side in range(4)]
        zero = jnp.zeros((1, cols_low, chan), jnp.float32)
        parts = []
        for j in range(3):
            even = column_pair(own[0], own[1], j, at, cols_low - 1).reshape(rows_low, cols_low, chan)
            odd = column_pair(own[2], own[3], j, at, cols_low - 1).reshape(rows_low, cols_low, chan)
            below = jnp.concatenate([even[1:], zero], axis=0)
            above = jnp.concatenate([zero, odd[:-1]], axis=0)
            for value in (odd + below, even + odd, above + even):
                parts.append(jnp.concatenate(split(value.reshape(count, chan)), axis=0))
        sums = product(jnp.concatenate(parts, axis=1), turned)
        copies[frame].wait()
        total = sum(cot_ref[frame, side].astype(jnp.float32) for side in range(4))
        total = total + (sums[:count] + sums[count:])
        out_ref[frame] = total.reshape(rows_low, cols_low, chan)


def input_own(pg, ext, ws, before, low_shape):
    return pl.pallas_call(
        input_kernel,
        in_specs=[FULL, HBM, FULL, UNREAD],
        out_specs=FULL,
        out_shape=like(low_shape, jnp.float32),
        scratch_shapes=[pltpu.VMEM(pg.shape, ext.dtype), pltpu.SemaphoreType.DMA((pg.shape[0],))],
        compiler_params=grant(16),
        cost_estimate=cost(6, 4),
        name="input_own",
    )(pg, in_hbm(ext), ws, before)


def finish_kernel(place_ref, own_ref, ws_ref, inner_hbm, outer_hbm, edge_hbm, act_hbm, wt_hbm, sort_hbm, low_hbm, _,
                  section_ref, input_ref, token_ref,
                  inner_ref, outer_ref, edge_ref, act_ref, wt_ref, wide_ref, low_ref, earlier, held, input_held, sems):
    frames, rows_low, cols_low, chan = low_ref.shape
    group = rows_at_once(rows_low, cols_low)
    span, count = group * cols_low, rows_low * cols_low
    pairs = [(inner_hbm, inner_ref), (outer_hbm, outer_ref)]
    pairs += [(edge_hbm, edge_ref), (wt_hbm, wt_ref)]
    pairs += [(act_hbm.at[n], act_ref.at[n]) for n in range(frames)] + [(sort_hbm, wide_ref), (low_hbm, low_ref)]
    copies = [pltpu.make_async_copy(a, b, sems.at[n]) for n, (a, b) in enumerate(pairs)]
    for copy in copies:
        copy.start()
    token_ref[...] = jnp.zeros_like(token_ref)

    for copy in copies[:2]:
        copy.wait()
    odd_place = place_ref[1] == 1
    flat = (frames * cols_low, chan)
    at = column(flat[0], cols_low, chan)
    inner = [inner_ref[:, b].reshape(flat).astype(jnp.float32) for b in range(2)]
    outer = [outer_ref[:, b].reshape(flat).astype(jnp.float32) for b in range(2)]
    above = [jnp.where(odd_place, inner[b], outer[b]) for b in range(2)]
    below = [jnp.where(odd_place, outer[b], inner[b]) for b in range(2)]
    terms = []
    for (first, second), i in ((above, 2), (below, 0)):
        total = jnp.zeros(flat, jnp.float32)
        for j in range(3):
            parts = jnp.concatenate(split(column_pair(first, second, j, at, cols_low - 1)), axis=0)
            sums = product_nt(parts, ws_ref[i, j])
            total = total + (sums[: flat[0]] + sums[flat[0] :])
        terms.append(total.reshape(frames, cols_low, chan))
    for row in range(rows_low):
        value = own_ref[:, row]
        if row == 0:
            value = value + terms[0]
        if row == rows_low - 1:
            value = value + terms[1]
        input_held[:, row] = value.astype(jnp.bfloat16)
    leaving = [pltpu.make_async_copy(input_held, input_ref, sems.at[len(copies)])]
    leaving[0].start()

    for copy in copies[2:3]:
        copy.wait()
    for frame in range(2):
        for side, pre in enumerate(spatial(edge_ref[frame], ws_ref)):
            earlier[frame, side] = (pre * jax.nn.sigmoid(pre)).astype(jnp.bfloat16)
    for copy in copies[3:]:
        copy.wait()
    merge = wide_ref[...].T.astype(jnp.bfloat16)
    wt = wt_ref[...].reshape(3 * chan, chan)
    for frame in range(frames):
        acts = [act_ref[frame - k] if frame >= k else earlier[frame - k + 2] for k in range(3)]
        acts = jnp.concatenate([act.reshape(4 * count, chan) for act in acts], axis=1)
        low = low_ref[frame].reshape(1, count, chan).astype(jnp.float32)
        mixed = (product(acts, wt).reshape(4, count, chan) + low).astype(jnp.bfloat16)
        for n in range(rows_low // group):
            block = mixed[:, n * span : (n + 1) * span].reshape(4 * span, chan)
            block = product(merge, block).astype(jnp.bfloat16)
            held[frame, 2 * group * n : 2 * group * (n + 1)] = block.reshape(2 * group, 2 * cols_low, chan)
        leaving.append(pltpu.make_async_copy(held.at[frame], section_ref.at[frame], sems.at[len(copies) + 1 + frame]))
        leaving[-1].start()
    for copy in leaving:
        copy.wait()


def finish(place, own, ws, inner, outer, edge, act, wt, sort, low, before):
    frames, rows_low, cols_low, chan = low.shape
    out = (frames, 2 * rows_low, 2 * cols_low, chan)
    fetched = [inner, outer, edge, act, wt, sort, low]
    return pl.pallas_call(
        finish_kernel,
        in_specs=[SCALAR, FULL, FULL] + [HBM] * 7 + [UNREAD],
        out_specs=[HBM, HBM, FULL],
        out_shape=[like(out, jnp.bfloat16), like(low.shape, jnp.bfloat16), TOKEN],
        scratch_shapes=[pltpu.VMEM(a.shape, a.dtype) for a in fetched]
        + [pltpu.VMEM((2,) + act.shape[1:], act.dtype), pltpu.VMEM(out, jnp.bfloat16),
           pltpu.VMEM(low.shape, jnp.bfloat16), pltpu.SemaphoreType.DMA((7 + 2 * frames,))],
        compiler_params=grant(16),
        cost_estimate=cost(8, 4),
        name="finish",
    )(place, own, ws, inner, outer, edge, *[in_hbm(a) for a in (act, wt, sort, low)], before)


def put_kernel(place_ref, half_ref, *refs):
    spatial_ref, temporal_ref, wide, sems = refs[-4:]
    taps, half, _ = half_ref.shape
    to = pl.ds(pl.multiple_of(place_ref[0] * half, half), half)
    copies = []
    for tap in range(taps):
        wide[tap] = half_ref[tap].astype(jnp.float32)
        if tap < 9:
            target = spatial_ref.at[tap // 3, tap % 3, to]
        else:
            target = temporal_ref.at[tap - 9, to]
        copies.append(pltpu.make_async_copy(wide.at[tap], target, sems.at[tap]))
        copies[-1].start()
    for copy in copies:
        copy.wait()


def put(place, half, *done):
    chan = half.shape[-1]
    return pl.pallas_call(
        put_kernel,
        in_specs=[SCALAR, FULL] + [HBM] * len(done),
        out_specs=[HBM, HBM],
        out_shape=[like((3, 3, chan, chan), jnp.float32), like((3, chan, chan), jnp.float32)],
        input_output_aliases={2 + n: n for n in range(len(done))},
        scratch_shapes=[pltpu.VMEM((12, chan // 2, chan), jnp.float32), pltpu.SemaphoreType.DMA((12,))],
        compiler_params=grant(6),
        name="put",
    )(place, half, *done)


def add_kernel(mine_ref, theirs_ref, out_ref):
    out_ref[...] = (mine_ref[...] + theirs_ref[...]).astype(jnp.bfloat16)


def add_halves(mine, theirs):
    full = pl.BlockSpec(memory_space=pltpu.VMEM)
    return pl.pallas_call(
        add_kernel,
        in_specs=[full, full],
        out_specs=full,
        out_shape=like(mine.shape, jnp.bfloat16),
        compiler_params=grant(8),
        name="add_halves",
    )(mine, theirs)


def sum_kernel(got_ref, _, out_ref):
    total = got_ref[0].astype(jnp.float32)
    for n in range(1, got_ref.shape[0]):
        total = total + got_ref[n].astype(jnp.float32)
    out_ref[...] = total.astype(jnp.bfloat16)


def sum_parts(got, before):
    return pl.pallas_call(
        sum_kernel,
        in_specs=[FULL, UNREAD],
        out_specs=FULL,
        out_shape=like(got.shape[1:], jnp.bfloat16),
        compiler_params=grant(4),
        name="sum_parts",
    )(got, before)


def spread_kernel(own_ref, theirs_ref, *refs):
    total = (own_ref[...].astype(jnp.float32) + theirs_ref[...].astype(jnp.float32)).astype(jnp.bfloat16)
    for n in range(refs[-1].shape[0]):
        refs[-1][n] = total


def spread(own, theirs, parts, *before):
    return pl.pallas_call(
        spread_kernel,
        in_specs=[FULL, FULL] + [UNREAD] * len(before),
        out_specs=FULL,
        out_shape=like((parts,) + own.shape, jnp.bfloat16),
        compiler_params=grant(4),
        name="spread",
    )(own, theirs, *before)


def on_device(bits, low_frames, spatial_weight, temporal_weight, cotangent):
    low, cot = low_frames[0], cotangent[0]
    frames, rows_low, cols_low, chan = low.shape
    core = lax.axis_index(bits.core).astype(jnp.int32)
    odd = lax.axis_index(bits.axes["height"][-1]).astype(jnp.int32)
    mine, other = jnp.stack([core, odd]), jnp.stack([1 - core, odd])
    parts = 1 << len(bits.near)

    inner, outer, later = first_messages(mine, low, cot)
    later = bits.shift(later, "tm", -1)
    inner, outer = bits.pairs(inner, outer)
    order = jnp.asarray(side_order(rows_low, cols_low))
    low_in, ws, sort, turned, cot_side = load(low, cot, spatial_weight, temporal_weight, order)
    act, slope = forward(mine, low_in, inner, outer, ws)
    pg, ext, theirs = backward(
        other, low_in, inner, outer, act, slope, cot_side, later, turned, sort
    )
    theirs = bits.swap(theirs, bits.core)
    own, act = half_grads(mine, low_in, inner, outer, act, pg, ext)
    kept = add_halves(own, theirs)
    got = bits.exchange(kept.reshape(parts, -1, chan))
    edge, pg_inner, pg_outer = edges(mine, low_in, inner, outer, pg, kept)
    edge = bits.shift(edge, "tm", 1)
    pg_inner, pg_outer = bits.pairs(pg_inner, pg_outer)
    own_part = input_own(pg, ext, ws, kept, low.shape)
    total, far = bits.far_sums(sum_parts(got, own_part))
    section_out, input_grad, done = finish(
        mine, own_part, ws, pg_inner, pg_outer, edge, act, temporal_weight, order, low, total
    )
    totals = spread(total, far, parts, done)
    half = bits.exchange(totals).reshape(kept.shape)
    theirs = bits.swap(half, bits.core)
    spatial_grad, temporal_grad = put(other, theirs, *put(mine, half))
    return section_out[None], input_grad[None], spatial_grad, temporal_grad


def solution(mesh):
    bits = Bits(mesh)
    block = P(*(bits.axes[name] for name in ("dp", "tm", "height")), None, None)
    return jax.shard_map(
        functools.partial(on_device, bits),
        mesh=bits.mesh,
        in_specs=(block, P(), P(), block),
        out_specs=(block, block, P(), P()),
        check_vma=False,
    )
```

```python
import functools

import jax
import jax.numpy as jnp
import numpy as np
from jax import lax
from jax.experimental import pallas as pl
from jax.experimental.pallas import tpu as pltpu
from jax.sharding import Mesh
from jax.sharding import PartitionSpec as P


class Bits:
    def __init__(self, mesh):
        self.axes = {}
        for name in mesh.axis_names:
            count = mesh.shape[name].bit_length() - 1
            self.axes[name] = tuple(f"{name}{bit}" for bit in reversed(range(count)))
        names = [bit for bits in self.axes.values() for bit in bits]
        self.mesh = Mesh(mesh.devices.reshape([2] * len(names)), tuple(names))
        self.core = next((n for n in names if self.same_chip(n)), self.axes["tm"][-1])
        others = [[b for b in reversed(bits) if b != self.core] for bits in self.axes.values()]
        turns = [bits[turn] for turn in range(len(names)) for bits in others if turn < len(bits)]
        self.near = [n for n in names if n in turns[:3]]
        self.far = turns[3:]

    def same_chip(self, name):
        at = [1 if n == name else 0 for n in self.mesh.axis_names]
        here = self.mesh.devices[tuple([0] * len(at))]
        there = self.mesh.devices[tuple(at)]
        return tuple(getattr(here, "coords", (0,))) == tuple(getattr(there, "coords", (1,)))

    def swap(self, block, axis):
        return lax.ppermute(block, axis, [(0, 1), (1, 0)])

    def shift(self, block, name, distance):
        axes = self.axes[name]
        devices = range(1 << len(axes))
        route = [(i - distance, i) for i in devices if i - distance in devices]
        return lax.ppermute(block, axes, route)

    def exchange(self, parts):
        return lax.all_to_all(parts, tuple(self.near), 0, 0, tiled=True)

    def pairs(self, inner, outer):
        axes = self.axes["height"]
        low = range(1, (1 << len(axes)) - 1, 2)
        route = [(i, i + 1) for i in low] + [(i + 1, i) for i in low]
        outer = lax.ppermute(outer, axes, route)
        return self.swap(inner, axes[-1]), outer

    def far_sums(self, total):
        for axis in self.far[:-1]:
            total = total.astype(jnp.float32) + self.swap(total, axis).astype(jnp.float32)
            total = lax.reduce_precision(total, 8, 7).astype(jnp.bfloat16)
        return total, self.swap(total, self.far[-1])


SIDES = ((0, 0), (0, 1), (1, 0), (1, 1))


def grant(mib):
    return pltpu.CompilerParams(vmem_limit_bytes=mib * 2**20)


def product(left, right):
    return jnp.dot(left, right, preferred_element_type=jnp.float32)


def product_nt(left, right):
    return lax.dot_general(left, right, (((1,), (1,)), ((), ())), preferred_element_type=jnp.float32)


def rows_at_once(rows_low, cols_low):
    return max(n for n in (1, 2, 4, 8) if rows_low % n == 0 and (n == 1 or 4 * n * cols_low <= 256))


def side_order(rows_low, cols_low):
    count = rows_at_once(rows_low, cols_low)
    size = 4 * count * cols_low
    at = np.arange(size).reshape(count, 2, cols_low, 2).transpose(1, 3, 0, 2).reshape(-1)
    return (at[:, None] == np.arange(size)[None, :]).astype(np.float32)


def column(rows, cols_low, chan):
    return lax.broadcasted_iota(jnp.int32, (rows // cols_low, cols_low, chan), 1).reshape(rows, chan)


def from_left(x, at):
    return jnp.where(at == 0, 0.0, pltpu.roll(x, 1, 0))


def from_right(x, at, last):
    return jnp.where(at == last, 0.0, pltpu.roll(x, x.shape[0] - 1, 0))


def sort_columns(source, target, cols_low, order):
    rows_low, chan = source.shape[0] // 2, source.shape[2]
    group = rows_at_once(rows_low, cols_low)
    span = group * cols_low
    for n in range(rows_low // group):
        block = source[2 * group * n : 2 * group * (n + 1)].reshape(4 * span, chan)
        block = product(order, block).astype(jnp.bfloat16).reshape(4, span, chan)
        target[:, n * span : (n + 1) * span, :] = block


def tall(place_ref, low_ref, inner_ref, outer_ref, frame, lanes=slice(None)):
    odd = place_ref[1] == 1
    inner, outer = inner_ref[frame, :, :, lanes], outer_ref[frame, :, :, lanes]
    up, down = jnp.where(odd, inner, outer), jnp.where(odd, outer, inner)
    return jnp.concatenate([up, low_ref[frame, :, :, lanes], down], axis=0)


def spatial(low, ws_ref):
    rows_low, cols_low, chan = low.shape[0] - 2, low.shape[1], low.shape[2]
    count = rows_low * cols_low
    flat = low.reshape(-1, chan)
    rows = [[], []]
    for j in range(3):
        taps = [product(flat, ws_ref[i, j]).reshape(low.shape) for i in range(3)]
        even = taps[0][:rows_low] + (taps[1] + taps[2])[1 : rows_low + 1]
        odd = (taps[0] + taps[1])[1 : rows_low + 1] + taps[2][2:]
        rows[0].append(even.reshape(count, chan))
        rows[1].append(odd.reshape(count, chan))
    at = column(count, cols_low, chan)
    for first, second, third in rows:
        yield from_left(first, at) + (second + third)
        yield (first + second) + from_right(third, at, cols_low - 1)


def forward_kernel(place_ref, low_ref, inner_ref, outer_ref, ws_ref, act_ref, slope_ref):
    for frame in range(low_ref.shape[0]):
        low = tall(place_ref, low_ref, inner_ref, outer_ref, frame)
        for side, pre in enumerate(spatial(low, ws_ref)):
            sig = jax.nn.sigmoid(pre)
            act_ref[frame, side] = (pre * sig).astype(jnp.bfloat16)
            slope_ref[frame, side] = sig * (1.0 + pre * (1.0 - sig))


def half_sums(place_ref, low_ref, inner_ref, outer_ref, act_ref, pg_ref, ext_ref, out_ref):
    frames, rows_low, cols_low, chan = low_ref.shape
    count, half = rows_low * cols_low, chan // 2
    lanes = pl.ds(pl.multiple_of(place_ref[0] * half, half), half)
    lefts = [[] for _ in range(9)]
    acts = []
    at = column((rows_low + 2) * cols_low, cols_low, half)
    for frame in range(frames):
        low = tall(place_ref, low_ref, inner_ref, outer_ref, frame, lanes)
        wide = low.reshape(-1, half).astype(jnp.float32)
        moved = [from_left(wide, at), wide, from_right(wide, at, cols_low - 1)]
        turned = {}
        for dc in range(3):
            view = moved[dc].astype(jnp.bfloat16).reshape(low.shape)
            for dr in range(3):
                turned[dr - 1, dc - 1] = view[dr : dr + rows_low].reshape(count, half).T
        for i in range(3):
            for j in range(3):
                lefts[3 * i + j] += [turned[(a + i - 1) // 2, (b + j - 1) // 2] for a, b in SIDES]
        acts.append(act_ref[frame, :, :, lanes].reshape(4 * count, half).T)
    pg = pg_ref[...].reshape(frames * 4 * count, chan)
    left = jnp.concatenate([jnp.concatenate(left, axis=1) for left in lefts], axis=0)
    out_ref[:9] = product(left, pg).reshape(9, half, chan)
    act = jnp.concatenate(acts, axis=1)
    for k in range(3):
        out_ref[9 + k] = product(act, ext_ref[k : k + frames].reshape(frames * 4 * count, chan))


def half_kernel(place_ref, low_ref, inner_ref, outer_ref, act_ref, pg_ref, ext_ref, out_ref, act_out, box_ref, sem):
    copy = pltpu.make_async_copy(act_ref, act_out, sem)
    copy.start()
    for frame in range(box_ref.shape[0]):
        box_ref[frame] = sum(ext_ref[frame, side].astype(jnp.float32) for side in range(4))
    half_sums(place_ref, low_ref, inner_ref, outer_ref, act_ref, pg_ref, ext_ref, out_ref)
    copy.wait()


def backward_kernel(place_ref, low_ref, inner_ref, outer_ref, act_ref, slope_ref, cot_ref, later_ref, turned_ref, sort_ref,
                    pg_ref, ext_ref, out_ref):
    frames, _, count, chan = cot_ref.shape
    ext_ref[:frames] = cot_ref[...]
    for n in range(2):
        sort_columns(later_ref.at[n], ext_ref.at[frames + n], low_ref.shape[2], sort_ref[...])
    for frame in range(frames):
        cots = [ext_ref[frame + k].reshape(4 * count, chan) for k in range(3)]
        act_grad = product(jnp.concatenate(cots, axis=1), turned_ref[...])
        slope = slope_ref[frame].reshape(4 * count, chan)
        pg_ref[frame] = (act_grad * slope).astype(jnp.bfloat16).reshape(4, count, chan)
    half_sums(place_ref, low_ref, inner_ref, outer_ref, act_ref, pg_ref, ext_ref, out_ref)


SCALAR = pl.BlockSpec(memory_space=pltpu.SMEM)
UNREAD = pl.BlockSpec(memory_space=pl.ANY)


def like(shape, dtype):
    return jax.ShapeDtypeStruct(shape, dtype)


TOKEN = like((8, 128), jnp.float32)


def cost(units, mib):
    return pl.CostEstimate(flops=units * 2 * 2048 * 256 * 256, bytes_accessed=mib * 2**20, transcendentals=0)


def in_hbm(array):
    return pltpu.with_memory_space_constraint(array, pltpu.HBM)


FULL = pl.BlockSpec(memory_space=pltpu.VMEM)


def first_kernel(place_ref, low_ref, cot_ref, inner_ref, outer_ref, later_ref, sems):
    last = low_ref.shape[1] - 1
    odd = place_ref[1]
    copies = [
        (low_ref.at[:, pl.ds(last * (1 - odd), 1)], inner_ref),
        (low_ref.at[:, pl.ds(last * odd, 1)], outer_ref),
    ]
    copies += [(cot_ref.at[n, r], later_ref.at[n, r]) for n in range(2) for r in range(cot_ref.shape[1])]
    copies = [pltpu.make_async_copy(a, b, sems.at[n]) for n, (a, b) in enumerate(copies)]
    for copy in copies:
        copy.start()
    for copy in copies:
        copy.wait()


def first_messages(place, low, cot):
    row = like(low[:, :1].shape, low.dtype)
    return pl.pallas_call(
        first_kernel,
        in_specs=[SCALAR, UNREAD, UNREAD],
        out_specs=[FULL] * 3,
        out_shape=[row, row, like(cot[:2].shape, cot.dtype)],
        scratch_shapes=[pltpu.SemaphoreType.DMA((2 + 2 * cot.shape[1],))],
        compiler_params=grant(4),
        name="first_messages",
    )(place, in_hbm(low), in_hbm(cot))


def load_kernel(low_hbm, cot_hbm, ws_hbm, wt_hbm, sort_hbm,
                low_ref, ws_ref, sort_ref, turned_ref, side_ref, cot_ref, wide_ref, wt_ref, sems):
    frames, cols_low, chan = low_ref.shape[0], low_ref.shape[2], low_ref.shape[3]
    pairs = [(sort_hbm, wide_ref)] + [(cot_hbm.at[n], cot_ref.at[n]) for n in range(frames)]
    pairs += [(wt_hbm.at[k], wt_ref.at[k]) for k in range(3)] + [(low_hbm, low_ref)]
    pairs += [(ws_hbm.at[i, j], ws_ref.at[i, j]) for i in range(3) for j in range(3)]
    copies = [pltpu.make_async_copy(a, b, sems.at[n]) for n, (a, b) in enumerate(pairs)]
    for copy in copies:
        copy.start()
    copies[0].wait()
    sort_ref[...] = wide_ref[...].astype(jnp.bfloat16)
    for n in range(frames):
        copies[1 + n].wait()
        sort_columns(cot_ref.at[n], side_ref.at[n], cols_low, sort_ref[...])
    for k in range(3):
        copies[1 + frames + k].wait()
        turned_ref[k * chan : (k + 1) * chan] = wt_ref[k].T
    for copy in copies[4 + frames :]:
        copy.wait()


def load(low, cot, ws, wt, sort):
    frames, rows_low, cols_low, chan = low.shape
    order = like(sort.shape, jnp.bfloat16)
    shapes = [low, ws, order, like((3 * chan, chan), wt.dtype),
              like((frames, 4, rows_low * cols_low, chan), jnp.bfloat16)]
    return pl.pallas_call(
        load_kernel,
        in_specs=[UNREAD] * 5,
        out_specs=[FULL] * 5,
        out_shape=[like(a.shape, a.dtype) for a in shapes],
        scratch_shapes=[pltpu.VMEM(cot.shape, cot.dtype), pltpu.VMEM(sort.shape, sort.dtype), pltpu.VMEM(wt.shape, wt.dtype),
                        pltpu.SemaphoreType.DMA((frames + 14,))],
        compiler_params=grant(14),
        cost_estimate=cost(2, 4),
        name="load",
    )(*[in_hbm(a) for a in (low, cot, ws, wt, sort)])


def forward(place, low, inner, outer, ws):
    frames, rows_low, cols_low, chan = low.shape
    side = (frames, 4, rows_low * cols_low, chan)
    return pl.pallas_call(
        forward_kernel,
        in_specs=[SCALAR] + [FULL] * 4,
        out_specs=[FULL] * 2,
        out_shape=[like(side, jnp.bfloat16), like(side, jnp.float32)],
        compiler_params=grant(20),
        cost_estimate=cost(10, 8),
        name="forward",
    )(place, low, inner, outer, ws)


def edges_kernel(place_ref, low_ref, inner_ref, outer_ref, pg_ref, _, tall_ref, pg_inner, pg_outer):
    cols_low = low_ref.shape[2]
    first = low_ref.shape[0] - tall_ref.shape[0]
    for n in range(tall_ref.shape[0]):
        tall_ref[n] = tall(place_ref, low_ref, inner_ref, outer_ref, first + n)
    odd = place_ref[1] == 1
    top, bottom = pg_ref[:, :2, :cols_low, :], pg_ref[:, 2:, -cols_low:, :]
    pg_inner[...] = jnp.where(odd, top, bottom)
    pg_outer[...] = jnp.where(odd, bottom, top)


def edges(place, low, inner, outer, pg, before):
    frames, rows_low, cols_low, chan = low.shape
    full = pl.BlockSpec(memory_space=pltpu.VMEM)
    rows = like((frames, 2, cols_low, chan), jnp.bfloat16)
    return pl.pallas_call(
        edges_kernel,
        in_specs=[SCALAR, full, full, full, full, UNREAD],
        out_specs=[full] * 3,
        out_shape=[like((2, rows_low + 2, cols_low, chan), jnp.bfloat16), rows, rows],
        compiler_params=grant(8),
        name="edges",
    )(place, low, inner, outer, pg, before)


def backward(place, low, inner, outer, act, slope, cot, later, turned, sort):
    frames, _, count, chan = act.shape
    ext = (frames + 2,) + act.shape[1:]
    return pl.pallas_call(
        backward_kernel,
        in_specs=[SCALAR] + [FULL] * 9,
        out_specs=[FULL] * 3,
        out_shape=[like(act.shape, jnp.bfloat16), like(ext, jnp.bfloat16), like((12, chan // 2, chan), jnp.float32)],
        compiler_params=grant(24),
        cost_estimate=cost(15, 10),
        name="backward",
    )(place, low, inner, outer, act, slope, cot, later, turned, sort)


def half_grads(place, low, inner, outer, act, pg, ext):
    chan = low.shape[-1]
    return pl.pallas_call(
        half_kernel,
        in_specs=[SCALAR] + [FULL] * 6,
        out_specs=[FULL, HBM, FULL],
        out_shape=[like((12, chan // 2, chan), jnp.float32), pltpu.HBM(act.shape, act.dtype),
                   like((act.shape[0],) + act.shape[2:], jnp.float32)],
        scratch_shapes=[pltpu.SemaphoreType.DMA],
        compiler_params=grant(20),
        cost_estimate=cost(10, 6),
        name="half_grads",
    )(place, low, inner, outer, act, pg, ext)


HBM = pl.BlockSpec(memory_space=pltpu.HBM)


def split(value):
    high = value.astype(jnp.bfloat16)
    return high, (value - high.astype(jnp.float32)).astype(jnp.bfloat16)


def column_pair(first, second, j, at, last):
    if j == 0:
        return second + from_right(first, at, last)
    if j == 1:
        return first + second
    return first + from_left(second, at)


def input_kernel(pg_ref, box_ref, ws_ref, _, out_ref):
    frames, _, count, chan = pg_ref.shape
    cols_low = out_ref.shape[2]
    rows_low = count // cols_low
    at = column(count, cols_low, chan)
    turned = jnp.concatenate([ws_ref[i, j].T for j in range(3) for i in range(3)], axis=0)
    for frame in range(frames):
        own = [pg_ref[frame, side].astype(jnp.float32) for side in range(4)]
        zero = jnp.zeros((1, cols_low, chan), jnp.float32)
        parts = []
        for j in range(3):
            even = column_pair(own[0], own[1], j, at, cols_low - 1).reshape(rows_low, cols_low, chan)
            odd = column_pair(own[2], own[3], j, at, cols_low - 1).reshape(rows_low, cols_low, chan)
            below = jnp.concatenate([even[1:], zero], axis=0)
            above = jnp.concatenate([zero, odd[:-1]], axis=0)
            for value in (odd + below, even + odd, above + even):
                parts.append(jnp.concatenate(split(value.reshape(count, chan)), axis=0))
        sums = product(jnp.concatenate(parts, axis=1), turned)
        total = box_ref[frame] + (sums[:count] + sums[count:])
        out_ref[frame] = total.reshape(rows_low, cols_low, chan)


def input_own(pg, box, ws, before, low_shape):
    return pl.pallas_call(
        input_kernel,
        in_specs=[FULL] * 3 + [UNREAD],
        out_specs=FULL,
        out_shape=like(low_shape, jnp.float32),
        compiler_params=grant(16),
        cost_estimate=cost(6, 4),
        name="input_own",
    )(pg, box, ws, before)


def finish_kernel(place_ref, own_ref, ws_ref, inner_hbm, outer_hbm, edge_hbm, act_hbm, wt_hbm, sort_hbm, low_hbm, _,
                  section_ref, input_ref, token_ref,
                  inner_ref, outer_ref, edge_ref, act_ref, wt_ref, wide_ref, low_ref, earlier, held, input_held, sems):
    frames, rows_low, cols_low, chan = low_ref.shape
    group = rows_at_once(rows_low, cols_low)
    span, count = group * cols_low, rows_low * cols_low
    pairs = [(inner_hbm, inner_ref), (outer_hbm, outer_ref)]
    pairs += [(edge_hbm, edge_ref), (wt_hbm, wt_ref)]
    pairs += [(act_hbm.at[n], act_ref.at[n]) for n in range(frames)] + [(sort_hbm, wide_ref), (low_hbm, low_ref)]
    copies = [pltpu.make_async_copy(a, b, sems.at[n]) for n, (a, b) in enumerate(pairs)]
    for copy in copies:
        copy.start()
    token_ref[...] = jnp.zeros_like(token_ref)

    for copy in copies[:2]:
        copy.wait()
    odd_place = place_ref[1] == 1
    flat = (frames * cols_low, chan)
    at = column(flat[0], cols_low, chan)
    inner = [inner_ref[:, b].reshape(flat).astype(jnp.float32) for b in range(2)]
    outer = [outer_ref[:, b].reshape(flat).astype(jnp.float32) for b in range(2)]
    above = [jnp.where(odd_place, inner[b], outer[b]) for b in range(2)]
    below = [jnp.where(odd_place, outer[b], inner[b]) for b in range(2)]
    terms = []
    for (first, second), i in ((above, 2), (below, 0)):
        total = jnp.zeros(flat, jnp.float32)
        for j in range(3):
            parts = jnp.concatenate(split(column_pair(first, second, j, at, cols_low - 1)), axis=0)
            sums = product_nt(parts, ws_ref[i, j])
            total = total + (sums[: flat[0]] + sums[flat[0] :])
        terms.append(total.reshape(frames, cols_low, chan))
    for row in range(rows_low):
        value = own_ref[:, row]
        if row == 0:
            value = value + terms[0]
        if row == rows_low - 1:
            value = value + terms[1]
        input_held[:, row] = value.astype(jnp.bfloat16)
    leaving = [pltpu.make_async_copy(input_held, input_ref, sems.at[len(copies)])]
    leaving[0].start()

    for copy in copies[2:3]:
        copy.wait()
    for frame in range(2):
        for side, pre in enumerate(spatial(edge_ref[frame], ws_ref)):
            earlier[frame, side] = (pre * jax.nn.sigmoid(pre)).astype(jnp.bfloat16)
    for copy in copies[3:]:
        copy.wait()
    merge = wide_ref[...].T.astype(jnp.bfloat16)
    wt = wt_ref[...].reshape(3 * chan, chan)
    for frame in range(frames):
        acts = [act_ref[frame - k] if frame >= k else earlier[frame - k + 2] for k in range(3)]
        acts = jnp.concatenate([act.reshape(4 * count, chan) for act in acts], axis=1)
        low = low_ref[frame].reshape(1, count, chan).astype(jnp.float32)
        mixed = (product(acts, wt).reshape(4, count, chan) + low).astype(jnp.bfloat16)
        for n in range(rows_low // group):
            block = mixed[:, n * span : (n + 1) * span].reshape(4 * span, chan)
            block = product(merge, block).astype(jnp.bfloat16)
            held[frame, 2 * group * n : 2 * group * (n + 1)] = block.reshape(2 * group, 2 * cols_low, chan)
        leaving.append(pltpu.make_async_copy(held.at[frame], section_ref.at[frame], sems.at[len(copies) + 1 + frame]))
        leaving[-1].start()
    for copy in leaving:
        copy.wait()


def finish(place, own, ws, inner, outer, edge, act, wt, sort, low, before):
    frames, rows_low, cols_low, chan = low.shape
    out = (frames, 2 * rows_low, 2 * cols_low, chan)
    fetched = [inner, outer, edge, act, wt, sort, low]
    return pl.pallas_call(
        finish_kernel,
        in_specs=[SCALAR, FULL, FULL] + [HBM] * 7 + [UNREAD],
        out_specs=[HBM, HBM, FULL],
        out_shape=[like(out, jnp.bfloat16), like(low.shape, jnp.bfloat16), TOKEN],
        scratch_shapes=[pltpu.VMEM(a.shape, a.dtype) for a in fetched]
        + [pltpu.VMEM((2,) + act.shape[1:], act.dtype), pltpu.VMEM(out, jnp.bfloat16),
           pltpu.VMEM(low.shape, jnp.bfloat16), pltpu.SemaphoreType.DMA((7 + 2 * frames,))],
        compiler_params=grant(16),
        cost_estimate=cost(8, 4),
        name="finish",
    )(place, own, ws, inner, outer, edge, *[in_hbm(a) for a in (act, wt, sort, low)], before)


def put_kernel(place_ref, half_ref, *refs):
    spatial_ref, temporal_ref, wide, sems = refs[-4:]
    taps, half, _ = half_ref.shape
    to = pl.ds(pl.multiple_of(place_ref[0] * half, half), half)
    copies = []
    for tap in range(taps):
        wide[tap] = half_ref[tap].astype(jnp.float32)
        if tap < 9:
            target = spatial_ref.at[tap // 3, tap % 3, to]
        else:
            target = temporal_ref.at[tap - 9, to]
        copies.append(pltpu.make_async_copy(wide.at[tap], target, sems.at[tap]))
        copies[-1].start()
    for copy in copies:
        copy.wait()


def put(place, half, *done):
    chan = half.shape[-1]
    return pl.pallas_call(
        put_kernel,
        in_specs=[SCALAR, FULL] + [HBM] * len(done),
        out_specs=[HBM, HBM],
        out_shape=[like((3, 3, chan, chan), jnp.float32), like((3, chan, chan), jnp.float32)],
        input_output_aliases={2 + n: n for n in range(len(done))},
        scratch_shapes=[pltpu.VMEM((12, chan // 2, chan), jnp.float32), pltpu.SemaphoreType.DMA((12,))],
        compiler_params=grant(6),
        name="put",
    )(place, half, *done)


def add_kernel(mine_ref, theirs_ref, out_ref):
    out_ref[...] = (mine_ref[...] + theirs_ref[...]).astype(jnp.bfloat16)


def add_halves(mine, theirs):
    full = pl.BlockSpec(memory_space=pltpu.VMEM)
    return pl.pallas_call(
        add_kernel,
        in_specs=[full, full],
        out_specs=full,
        out_shape=like(mine.shape, jnp.bfloat16),
        compiler_params=grant(8),
        name="add_halves",
    )(mine, theirs)


def sum_kernel(got_ref, _, out_ref):
    total = got_ref[0].astype(jnp.float32)
    for n in range(1, got_ref.shape[0]):
        total = total + got_ref[n].astype(jnp.float32)
    out_ref[...] = total.astype(jnp.bfloat16)


def sum_parts(got, before):
    return pl.pallas_call(
        sum_kernel,
        in_specs=[FULL, UNREAD],
        out_specs=FULL,
        out_shape=like(got.shape[1:], jnp.bfloat16),
        compiler_params=grant(4),
        name="sum_parts",
    )(got, before)


def spread_kernel(own_ref, theirs_ref, *refs):
    total = (own_ref[...].astype(jnp.float32) + theirs_ref[...].astype(jnp.float32)).astype(jnp.bfloat16)
    for n in range(refs[-1].shape[0]):
        refs[-1][n] = total


def spread(own, theirs, parts, *before):
    return pl.pallas_call(
        spread_kernel,
        in_specs=[FULL, FULL] + [UNREAD] * len(before),
        out_specs=FULL,
        out_shape=like((parts,) + own.shape, jnp.bfloat16),
        compiler_params=grant(4),
        name="spread",
    )(own, theirs, *before)


def on_device(bits, low_frames, spatial_weight, temporal_weight, cotangent):
    low, cot = low_frames[0], cotangent[0]
    frames, rows_low, cols_low, chan = low.shape
    core = lax.axis_index(bits.core).astype(jnp.int32)
    odd = lax.axis_index(bits.axes["height"][-1]).astype(jnp.int32)
    mine, other = jnp.stack([core, odd]), jnp.stack([1 - core, odd])
    parts = 1 << len(bits.near)

    inner, outer, later = first_messages(mine, low, cot)
    later = bits.shift(later, "tm", -1)
    inner, outer = bits.pairs(inner, outer)
    order = jnp.asarray(side_order(rows_low, cols_low))
    low_in, ws, sort, turned, cot_side = load(low, cot, spatial_weight, temporal_weight, order)
    act, slope = forward(mine, low_in, inner, outer, ws)
    pg, ext, theirs = backward(
        other, low_in, inner, outer, act, slope, cot_side, later, turned, sort
    )
    theirs = bits.swap(theirs, bits.core)
    own, act, box = half_grads(mine, low_in, inner, outer, act, pg, ext)
    kept = add_halves(own, theirs)
    got = bits.exchange(kept.reshape(parts, -1, chan))
    edge, pg_inner, pg_outer = edges(mine, low_in, inner, outer, pg, kept)
    edge = bits.shift(edge, "tm", 1)
    pg_inner, pg_outer = bits.pairs(pg_inner, pg_outer)
    own_part = input_own(pg, box, ws, kept, low.shape)
    total, far = bits.far_sums(sum_parts(got, own_part))
    section_out, input_grad, done = finish(
        mine, own_part, ws, pg_inner, pg_outer, edge, act, temporal_weight, order, low, total
    )
    totals = spread(total, far, parts, done)
    half = bits.exchange(totals).reshape(kept.shape)
    theirs = bits.swap(half, bits.core)
    spatial_grad, temporal_grad = put(other, theirs, *put(mine, half))
    return section_out[None], input_grad[None], spatial_grad, temporal_grad


def solution(mesh):
    bits = Bits(mesh)
    block = P(*(bits.axes[name] for name in ("dp", "tm", "height")), None, None)
    return jax.shard_map(
        functools.partial(on_device, bits),
        mesh=bits.mesh,
        in_specs=(block, P(), P(), block),
        out_specs=(block, block, P(), P()),
        check_vma=False,
    )
```

```python
import functools

import jax
import jax.numpy as jnp
import numpy as np
from jax import lax
from jax.experimental import pallas as pl
from jax.experimental.pallas import tpu as pltpu
from jax.sharding import Mesh
from jax.sharding import PartitionSpec as P


class Bits:
    def __init__(self, mesh):
        self.axes = {}
        for name in mesh.axis_names:
            count = mesh.shape[name].bit_length() - 1
            self.axes[name] = tuple(f"{name}{bit}" for bit in reversed(range(count)))
        names = [bit for bits in self.axes.values() for bit in bits]
        self.mesh = Mesh(mesh.devices.reshape([2] * len(names)), tuple(names))
        self.core = next((n for n in names if self.same_chip(n)), self.axes["tm"][-1])
        others = [[b for b in reversed(bits) if b != self.core] for bits in self.axes.values()]
        turns = [bits[turn] for turn in range(len(names)) for bits in others if turn < len(bits)]
        self.near = [n for n in names if n in turns[:3]]
        self.far = turns[3:]

    def same_chip(self, name):
        at = [1 if n == name else 0 for n in self.mesh.axis_names]
        here = self.mesh.devices[tuple([0] * len(at))]
        there = self.mesh.devices[tuple(at)]
        return tuple(getattr(here, "coords", (0,))) == tuple(getattr(there, "coords", (1,)))

    def swap(self, block, axis):
        return lax.ppermute(block, axis, [(0, 1), (1, 0)])

    def shift(self, block, name, distance):
        axes = self.axes[name]
        devices = range(1 << len(axes))
        route = [(i - distance, i) for i in devices if i - distance in devices]
        return lax.ppermute(block, axes, route)

    def exchange(self, parts):
        return lax.all_to_all(parts, tuple(self.near), 0, 0, tiled=True)

    def pairs(self, inner, outer):
        axes = self.axes["height"]
        low = range(1, (1 << len(axes)) - 1, 2)
        route = [(i, i + 1) for i in low] + [(i + 1, i) for i in low]
        outer = lax.ppermute(outer, axes, route)
        return self.swap(inner, axes[-1]), outer

    def far_sums(self, total):
        for axis in self.far[:-1]:
            total = total.astype(jnp.float32) + self.swap(total, axis).astype(jnp.float32)
            total = lax.reduce_precision(total, 8, 7).astype(jnp.bfloat16)
        return total, self.swap(total, self.far[-1])


SIDES = ((0, 0), (0, 1), (1, 0), (1, 1))


def grant(mib):
    return pltpu.CompilerParams(vmem_limit_bytes=mib * 2**20)


def product(left, right):
    return jnp.dot(left, right, preferred_element_type=jnp.float32)


def product_nt(left, right):
    return lax.dot_general(left, right, (((1,), (1,)), ((), ())), preferred_element_type=jnp.float32)


def rows_at_once(rows_low, cols_low):
    return max(n for n in (1, 2, 4, 8) if rows_low % n == 0 and (n == 1 or 4 * n * cols_low <= 256))


def side_order(rows_low, cols_low):
    count = rows_at_once(rows_low, cols_low)
    size = 4 * count * cols_low
    at = np.arange(size).reshape(count, 2, cols_low, 2).transpose(1, 3, 0, 2).reshape(-1)
    return (at[:, None] == np.arange(size)[None, :]).astype(np.float32)


def column(rows, cols_low, chan):
    return lax.broadcasted_iota(jnp.int32, (rows // cols_low, cols_low, chan), 1).reshape(rows, chan)


def from_left(x, at):
    return jnp.where(at == 0, 0.0, pltpu.roll(x, 1, 0))


def from_right(x, at, last):
    return jnp.where(at == last, 0.0, pltpu.roll(x, x.shape[0] - 1, 0))


def sort_columns(source, target, cols_low, order):
    rows_low, chan = source.shape[0] // 2, source.shape[2]
    group = rows_at_once(rows_low, cols_low)
    span = group * cols_low
    for n in range(rows_low // group):
        block = source[2 * group * n : 2 * group * (n + 1)].reshape(4 * span, chan)
        block = product(order, block).astype(jnp.bfloat16).reshape(4, span, chan)
        target[:, n * span : (n + 1) * span, :] = block


def tall(place_ref, low_ref, inner_ref, outer_ref, frame, lanes=slice(None)):
    odd = place_ref[1] == 1
    inner, outer = inner_ref[frame, :, :, lanes], outer_ref[frame, :, :, lanes]
    up, down = jnp.where(odd, inner, outer), jnp.where(odd, outer, inner)
    return jnp.concatenate([up, low_ref[frame, :, :, lanes], down], axis=0)


def spatial(low, ws_ref):
    frames, rows_tall, cols_low, chan = low.shape
    rows_low = rows_tall - 2
    count = frames * rows_low * cols_low
    flat = low.reshape(-1, chan)
    rows = [[], []]
    for j in range(3):
        taps = [product(flat, ws_ref[i, j]).reshape(low.shape) for i in range(3)]
        even = taps[0][:, :rows_low] + (taps[1] + taps[2])[:, 1 : rows_low + 1]
        odd = (taps[0] + taps[1])[:, 1 : rows_low + 1] + taps[2][:, 2:]
        rows[0].append(even.reshape(count, chan))
        rows[1].append(odd.reshape(count, chan))
    at = column(count, cols_low, chan)
    for first, second, third in rows:
        yield from_left(first, at) + (second + third)
        yield (first + second) + from_right(third, at, cols_low - 1)


def forward_kernel(place_ref, low_ref, inner_ref, outer_ref, ws_ref, act_ref, slope_ref):
    frames, rows_low, cols_low, chan = low_ref.shape
    shape = (frames, rows_low * cols_low, chan)
    low = jnp.stack([tall(place_ref, low_ref, inner_ref, outer_ref, frame) for frame in range(frames)])
    for side, pre in enumerate(spatial(low, ws_ref)):
        sig = jax.nn.sigmoid(pre)
        act_ref[:, side] = (pre * sig).astype(jnp.bfloat16).reshape(shape)
        slope_ref[:, side] = (sig * (1.0 + pre * (1.0 - sig))).reshape(shape)


def half_sums(place_ref, low_ref, inner_ref, outer_ref, act_ref, pg_ref, ext_ref, out_ref):
    frames, rows_low, cols_low, chan = low_ref.shape
    count, half = rows_low * cols_low, chan // 2
    lanes = pl.ds(pl.multiple_of(place_ref[0] * half, half), half)
    lefts = [[] for _ in range(9)]
    acts = []
    at = column((rows_low + 2) * cols_low, cols_low, half)
    for frame in range(frames):
        low = tall(place_ref, low_ref, inner_ref, outer_ref, frame, lanes)
        wide = low.reshape(-1, half).astype(jnp.float32)
        moved = [from_left(wide, at), wide, from_right(wide, at, cols_low - 1)]
        turned = {}
        for dc in range(3):
            view = moved[dc].astype(jnp.bfloat16).reshape(low.shape)
            for dr in range(3):
                turned[dr - 1, dc - 1] = view[dr : dr + rows_low].reshape(count, half).T
        for i in range(3):
            for j in range(3):
                lefts[3 * i + j] += [turned[(a + i - 1) // 2, (b + j - 1) // 2] for a, b in SIDES]
        acts.append(act_ref[frame, :, :, lanes].reshape(4 * count, half).T)
    pg = pg_ref[...].reshape(frames * 4 * count, chan)
    left = jnp.concatenate([jnp.concatenate(left, axis=1) for left in lefts], axis=0)
    out_ref[:9] = product(left, pg).reshape(9, half, chan)
    act = jnp.concatenate(acts, axis=1)
    for k in range(3):
        out_ref[9 + k] = product(act, ext_ref[k : k + frames].reshape(frames * 4 * count, chan))


def half_kernel(place_ref, low_ref, inner_ref, outer_ref, act_ref, pg_ref, ext_ref, out_ref, act_out, box_ref, sem):
    copy = pltpu.make_async_copy(act_ref, act_out, sem)
    copy.start()
    for frame in range(box_ref.shape[0]):
        box_ref[frame] = sum(ext_ref[frame, side].astype(jnp.float32) for side in range(4))
    half_sums(place_ref, low_ref, inner_ref, outer_ref, act_ref, pg_ref, ext_ref, out_ref)
    copy.wait()


def backward_kernel(place_ref, low_ref, inner_ref, outer_ref, act_ref, slope_ref, cot_ref, later_ref, turned_ref, sort_ref,
                    pg_ref, ext_ref, out_ref):
    frames, _, count, chan = cot_ref.shape
    ext_ref[:frames] = cot_ref[...]
    for n in range(2):
        sort_columns(later_ref.at[n], ext_ref.at[frames + n], low_ref.shape[2], sort_ref[...])
    for frame in range(frames):
        cots = [ext_ref[frame + k].reshape(4 * count, chan) for k in range(3)]
        act_grad = product(jnp.concatenate(cots, axis=1), turned_ref[...])
        slope = slope_ref[frame].reshape(4 * count, chan)
        pg_ref[frame] = (act_grad * slope).astype(jnp.bfloat16).reshape(4, count, chan)
    half_sums(place_ref, low_ref, inner_ref, outer_ref, act_ref, pg_ref, ext_ref, out_ref)


SCALAR = pl.BlockSpec(memory_space=pltpu.SMEM)
UNREAD = pl.BlockSpec(memory_space=pl.ANY)


def like(shape, dtype):
    return jax.ShapeDtypeStruct(shape, dtype)


TOKEN = like((8, 128), jnp.float32)


def cost(units, mib):
    return pl.CostEstimate(flops=units * 2 * 2048 * 256 * 256, bytes_accessed=mib * 2**20, transcendentals=0)


def in_hbm(array):
    return pltpu.with_memory_space_constraint(array, pltpu.HBM)


FULL = pl.BlockSpec(memory_space=pltpu.VMEM)


def first_kernel(place_ref, low_ref, cot_ref, inner_ref, outer_ref, later_ref, sems):
    last = low_ref.shape[1] - 1
    odd = place_ref[1]
    copies = [
        (low_ref.at[:, pl.ds(last * (1 - odd), 1)], inner_ref),
        (low_ref.at[:, pl.ds(last * odd, 1)], outer_ref),
    ]
    copies += [(cot_ref.at[n, r], later_ref.at[n, r]) for n in range(2) for r in range(cot_ref.shape[1])]
    copies = [pltpu.make_async_copy(a, b, sems.at[n]) for n, (a, b) in enumerate(copies)]
    for copy in copies:
        copy.start()
    for copy in copies:
        copy.wait()


def first_messages(place, low, cot):
    row = like(low[:, :1].shape, low.dtype)
    return pl.pallas_call(
        first_kernel,
        in_specs=[SCALAR, UNREAD, UNREAD],
        out_specs=[FULL] * 3,
        out_shape=[row, row, like(cot[:2].shape, cot.dtype)],
        scratch_shapes=[pltpu.SemaphoreType.DMA((2 + 2 * cot.shape[1],))],
        compiler_params=grant(4),
        name="first_messages",
    )(place, in_hbm(low), in_hbm(cot))


def load_kernel(low_hbm, cot_hbm, ws_hbm, wt_hbm, sort_hbm,
                low_ref, ws_ref, sort_ref, turned_ref, side_ref, cot_ref, wide_ref, wt_ref, sems):
    frames, cols_low, chan = low_ref.shape[0], low_ref.shape[2], low_ref.shape[3]
    pairs = [(sort_hbm, wide_ref)] + [(cot_hbm.at[n], cot_ref.at[n]) for n in range(frames)]
    pairs += [(wt_hbm.at[k], wt_ref.at[k]) for k in range(3)] + [(low_hbm, low_ref)]
    pairs += [(ws_hbm.at[i, j], ws_ref.at[i, j]) for i in range(3) for j in range(3)]
    copies = [pltpu.make_async_copy(a, b, sems.at[n]) for n, (a, b) in enumerate(pairs)]
    for copy in copies:
        copy.start()
    copies[0].wait()
    sort_ref[...] = wide_ref[...].astype(jnp.bfloat16)
    for n in range(frames):
        copies[1 + n].wait()
        sort_columns(cot_ref.at[n], side_ref.at[n], cols_low, sort_ref[...])
    for k in range(3):
        copies[1 + frames + k].wait()
        turned_ref[k * chan : (k + 1) * chan] = wt_ref[k].T
    for copy in copies[4 + frames :]:
        copy.wait()


def load(low, cot, ws, wt, sort):
    frames, rows_low, cols_low, chan = low.shape
    order = like(sort.shape, jnp.bfloat16)
    shapes = [low, ws, order, like((3 * chan, chan), wt.dtype),
              like((frames, 4, rows_low * cols_low, chan), jnp.bfloat16)]
    return pl.pallas_call(
        load_kernel,
        in_specs=[UNREAD] * 5,
        out_specs=[FULL] * 5,
        out_shape=[like(a.shape, a.dtype) for a in shapes],
        scratch_shapes=[pltpu.VMEM(cot.shape, cot.dtype), pltpu.VMEM(sort.shape, sort.dtype), pltpu.VMEM(wt.shape, wt.dtype),
                        pltpu.SemaphoreType.DMA((frames + 14,))],
        compiler_params=grant(14),
        cost_estimate=cost(2, 4),
        name="load",
    )(*[in_hbm(a) for a in (low, cot, ws, wt, sort)])


def forward(place, low, inner, outer, ws):
    frames, rows_low, cols_low, chan = low.shape
    side = (frames, 4, rows_low * cols_low, chan)
    return pl.pallas_call(
        forward_kernel,
        in_specs=[SCALAR] + [FULL] * 4,
        out_specs=[FULL] * 2,
        out_shape=[like(side, jnp.bfloat16), like(side, jnp.float32)],
        compiler_params=grant(20),
        cost_estimate=cost(10, 8),
        name="forward",
    )(place, low, inner, outer, ws)


def edges_kernel(place_ref, low_ref, inner_ref, outer_ref, pg_ref, _, tall_ref, pg_inner, pg_outer):
    cols_low = low_ref.shape[2]
    first = low_ref.shape[0] - tall_ref.shape[0]
    for n in range(tall_ref.shape[0]):
        tall_ref[n] = tall(place_ref, low_ref, inner_ref, outer_ref, first + n)
    odd = place_ref[1] == 1
    top, bottom = pg_ref[:, :2, :cols_low, :], pg_ref[:, 2:, -cols_low:, :]
    pg_inner[...] = jnp.where(odd, top, bottom)
    pg_outer[...] = jnp.where(odd, bottom, top)


def edges(place, low, inner, outer, pg, before):
    frames, rows_low, cols_low, chan = low.shape
    full = pl.BlockSpec(memory_space=pltpu.VMEM)
    rows = like((frames, 2, cols_low, chan), jnp.bfloat16)
    return pl.pallas_call(
        edges_kernel,
        in_specs=[SCALAR, full, full, full, full, UNREAD],
        out_specs=[full] * 3,
        out_shape=[like((2, rows_low + 2, cols_low, chan), jnp.bfloat16), rows, rows],
        compiler_params=grant(8),
        name="edges",
    )(place, low, inner, outer, pg, before)


def backward(place, low, inner, outer, act, slope, cot, later, turned, sort):
    frames, _, count, chan = act.shape
    ext = (frames + 2,) + act.shape[1:]
    return pl.pallas_call(
        backward_kernel,
        in_specs=[SCALAR] + [FULL] * 9,
        out_specs=[FULL] * 3,
        out_shape=[like(act.shape, jnp.bfloat16), like(ext, jnp.bfloat16), like((12, chan // 2, chan), jnp.float32)],
        compiler_params=grant(24),
        cost_estimate=cost(15, 10),
        name="backward",
    )(place, low, inner, outer, act, slope, cot, later, turned, sort)


def half_grads(place, low, inner, outer, act, pg, ext):
    chan = low.shape[-1]
    return pl.pallas_call(
        half_kernel,
        in_specs=[SCALAR] + [FULL] * 6,
        out_specs=[FULL, HBM, FULL],
        out_shape=[like((12, chan // 2, chan), jnp.float32), pltpu.HBM(act.shape, act.dtype),
                   like((act.shape[0],) + act.shape[2:], jnp.float32)],
        scratch_shapes=[pltpu.SemaphoreType.DMA],
        compiler_params=grant(20),
        cost_estimate=cost(10, 6),
        name="half_grads",
    )(place, low, inner, outer, act, pg, ext)


HBM = pl.BlockSpec(memory_space=pltpu.HBM)


def split(value):
    high = value.astype(jnp.bfloat16)
    return high, (value - high.astype(jnp.float32)).astype(jnp.bfloat16)


def column_pair(first, second, j, at, last):
    if j == 0:
        return second + from_right(first, at, last)
    if j == 1:
        return first + second
    return first + from_left(second, at)


def input_kernel(pg_ref, box_ref, ws_ref, _, out_ref):
    frames, _, count, chan = pg_ref.shape
    cols_low = out_ref.shape[2]
    rows_low = count // cols_low
    at = column(count, cols_low, chan)
    turned = jnp.concatenate([ws_ref[i, j].T for j in range(3) for i in range(3)], axis=0)
    for frame in range(frames):
        own = [pg_ref[frame, side].astype(jnp.float32) for side in range(4)]
        zero = jnp.zeros((1, cols_low, chan), jnp.float32)
        parts = []
        for j in range(3):
            even = column_pair(own[0], own[1], j, at, cols_low - 1).reshape(rows_low, cols_low, chan)
            odd = column_pair(own[2], own[3], j, at, cols_low - 1).reshape(rows_low, cols_low, chan)
            below = jnp.concatenate([even[1:], zero], axis=0)
            above = jnp.concatenate([zero, odd[:-1]], axis=0)
            for value in (odd + below, even + odd, above + even):
                parts.append(jnp.concatenate(split(value.reshape(count, chan)), axis=0))
        sums = product(jnp.concatenate(parts, axis=1), turned)
        total = box_ref[frame] + (sums[:count] + sums[count:])
        out_ref[frame] = total.reshape(rows_low, cols_low, chan)


def input_own(pg, box, ws, before, low_shape):
    return pl.pallas_call(
        input_kernel,
        in_specs=[FULL] * 3 + [UNREAD],
        out_specs=FULL,
        out_shape=like(low_shape, jnp.float32),
        compiler_params=grant(16),
        cost_estimate=cost(6, 4),
        name="input_own",
    )(pg, box, ws, before)


def finish_kernel(place_ref, own_ref, ws_ref, sort_ref, low_ref, inner_hbm, outer_hbm, edge_hbm, act_hbm, wt_hbm, _,
                  section_ref, input_ref, token_ref,
                  inner_ref, outer_ref, edge_ref, act_ref, wt_ref, earlier, held, input_held, sems):
    frames, rows_low, cols_low, chan = low_ref.shape
    group = rows_at_once(rows_low, cols_low)
    span, count = group * cols_low, rows_low * cols_low
    pairs = [(inner_hbm, inner_ref), (outer_hbm, outer_ref)]
    pairs += [(edge_hbm, edge_ref), (wt_hbm, wt_ref)]
    pairs += [(act_hbm.at[n], act_ref.at[n]) for n in range(frames)]
    copies = [pltpu.make_async_copy(a, b, sems.at[n]) for n, (a, b) in enumerate(pairs)]
    for copy in copies:
        copy.start()
    token_ref[...] = jnp.zeros_like(token_ref)

    for copy in copies[:2]:
        copy.wait()
    odd_place = place_ref[1] == 1
    flat = (frames * cols_low, chan)
    at = column(flat[0], cols_low, chan)
    inner = [inner_ref[:, b].reshape(flat).astype(jnp.float32) for b in range(2)]
    outer = [outer_ref[:, b].reshape(flat).astype(jnp.float32) for b in range(2)]
    above = [jnp.where(odd_place, inner[b], outer[b]) for b in range(2)]
    below = [jnp.where(odd_place, outer[b], inner[b]) for b in range(2)]
    terms = []
    for (first, second), i in ((above, 2), (below, 0)):
        parts = [split(column_pair(first, second, j, at, cols_low - 1)) for j in range(3)]
        parts = jnp.concatenate([jnp.concatenate(part, axis=0) for part in parts], axis=1)
        sums = product(parts, jnp.concatenate([ws_ref[i, j].T for j in range(3)], axis=0))
        terms.append((sums[: flat[0]] + sums[flat[0] :]).reshape(frames, cols_low, chan))
    for row in range(rows_low):
        value = own_ref[:, row]
        if row == 0:
            value = value + terms[0]
        if row == rows_low - 1:
            value = value + terms[1]
        input_held[:, row] = value.astype(jnp.bfloat16)
    leaving = [pltpu.make_async_copy(input_held, input_ref, sems.at[len(copies)])]
    leaving[0].start()

    for copy in copies[2:3]:
        copy.wait()
    for side, pre in enumerate(spatial(edge_ref[...], ws_ref)):
        earlier[:, side] = (pre * jax.nn.sigmoid(pre)).astype(jnp.bfloat16).reshape(2, count, chan)
    for copy in copies[3:]:
        copy.wait()
    merge = sort_ref[...].T
    wt = wt_ref[...].reshape(3 * chan, chan)
    for frame in range(frames):
        acts = [act_ref[frame - k] if frame >= k else earlier[frame - k + 2] for k in range(3)]
        acts = jnp.concatenate([act.reshape(4 * count, chan) for act in acts], axis=1)
        low = low_ref[frame].reshape(1, count, chan).astype(jnp.float32)
        mixed = (product(acts, wt).reshape(4, count, chan) + low).astype(jnp.bfloat16)
        for n in range(rows_low // group):
            block = mixed[:, n * span : (n + 1) * span].reshape(4 * span, chan)
            block = product(merge, block).astype(jnp.bfloat16)
            held[frame, 2 * group * n : 2 * group * (n + 1)] = block.reshape(2 * group, 2 * cols_low, chan)
        leaving.append(pltpu.make_async_copy(held.at[frame], section_ref.at[frame], sems.at[len(copies) + 1 + frame]))
        leaving[-1].start()
    for copy in leaving:
        copy.wait()


def finish(place, own, ws, sort, low, inner, outer, edge, act, wt, before):
    frames, rows_low, cols_low, chan = low.shape
    out = (frames, 2 * rows_low, 2 * cols_low, chan)
    fetched = [inner, outer, edge, act, wt]
    return pl.pallas_call(
        finish_kernel,
        in_specs=[SCALAR] + [FULL] * 4 + [HBM] * 5 + [UNREAD],
        out_specs=[HBM, HBM, FULL],
        out_shape=[like(out, jnp.bfloat16), like(low.shape, jnp.bfloat16), TOKEN],
        scratch_shapes=[pltpu.VMEM(a.shape, a.dtype) for a in fetched]
        + [pltpu.VMEM((2,) + act.shape[1:], act.dtype), pltpu.VMEM(out, jnp.bfloat16),
           pltpu.VMEM(low.shape, jnp.bfloat16), pltpu.SemaphoreType.DMA((7 + 2 * frames,))],
        compiler_params=grant(16),
        cost_estimate=cost(8, 4),
        name="finish",
    )(place, own, ws, sort, low, inner, outer, edge, in_hbm(act), in_hbm(wt), before)


def put_kernel(place_ref, half_ref, *refs):
    spatial_ref, temporal_ref, wide, sems = refs[-4:]
    taps, half, _ = half_ref.shape
    to = pl.ds(pl.multiple_of(place_ref[0] * half, half), half)
    copies = []
    for tap in range(taps):
        wide[tap] = half_ref[tap].astype(jnp.float32)
        if tap < 9:
            target = spatial_ref.at[tap // 3, tap % 3, to]
        else:
            target = temporal_ref.at[tap - 9, to]
        copies.append(pltpu.make_async_copy(wide.at[tap], target, sems.at[tap]))
        copies[-1].start()
    for copy in copies:
        copy.wait()


def put(place, half, *done):
    chan = half.shape[-1]
    return pl.pallas_call(
        put_kernel,
        in_specs=[SCALAR, FULL] + [HBM] * len(done),
        out_specs=[HBM, HBM],
        out_shape=[like((3, 3, chan, chan), jnp.float32), like((3, chan, chan), jnp.float32)],
        input_output_aliases={2 + n: n for n in range(len(done))},
        scratch_shapes=[pltpu.VMEM((12, chan // 2, chan), jnp.float32), pltpu.SemaphoreType.DMA((12,))],
        compiler_params=grant(6),
        name="put",
    )(place, half, *done)


def add_kernel(mine_ref, theirs_ref, out_ref):
    out_ref[...] = (mine_ref[...] + theirs_ref[...]).astype(jnp.bfloat16)


def add_halves(mine, theirs):
    full = pl.BlockSpec(memory_space=pltpu.VMEM)
    return pl.pallas_call(
        add_kernel,
        in_specs=[full, full],
        out_specs=full,
        out_shape=like(mine.shape, jnp.bfloat16),
        compiler_params=grant(8),
        name="add_halves",
    )(mine, theirs)


def sum_kernel(got_ref, _, out_ref):
    total = got_ref[0].astype(jnp.float32)
    for n in range(1, got_ref.shape[0]):
        total = total + got_ref[n].astype(jnp.float32)
    out_ref[...] = total.astype(jnp.bfloat16)


def sum_parts(got, before):
    return pl.pallas_call(
        sum_kernel,
        in_specs=[FULL, UNREAD],
        out_specs=FULL,
        out_shape=like(got.shape[1:], jnp.bfloat16),
        compiler_params=grant(4),
        name="sum_parts",
    )(got, before)


def spread_kernel(own_ref, theirs_ref, *refs):
    total = (own_ref[...].astype(jnp.float32) + theirs_ref[...].astype(jnp.float32)).astype(jnp.bfloat16)
    for n in range(refs[-1].shape[0]):
        refs[-1][n] = total


def spread(own, theirs, parts, *before):
    return pl.pallas_call(
        spread_kernel,
        in_specs=[FULL, FULL] + [UNREAD] * len(before),
        out_specs=FULL,
        out_shape=like((parts,) + own.shape, jnp.bfloat16),
        compiler_params=grant(4),
        name="spread",
    )(own, theirs, *before)


def on_device(bits, low_frames, spatial_weight, temporal_weight, cotangent):
    low, cot = low_frames[0], cotangent[0]
    frames, rows_low, cols_low, chan = low.shape
    core = lax.axis_index(bits.core).astype(jnp.int32)
    odd = lax.axis_index(bits.axes["height"][-1]).astype(jnp.int32)
    mine, other = jnp.stack([core, odd]), jnp.stack([1 - core, odd])
    parts = 1 << len(bits.near)

    inner, outer, later = first_messages(mine, low, cot)
    later = bits.shift(later, "tm", -1)
    inner, outer = bits.pairs(inner, outer)
    order = jnp.asarray(side_order(rows_low, cols_low))
    low_in, ws, sort, turned, cot_side = load(low, cot, spatial_weight, temporal_weight, order)
    act, slope = forward(mine, low_in, inner, outer, ws)
    pg, ext, theirs = backward(
        other, low_in, inner, outer, act, slope, cot_side, later, turned, sort
    )
    theirs = bits.swap(theirs, bits.core)
    own, act, box = half_grads(mine, low_in, inner, outer, act, pg, ext)
    kept = add_halves(own, theirs)
    got = bits.exchange(kept.reshape(parts, -1, chan))
    edge, pg_inner, pg_outer = edges(mine, low_in, inner, outer, pg, kept)
    edge = bits.shift(edge, "tm", 1)
    pg_inner, pg_outer = bits.pairs(pg_inner, pg_outer)
    own_part = input_own(pg, box, ws, kept, low.shape)
    total, far = bits.far_sums(sum_parts(got, own_part))
    section_out, input_grad, done = finish(
        mine, own_part, ws, sort, low_in, pg_inner, pg_outer, edge, act, temporal_weight, total
    )
    totals = spread(total, far, parts, done)
    half = bits.exchange(totals).reshape(kept.shape)
    theirs = bits.swap(half, bits.core)
    spatial_grad, temporal_grad = put(other, theirs, *put(mine, half))
    return section_out[None], input_grad[None], spatial_grad, temporal_grad


def solution(mesh):
    bits = Bits(mesh)
    block = P(*(bits.axes[name] for name in ("dp", "tm", "height")), None, None)
    return jax.shard_map(
        functools.partial(on_device, bits),
        mesh=bits.mesh,
        in_specs=(block, P(), P(), block),
        out_specs=(block, block, P(), P()),
        check_vma=False,
    )
```

```python
import functools

import jax
import jax.numpy as jnp
import numpy as np
from jax import lax
from jax.experimental import pallas as pl
from jax.experimental.pallas import tpu as pltpu
from jax.sharding import Mesh
from jax.sharding import PartitionSpec as P


class Bits:
    def __init__(self, mesh):
        self.axes = {}
        for name in mesh.axis_names:
            count = mesh.shape[name].bit_length() - 1
            self.axes[name] = tuple(f"{name}{bit}" for bit in reversed(range(count)))
        names = [bit for bits in self.axes.values() for bit in bits]
        self.mesh = Mesh(mesh.devices.reshape([2] * len(names)), tuple(names))
        self.core = next((n for n in names if self.same_chip(n)), self.axes["tm"][-1])
        others = [[b for b in reversed(bits) if b != self.core] for bits in self.axes.values()]
        turns = [bits[turn] for turn in range(len(names)) for bits in others if turn < len(bits)]
        self.near = [n for n in names if n in turns[:3]]
        self.far = turns[3:]

    def same_chip(self, name):
        at = [1 if n == name else 0 for n in self.mesh.axis_names]
        here = self.mesh.devices[tuple([0] * len(at))]
        there = self.mesh.devices[tuple(at)]
        return tuple(getattr(here, "coords", (0,))) == tuple(getattr(there, "coords", (1,)))

    def swap(self, block, axis):
        return lax.ppermute(block, axis, [(0, 1), (1, 0)])

    def shift(self, block, name, distance):
        axes = self.axes[name]
        devices = range(1 << len(axes))
        route = [(i - distance, i) for i in devices if i - distance in devices]
        return lax.ppermute(block, axes, route)

    def exchange(self, parts):
        return lax.all_to_all(parts, tuple(self.near), 0, 0, tiled=True)

    def pairs(self, inner, outer):
        axes = self.axes["height"]
        low = range(1, (1 << len(axes)) - 1, 2)
        route = [(i, i + 1) for i in low] + [(i + 1, i) for i in low]
        outer = lax.ppermute(outer, axes, route)
        return self.swap(inner, axes[-1]), outer

    def far_sums(self, total):
        for axis in self.far[:-1]:
            total = total.astype(jnp.float32) + self.swap(total, axis).astype(jnp.float32)
            total = lax.reduce_precision(total, 8, 7).astype(jnp.bfloat16)
        return total, self.swap(total, self.far[-1])


SIDES = ((0, 0), (0, 1), (1, 0), (1, 1))


def grant(mib):
    return pltpu.CompilerParams(vmem_limit_bytes=mib * 2**20)


def product(left, right):
    return jnp.dot(left, right, preferred_element_type=jnp.float32)


def product_nt(left, right):
    return lax.dot_general(left, right, (((1,), (1,)), ((), ())), preferred_element_type=jnp.float32)


def rows_at_once(rows_low, cols_low):
    return max(n for n in (1, 2, 4, 8) if rows_low % n == 0 and (n == 1 or 4 * n * cols_low <= 256))


def side_order(rows_low, cols_low):
    count = rows_at_once(rows_low, cols_low)
    size = 4 * count * cols_low
    at = np.arange(size).reshape(count, 2, cols_low, 2).transpose(1, 3, 0, 2).reshape(-1)
    return (at[:, None] == np.arange(size)[None, :]).astype(np.float32)


def column(rows, cols_low, chan):
    return lax.broadcasted_iota(jnp.int32, (rows // cols_low, cols_low, chan), 1).reshape(rows, chan)


def from_left(x, at):
    return jnp.where(at == 0, 0.0, pltpu.roll(x, 1, 0))


def from_right(x, at, last):
    return jnp.where(at == last, 0.0, pltpu.roll(x, x.shape[0] - 1, 0))


def sort_columns(source, target, cols_low, order):
    rows_low, chan = source.shape[0] // 2, source.shape[2]
    group = rows_at_once(rows_low, cols_low)
    span = group * cols_low
    for n in range(rows_low // group):
        block = source[2 * group * n : 2 * group * (n + 1)].reshape(4 * span, chan)
        block = product(order, block).astype(jnp.bfloat16).reshape(4, span, chan)
        target[:, n * span : (n + 1) * span, :] = block


def tall(place_ref, low_ref, inner_ref, outer_ref, frame, lanes=slice(None)):
    odd = place_ref[1] == 1
    inner, outer = inner_ref[frame, :, :, lanes], outer_ref[frame, :, :, lanes]
    up, down = jnp.where(odd, inner, outer), jnp.where(odd, outer, inner)
    return jnp.concatenate([up, low_ref[frame, :, :, lanes], down], axis=0)


def spatial(low, ws_ref):
    frames, rows_tall, cols_low, chan = low.shape
    rows_low = rows_tall - 2
    count = frames * rows_low * cols_low
    flat = low.reshape(-1, chan)
    rows = [[], []]
    for j in range(3):
        taps = [product(flat, ws_ref[i, j]).reshape(low.shape) for i in range(3)]
        even = taps[0][:, :rows_low] + (taps[1] + taps[2])[:, 1 : rows_low + 1]
        odd = (taps[0] + taps[1])[:, 1 : rows_low + 1] + taps[2][:, 2:]
        rows[0].append(even.reshape(count, chan))
        rows[1].append(odd.reshape(count, chan))
    at = column(count, cols_low, chan)
    for first, second, third in rows:
        yield from_left(first, at) + (second + third)
        yield (first + second) + from_right(third, at, cols_low - 1)


def forward_kernel(place_ref, low_ref, inner_ref, outer_ref, ws_ref, act_ref, slope_ref):
    frames, rows_low, cols_low, chan = low_ref.shape
    shape = (frames, rows_low * cols_low, chan)
    low = jnp.stack([tall(place_ref, low_ref, inner_ref, outer_ref, frame) for frame in range(frames)])
    for side, pre in enumerate(spatial(low, ws_ref)):
        sig = jax.nn.sigmoid(pre)
        act_ref[:, side] = (pre * sig).astype(jnp.bfloat16).reshape(shape)
        slope_ref[:, side] = (sig * (1.0 + pre * (1.0 - sig))).reshape(shape)


def half_sums(place_ref, low_ref, inner_ref, outer_ref, act_ref, pg_ref, ext_ref, out_ref):
    frames, rows_low, cols_low, chan = low_ref.shape
    count, half = rows_low * cols_low, chan // 2
    lanes = pl.ds(pl.multiple_of(place_ref[0] * half, half), half)
    lefts = [[] for _ in range(9)]
    acts = []
    at = column((rows_low + 2) * cols_low, cols_low, half)
    for frame in range(frames):
        low = tall(place_ref, low_ref, inner_ref, outer_ref, frame, lanes)
        wide = low.reshape(-1, half).astype(jnp.float32)
        moved = [from_left(wide, at), wide, from_right(wide, at, cols_low - 1)]
        turned = {}
        for dc in range(3):
            view = moved[dc].astype(jnp.bfloat16).reshape(low.shape)
            for dr in range(3):
                turned[dr - 1, dc - 1] = view[dr : dr + rows_low].reshape(count, half).T
        for i in range(3):
            for j in range(3):
                lefts[3 * i + j] += [turned[(a + i - 1) // 2, (b + j - 1) // 2] for a, b in SIDES]
        acts.append(act_ref[frame, :, :, lanes].reshape(4 * count, half).T)
    pg = pg_ref[...].reshape(frames * 4 * count, chan)
    left = jnp.concatenate([jnp.concatenate(left, axis=1) for left in lefts], axis=0)
    out_ref[:9] = product(left, pg).reshape(9, half, chan)
    act = jnp.concatenate(acts, axis=1)
    for k in range(3):
        out_ref[9 + k] = product(act, ext_ref[k : k + frames].reshape(frames * 4 * count, chan))


def half_kernel(place_ref, low_ref, inner_ref, outer_ref, act_ref, pg_ref, ext_ref, out_ref, act_out, box_ref, sem):
    copy = pltpu.make_async_copy(act_ref, act_out, sem)
    copy.start()
    for frame in range(box_ref.shape[0]):
        box_ref[frame] = sum(ext_ref[frame, side].astype(jnp.float32) for side in range(4))
    half_sums(place_ref, low_ref, inner_ref, outer_ref, act_ref, pg_ref, ext_ref, out_ref)
    copy.wait()


def backward_kernel(place_ref, low_ref, inner_ref, outer_ref, act_ref, slope_ref, cot_ref, later_ref, turned_ref, sort_ref,
                    pg_ref, ext_ref, out_ref):
    frames, _, count, chan = cot_ref.shape
    ext_ref[:frames] = cot_ref[...]
    for n in range(2):
        sort_columns(later_ref.at[n], ext_ref.at[frames + n], low_ref.shape[2], sort_ref[...])
    for frame in range(frames):
        cots = [ext_ref[frame + k].reshape(4 * count, chan) for k in range(3)]
        act_grad = product(jnp.concatenate(cots, axis=1), turned_ref[...])
        slope = slope_ref[frame].reshape(4 * count, chan)
        pg_ref[frame] = (act_grad * slope).astype(jnp.bfloat16).reshape(4, count, chan)
    half_sums(place_ref, low_ref, inner_ref, outer_ref, act_ref, pg_ref, ext_ref, out_ref)


SCALAR = pl.BlockSpec(memory_space=pltpu.SMEM)
UNREAD = pl.BlockSpec(memory_space=pl.ANY)


def like(shape, dtype):
    return jax.ShapeDtypeStruct(shape, dtype)


TOKEN = like((8, 128), jnp.float32)


def cost(units, mib):
    return pl.CostEstimate(flops=units * 2 * 2048 * 256 * 256, bytes_accessed=mib * 2**20, transcendentals=0)


def in_hbm(array):
    return pltpu.with_memory_space_constraint(array, pltpu.HBM)


FULL = pl.BlockSpec(memory_space=pltpu.VMEM)


def first_kernel(place_ref, low_ref, cot_ref, inner_ref, outer_ref, later_ref, sems):
    last = low_ref.shape[1] - 1
    odd = place_ref[1]
    copies = [
        (low_ref.at[:, pl.ds(last * (1 - odd), 1)], inner_ref),
        (low_ref.at[:, pl.ds(last * odd, 1)], outer_ref),
    ]
    copies += [(cot_ref.at[0:2], later_ref)]
    copies = [pltpu.make_async_copy(a, b, sems.at[n]) for n, (a, b) in enumerate(copies)]
    for copy in copies:
        copy.start()
    for copy in copies:
        copy.wait()


def first_messages(place, low, cot):
    row = like(low[:, :1].shape, low.dtype)
    return pl.pallas_call(
        first_kernel,
        in_specs=[SCALAR, UNREAD, UNREAD],
        out_specs=[FULL] * 3,
        out_shape=[row, row, like(cot[:2].shape, cot.dtype)],
        scratch_shapes=[pltpu.SemaphoreType.DMA((3,))],
        compiler_params=grant(4),
        name="first_messages",
    )(place, in_hbm(low), in_hbm(cot))


def load_kernel(low_hbm, cot_hbm, ws_hbm, wt_hbm, sort_hbm,
                low_ref, ws_ref, sort_ref, turned_ref, side_ref, cot_ref, wide_ref, wt_ref, sems):
    frames, cols_low, chan = low_ref.shape[0], low_ref.shape[2], low_ref.shape[3]
    pairs = [(sort_hbm, wide_ref)] + [(cot_hbm.at[n], cot_ref.at[n]) for n in range(frames)]
    pairs += [(wt_hbm.at[k], wt_ref.at[k]) for k in range(3)] + [(low_hbm, low_ref)]
    pairs += [(ws_hbm.at[i, j], ws_ref.at[i, j]) for i in range(3) for j in range(3)]
    copies = [pltpu.make_async_copy(a, b, sems.at[n]) for n, (a, b) in enumerate(pairs)]
    for copy in copies:
        copy.start()
    copies[0].wait()
    sort_ref[...] = wide_ref[...].astype(jnp.bfloat16)
    for n in range(frames):
        copies[1 + n].wait()
        sort_columns(cot_ref.at[n], side_ref.at[n], cols_low, sort_ref[...])
    for k in range(3):
        copies[1 + frames + k].wait()
        turned_ref[k * chan : (k + 1) * chan] = wt_ref[k].T
    for copy in copies[4 + frames :]:
        copy.wait()


def load(low, cot, ws, wt, sort):
    frames, rows_low, cols_low, chan = low.shape
    order = like(sort.shape, jnp.bfloat16)
    shapes = [low, ws, order, like((3 * chan, chan), wt.dtype),
              like((frames, 4, rows_low * cols_low, chan), jnp.bfloat16)]
    return pl.pallas_call(
        load_kernel,
        in_specs=[UNREAD] * 5,
        out_specs=[FULL] * 5,
        out_shape=[like(a.shape, a.dtype) for a in shapes],
        scratch_shapes=[pltpu.VMEM(cot.shape, cot.dtype), pltpu.VMEM(sort.shape, sort.dtype), pltpu.VMEM(wt.shape, wt.dtype),
                        pltpu.SemaphoreType.DMA((frames + 14,))],
        compiler_params=grant(14),
        cost_estimate=cost(2, 4),
        name="load",
    )(*[in_hbm(a) for a in (low, cot, ws, wt, sort)])


def forward(place, low, inner, outer, ws):
    frames, rows_low, cols_low, chan = low.shape
    side = (frames, 4, rows_low * cols_low, chan)
    return pl.pallas_call(
        forward_kernel,
        in_specs=[SCALAR] + [FULL] * 4,
        out_specs=[FULL] * 2,
        out_shape=[like(side, jnp.bfloat16), like(side, jnp.float32)],
        compiler_params=grant(20),
        cost_estimate=cost(10, 8),
        name="forward",
    )(place, low, inner, outer, ws)


def edges_kernel(place_ref, low_ref, inner_ref, outer_ref, pg_ref, _, tall_ref, pg_inner, pg_outer):
    cols_low = low_ref.shape[2]
    first = low_ref.shape[0] - tall_ref.shape[0]
    for n in range(tall_ref.shape[0]):
        tall_ref[n] = tall(place_ref, low_ref, inner_ref, outer_ref, first + n)
    odd = place_ref[1] == 1
    top, bottom = pg_ref[:, :2, :cols_low, :], pg_ref[:, 2:, -cols_low:, :]
    pg_inner[...] = jnp.where(odd, top, bottom)
    pg_outer[...] = jnp.where(odd, bottom, top)


def edges(place, low, inner, outer, pg, before):
    frames, rows_low, cols_low, chan = low.shape
    full = pl.BlockSpec(memory_space=pltpu.VMEM)
    rows = like((frames, 2, cols_low, chan), jnp.bfloat16)
    return pl.pallas_call(
        edges_kernel,
        in_specs=[SCALAR, full, full, full, full, UNREAD],
        out_specs=[full] * 3,
        out_shape=[like((2, rows_low + 2, cols_low, chan), jnp.bfloat16), rows, rows],
        compiler_params=grant(8),
        name="edges",
    )(place, low, inner, outer, pg, before)


def backward(place, low, inner, outer, act, slope, cot, later, turned, sort):
    frames, _, count, chan = act.shape
    ext = (frames + 2,) + act.shape[1:]
    return pl.pallas_call(
        backward_kernel,
        in_specs=[SCALAR] + [FULL] * 9,
        out_specs=[FULL] * 3,
        out_shape=[like(act.shape, jnp.bfloat16), like(ext, jnp.bfloat16), like((12, chan // 2, chan), jnp.float32)],
        compiler_params=grant(24),
        cost_estimate=cost(15, 10),
        name="backward",
    )(place, low, inner, outer, act, slope, cot, later, turned, sort)


def half_grads(place, low, inner, outer, act, pg, ext):
    chan = low.shape[-1]
    return pl.pallas_call(
        half_kernel,
        in_specs=[SCALAR] + [FULL] * 6,
        out_specs=[FULL, HBM, FULL],
        out_shape=[like((12, chan // 2, chan), jnp.float32), pltpu.HBM(act.shape, act.dtype),
                   like((act.shape[0],) + act.shape[2:], jnp.float32)],
        scratch_shapes=[pltpu.SemaphoreType.DMA],
        compiler_params=grant(20),
        cost_estimate=cost(10, 6),
        name="half_grads",
    )(place, low, inner, outer, act, pg, ext)


HBM = pl.BlockSpec(memory_space=pltpu.HBM)


def split(value):
    high = value.astype(jnp.bfloat16)
    return high, (value - high.astype(jnp.float32)).astype(jnp.bfloat16)


def column_pair(first, second, j, at, last):
    if j == 0:
        return second + from_right(first, at, last)
    if j == 1:
        return first + second
    return first + from_left(second, at)


def input_kernel(pg_ref, box_ref, ws_ref, _, out_ref):
    frames, _, count, chan = pg_ref.shape
    cols_low = out_ref.shape[2]
    rows_low = count // cols_low
    at = column(count, cols_low, chan)
    turned = jnp.concatenate([ws_ref[i, j].T for j in range(3) for i in range(3)], axis=0)
    for frame in range(frames):
        own = [pg_ref[frame, side].astype(jnp.float32) for side in range(4)]
        zero = jnp.zeros((1, cols_low, chan), jnp.float32)
        parts = []
        for j in range(3):
            even = column_pair(own[0], own[1], j, at, cols_low - 1).reshape(rows_low, cols_low, chan)
            odd = column_pair(own[2], own[3], j, at, cols_low - 1).reshape(rows_low, cols_low, chan)
            below = jnp.concatenate([even[1:], zero], axis=0)
            above = jnp.concatenate([zero, odd[:-1]], axis=0)
            for value in (odd + below, even + odd, above + even):
                parts.append(jnp.concatenate(split(value.reshape(count, chan)), axis=0))
        sums = product(jnp.concatenate(parts, axis=1), turned)
        total = box_ref[frame] + (sums[:count] + sums[count:])
        out_ref[frame] = total.reshape(rows_low, cols_low, chan)


def input_own(pg, box, ws, before, low_shape):
    return pl.pallas_call(
        input_kernel,
        in_specs=[FULL] * 3 + [UNREAD],
        out_specs=FULL,
        out_shape=like(low_shape, jnp.float32),
        compiler_params=grant(16),
        cost_estimate=cost(6, 4),
        name="input_own",
    )(pg, box, ws, before)


def finish_kernel(place_ref, own_ref, ws_ref, inner_hbm, outer_hbm, edge_hbm, act_hbm, wt_hbm, sort_hbm, low_hbm, _,
                  section_ref, input_ref, token_ref,
                  inner_ref, outer_ref, edge_ref, act_ref, wt_ref, wide_ref, low_ref, earlier, held, input_held, sems):
    frames, rows_low, cols_low, chan = low_ref.shape
    group = rows_at_once(rows_low, cols_low)
    span, count = group * cols_low, rows_low * cols_low
    pairs = [(inner_hbm, inner_ref), (outer_hbm, outer_ref)]
    pairs += [(edge_hbm, edge_ref), (wt_hbm, wt_ref)]
    pairs += [(act_hbm.at[n], act_ref.at[n]) for n in range(frames)] + [(sort_hbm, wide_ref), (low_hbm, low_ref)]
    copies = [pltpu.make_async_copy(a, b, sems.at[n]) for n, (a, b) in enumerate(pairs)]
    for copy in copies:
        copy.start()
    token_ref[...] = jnp.zeros_like(token_ref)

    for copy in copies[:2]:
        copy.wait()
    odd_place = place_ref[1] == 1
    flat = (frames * cols_low, chan)
    at = column(flat[0], cols_low, chan)
    inner = [inner_ref[:, b].reshape(flat).astype(jnp.float32) for b in range(2)]
    outer = [outer_ref[:, b].reshape(flat).astype(jnp.float32) for b in range(2)]
    above = [jnp.where(odd_place, inner[b], outer[b]) for b in range(2)]
    below = [jnp.where(odd_place, outer[b], inner[b]) for b in range(2)]
    terms = []
    for (first, second), i in ((above, 2), (below, 0)):
        parts = [split(column_pair(first, second, j, at, cols_low - 1)) for j in range(3)]
        parts = jnp.concatenate([jnp.concatenate(part, axis=0) for part in parts], axis=1)
        sums = product(parts, jnp.concatenate([ws_ref[i, j].T for j in range(3)], axis=0))
        terms.append((sums[: flat[0]] + sums[flat[0] :]).reshape(frames, cols_low, chan))
    for row in range(rows_low):
        value = own_ref[:, row]
        if row == 0:
            value = value + terms[0]
        if row == rows_low - 1:
            value = value + terms[1]
        input_held[:, row] = value.astype(jnp.bfloat16)
    leaving = [pltpu.make_async_copy(input_held, input_ref, sems.at[len(copies)])]
    leaving[0].start()

    for copy in copies[2:3]:
        copy.wait()
    for side, pre in enumerate(spatial(edge_ref[...], ws_ref)):
        earlier[:, side] = (pre * jax.nn.sigmoid(pre)).astype(jnp.bfloat16).reshape(2, count, chan)
    for copy in copies[3:]:
        copy.wait()
    merge = wide_ref[...].T.astype(jnp.bfloat16)
    wt = wt_ref[...].reshape(3 * chan, chan)
    for frame in range(frames):
        acts = [act_ref[frame - k] if frame >= k else earlier[frame - k + 2] for k in range(3)]
        acts = jnp.concatenate([act.reshape(4 * count, chan) for act in acts], axis=1)
        low = low_ref[frame].reshape(1, count, chan).astype(jnp.float32)
        mixed = (product(acts, wt).reshape(4, count, chan) + low).astype(jnp.bfloat16)
        for n in range(rows_low // group):
            block = mixed[:, n * span : (n + 1) * span].reshape(4 * span, chan)
            block = product(merge, block).astype(jnp.bfloat16)
            held[frame, 2 * group * n : 2 * group * (n + 1)] = block.reshape(2 * group, 2 * cols_low, chan)
        leaving.append(pltpu.make_async_copy(held.at[frame], section_ref.at[frame], sems.at[len(copies) + 1 + frame]))
        leaving[-1].start()
    for copy in leaving:
        copy.wait()


def finish(place, own, ws, inner, outer, edge, act, wt, sort, low, before):
    frames, rows_low, cols_low, chan = low.shape
    out = (frames, 2 * rows_low, 2 * cols_low, chan)
    fetched = [inner, outer, edge, act, wt, sort, low]
    return pl.pallas_call(
        finish_kernel,
        in_specs=[SCALAR, FULL, FULL] + [HBM] * 7 + [UNREAD],
        out_specs=[HBM, HBM, FULL],
        out_shape=[like(out, jnp.bfloat16), like(low.shape, jnp.bfloat16), TOKEN],
        scratch_shapes=[pltpu.VMEM(a.shape, a.dtype) for a in fetched]
        + [pltpu.VMEM((2,) + act.shape[1:], act.dtype), pltpu.VMEM(out, jnp.bfloat16),
           pltpu.VMEM(low.shape, jnp.bfloat16), pltpu.SemaphoreType.DMA((7 + 2 * frames,))],
        compiler_params=grant(16),
        cost_estimate=cost(8, 4),
        name="finish",
    )(place, own, ws, inner, outer, edge, *[in_hbm(a) for a in (act, wt, sort, low)], before)


def put_kernel(place_ref, half_ref, *refs):
    spatial_ref, temporal_ref, wide, sems = refs[-4:]
    taps, half, _ = half_ref.shape
    to = pl.ds(pl.multiple_of(place_ref[0] * half, half), half)
    copies = []
    for tap in range(taps):
        wide[tap] = half_ref[tap].astype(jnp.float32)
        if tap < 9:
            target = spatial_ref.at[tap // 3, tap % 3, to]
        else:
            target = temporal_ref.at[tap - 9, to]
        copies.append(pltpu.make_async_copy(wide.at[tap], target, sems.at[tap]))
        copies[-1].start()
    for copy in copies:
        copy.wait()


def put(place, half, *done):
    chan = half.shape[-1]
    return pl.pallas_call(
        put_kernel,
        in_specs=[SCALAR, FULL] + [HBM] * len(done),
        out_specs=[HBM, HBM],
        out_shape=[like((3, 3, chan, chan), jnp.float32), like((3, chan, chan), jnp.float32)],
        input_output_aliases={2 + n: n for n in range(len(done))},
        scratch_shapes=[pltpu.VMEM((12, chan // 2, chan), jnp.float32), pltpu.SemaphoreType.DMA((12,))],
        compiler_params=grant(6),
        name="put",
    )(place, half, *done)


def add_kernel(mine_ref, theirs_ref, out_ref):
    out_ref[...] = (mine_ref[...] + theirs_ref[...]).astype(jnp.bfloat16)


def add_halves(mine, theirs):
    full = pl.BlockSpec(memory_space=pltpu.VMEM)
    return pl.pallas_call(
        add_kernel,
        in_specs=[full, full],
        out_specs=full,
        out_shape=like(mine.shape, jnp.bfloat16),
        compiler_params=grant(8),
        name="add_halves",
    )(mine, theirs)


def sum_kernel(got_ref, _, out_ref):
    total = got_ref[0].astype(jnp.float32)
    for n in range(1, got_ref.shape[0]):
        total = total + got_ref[n].astype(jnp.float32)
    out_ref[...] = total.astype(jnp.bfloat16)


def sum_parts(got, before):
    return pl.pallas_call(
        sum_kernel,
        in_specs=[FULL, UNREAD],
        out_specs=FULL,
        out_shape=like(got.shape[1:], jnp.bfloat16),
        compiler_params=grant(4),
        name="sum_parts",
    )(got, before)


def spread_kernel(own_ref, theirs_ref, *refs):
    total = (own_ref[...].astype(jnp.float32) + theirs_ref[...].astype(jnp.float32)).astype(jnp.bfloat16)
    for n in range(refs[-1].shape[0]):
        refs[-1][n] = total


def spread(own, theirs, parts, *before):
    return pl.pallas_call(
        spread_kernel,
        in_specs=[FULL, FULL] + [UNREAD] * len(before),
        out_specs=FULL,
        out_shape=like((parts,) + own.shape, jnp.bfloat16),
        compiler_params=grant(4),
        name="spread",
    )(own, theirs, *before)


def on_device(bits, low_frames, spatial_weight, temporal_weight, cotangent):
    low, cot = low_frames[0], cotangent[0]
    frames, rows_low, cols_low, chan = low.shape
    core = lax.axis_index(bits.core).astype(jnp.int32)
    odd = lax.axis_index(bits.axes["height"][-1]).astype(jnp.int32)
    mine, other = jnp.stack([core, odd]), jnp.stack([1 - core, odd])
    parts = 1 << len(bits.near)

    inner, outer, later = first_messages(mine, low, cot)
    later = bits.shift(later, "tm", -1)
    inner, outer = bits.pairs(inner, outer)
    order = jnp.asarray(side_order(rows_low, cols_low))
    low_in, ws, sort, turned, cot_side = load(low, cot, spatial_weight, temporal_weight, order)
    act, slope = forward(mine, low_in, inner, outer, ws)
    pg, ext, theirs = backward(
        other, low_in, inner, outer, act, slope, cot_side, later, turned, sort
    )
    theirs = bits.swap(theirs, bits.core)
    own, act, box = half_grads(mine, low_in, inner, outer, act, pg, ext)
    kept = add_halves(own, theirs)
    got = bits.exchange(kept.reshape(parts, -1, chan))
    edge, pg_inner, pg_outer = edges(mine, low_in, inner, outer, pg, kept)
    edge = bits.shift(edge, "tm", 1)
    pg_inner, pg_outer = bits.pairs(pg_inner, pg_outer)
    own_part = input_own(pg, box, ws, kept, low.shape)
    total, far = bits.far_sums(sum_parts(got, own_part))
    section_out, input_grad, done = finish(
        mine, own_part, ws, pg_inner, pg_outer, edge, act, temporal_weight, order, low, total
    )
    totals = spread(total, far, parts, done)
    half = bits.exchange(totals).reshape(kept.shape)
    theirs = bits.swap(half, bits.core)
    spatial_grad, temporal_grad = put(other, theirs, *put(mine, half))
    return section_out[None], input_grad[None], spatial_grad, temporal_grad


def solution(mesh):
    bits = Bits(mesh)
    block = P(*(bits.axes[name] for name in ("dp", "tm", "height")), None, None)
    return jax.shard_map(
        functools.partial(on_device, bits),
        mesh=bits.mesh,
        in_specs=(block, P(), P(), block),
        out_specs=(block, block, P(), P()),
        check_vma=False,
    )
```

```python
import functools

import jax
import jax.numpy as jnp
import numpy as np
from jax import lax
from jax.experimental import pallas as pl
from jax.experimental.pallas import tpu as pltpu
from jax.sharding import Mesh
from jax.sharding import PartitionSpec as P


class Bits:
    def __init__(self, mesh):
        self.axes = {}
        for name in mesh.axis_names:
            count = mesh.shape[name].bit_length() - 1
            self.axes[name] = tuple(f"{name}{bit}" for bit in reversed(range(count)))
        names = [bit for bits in self.axes.values() for bit in bits]
        self.mesh = Mesh(mesh.devices.reshape([2] * len(names)), tuple(names))
        self.core = next((n for n in names if self.same_chip(n)), self.axes["tm"][-1])
        others = [[b for b in reversed(bits) if b != self.core] for bits in self.axes.values()]
        turns = [bits[turn] for turn in range(len(names)) for bits in others if turn < len(bits)]
        self.near = [n for n in names if n in turns[:3]]
        self.far = turns[3:]

    def same_chip(self, name):
        at = [1 if n == name else 0 for n in self.mesh.axis_names]
        here = self.mesh.devices[tuple([0] * len(at))]
        there = self.mesh.devices[tuple(at)]
        return tuple(getattr(here, "coords", (0,))) == tuple(getattr(there, "coords", (1,)))

    def swap(self, block, axis):
        return lax.ppermute(block, axis, [(0, 1), (1, 0)])

    def shift(self, block, name, distance):
        axes = self.axes[name]
        devices = range(1 << len(axes))
        route = [(i - distance, i) for i in devices if i - distance in devices]
        return lax.ppermute(block, axes, route)

    def exchange(self, parts):
        return lax.all_to_all(parts, tuple(self.near), 0, 0, tiled=True)

    def pairs(self, inner, outer):
        axes = self.axes["height"]
        low = range(1, (1 << len(axes)) - 1, 2)
        route = [(i, i + 1) for i in low] + [(i + 1, i) for i in low]
        outer = lax.ppermute(outer, axes, route)
        return self.swap(inner, axes[-1]), outer

    def far_sums(self, total):
        for axis in self.far[:-1]:
            total = total.astype(jnp.float32) + self.swap(total, axis).astype(jnp.float32)
            total = lax.reduce_precision(total, 8, 7).astype(jnp.bfloat16)
        return total, self.swap(total, self.far[-1])


SIDES = ((0, 0), (0, 1), (1, 0), (1, 1))


def grant(mib):
    return pltpu.CompilerParams(vmem_limit_bytes=mib * 2**20)


def product(left, right):
    return jnp.dot(left, right, preferred_element_type=jnp.float32)


def product_nt(left, right):
    return lax.dot_general(left, right, (((1,), (1,)), ((), ())), preferred_element_type=jnp.float32)


def rows_at_once(rows_low, cols_low):
    return max(n for n in (1, 2, 4, 8) if rows_low % n == 0 and (n == 1 or 4 * n * cols_low <= 256))


def side_order(rows_low, cols_low):
    count = rows_at_once(rows_low, cols_low)
    size = 4 * count * cols_low
    at = np.arange(size).reshape(count, 2, cols_low, 2).transpose(1, 3, 0, 2).reshape(-1)
    return (at[:, None] == np.arange(size)[None, :]).astype(np.float32)


def column(rows, cols_low, chan):
    return lax.broadcasted_iota(jnp.int32, (rows // cols_low, cols_low, chan), 1).reshape(rows, chan)


def from_left(x, at):
    return jnp.where(at == 0, 0.0, pltpu.roll(x, 1, 0))


def from_right(x, at, last):
    return jnp.where(at == last, 0.0, pltpu.roll(x, x.shape[0] - 1, 0))


def sort_columns(source, target, cols_low, order):
    rows_low, chan = source.shape[0] // 2, source.shape[2]
    group = rows_at_once(rows_low, cols_low)
    span = group * cols_low
    for n in range(rows_low // group):
        block = source[2 * group * n : 2 * group * (n + 1)].reshape(4 * span, chan)
        block = product(order, block).astype(jnp.bfloat16).reshape(4, span, chan)
        target[:, n * span : (n + 1) * span, :] = block


def tall(place_ref, low_ref, inner_ref, outer_ref, frame, lanes=slice(None)):
    odd = place_ref[1] == 1
    inner, outer = inner_ref[frame, :, :, lanes], outer_ref[frame, :, :, lanes]
    up, down = jnp.where(odd, inner, outer), jnp.where(odd, outer, inner)
    return jnp.concatenate([up, low_ref[frame, :, :, lanes], down], axis=0)


def spatial(low, ws_ref):
    frames, rows_tall, cols_low, chan = low.shape
    rows_low = rows_tall - 2
    count = frames * rows_low * cols_low
    flat = low.reshape(-1, chan)
    rows = [[], []]
    for j in range(3):
        taps = [product(flat, ws_ref[i, j]).reshape(low.shape) for i in range(3)]
        even = taps[0][:, :rows_low] + (taps[1] + taps[2])[:, 1 : rows_low + 1]
        odd = (taps[0] + taps[1])[:, 1 : rows_low + 1] + taps[2][:, 2:]
        rows[0].append(even.reshape(count, chan))
        rows[1].append(odd.reshape(count, chan))
    at = column(count, cols_low, chan)
    for first, second, third in rows:
        yield from_left(first, at) + (second + third)
        yield (first + second) + from_right(third, at, cols_low - 1)


def forward_kernel(place_ref, low_ref, inner_ref, outer_ref, ws_ref, act_ref, slope_ref):
    frames, rows_low, cols_low, chan = low_ref.shape
    shape = (frames, rows_low * cols_low, chan)
    low = jnp.stack([tall(place_ref, low_ref, inner_ref, outer_ref, frame) for frame in range(frames)])
    for side, pre in enumerate(spatial(low, ws_ref)):
        sig = jax.nn.sigmoid(pre)
        act_ref[:, side] = (pre * sig).astype(jnp.bfloat16).reshape(shape)
        slope_ref[:, side] = (sig * (1.0 + pre * (1.0 - sig))).reshape(shape)


def half_sums(place_ref, low_ref, inner_ref, outer_ref, act_ref, pg_ref, ext_ref, out_ref):
    frames, rows_low, cols_low, chan = low_ref.shape
    count, half = rows_low * cols_low, chan // 2
    lanes = pl.ds(pl.multiple_of(place_ref[0] * half, half), half)
    lefts = [[] for _ in range(9)]
    acts = []
    at = column((rows_low + 2) * cols_low, cols_low, half)
    for frame in range(frames):
        low = tall(place_ref, low_ref, inner_ref, outer_ref, frame, lanes)
        wide = low.reshape(-1, half).astype(jnp.float32)
        moved = [from_left(wide, at), wide, from_right(wide, at, cols_low - 1)]
        turned = {}
        for dc in range(3):
            view = moved[dc].astype(jnp.bfloat16).reshape(low.shape)
            for dr in range(3):
                turned[dr - 1, dc - 1] = view[dr : dr + rows_low].reshape(count, half).T
        for i in range(3):
            for j in range(3):
                lefts[3 * i + j] += [turned[(a + i - 1) // 2, (b + j - 1) // 2] for a, b in SIDES]
        acts.append(act_ref[frame, :, :, lanes].reshape(4 * count, half).T)
    pg = pg_ref[...].reshape(frames * 4 * count, chan)
    left = jnp.concatenate([jnp.concatenate(left, axis=1) for left in lefts], axis=0)
    out_ref[:9] = product(left, pg).reshape(9, half, chan)
    act = jnp.concatenate(acts, axis=1)
    for k in range(3):
        out_ref[9 + k] = product(act, ext_ref[k : k + frames].reshape(frames * 4 * count, chan))


def half_kernel(place_ref, low_ref, inner_ref, outer_ref, act_ref, pg_ref, ext_ref, out_ref, act_out, box_ref, sem):
    copy = pltpu.make_async_copy(act_ref, act_out, sem)
    copy.start()
    for frame in range(box_ref.shape[0]):
        box_ref[frame] = sum(ext_ref[frame, side].astype(jnp.float32) for side in range(4))
    half_sums(place_ref, low_ref, inner_ref, outer_ref, act_ref, pg_ref, ext_ref, out_ref)
    copy.wait()


def backward_kernel(place_ref, low_ref, inner_ref, outer_ref, act_ref, slope_ref, cot_ref, later_ref, turned_ref, sort_ref,
                    pg_ref, ext_ref, out_ref):
    frames, _, count, chan = cot_ref.shape
    ext_ref[:frames] = cot_ref[...]
    for n in range(2):
        sort_columns(later_ref.at[n], ext_ref.at[frames + n], low_ref.shape[2], sort_ref[...])
    for frame in range(frames):
        cots = [ext_ref[frame + k].reshape(4 * count, chan) for k in range(3)]
        act_grad = product(jnp.concatenate(cots, axis=1), turned_ref[...])
        slope = slope_ref[frame].reshape(4 * count, chan)
        pg_ref[frame] = (act_grad * slope).astype(jnp.bfloat16).reshape(4, count, chan)
    half_sums(place_ref, low_ref, inner_ref, outer_ref, act_ref, pg_ref, ext_ref, out_ref)


SCALAR = pl.BlockSpec(memory_space=pltpu.SMEM)
UNREAD = pl.BlockSpec(memory_space=pl.ANY)


def like(shape, dtype):
    return jax.ShapeDtypeStruct(shape, dtype)


TOKEN = like((8, 128), jnp.float32)


def cost(units, mib):
    return pl.CostEstimate(flops=units * 2 * 2048 * 256 * 256, bytes_accessed=mib * 2**20, transcendentals=0)


def in_hbm(array):
    return pltpu.with_memory_space_constraint(array, pltpu.HBM)


FULL = pl.BlockSpec(memory_space=pltpu.VMEM)


def first_kernel(place_ref, low_ref, cot_ref, inner_ref, outer_ref, later_ref, sems):
    last = low_ref.shape[1] - 1
    odd = place_ref[1]
    copies = [
        (low_ref.at[:, pl.ds(last * (1 - odd), 1)], inner_ref),
        (low_ref.at[:, pl.ds(last * odd, 1)], outer_ref),
    ]
    copies += [(cot_ref.at[0:2], later_ref)]
    copies = [pltpu.make_async_copy(a, b, sems.at[n]) for n, (a, b) in enumerate(copies)]
    for copy in copies:
        copy.start()
    for copy in copies:
        copy.wait()


def first_messages(place, low, cot):
    row = like(low[:, :1].shape, low.dtype)
    return pl.pallas_call(
        first_kernel,
        in_specs=[SCALAR, UNREAD, UNREAD],
        out_specs=[FULL] * 3,
        out_shape=[row, row, like(cot[:2].shape, cot.dtype)],
        scratch_shapes=[pltpu.SemaphoreType.DMA((3,))],
        compiler_params=grant(4),
        name="first_messages",
    )(place, in_hbm(low), in_hbm(cot))


def load_kernel(low_hbm, cot_hbm, ws_hbm, wt_hbm, sort_hbm,
                low_ref, ws_ref, sort_ref, turned_ref, side_ref, cot_ref, wide_ref, wt_ref, sems):
    frames, cols_low, chan = low_ref.shape[0], low_ref.shape[2], low_ref.shape[3]
    pairs = [(sort_hbm, wide_ref)] + [(cot_hbm.at[n], cot_ref.at[n]) for n in range(frames)]
    pairs += [(wt_hbm.at[k], wt_ref.at[k]) for k in range(3)] + [(low_hbm, low_ref)]
    pairs += [(ws_hbm.at[i, j], ws_ref.at[i, j]) for i in range(3) for j in range(3)]
    copies = [pltpu.make_async_copy(a, b, sems.at[n]) for n, (a, b) in enumerate(pairs)]
    for copy in copies:
        copy.start()
    copies[0].wait()
    sort_ref[...] = wide_ref[...].astype(jnp.bfloat16)
    for n in range(frames):
        copies[1 + n].wait()
        sort_columns(cot_ref.at[n], side_ref.at[n], cols_low, sort_ref[...])
    for k in range(3):
        copies[1 + frames + k].wait()
        turned_ref[k * chan : (k + 1) * chan] = wt_ref[k].T
    for copy in copies[4 + frames :]:
        copy.wait()


def load(low, cot, ws, wt, sort):
    frames, rows_low, cols_low, chan = low.shape
    order = like(sort.shape, jnp.bfloat16)
    shapes = [low, ws, order, like((3 * chan, chan), wt.dtype),
              like((frames, 4, rows_low * cols_low, chan), jnp.bfloat16)]
    return pl.pallas_call(
        load_kernel,
        in_specs=[UNREAD] * 5,
        out_specs=[FULL] * 5,
        out_shape=[like(a.shape, a.dtype) for a in shapes],
        scratch_shapes=[pltpu.VMEM(cot.shape, cot.dtype), pltpu.VMEM(sort.shape, sort.dtype), pltpu.VMEM(wt.shape, wt.dtype),
                        pltpu.SemaphoreType.DMA((frames + 14,))],
        compiler_params=grant(14),
        cost_estimate=cost(2, 4),
        name="load",
    )(*[in_hbm(a) for a in (low, cot, ws, wt, sort)])


def forward(place, low, inner, outer, ws):
    frames, rows_low, cols_low, chan = low.shape
    side = (frames, 4, rows_low * cols_low, chan)
    return pl.pallas_call(
        forward_kernel,
        in_specs=[SCALAR] + [FULL] * 4,
        out_specs=[FULL] * 2,
        out_shape=[like(side, jnp.bfloat16), like(side, jnp.float32)],
        compiler_params=grant(20),
        cost_estimate=cost(10, 8),
        name="forward",
    )(place, low, inner, outer, ws)


def edges_kernel(place_ref, low_ref, inner_ref, outer_ref, pg_ref, _, tall_ref, pg_inner, pg_outer):
    cols_low = low_ref.shape[2]
    first = low_ref.shape[0] - tall_ref.shape[0]
    for n in range(tall_ref.shape[0]):
        tall_ref[n] = tall(place_ref, low_ref, inner_ref, outer_ref, first + n)
    odd = place_ref[1] == 1
    top, bottom = pg_ref[:, :2, :cols_low, :], pg_ref[:, 2:, -cols_low:, :]
    pg_inner[...] = jnp.where(odd, top, bottom)
    pg_outer[...] = jnp.where(odd, bottom, top)


def edges(place, low, inner, outer, pg, before):
    frames, rows_low, cols_low, chan = low.shape
    full = pl.BlockSpec(memory_space=pltpu.VMEM)
    rows = like((frames, 2, cols_low, chan), jnp.bfloat16)
    return pl.pallas_call(
        edges_kernel,
        in_specs=[SCALAR, full, full, full, full, UNREAD],
        out_specs=[full] * 3,
        out_shape=[like((2, rows_low + 2, cols_low, chan), jnp.bfloat16), rows, rows],
        compiler_params=grant(8),
        name="edges",
    )(place, low, inner, outer, pg, before)


def backward(place, low, inner, outer, act, slope, cot, later, turned, sort):
    frames, _, count, chan = act.shape
    ext = (frames + 2,) + act.shape[1:]
    return pl.pallas_call(
        backward_kernel,
        in_specs=[SCALAR] + [FULL] * 9,
        out_specs=[FULL] * 3,
        out_shape=[like(act.shape, jnp.bfloat16), like(ext, jnp.bfloat16), like((12, chan // 2, chan), jnp.float32)],
        compiler_params=grant(24),
        cost_estimate=cost(15, 10),
        name="backward",
    )(place, low, inner, outer, act, slope, cot, later, turned, sort)


def half_grads(place, low, inner, outer, act, pg, ext):
    chan = low.shape[-1]
    return pl.pallas_call(
        half_kernel,
        in_specs=[SCALAR] + [FULL] * 6,
        out_specs=[FULL, HBM, FULL],
        out_shape=[like((12, chan // 2, chan), jnp.float32), pltpu.HBM(act.shape, act.dtype),
                   like((act.shape[0],) + act.shape[2:], jnp.float32)],
        scratch_shapes=[pltpu.SemaphoreType.DMA],
        compiler_params=grant(20),
        cost_estimate=cost(10, 6),
        name="half_grads",
    )(place, low, inner, outer, act, pg, ext)


HBM = pl.BlockSpec(memory_space=pltpu.HBM)


def split(value):
    high = value.astype(jnp.bfloat16)
    return high, (value - high.astype(jnp.float32)).astype(jnp.bfloat16)


def column_pair(first, second, j, at, last):
    if j == 0:
        return second + from_right(first, at, last)
    if j == 1:
        return first + second
    return first + from_left(second, at)


def input_kernel(pg_ref, box_ref, ws_ref, _, out_ref):
    frames, _, count, chan = pg_ref.shape
    cols_low = out_ref.shape[2]
    rows_low = count // cols_low
    at = column(count, cols_low, chan)
    turned = jnp.concatenate([ws_ref[i, j].T for j in range(3) for i in range(3)], axis=0)
    for frame in range(frames):
        own = [pg_ref[frame, side].astype(jnp.float32) for side in range(4)]
        zero = jnp.zeros((1, cols_low, chan), jnp.float32)
        parts = []
        for j in range(3):
            even = column_pair(own[0], own[1], j, at, cols_low - 1).reshape(rows_low, cols_low, chan)
            odd = column_pair(own[2], own[3], j, at, cols_low - 1).reshape(rows_low, cols_low, chan)
            below = jnp.concatenate([even[1:], zero], axis=0)
            above = jnp.concatenate([zero, odd[:-1]], axis=0)
            for value in (odd + below, even + odd, above + even):
                parts.append(jnp.concatenate(split(value.reshape(count, chan)), axis=0))
        sums = product(jnp.concatenate(parts, axis=1), turned)
        total = box_ref[frame] + (sums[:count] + sums[count:])
        out_ref[frame] = total.reshape(rows_low, cols_low, chan)


def input_own(pg, box, ws, before, low_shape):
    return pl.pallas_call(
        input_kernel,
        in_specs=[FULL] * 3 + [UNREAD],
        out_specs=FULL,
        out_shape=like(low_shape, jnp.float32),
        compiler_params=grant(16),
        cost_estimate=cost(6, 4),
        name="input_own",
    )(pg, box, ws, before)


def finish_kernel(place_ref, own_ref, ws_ref, inner_hbm, outer_hbm, edge_hbm, act_hbm, wt_hbm, sort_hbm, low_hbm, _,
                  section_ref, input_ref, token_ref,
                  inner_ref, outer_ref, edge_ref, act_ref, wt_ref, wide_ref, low_ref, earlier, held, input_held, sems):
    frames, rows_low, cols_low, chan = low_ref.shape
    group = rows_at_once(rows_low, cols_low)
    span, count = group * cols_low, rows_low * cols_low
    pairs = [(inner_hbm, inner_ref), (outer_hbm, outer_ref)]
    pairs += [(edge_hbm, edge_ref), (wt_hbm, wt_ref), (sort_hbm, wide_ref), (low_hbm, low_ref)]
    pairs += [(act_hbm.at[n], act_ref.at[n]) for n in range(frames)]
    copies = [pltpu.make_async_copy(a, b, sems.at[n]) for n, (a, b) in enumerate(pairs)]
    for copy in copies:
        copy.start()
    token_ref[...] = jnp.zeros_like(token_ref)

    for copy in copies[:2]:
        copy.wait()
    odd_place = place_ref[1] == 1
    flat = (frames * cols_low, chan)
    at = column(flat[0], cols_low, chan)
    inner = [inner_ref[:, b].reshape(flat).astype(jnp.float32) for b in range(2)]
    outer = [outer_ref[:, b].reshape(flat).astype(jnp.float32) for b in range(2)]
    above = [jnp.where(odd_place, inner[b], outer[b]) for b in range(2)]
    below = [jnp.where(odd_place, outer[b], inner[b]) for b in range(2)]
    terms = []
    for (first, second), i in ((above, 2), (below, 0)):
        parts = [split(column_pair(first, second, j, at, cols_low - 1)) for j in range(3)]
        parts = jnp.concatenate([jnp.concatenate(part, axis=0) for part in parts], axis=1)
        sums = product(parts, jnp.concatenate([ws_ref[i, j].T for j in range(3)], axis=0))
        terms.append((sums[: flat[0]] + sums[flat[0] :]).reshape(frames, cols_low, chan))
    for row in range(rows_low):
        value = own_ref[:, row]
        if row == 0:
            value = value + terms[0]
        if row == rows_low - 1:
            value = value + terms[1]
        input_held[:, row] = value.astype(jnp.bfloat16)
    leaving = [pltpu.make_async_copy(input_held, input_ref, sems.at[len(copies)])]
    leaving[0].start()

    for copy in copies[2:3]:
        copy.wait()
    for side, pre in enumerate(spatial(edge_ref[...], ws_ref)):
        earlier[:, side] = (pre * jax.nn.sigmoid(pre)).astype(jnp.bfloat16).reshape(2, count, chan)
    for copy in copies[3:6]:
        copy.wait()
    merge = wide_ref[...].T.astype(jnp.bfloat16)
    wt = wt_ref[...].reshape(3 * chan, chan)
    for frame in range(frames):
        copies[6 + frame].wait()
        acts = [act_ref[frame - k] if frame >= k else earlier[frame - k + 2] for k in range(3)]
        acts = jnp.concatenate([act.reshape(4 * count, chan) for act in acts], axis=1)
        low = low_ref[frame].reshape(1, count, chan).astype(jnp.float32)
        mixed = (product(acts, wt).reshape(4, count, chan) + low).astype(jnp.bfloat16)
        for n in range(rows_low // group):
            block = mixed[:, n * span : (n + 1) * span].reshape(4 * span, chan)
            block = product(merge, block).astype(jnp.bfloat16)
            held[frame, 2 * group * n : 2 * group * (n + 1)] = block.reshape(2 * group, 2 * cols_low, chan)
        leaving.append(pltpu.make_async_copy(held.at[frame], section_ref.at[frame], sems.at[len(copies) + 1 + frame]))
        leaving[-1].start()
    for copy in leaving:
        copy.wait()


def finish(place, own, ws, inner, outer, edge, act, wt, sort, low, before):
    frames, rows_low, cols_low, chan = low.shape
    out = (frames, 2 * rows_low, 2 * cols_low, chan)
    fetched = [inner, outer, edge, act, wt, sort, low]
    return pl.pallas_call(
        finish_kernel,
        in_specs=[SCALAR, FULL, FULL] + [HBM] * 7 + [UNREAD],
        out_specs=[HBM, HBM, FULL],
        out_shape=[like(out, jnp.bfloat16), like(low.shape, jnp.bfloat16), TOKEN],
        scratch_shapes=[pltpu.VMEM(a.shape, a.dtype) for a in fetched]
        + [pltpu.VMEM((2,) + act.shape[1:], act.dtype), pltpu.VMEM(out, jnp.bfloat16),
           pltpu.VMEM(low.shape, jnp.bfloat16), pltpu.SemaphoreType.DMA((7 + 2 * frames,))],
        compiler_params=grant(16),
        cost_estimate=cost(8, 4),
        name="finish",
    )(place, own, ws, inner, outer, edge, *[in_hbm(a) for a in (act, wt, sort, low)], before)


def put_kernel(place_ref, half_ref, *refs):
    spatial_ref, temporal_ref, wide, sems = refs[-4:]
    taps, half, _ = half_ref.shape
    to = pl.ds(pl.multiple_of(place_ref[0] * half, half), half)
    copies = []
    for tap in range(taps):
        wide[tap] = half_ref[tap].astype(jnp.float32)
        if tap < 9:
            target = spatial_ref.at[tap // 3, tap % 3, to]
        else:
            target = temporal_ref.at[tap - 9, to]
        copies.append(pltpu.make_async_copy(wide.at[tap], target, sems.at[tap]))
        copies[-1].start()
    for copy in copies:
        copy.wait()


def put(place, half, *done):
    chan = half.shape[-1]
    return pl.pallas_call(
        put_kernel,
        in_specs=[SCALAR, FULL] + [HBM] * len(done),
        out_specs=[HBM, HBM],
        out_shape=[like((3, 3, chan, chan), jnp.float32), like((3, chan, chan), jnp.float32)],
        input_output_aliases={2 + n: n for n in range(len(done))},
        scratch_shapes=[pltpu.VMEM((12, chan // 2, chan), jnp.float32), pltpu.SemaphoreType.DMA((12,))],
        compiler_params=grant(6),
        name="put",
    )(place, half, *done)


def add_kernel(mine_ref, theirs_ref, out_ref, held, sems):
    size = held.shape[0] // 4
    copies = []
    for n in range(4):
        at = pl.ds(n * size, size)
        held[at] = (mine_ref[at] + theirs_ref[at]).astype(jnp.bfloat16)
        copies.append(pltpu.make_async_copy(held.at[at], out_ref.at[at], sems.at[n]))
        copies[-1].start()
    for copy in copies:
        copy.wait()


def add_halves(mine, theirs):
    return pl.pallas_call(
        add_kernel,
        in_specs=[FULL, FULL],
        out_specs=HBM,
        out_shape=pltpu.HBM(mine.shape, jnp.bfloat16),
        scratch_shapes=[pltpu.VMEM(mine.shape, jnp.bfloat16), pltpu.SemaphoreType.DMA((4,))],
        compiler_params=grant(6),
        name="add_halves",
    )(mine, theirs)


def sum_kernel(got_ref, _, out_ref):
    total = got_ref[0].astype(jnp.float32)
    for n in range(1, got_ref.shape[0]):
        total = total + got_ref[n].astype(jnp.float32)
    out_ref[...] = total.astype(jnp.bfloat16)


def sum_parts(got, before):
    return pl.pallas_call(
        sum_kernel,
        in_specs=[FULL, UNREAD],
        out_specs=FULL,
        out_shape=like(got.shape[1:], jnp.bfloat16),
        compiler_params=grant(4),
        name="sum_parts",
    )(got, before)


def spread_kernel(own_ref, theirs_ref, *refs):
    total = (own_ref[...].astype(jnp.float32) + theirs_ref[...].astype(jnp.float32)).astype(jnp.bfloat16)
    for n in range(refs[-1].shape[0]):
        refs[-1][n] = total


def spread(own, theirs, parts, *before):
    return pl.pallas_call(
        spread_kernel,
        in_specs=[FULL, FULL] + [UNREAD] * len(before),
        out_specs=FULL,
        out_shape=like((parts,) + own.shape, jnp.bfloat16),
        compiler_params=grant(4),
        name="spread",
    )(own, theirs, *before)


def on_device(bits, low_frames, spatial_weight, temporal_weight, cotangent):
    low, cot = low_frames[0], cotangent[0]
    frames, rows_low, cols_low, chan = low.shape
    core = lax.axis_index(bits.core).astype(jnp.int32)
    odd = lax.axis_index(bits.axes["height"][-1]).astype(jnp.int32)
    mine, other = jnp.stack([core, odd]), jnp.stack([1 - core, odd])
    parts = 1 << len(bits.near)

    inner, outer, later = first_messages(mine, low, cot)
    later = bits.shift(later, "tm", -1)
    inner, outer = bits.pairs(inner, outer)
    order = jnp.asarray(side_order(rows_low, cols_low))
    low_in, ws, sort, turned, cot_side = load(low, cot, spatial_weight, temporal_weight, order)
    act, slope = forward(mine, low_in, inner, outer, ws)
    pg, ext, theirs = backward(
        other, low_in, inner, outer, act, slope, cot_side, later, turned, sort
    )
    theirs = bits.swap(theirs, bits.core)
    own, act, box = half_grads(mine, low_in, inner, outer, act, pg, ext)
    kept = add_halves(own, theirs)
    got = bits.exchange(kept.reshape(parts, -1, chan))
    edge, pg_inner, pg_outer = edges(mine, low_in, inner, outer, pg, in_hbm(kept))
    edge = bits.shift(edge, "tm", 1)
    pg_inner, pg_outer = bits.pairs(pg_inner, pg_outer)
    own_part = input_own(pg, box, ws, in_hbm(kept), low.shape)
    total, far = bits.far_sums(sum_parts(got, own_part))
    section_out, input_grad, done = finish(
        mine, own_part, ws, pg_inner, pg_outer, edge, act, temporal_weight, order, low, total
    )
    totals = spread(total, far, parts, done)
    half = bits.exchange(totals).reshape(kept.shape)
    theirs = bits.swap(half, bits.core)
    spatial_grad, temporal_grad = put(other, theirs, *put(mine, half))
    return section_out[None], input_grad[None], spatial_grad, temporal_grad


def solution(mesh):
    bits = Bits(mesh)
    block = P(*(bits.axes[name] for name in ("dp", "tm", "height")), None, None)
    return jax.shard_map(
        functools.partial(on_device, bits),
        mesh=bits.mesh,
        in_specs=(block, P(), P(), block),
        out_specs=(block, block, P(), P()),
        check_vma=False,
    )
```

```python
import functools

import jax
import jax.numpy as jnp
import numpy as np
from jax import lax
from jax.experimental import pallas as pl
from jax.experimental.pallas import tpu as pltpu
from jax.sharding import Mesh
from jax.sharding import PartitionSpec as P


class Bits:
    def __init__(self, mesh):
        self.axes = {}
        for name in mesh.axis_names:
            count = mesh.shape[name].bit_length() - 1
            self.axes[name] = tuple(f"{name}{bit}" for bit in reversed(range(count)))
        names = [bit for bits in self.axes.values() for bit in bits]
        self.mesh = Mesh(mesh.devices.reshape([2] * len(names)), tuple(names))
        self.core = next((n for n in names if self.same_chip(n)), self.axes["tm"][-1])
        others = [[b for b in reversed(bits) if b != self.core] for bits in self.axes.values()]
        turns = [bits[turn] for turn in range(len(names)) for bits in others if turn < len(bits)]
        self.near = [n for n in names if n in turns[:3]]
        self.far = turns[3:]

    def same_chip(self, name):
        at = [1 if n == name else 0 for n in self.mesh.axis_names]
        here = self.mesh.devices[tuple([0] * len(at))]
        there = self.mesh.devices[tuple(at)]
        return tuple(getattr(here, "coords", (0,))) == tuple(getattr(there, "coords", (1,)))

    def swap(self, block, axis):
        return lax.ppermute(block, axis, [(0, 1), (1, 0)])

    def shift(self, block, name, distance):
        axes = self.axes[name]
        devices = range(1 << len(axes))
        route = [(i - distance, i) for i in devices if i - distance in devices]
        return lax.ppermute(block, axes, route)

    def exchange(self, parts):
        return lax.all_to_all(parts, tuple(self.near), 0, 0, tiled=True)

    def pairs(self, inner, outer):
        axes = self.axes["height"]
        low = range(1, (1 << len(axes)) - 1, 2)
        route = [(i, i + 1) for i in low] + [(i + 1, i) for i in low]
        outer = lax.ppermute(outer, axes, route)
        return self.swap(inner, axes[-1]), outer

    def far_sums(self, total):
        for axis in self.far[:-1]:
            total = total.astype(jnp.float32) + self.swap(total, axis).astype(jnp.float32)
            total = lax.reduce_precision(total, 8, 7).astype(jnp.bfloat16)
        return total, self.swap(total, self.far[-1])


SIDES = ((0, 0), (0, 1), (1, 0), (1, 1))


def grant(mib):
    return pltpu.CompilerParams(vmem_limit_bytes=mib * 2**20)


def product(left, right):
    return jnp.dot(left, right, preferred_element_type=jnp.float32)


def product_nt(left, right):
    return lax.dot_general(left, right, (((1,), (1,)), ((), ())), preferred_element_type=jnp.float32)


def rows_at_once(rows_low, cols_low):
    return max(n for n in (1, 2, 4, 8) if rows_low % n == 0 and (n == 1 or 4 * n * cols_low <= 256))


def side_order(rows_low, cols_low):
    count = rows_at_once(rows_low, cols_low)
    size = 4 * count * cols_low
    at = np.arange(size).reshape(count, 2, cols_low, 2).transpose(1, 3, 0, 2).reshape(-1)
    return (at[:, None] == np.arange(size)[None, :]).astype(np.float32)


def column(rows, cols_low, chan):
    return lax.broadcasted_iota(jnp.int32, (rows // cols_low, cols_low, chan), 1).reshape(rows, chan)


def from_left(x, at):
    return jnp.where(at == 0, 0.0, pltpu.roll(x, 1, 0))


def from_right(x, at, last):
    return jnp.where(at == last, 0.0, pltpu.roll(x, x.shape[0] - 1, 0))


def sort_columns(source, target, cols_low, order):
    rows_low, chan = source.shape[0] // 2, source.shape[2]
    group = rows_at_once(rows_low, cols_low)
    span = group * cols_low
    for n in range(rows_low // group):
        block = source[2 * group * n : 2 * group * (n + 1)].reshape(4 * span, chan)
        block = product(order, block).astype(jnp.bfloat16).reshape(4, span, chan)
        target[:, n * span : (n + 1) * span, :] = block


def tall(place_ref, low_ref, inner_ref, outer_ref, frame, lanes=slice(None)):
    odd = place_ref[1] == 1
    inner, outer = inner_ref[frame, :, :, lanes], outer_ref[frame, :, :, lanes]
    up, down = jnp.where(odd, inner, outer), jnp.where(odd, outer, inner)
    return jnp.concatenate([up, low_ref[frame, :, :, lanes], down], axis=0)


def spatial(low, ws_ref):
    frames, rows_tall, cols_low, chan = low.shape
    rows_low = rows_tall - 2
    count = frames * rows_low * cols_low
    flat = low.reshape(-1, chan)
    rows = [[], []]
    for j in range(3):
        taps = [product(flat, ws_ref[i, j]).reshape(low.shape) for i in range(3)]
        even = taps[0][:, :rows_low] + (taps[1] + taps[2])[:, 1 : rows_low + 1]
        odd = (taps[0] + taps[1])[:, 1 : rows_low + 1] + taps[2][:, 2:]
        rows[0].append(even.reshape(count, chan))
        rows[1].append(odd.reshape(count, chan))
    at = column(count, cols_low, chan)
    for first, second, third in rows:
        yield from_left(first, at) + (second + third)
        yield (first + second) + from_right(third, at, cols_low - 1)


def forward_kernel(place_ref, low_ref, inner_ref, outer_ref, ws_ref, act_ref, slope_ref):
    frames, rows_low, cols_low, chan = low_ref.shape
    shape = (frames, rows_low * cols_low, chan)
    low = jnp.stack([tall(place_ref, low_ref, inner_ref, outer_ref, frame) for frame in range(frames)])
    for side, pre in enumerate(spatial(low, ws_ref)):
        sig = jax.nn.sigmoid(pre)
        act_ref[:, side] = (pre * sig).astype(jnp.bfloat16).reshape(shape)
        slope_ref[:, side] = (sig * (1.0 + pre * (1.0 - sig))).reshape(shape)


def half_sums(place_ref, low_ref, inner_ref, outer_ref, act_ref, pg_ref, ext_ref, out_ref):
    frames, rows_low, cols_low, chan = low_ref.shape
    count, half = rows_low * cols_low, chan // 2
    lanes = pl.ds(pl.multiple_of(place_ref[0] * half, half), half)
    lefts = [[] for _ in range(9)]
    acts = []
    at = column((rows_low + 2) * cols_low, cols_low, half)
    for frame in range(frames):
        low = tall(place_ref, low_ref, inner_ref, outer_ref, frame, lanes)
        wide = low.reshape(-1, half).astype(jnp.float32)
        moved = [from_left(wide, at), wide, from_right(wide, at, cols_low - 1)]
        turned = {}
        for dc in range(3):
            view = moved[dc].astype(jnp.bfloat16).reshape(low.shape)
            for dr in range(3):
                turned[dr - 1, dc - 1] = view[dr : dr + rows_low].reshape(count, half).T
        for i in range(3):
            for j in range(3):
                lefts[3 * i + j] += [turned[(a + i - 1) // 2, (b + j - 1) // 2] for a, b in SIDES]
        acts.append(act_ref[frame, :, :, lanes].reshape(4 * count, half).T)
    pg = pg_ref[...].reshape(frames * 4 * count, chan)
    left = jnp.concatenate([jnp.concatenate(left, axis=1) for left in lefts], axis=0)
    out_ref[:9] = product(left, pg).reshape(9, half, chan)
    act = jnp.concatenate(acts, axis=1)
    for k in range(3):
        out_ref[9 + k] = product(act, ext_ref[k : k + frames].reshape(frames * 4 * count, chan))


def half_kernel(place_ref, low_ref, inner_ref, outer_ref, act_ref, pg_ref, ext_ref, out_ref, act_out, box_ref, sem):
    copy = pltpu.make_async_copy(act_ref, act_out, sem)
    copy.start()
    for frame in range(box_ref.shape[0]):
        box_ref[frame] = sum(ext_ref[frame, side].astype(jnp.float32) for side in range(4))
    half_sums(place_ref, low_ref, inner_ref, outer_ref, act_ref, pg_ref, ext_ref, out_ref)
    copy.wait()


def backward_kernel(place_ref, low_ref, inner_ref, outer_ref, act_ref, slope_ref, cot_ref, later_ref, turned_ref, sort_ref,
                    pg_ref, ext_ref, out_ref):
    frames, _, count, chan = cot_ref.shape
    ext_ref[:frames] = cot_ref[...]
    for n in range(2):
        sort_columns(later_ref.at[n], ext_ref.at[frames + n], low_ref.shape[2], sort_ref[...])
    for frame in range(frames):
        cots = [ext_ref[frame + k].reshape(4 * count, chan) for k in range(3)]
        act_grad = product(jnp.concatenate(cots, axis=1), turned_ref[...])
        slope = slope_ref[frame].reshape(4 * count, chan)
        pg_ref[frame] = (act_grad * slope).astype(jnp.bfloat16).reshape(4, count, chan)
    half_sums(place_ref, low_ref, inner_ref, outer_ref, act_ref, pg_ref, ext_ref, out_ref)


SCALAR = pl.BlockSpec(memory_space=pltpu.SMEM)
UNREAD = pl.BlockSpec(memory_space=pl.ANY)


def like(shape, dtype):
    return jax.ShapeDtypeStruct(shape, dtype)


TOKEN = like((8, 128), jnp.float32)


def cost(units, mib):
    return pl.CostEstimate(flops=units * 2 * 2048 * 256 * 256, bytes_accessed=mib * 2**20, transcendentals=0)


def in_hbm(array):
    return pltpu.with_memory_space_constraint(array, pltpu.HBM)


FULL = pl.BlockSpec(memory_space=pltpu.VMEM)


def first_kernel(place_ref, low_ref, cot_ref, inner_ref, outer_ref, later_ref, sems):
    last = low_ref.shape[1] - 1
    odd = place_ref[1]
    copies = [
        (low_ref.at[:, pl.ds(last * (1 - odd), 1)], inner_ref),
        (low_ref.at[:, pl.ds(last * odd, 1)], outer_ref),
    ]
    copies += [(cot_ref.at[0:2], later_ref)]
    copies = [pltpu.make_async_copy(a, b, sems.at[n]) for n, (a, b) in enumerate(copies)]
    for copy in copies:
        copy.start()
    for copy in copies:
        copy.wait()


def first_messages(place, low, cot):
    row = like(low[:, :1].shape, low.dtype)
    return pl.pallas_call(
        first_kernel,
        in_specs=[SCALAR, UNREAD, UNREAD],
        out_specs=[FULL] * 3,
        out_shape=[row, row, like(cot[:2].shape, cot.dtype)],
        scratch_shapes=[pltpu.SemaphoreType.DMA((3,))],
        compiler_params=grant(4),
        name="first_messages",
    )(place, in_hbm(low), in_hbm(cot))


def load_kernel(low_hbm, cot_hbm, ws_hbm, wt_hbm, sort_hbm,
                low_ref, ws_ref, sort_ref, turned_ref, side_ref, cot_ref, wide_ref, wt_ref, sems):
    frames, cols_low, chan = low_ref.shape[0], low_ref.shape[2], low_ref.shape[3]
    pairs = [(sort_hbm, wide_ref)] + [(cot_hbm.at[n], cot_ref.at[n]) for n in range(frames)]
    pairs += [(wt_hbm.at[k], wt_ref.at[k]) for k in range(3)] + [(low_hbm, low_ref)]
    pairs += [(ws_hbm.at[i, j], ws_ref.at[i, j]) for i in range(3) for j in range(3)]
    copies = [pltpu.make_async_copy(a, b, sems.at[n]) for n, (a, b) in enumerate(pairs)]
    for copy in copies:
        copy.start()
    copies[0].wait()
    sort_ref[...] = wide_ref[...].astype(jnp.bfloat16)
    for n in range(frames):
        copies[1 + n].wait()
        sort_columns(cot_ref.at[n], side_ref.at[n], cols_low, sort_ref[...])
    for k in range(3):
        copies[1 + frames + k].wait()
        turned_ref[k * chan : (k + 1) * chan] = wt_ref[k].T
    for copy in copies[4 + frames :]:
        copy.wait()


def load(low, cot, ws, wt, sort):
    frames, rows_low, cols_low, chan = low.shape
    order = like(sort.shape, jnp.bfloat16)
    shapes = [low, ws, order, like((3 * chan, chan), wt.dtype),
              like((frames, 4, rows_low * cols_low, chan), jnp.bfloat16)]
    return pl.pallas_call(
        load_kernel,
        in_specs=[UNREAD] * 5,
        out_specs=[FULL] * 5,
        out_shape=[like(a.shape, a.dtype) for a in shapes],
        scratch_shapes=[pltpu.VMEM(cot.shape, cot.dtype), pltpu.VMEM(sort.shape, sort.dtype), pltpu.VMEM(wt.shape, wt.dtype),
                        pltpu.SemaphoreType.DMA((frames + 14,))],
        compiler_params=grant(14),
        cost_estimate=cost(2, 4),
        name="load",
    )(*[in_hbm(a) for a in (low, cot, ws, wt, sort)])


def forward(place, low, inner, outer, ws):
    frames, rows_low, cols_low, chan = low.shape
    side = (frames, 4, rows_low * cols_low, chan)
    return pl.pallas_call(
        forward_kernel,
        in_specs=[SCALAR] + [FULL] * 4,
        out_specs=[FULL] * 2,
        out_shape=[like(side, jnp.bfloat16), like(side, jnp.float32)],
        compiler_params=grant(20),
        cost_estimate=cost(10, 8),
        name="forward",
    )(place, low, inner, outer, ws)


def edges_kernel(place_ref, low_ref, inner_ref, outer_ref, pg_ref, _, tall_ref, pg_inner, pg_outer):
    cols_low = low_ref.shape[2]
    first = low_ref.shape[0] - tall_ref.shape[0]
    for n in range(tall_ref.shape[0]):
        tall_ref[n] = tall(place_ref, low_ref, inner_ref, outer_ref, first + n)
    odd = place_ref[1] == 1
    top, bottom = pg_ref[:, :2, :cols_low, :], pg_ref[:, 2:, -cols_low:, :]
    pg_inner[...] = jnp.where(odd, top, bottom)
    pg_outer[...] = jnp.where(odd, bottom, top)


def edges(place, low, inner, outer, pg, before):
    frames, rows_low, cols_low, chan = low.shape
    full = pl.BlockSpec(memory_space=pltpu.VMEM)
    rows = like((frames, 2, cols_low, chan), jnp.bfloat16)
    return pl.pallas_call(
        edges_kernel,
        in_specs=[SCALAR, full, full, full, full, UNREAD],
        out_specs=[full] * 3,
        out_shape=[like((2, rows_low + 2, cols_low, chan), jnp.bfloat16), rows, rows],
        compiler_params=grant(8),
        name="edges",
    )(place, low, inner, outer, pg, before)


def backward(place, low, inner, outer, act, slope, cot, later, turned, sort):
    frames, _, count, chan = act.shape
    ext = (frames + 2,) + act.shape[1:]
    return pl.pallas_call(
        backward_kernel,
        in_specs=[SCALAR] + [FULL] * 9,
        out_specs=[FULL] * 3,
        out_shape=[like(act.shape, jnp.bfloat16), like(ext, jnp.bfloat16), like((12, chan // 2, chan), jnp.float32)],
        compiler_params=grant(24),
        cost_estimate=cost(15, 10),
        name="backward",
    )(place, low, inner, outer, act, slope, cot, later, turned, sort)


def half_grads(place, low, inner, outer, act, pg, ext):
    chan = low.shape[-1]
    return pl.pallas_call(
        half_kernel,
        in_specs=[SCALAR] + [FULL] * 6,
        out_specs=[FULL, HBM, FULL],
        out_shape=[like((12, chan // 2, chan), jnp.float32), pltpu.HBM(act.shape, act.dtype),
                   like((act.shape[0],) + act.shape[2:], jnp.float32)],
        scratch_shapes=[pltpu.SemaphoreType.DMA],
        compiler_params=grant(20),
        cost_estimate=cost(10, 6),
        name="half_grads",
    )(place, low, inner, outer, act, pg, ext)


HBM = pl.BlockSpec(memory_space=pltpu.HBM)


def split(value):
    high = value.astype(jnp.bfloat16)
    return high, (value - high.astype(jnp.float32)).astype(jnp.bfloat16)


def column_pair(first, second, j, at, last):
    if j == 0:
        return second + from_right(first, at, last)
    if j == 1:
        return first + second
    return first + from_left(second, at)


def input_kernel(pg_ref, box_ref, ws_ref, _, out_ref):
    frames, _, count, chan = pg_ref.shape
    cols_low = out_ref.shape[2]
    rows_low = count // cols_low
    at = column(count, cols_low, chan)
    turned = jnp.concatenate([ws_ref[i, j].T for j in range(3) for i in range(3)], axis=0)
    for frame in range(frames):
        own = [pg_ref[frame, side].astype(jnp.float32) for side in range(4)]
        zero = jnp.zeros((1, cols_low, chan), jnp.float32)
        parts = []
        for j in range(3):
            even = column_pair(own[0], own[1], j, at, cols_low - 1).reshape(rows_low, cols_low, chan)
            odd = column_pair(own[2], own[3], j, at, cols_low - 1).reshape(rows_low, cols_low, chan)
            below = jnp.concatenate([even[1:], zero], axis=0)
            above = jnp.concatenate([zero, odd[:-1]], axis=0)
            for value in (odd + below, even + odd, above + even):
                parts.append(jnp.concatenate(split(value.reshape(count, chan)), axis=0))
        sums = product(jnp.concatenate(parts, axis=1), turned)
        total = box_ref[frame] + (sums[:count] + sums[count:])
        out_ref[frame] = total.reshape(rows_low, cols_low, chan)


def input_own(pg, box, ws, before, low_shape):
    return pl.pallas_call(
        input_kernel,
        in_specs=[FULL] * 3 + [UNREAD],
        out_specs=FULL,
        out_shape=like(low_shape, jnp.float32),
        compiler_params=grant(16),
        cost_estimate=cost(6, 4),
        name="input_own",
    )(pg, box, ws, before)


def finish_kernel(place_ref, own_ref, ws_ref, inner_hbm, outer_hbm, edge_hbm, act_hbm, wt_hbm, sort_hbm, low_hbm, _,
                  section_ref, input_ref, token_ref,
                  inner_ref, outer_ref, edge_ref, act_ref, wt_ref, wide_ref, low_ref, earlier, held, input_held, sems):
    frames, rows_low, cols_low, chan = low_ref.shape
    group = rows_at_once(rows_low, cols_low)
    span, count = group * cols_low, rows_low * cols_low
    pairs = [(inner_hbm, inner_ref), (outer_hbm, outer_ref)]
    pairs += [(edge_hbm, edge_ref), (wt_hbm, wt_ref)]
    pairs += [(act_hbm.at[n], act_ref.at[n]) for n in range(frames)] + [(sort_hbm, wide_ref), (low_hbm, low_ref)]
    copies = [pltpu.make_async_copy(a, b, sems.at[n]) for n, (a, b) in enumerate(pairs)]
    for copy in copies:
        copy.start()
    token_ref[...] = jnp.zeros_like(token_ref)

    for copy in copies[:3]:
        copy.wait()
    odd_place = place_ref[1] == 1
    flat = (frames * cols_low, chan)
    at = column(flat[0], cols_low, chan)
    inner = [inner_ref[:, b].reshape(flat).astype(jnp.float32) for b in range(2)]
    outer = [outer_ref[:, b].reshape(flat).astype(jnp.float32) for b in range(2)]
    above = [jnp.where(odd_place, inner[b], outer[b]) for b in range(2)]
    below = [jnp.where(odd_place, outer[b], inner[b]) for b in range(2)]
    terms = []
    for (first, second), i in ((above, 2), (below, 0)):
        parts = [split(column_pair(first, second, j, at, cols_low - 1)) for j in range(3)]
        parts = jnp.concatenate([jnp.concatenate(part, axis=0) for part in parts], axis=1)
        sums = product(parts, jnp.concatenate([ws_ref[i, j].T for j in range(3)], axis=0))
        terms.append((sums[: flat[0]] + sums[flat[0] :]).reshape(frames, cols_low, chan))
    for row in range(rows_low):
        value = own_ref[:, row]
        if row == 0:
            value = value + terms[0]
        if row == rows_low - 1:
            value = value + terms[1]
        input_held[:, row] = value.astype(jnp.bfloat16)
    leaving = [pltpu.make_async_copy(input_held, input_ref, sems.at[len(copies)])]
    leaving[0].start()

    for side, pre in enumerate(spatial(edge_ref[...], ws_ref)):
        earlier[:, side] = (pre * jax.nn.sigmoid(pre)).astype(jnp.bfloat16).reshape(2, count, chan)
    for copy in copies[3:]:
        copy.wait()
    merge = wide_ref[...].T.astype(jnp.bfloat16)
    wt = wt_ref[...].reshape(3 * chan, chan)
    for frame in range(frames):
        acts = [act_ref[frame - k] if frame >= k else earlier[frame - k + 2] for k in range(3)]
        acts = jnp.concatenate([act.reshape(4 * count, chan) for act in acts], axis=1)
        low = low_ref[frame].reshape(1, count, chan).astype(jnp.float32)
        mixed = (product(acts, wt).reshape(4, count, chan) + low).astype(jnp.bfloat16)
        for n in range(rows_low // group):
            block = mixed[:, n * span : (n + 1) * span].reshape(4 * span, chan)
            block = product(merge, block).astype(jnp.bfloat16)
            held[frame, 2 * group * n : 2 * group * (n + 1)] = block.reshape(2 * group, 2 * cols_low, chan)
        leaving.append(pltpu.make_async_copy(held.at[frame], section_ref.at[frame], sems.at[len(copies) + 1 + frame]))
        leaving[-1].start()
    for copy in leaving:
        copy.wait()


def finish(place, own, ws, inner, outer, edge, act, wt, sort, low, before):
    frames, rows_low, cols_low, chan = low.shape
    out = (frames, 2 * rows_low, 2 * cols_low, chan)
    fetched = [inner, outer, edge, act, wt, sort, low]
    return pl.pallas_call(
        finish_kernel,
        in_specs=[SCALAR, FULL, FULL] + [HBM] * 7 + [UNREAD],
        out_specs=[HBM, HBM, FULL],
        out_shape=[like(out, jnp.bfloat16), like(low.shape, jnp.bfloat16), TOKEN],
        scratch_shapes=[pltpu.VMEM(a.shape, a.dtype) for a in fetched]
        + [pltpu.VMEM((2,) + act.shape[1:], act.dtype), pltpu.VMEM(out, jnp.bfloat16),
           pltpu.VMEM(low.shape, jnp.bfloat16), pltpu.SemaphoreType.DMA((7 + 2 * frames,))],
        compiler_params=grant(16),
        cost_estimate=cost(8, 4),
        name="finish",
    )(place, own, ws, inner, outer, edge, *[in_hbm(a) for a in (act, wt, sort, low)], before)


def put_kernel(place_ref, half_ref, *refs):
    spatial_ref, temporal_ref, wide, sems = refs[-4:]
    taps, half, _ = half_ref.shape
    to = pl.ds(pl.multiple_of(place_ref[0] * half, half), half)
    copies = []
    for tap in range(taps):
        wide[tap] = half_ref[tap].astype(jnp.float32)
        if tap < 9:
            target = spatial_ref.at[tap // 3, tap % 3, to]
        else:
            target = temporal_ref.at[tap - 9, to]
        copies.append(pltpu.make_async_copy(wide.at[tap], target, sems.at[tap]))
        copies[-1].start()
    for copy in copies:
        copy.wait()


def put(place, half, *done):
    chan = half.shape[-1]
    return pl.pallas_call(
        put_kernel,
        in_specs=[SCALAR, FULL] + [HBM] * len(done),
        out_specs=[HBM, HBM],
        out_shape=[like((3, 3, chan, chan), jnp.float32), like((3, chan, chan), jnp.float32)],
        input_output_aliases={2 + n: n for n in range(len(done))},
        scratch_shapes=[pltpu.VMEM((12, chan // 2, chan), jnp.float32), pltpu.SemaphoreType.DMA((12,))],
        compiler_params=grant(6),
        name="put",
    )(place, half, *done)


def add_kernel(mine_ref, theirs_ref, out_ref):
    out_ref[...] = (mine_ref[...] + theirs_ref[...]).astype(jnp.bfloat16)


def add_halves(mine, theirs):
    full = pl.BlockSpec(memory_space=pltpu.VMEM)
    return pl.pallas_call(
        add_kernel,
        in_specs=[full, full],
        out_specs=full,
        out_shape=like(mine.shape, jnp.bfloat16),
        compiler_params=grant(8),
        name="add_halves",
    )(mine, theirs)


def sum_kernel(got_ref, _, out_ref):
    total = got_ref[0].astype(jnp.float32)
    for n in range(1, got_ref.shape[0]):
        total = total + got_ref[n].astype(jnp.float32)
    out_ref[...] = total.astype(jnp.bfloat16)


def sum_parts(got, before):
    return pl.pallas_call(
        sum_kernel,
        in_specs=[FULL, UNREAD],
        out_specs=FULL,
        out_shape=like(got.shape[1:], jnp.bfloat16),
        compiler_params=grant(4),
        name="sum_parts",
    )(got, before)


def spread_kernel(own_ref, theirs_ref, *refs):
    total = (own_ref[...].astype(jnp.float32) + theirs_ref[...].astype(jnp.float32)).astype(jnp.bfloat16)
    for n in range(refs[-1].shape[0]):
        refs[-1][n] = total


def spread(own, theirs, parts, *before):
    return pl.pallas_call(
        spread_kernel,
        in_specs=[FULL, FULL] + [UNREAD] * len(before),
        out_specs=FULL,
        out_shape=like((parts,) + own.shape, jnp.bfloat16),
        compiler_params=grant(4),
        name="spread",
    )(own, theirs, *before)


def on_device(bits, low_frames, spatial_weight, temporal_weight, cotangent):
    low, cot = low_frames[0], cotangent[0]
    frames, rows_low, cols_low, chan = low.shape
    core = lax.axis_index(bits.core).astype(jnp.int32)
    odd = lax.axis_index(bits.axes["height"][-1]).astype(jnp.int32)
    mine, other = jnp.stack([core, odd]), jnp.stack([1 - core, odd])
    parts = 1 << len(bits.near)

    inner, outer, later = first_messages(mine, low, cot)
    later = bits.shift(later, "tm", -1)
    inner, outer = bits.pairs(inner, outer)
    order = jnp.asarray(side_order(rows_low, cols_low))
    low_in, ws, sort, turned, cot_side = load(low, cot, spatial_weight, temporal_weight, order)
    act, slope = forward(mine, low_in, inner, outer, ws)
    pg, ext, theirs = backward(
        other, low_in, inner, outer, act, slope, cot_side, later, turned, sort
    )
    theirs = bits.swap(theirs, bits.core)
    own, act, box = half_grads(mine, low_in, inner, outer, act, pg, ext)
    kept = add_halves(own, theirs)
    got = bits.exchange(kept.reshape(parts, -1, chan))
    edge, pg_inner, pg_outer = edges(mine, low_in, inner, outer, pg, kept)
    edge = bits.shift(edge, "tm", 1)
    pg_inner, pg_outer = bits.pairs(pg_inner, pg_outer)
    own_part = input_own(pg, box, ws, kept, low.shape)
    total, far = bits.far_sums(sum_parts(got, own_part))
    section_out, input_grad, done = finish(
        mine, own_part, ws, pg_inner, pg_outer, edge, act, temporal_weight, order, low, total
    )
    totals = spread(total, far, parts, done)
    half = bits.exchange(totals).reshape(kept.shape)
    theirs = bits.swap(half, bits.core)
    spatial_grad, temporal_grad = put(other, theirs, *put(mine, half))
    return section_out[None], input_grad[None], spatial_grad, temporal_grad


def solution(mesh):
    bits = Bits(mesh)
    block = P(*(bits.axes[name] for name in ("dp", "tm", "height")), None, None)
    return jax.shard_map(
        functools.partial(on_device, bits),
        mesh=bits.mesh,
        in_specs=(block, P(), P(), block),
        out_specs=(block, block, P(), P()),
        check_vma=False,
    )
```

```python
import functools

import jax
import jax.numpy as jnp
import numpy as np
from jax import lax
from jax.experimental import pallas as pl
from jax.experimental.pallas import tpu as pltpu
from jax.sharding import Mesh
from jax.sharding import PartitionSpec as P


class Bits:
    def __init__(self, mesh):
        self.axes = {}
        for name in mesh.axis_names:
            count = mesh.shape[name].bit_length() - 1
            self.axes[name] = tuple(f"{name}{bit}" for bit in reversed(range(count)))
        names = [bit for bits in self.axes.values() for bit in bits]
        self.mesh = Mesh(mesh.devices.reshape([2] * len(names)), tuple(names))
        self.core = next((n for n in names if self.same_chip(n)), self.axes["tm"][-1])
        others = [[b for b in reversed(bits) if b != self.core] for bits in self.axes.values()]
        turns = [bits[turn] for turn in range(len(names)) for bits in others if turn < len(bits)]
        self.near = [n for n in names if n in turns[:3]]
        self.far = turns[3:]

    def same_chip(self, name):
        at = [1 if n == name else 0 for n in self.mesh.axis_names]
        here = self.mesh.devices[tuple([0] * len(at))]
        there = self.mesh.devices[tuple(at)]
        return tuple(getattr(here, "coords", (0,))) == tuple(getattr(there, "coords", (1,)))

    def swap(self, block, axis):
        return lax.ppermute(block, axis, [(0, 1), (1, 0)])

    def shift(self, block, name, distance):
        axes = self.axes[name]
        devices = range(1 << len(axes))
        route = [(i - distance, i) for i in devices if i - distance in devices]
        return lax.ppermute(block, axes, route)

    def exchange(self, parts):
        return lax.all_to_all(parts, tuple(self.near), 0, 0, tiled=True)

    def pairs(self, inner, outer):
        axes = self.axes["height"]
        low = range(1, (1 << len(axes)) - 1, 2)
        route = [(i, i + 1) for i in low] + [(i + 1, i) for i in low]
        outer = lax.ppermute(outer, axes, route)
        return self.swap(inner, axes[-1]), outer

    def far_sums(self, total):
        for axis in self.far[:-1]:
            total = total.astype(jnp.float32) + self.swap(total, axis).astype(jnp.float32)
            total = lax.reduce_precision(total, 8, 7).astype(jnp.bfloat16)
        return total, self.swap(total, self.far[-1])


SIDES = ((0, 0), (0, 1), (1, 0), (1, 1))


def grant(mib):
    return pltpu.CompilerParams(vmem_limit_bytes=mib * 2**20)


def product(left, right):
    return jnp.dot(left, right, preferred_element_type=jnp.float32)


def product_nt(left, right):
    return lax.dot_general(left, right, (((1,), (1,)), ((), ())), preferred_element_type=jnp.float32)


def rows_at_once(rows_low, cols_low):
    return max(n for n in (1, 2, 4, 8) if rows_low % n == 0 and (n == 1 or 4 * n * cols_low <= 256))


def side_order(rows_low, cols_low):
    count = rows_at_once(rows_low, cols_low)
    size = 4 * count * cols_low
    at = np.arange(size).reshape(count, 2, cols_low, 2).transpose(1, 3, 0, 2).reshape(-1)
    return (at[:, None] == np.arange(size)[None, :]).astype(np.float32)


def column(rows, cols_low, chan):
    return lax.broadcasted_iota(jnp.int32, (rows // cols_low, cols_low, chan), 1).reshape(rows, chan)


def from_left(x, at):
    return jnp.where(at == 0, 0.0, pltpu.roll(x, 1, 0))


def from_right(x, at, last):
    return jnp.where(at == last, 0.0, pltpu.roll(x, x.shape[0] - 1, 0))


def sort_columns(source, target, cols_low, order):
    rows_low, chan = source.shape[0] // 2, source.shape[2]
    group = rows_at_once(rows_low, cols_low)
    span = group * cols_low
    for n in range(rows_low // group):
        block = source[2 * group * n : 2 * group * (n + 1)].reshape(4 * span, chan)
        block = product(order, block).astype(jnp.bfloat16).reshape(4, span, chan)
        target[:, n * span : (n + 1) * span, :] = block


def tall(place_ref, low_ref, inner_ref, outer_ref, frame, lanes=slice(None)):
    odd = place_ref[1] == 1
    inner, outer = inner_ref[frame, :, :, lanes], outer_ref[frame, :, :, lanes]
    up, down = jnp.where(odd, inner, outer), jnp.where(odd, outer, inner)
    return jnp.concatenate([up, low_ref[frame, :, :, lanes], down], axis=0)


def spatial(low, ws_ref):
    frames, rows_tall, cols_low, chan = low.shape
    rows_low = rows_tall - 2
    count = frames * rows_low * cols_low
    flat = low.reshape(-1, chan)
    rows = [[], []]
    for j in range(3):
        taps = [product(flat, ws_ref[i, j]).reshape(low.shape) for i in range(3)]
        even = taps[0][:, :rows_low] + (taps[1] + taps[2])[:, 1 : rows_low + 1]
        odd = (taps[0] + taps[1])[:, 1 : rows_low + 1] + taps[2][:, 2:]
        rows[0].append(even.reshape(count, chan))
        rows[1].append(odd.reshape(count, chan))
    at = column(count, cols_low, chan)
    for first, second, third in rows:
        yield from_left(first, at) + (second + third)
        yield (first + second) + from_right(third, at, cols_low - 1)


def forward_kernel(place_ref, low_ref, inner_ref, outer_ref, ws_ref, act_ref, slope_ref):
    frames, rows_low, cols_low, chan = low_ref.shape
    shape = (frames, rows_low * cols_low, chan)
    low = jnp.stack([tall(place_ref, low_ref, inner_ref, outer_ref, frame) for frame in range(frames)])
    for side, pre in enumerate(spatial(low, ws_ref)):
        sig = jax.nn.sigmoid(pre)
        act_ref[:, side] = (pre * sig).astype(jnp.bfloat16).reshape(shape)
        slope_ref[:, side] = (sig * (1.0 + pre * (1.0 - sig))).reshape(shape)


def half_sums(place_ref, low_ref, inner_ref, outer_ref, act_ref, pg_ref, ext_ref, out_ref):
    frames, rows_low, cols_low, chan = low_ref.shape
    count, half = rows_low * cols_low, chan // 2
    lanes = pl.ds(pl.multiple_of(place_ref[0] * half, half), half)
    lefts = [[] for _ in range(9)]
    acts = []
    at = column((rows_low + 2) * cols_low, cols_low, half)
    for frame in range(frames):
        low = tall(place_ref, low_ref, inner_ref, outer_ref, frame, lanes)
        wide = low.reshape(-1, half).astype(jnp.float32)
        moved = [from_left(wide, at), wide, from_right(wide, at, cols_low - 1)]
        turned = {}
        for dc in range(3):
            view = moved[dc].astype(jnp.bfloat16).reshape(low.shape)
            for dr in range(3):
                turned[dr - 1, dc - 1] = view[dr : dr + rows_low].reshape(count, half).T
        for i in range(3):
            for j in range(3):
                lefts[3 * i + j] += [turned[(a + i - 1) // 2, (b + j - 1) // 2] for a, b in SIDES]
        acts.append(act_ref[frame, :, :, lanes].reshape(4 * count, half).T)
    pg = pg_ref[...].reshape(frames * 4 * count, chan)
    left = jnp.concatenate([jnp.concatenate(left, axis=1) for left in lefts], axis=0)
    out_ref[:9] = product(left, pg).reshape(9, half, chan)
    act = jnp.concatenate(acts, axis=1)
    for k in range(3):
        out_ref[9 + k] = product(act, ext_ref[k : k + frames].reshape(frames * 4 * count, chan))


def half_kernel(place_ref, low_ref, inner_ref, outer_ref, act_ref, pg_ref, ext_ref, out_ref, act_out, box_ref, sem):
    copy = pltpu.make_async_copy(act_ref, act_out, sem)
    copy.start()
    for frame in range(box_ref.shape[0]):
        box_ref[frame] = sum(ext_ref[frame, side].astype(jnp.float32) for side in range(4))
    half_sums(place_ref, low_ref, inner_ref, outer_ref, act_ref, pg_ref, ext_ref, out_ref)
    copy.wait()


def backward_kernel(place_ref, low_ref, inner_ref, outer_ref, act_ref, slope_ref, cot_ref, later_ref, turned_ref, sort_ref,
                    pg_ref, ext_ref, out_ref):
    frames, _, count, chan = cot_ref.shape
    ext_ref[:frames] = cot_ref[...]
    for n in range(2):
        sort_columns(later_ref.at[n], ext_ref.at[frames + n], low_ref.shape[2], sort_ref[...])
    for frame in range(frames):
        cots = [ext_ref[frame + k].reshape(4 * count, chan) for k in range(3)]
        act_grad = product(jnp.concatenate(cots, axis=1), turned_ref[...])
        slope = slope_ref[frame].reshape(4 * count, chan)
        pg_ref[frame] = (act_grad * slope).astype(jnp.bfloat16).reshape(4, count, chan)
    half_sums(place_ref, low_ref, inner_ref, outer_ref, act_ref, pg_ref, ext_ref, out_ref)


SCALAR = pl.BlockSpec(memory_space=pltpu.SMEM)
UNREAD = pl.BlockSpec(memory_space=pl.ANY)


def like(shape, dtype):
    return jax.ShapeDtypeStruct(shape, dtype)


TOKEN = like((8, 128), jnp.float32)


def cost(units, mib):
    return pl.CostEstimate(flops=units * 2 * 2048 * 256 * 256, bytes_accessed=mib * 2**20, transcendentals=0)


def in_hbm(array):
    return pltpu.with_memory_space_constraint(array, pltpu.HBM)


FULL = pl.BlockSpec(memory_space=pltpu.VMEM)


def first_kernel(place_ref, low_ref, cot_ref, inner_ref, outer_ref, later_ref, sems):
    last = low_ref.shape[1] - 1
    odd = place_ref[1]
    copies = [
        (low_ref.at[:, pl.ds(last * (1 - odd), 1)], inner_ref),
        (low_ref.at[:, pl.ds(last * odd, 1)], outer_ref),
    ]
    copies += [(cot_ref.at[0:2], later_ref)]
    copies = [pltpu.make_async_copy(a, b, sems.at[n]) for n, (a, b) in enumerate(copies)]
    for copy in copies:
        copy.start()
    for copy in copies:
        copy.wait()


def first_messages(place, low, cot):
    row = like(low[:, :1].shape, low.dtype)
    return pl.pallas_call(
        first_kernel,
        in_specs=[SCALAR, UNREAD, UNREAD],
        out_specs=[FULL] * 3,
        out_shape=[row, row, like(cot[:2].shape, cot.dtype)],
        scratch_shapes=[pltpu.SemaphoreType.DMA((3,))],
        compiler_params=grant(4),
        name="first_messages",
    )(place, in_hbm(low), in_hbm(cot))


def load_kernel(low_hbm, cot_hbm, ws_hbm, wt_hbm, sort_hbm,
                low_ref, ws_ref, sort_ref, turned_ref, side_ref, cot_ref, wide_ref, wt_ref, sems):
    frames, cols_low, chan = low_ref.shape[0], low_ref.shape[2], low_ref.shape[3]
    pairs = [(sort_hbm, wide_ref)] + [(cot_hbm.at[n], cot_ref.at[n]) for n in range(frames)]
    pairs += [(wt_hbm.at[k], wt_ref.at[k]) for k in range(3)] + [(low_hbm, low_ref)]
    pairs += [(ws_hbm.at[i, j], ws_ref.at[i, j]) for i in range(3) for j in range(3)]
    copies = [pltpu.make_async_copy(a, b, sems.at[n]) for n, (a, b) in enumerate(pairs)]
    for copy in copies:
        copy.start()
    copies[0].wait()
    sort_ref[...] = wide_ref[...].astype(jnp.bfloat16)
    for n in range(frames):
        copies[1 + n].wait()
        sort_columns(cot_ref.at[n], side_ref.at[n], cols_low, sort_ref[...])
    for k in range(3):
        copies[1 + frames + k].wait()
        turned_ref[k * chan : (k + 1) * chan] = wt_ref[k].T
    for copy in copies[4 + frames :]:
        copy.wait()


def load(low, cot, ws, wt, sort):
    frames, rows_low, cols_low, chan = low.shape
    order = like(sort.shape, jnp.bfloat16)
    shapes = [low, ws, order, like((3 * chan, chan), wt.dtype),
              like((frames, 4, rows_low * cols_low, chan), jnp.bfloat16)]
    return pl.pallas_call(
        load_kernel,
        in_specs=[UNREAD] * 5,
        out_specs=[FULL] * 5,
        out_shape=[like(a.shape, a.dtype) for a in shapes],
        scratch_shapes=[pltpu.VMEM(cot.shape, cot.dtype), pltpu.VMEM(sort.shape, sort.dtype), pltpu.VMEM(wt.shape, wt.dtype),
                        pltpu.SemaphoreType.DMA((frames + 14,))],
        compiler_params=grant(14),
        cost_estimate=cost(2, 4),
        name="load",
    )(*[in_hbm(a) for a in (low, cot, ws, wt, sort)])


def forward(place, low, inner, outer, ws):
    frames, rows_low, cols_low, chan = low.shape
    side = (frames, 4, rows_low * cols_low, chan)
    return pl.pallas_call(
        forward_kernel,
        in_specs=[SCALAR] + [FULL] * 4,
        out_specs=[FULL] * 2,
        out_shape=[like(side, jnp.bfloat16), like(side, jnp.float32)],
        compiler_params=grant(20),
        cost_estimate=cost(10, 8),
        name="forward",
    )(place, low, inner, outer, ws)


def edges_kernel(place_ref, low_ref, inner_ref, outer_ref, pg_ref, _, tall_ref, pg_inner, pg_outer):
    cols_low = low_ref.shape[2]
    first = low_ref.shape[0] - tall_ref.shape[0]
    for n in range(tall_ref.shape[0]):
        tall_ref[n] = tall(place_ref, low_ref, inner_ref, outer_ref, first + n)
    odd = place_ref[1] == 1
    top, bottom = pg_ref[:, :2, :cols_low, :], pg_ref[:, 2:, -cols_low:, :]
    pg_inner[...] = jnp.where(odd, top, bottom)
    pg_outer[...] = jnp.where(odd, bottom, top)


def edges(place, low, inner, outer, pg, before):
    frames, rows_low, cols_low, chan = low.shape
    full = pl.BlockSpec(memory_space=pltpu.VMEM)
    rows = like((frames, 2, cols_low, chan), jnp.bfloat16)
    return pl.pallas_call(
        edges_kernel,
        in_specs=[SCALAR, full, full, full, full, UNREAD],
        out_specs=[full] * 3,
        out_shape=[like((2, rows_low + 2, cols_low, chan), jnp.bfloat16), rows, rows],
        compiler_params=grant(8),
        name="edges",
    )(place, low, inner, outer, pg, before)


def backward(place, low, inner, outer, act, slope, cot, later, turned, sort):
    frames, _, count, chan = act.shape
    ext = (frames + 2,) + act.shape[1:]
    return pl.pallas_call(
        backward_kernel,
        in_specs=[SCALAR] + [FULL] * 9,
        out_specs=[FULL] * 3,
        out_shape=[like(act.shape, jnp.bfloat16), like(ext, jnp.bfloat16), like((12, chan // 2, chan), jnp.float32)],
        compiler_params=grant(24),
        cost_estimate=cost(15, 10),
        name="backward",
    )(place, low, inner, outer, act, slope, cot, later, turned, sort)


def half_grads(place, low, inner, outer, act, pg, ext):
    chan = low.shape[-1]
    return pl.pallas_call(
        half_kernel,
        in_specs=[SCALAR] + [FULL] * 6,
        out_specs=[FULL, HBM, FULL],
        out_shape=[like((12, chan // 2, chan), jnp.float32), pltpu.HBM(act.shape, act.dtype),
                   like((act.shape[0],) + act.shape[2:], jnp.float32)],
        scratch_shapes=[pltpu.SemaphoreType.DMA],
        compiler_params=grant(20),
        cost_estimate=cost(10, 6),
        name="half_grads",
    )(place, low, inner, outer, act, pg, ext)


HBM = pl.BlockSpec(memory_space=pltpu.HBM)


def split(value):
    high = value.astype(jnp.bfloat16)
    return high, (value - high.astype(jnp.float32)).astype(jnp.bfloat16)


def column_pair(first, second, j, at, last):
    if j == 0:
        return second + from_right(first, at, last)
    if j == 1:
        return first + second
    return first + from_left(second, at)


def input_kernel(pg_ref, box_ref, ws_ref, _, out_ref):
    frames, _, count, chan = pg_ref.shape
    cols_low = out_ref.shape[2]
    rows_low = count // cols_low
    at = column(count, cols_low, chan)
    turned = jnp.concatenate([ws_ref[i, j].T for j in range(3) for i in range(3)], axis=0)
    for frame in range(frames):
        own = [pg_ref[frame, side].astype(jnp.float32) for side in range(4)]
        zero = jnp.zeros((1, cols_low, chan), jnp.float32)
        parts = []
        for j in range(3):
            even = column_pair(own[0], own[1], j, at, cols_low - 1).reshape(rows_low, cols_low, chan)
            odd = column_pair(own[2], own[3], j, at, cols_low - 1).reshape(rows_low, cols_low, chan)
            below = jnp.concatenate([even[1:], zero], axis=0)
            above = jnp.concatenate([zero, odd[:-1]], axis=0)
            for value in (odd + below, even + odd, above + even):
                parts.append(jnp.concatenate(split(value.reshape(count, chan)), axis=0))
        sums = product(jnp.concatenate(parts, axis=1), turned)
        total = box_ref[frame] + (sums[:count] + sums[count:])
        out_ref[frame] = total.reshape(rows_low, cols_low, chan)


def input_own(pg, box, ws, before, low_shape):
    return pl.pallas_call(
        input_kernel,
        in_specs=[FULL] * 3 + [UNREAD],
        out_specs=FULL,
        out_shape=like(low_shape, jnp.float32),
        compiler_params=grant(16),
        cost_estimate=cost(6, 4),
        name="input_own",
    )(pg, box, ws, before)


def finish_kernel(place_ref, own_ref, ws_ref, inner_hbm, outer_hbm, edge_hbm, act_hbm, wt_hbm, sort_hbm, low_hbm, _,
                  section_ref, input_ref, token_ref,
                  inner_ref, outer_ref, edge_ref, act_ref, wt_ref, wide_ref, low_ref, earlier, held, input_held, sems):
    frames, rows_low, cols_low, chan = low_ref.shape
    group = rows_at_once(rows_low, cols_low)
    span, count = group * cols_low, rows_low * cols_low
    pairs = [(inner_hbm, inner_ref), (outer_hbm, outer_ref)]
    pairs += [(edge_hbm, edge_ref), (wt_hbm, wt_ref)]
    pairs += [(act_hbm.at[n], act_ref.at[n]) for n in range(frames)] + [(sort_hbm, wide_ref), (low_hbm, low_ref)]
    copies = [pltpu.make_async_copy(a, b, sems.at[n]) for n, (a, b) in enumerate(pairs)]
    for copy in copies:
        copy.start()
    token_ref[...] = jnp.zeros_like(token_ref)

    for copy in copies[:3]:
        copy.wait()
    odd_place = place_ref[1] == 1
    flat = (frames * cols_low, chan)
    at = column(flat[0], cols_low, chan)
    inner = [inner_ref[:, b].reshape(flat).astype(jnp.float32) for b in range(2)]
    outer = [outer_ref[:, b].reshape(flat).astype(jnp.float32) for b in range(2)]
    above = [jnp.where(odd_place, inner[b], outer[b]) for b in range(2)]
    below = [jnp.where(odd_place, outer[b], inner[b]) for b in range(2)]
    terms = []
    for (first, second), i in ((above, 2), (below, 0)):
        parts = [split(column_pair(first, second, j, at, cols_low - 1)) for j in range(3)]
        parts = jnp.concatenate([jnp.concatenate(part, axis=0) for part in parts], axis=1)
        sums = product(parts, jnp.concatenate([ws_ref[i, j].T for j in range(3)], axis=0))
        terms.append((sums[: flat[0]] + sums[flat[0] :]).reshape(frames, cols_low, chan))
    for row in range(rows_low):
        value = own_ref[:, row]
        if row == 0:
            value = value + terms[0]
        if row == rows_low - 1:
            value = value + terms[1]
        input_held[:, row] = value.astype(jnp.bfloat16)
    for side, pre in enumerate(spatial(edge_ref[...], ws_ref)):
        earlier[:, side] = (pre * jax.nn.sigmoid(pre)).astype(jnp.bfloat16).reshape(2, count, chan)
    leaving = [pltpu.make_async_copy(input_held, input_ref, sems.at[len(copies)])]
    leaving[0].start()
    for copy in copies[3:]:
        copy.wait()
    merge = wide_ref[...].T.astype(jnp.bfloat16)
    wt = wt_ref[...].reshape(3 * chan, chan)
    for frame in range(frames):
        acts = [act_ref[frame - k] if frame >= k else earlier[frame - k + 2] for k in range(3)]
        acts = jnp.concatenate([act.reshape(4 * count, chan) for act in acts], axis=1)
        low = low_ref[frame].reshape(1, count, chan).astype(jnp.float32)
        mixed = (product(acts, wt).reshape(4, count, chan) + low).astype(jnp.bfloat16)
        for n in range(rows_low // group):
            block = mixed[:, n * span : (n + 1) * span].reshape(4 * span, chan)
            block = product(merge, block).astype(jnp.bfloat16)
            held[frame, 2 * group * n : 2 * group * (n + 1)] = block.reshape(2 * group, 2 * cols_low, chan)
        leaving.append(pltpu.make_async_copy(held.at[frame], section_ref.at[frame], sems.at[len(copies) + 1 + frame]))
        leaving[-1].start()
    for copy in leaving:
        copy.wait()


def finish(place, own, ws, inner, outer, edge, act, wt, sort, low, before):
    frames, rows_low, cols_low, chan = low.shape
    out = (frames, 2 * rows_low, 2 * cols_low, chan)
    fetched = [inner, outer, edge, act, wt, sort, low]
    return pl.pallas_call(
        finish_kernel,
        in_specs=[SCALAR, FULL, FULL] + [HBM] * 7 + [UNREAD],
        out_specs=[HBM, HBM, FULL],
        out_shape=[like(out, jnp.bfloat16), like(low.shape, jnp.bfloat16), TOKEN],
        scratch_shapes=[pltpu.VMEM(a.shape, a.dtype) for a in fetched]
        + [pltpu.VMEM((2,) + act.shape[1:], act.dtype), pltpu.VMEM(out, jnp.bfloat16),
           pltpu.VMEM(low.shape, jnp.bfloat16), pltpu.SemaphoreType.DMA((7 + 2 * frames,))],
        compiler_params=grant(16),
        cost_estimate=cost(8, 4),
        name="finish",
    )(place, own, ws, inner, outer, edge, *[in_hbm(a) for a in (act, wt, sort, low)], before)


def put_kernel(place_ref, half_ref, *refs):
    spatial_ref, temporal_ref, wide, sems = refs[-4:]
    taps, half, _ = half_ref.shape
    to = pl.ds(pl.multiple_of(place_ref[0] * half, half), half)
    copies = []
    for tap in range(taps):
        wide[tap] = half_ref[tap].astype(jnp.float32)
        if tap < 9:
            target = spatial_ref.at[tap // 3, tap % 3, to]
        else:
            target = temporal_ref.at[tap - 9, to]
        copies.append(pltpu.make_async_copy(wide.at[tap], target, sems.at[tap]))
        copies[-1].start()
    for copy in copies:
        copy.wait()


def put(place, half, *done):
    chan = half.shape[-1]
    return pl.pallas_call(
        put_kernel,
        in_specs=[SCALAR, FULL] + [HBM] * len(done),
        out_specs=[HBM, HBM],
        out_shape=[like((3, 3, chan, chan), jnp.float32), like((3, chan, chan), jnp.float32)],
        input_output_aliases={2 + n: n for n in range(len(done))},
        scratch_shapes=[pltpu.VMEM((12, chan // 2, chan), jnp.float32), pltpu.SemaphoreType.DMA((12,))],
        compiler_params=grant(6),
        name="put",
    )(place, half, *done)


def add_kernel(mine_ref, theirs_ref, out_ref):
    out_ref[...] = (mine_ref[...] + theirs_ref[...]).astype(jnp.bfloat16)


def add_halves(mine, theirs):
    full = pl.BlockSpec(memory_space=pltpu.VMEM)
    return pl.pallas_call(
        add_kernel,
        in_specs=[full, full],
        out_specs=full,
        out_shape=like(mine.shape, jnp.bfloat16),
        compiler_params=grant(8),
        name="add_halves",
    )(mine, theirs)


def sum_kernel(got_ref, _, out_ref):
    total = got_ref[0].astype(jnp.float32)
    for n in range(1, got_ref.shape[0]):
        total = total + got_ref[n].astype(jnp.float32)
    out_ref[...] = total.astype(jnp.bfloat16)


def sum_parts(got, before):
    return pl.pallas_call(
        sum_kernel,
        in_specs=[FULL, UNREAD],
        out_specs=FULL,
        out_shape=like(got.shape[1:], jnp.bfloat16),
        compiler_params=grant(4),
        name="sum_parts",
    )(got, before)


def spread_kernel(own_ref, theirs_ref, *refs):
    total = (own_ref[...].astype(jnp.float32) + theirs_ref[...].astype(jnp.float32)).astype(jnp.bfloat16)
    for n in range(refs[-1].shape[0]):
        refs[-1][n] = total


def spread(own, theirs, parts, *before):
    return pl.pallas_call(
        spread_kernel,
        in_specs=[FULL, FULL] + [UNREAD] * len(before),
        out_specs=FULL,
        out_shape=like((parts,) + own.shape, jnp.bfloat16),
        compiler_params=grant(4),
        name="spread",
    )(own, theirs, *before)


def on_device(bits, low_frames, spatial_weight, temporal_weight, cotangent):
    low, cot = low_frames[0], cotangent[0]
    frames, rows_low, cols_low, chan = low.shape
    core = lax.axis_index(bits.core).astype(jnp.int32)
    odd = lax.axis_index(bits.axes["height"][-1]).astype(jnp.int32)
    mine, other = jnp.stack([core, odd]), jnp.stack([1 - core, odd])
    parts = 1 << len(bits.near)

    inner, outer, later = first_messages(mine, low, cot)
    later = bits.shift(later, "tm", -1)
    inner, outer = bits.pairs(inner, outer)
    order = jnp.asarray(side_order(rows_low, cols_low))
    low_in, ws, sort, turned, cot_side = load(low, cot, spatial_weight, temporal_weight, order)
    act, slope = forward(mine, low_in, inner, outer, ws)
    pg, ext, theirs = backward(
        other, low_in, inner, outer, act, slope, cot_side, later, turned, sort
    )
    theirs = bits.swap(theirs, bits.core)
    own, act, box = half_grads(mine, low_in, inner, outer, act, pg, ext)
    kept = add_halves(own, theirs)
    got = bits.exchange(kept.reshape(parts, -1, chan))
    edge, pg_inner, pg_outer = edges(mine, low_in, inner, outer, pg, kept)
    edge = bits.shift(edge, "tm", 1)
    pg_inner, pg_outer = bits.pairs(pg_inner, pg_outer)
    own_part = input_own(pg, box, ws, kept, low.shape)
    total, far = bits.far_sums(sum_parts(got, own_part))
    section_out, input_grad, done = finish(
        mine, own_part, ws, pg_inner, pg_outer, edge, act, temporal_weight, order, low, total
    )
    totals = spread(total, far, parts, done)
    half = bits.exchange(totals).reshape(kept.shape)
    theirs = bits.swap(half, bits.core)
    spatial_grad, temporal_grad = put(other, theirs, *put(mine, half))
    return section_out[None], input_grad[None], spatial_grad, temporal_grad


def solution(mesh):
    bits = Bits(mesh)
    block = P(*(bits.axes[name] for name in ("dp", "tm", "height")), None, None)
    return jax.shard_map(
        functools.partial(on_device, bits),
        mesh=bits.mesh,
        in_specs=(block, P(), P(), block),
        out_specs=(block, block, P(), P()),
        check_vma=False,
    )
```
